32 devices in a mesh: ctx: 8 (over z, core), fsdp: 4 (over y, x).
Axes of the slice: x: 2, y: 2, z: 4, core: 2. Of those that a mesh axis runs over, the one named last changes fastest.
Arguments:
- tokens: bfloat16 [4, 2048, 1600], P('fsdp', 'ctx'), may hold values from -6 to 6
- block_order: int32 [4, 16], P('fsdp'), may hold values from 0 to 15, as said below
- w_attn: bfloat16 [1600, 4800], P('fsdp'), may hold values from -0.21875 to 0.21875
- w_proj: bfloat16 [1600, 1600], P('fsdp'), may hold values from -0.4375 to 0.4375
- w_fc: bfloat16 [1600, 6400], P('fsdp'), may hold values from -0.15625 to 0.15625
- w_out: bfloat16 [6400, 1600], P('fsdp'), may hold values from -0.15625 to 0.15625
- norm_gains: bfloat16 [2, 1600], P(None, 'fsdp'), may hold values from 0.5 to 1.5
- biases: bfloat16 [6, 1600], P(None, 'fsdp'), may hold values from -4 to 4
- fc_bias: bfloat16 [6400], P('fsdp'), may hold values from -4 to 4
- cotangent: bfloat16 [4, 2048, 1600], P('fsdp', 'ctx'), may hold values from -6 to 6
Outputs:
- layer_out: bfloat16 [4, 2048, 1600], P('fsdp', 'ctx')
- tokens_grad: bfloat16 [4, 2048, 1600], P('fsdp', 'ctx')
- w_attn_grad: float32 [1600, 4800], P('fsdp')
- w_proj_grad: float32 [1600, 1600], P('fsdp')
- w_fc_grad: float32 [1600, 6400], P('fsdp')
- w_out_grad: float32 [6400, 1600], P('fsdp')
- gains_grad: float32 [2, 1600], P(None, 'fsdp')
- biases_grad: float32 [6, 1600], P(None, 'fsdp')
- fc_bias_grad: float32 [6400], P('fsdp')
The draws below stay inside these ranges and needn't reach their ends.
Inputs may be any that keep to these rules, and one draw needn't show every extreme that they name: `block_order`: each row is an ordering of the blocks 0 to 15 in which entries 2c and 2c + 1 are blocks p and 15 - p for some p, in either order.
All inputs are finite; a program needn't handle non-finite values.
Results may differ from the reference program's by a relative error of at most 0.02.
Values may be sent and summed in bfloat16 or wider, within the bound.
A program may use at most 384 MiB of HBM per device.

```python
import jax
import jax.numpy as jnp
from jax import lax

HEADS = 25
HEAD_DIM = 64
FF = 6400
D = 1600
SEQ_LEN = 2048
SEQS = 4
N_CTX = 8


def draw_block_order(key, part):
    key = jax.random.fold_in(key, 7)
    row_keys = jax.random.split(key, SEQS)

    def one_row(row_key):
        pair_key, flip_key = jax.random.split(row_key)
        pair_ids = jax.random.permutation(pair_key, N_CTX)
        flip_bits = jax.random.randint(flip_key, (N_CTX,), 0, 2)
        far_ids = 2 * N_CTX - 1 - pair_ids
        first_ids = jnp.where(flip_bits == 1, far_ids, pair_ids)
        second_ids = jnp.where(flip_bits == 1, pair_ids, far_ids)
        return jnp.stack([first_ids, second_ids], axis=1).reshape(2 * N_CTX).astype(jnp.int32)
    return jax.vmap(one_row)(row_keys)


def block_scale(key, dims, cuts, low, top_value):
    def one(position, blocks):
        heights = jax.random.uniform(jax.random.fold_in(jax.random.fold_in(key, 6), position), (blocks,), jnp.float32, low / len(cuts), top_value / len(cuts))
        return jnp.repeat(jnp.exp(heights), dims[position] // blocks).reshape((-1,) + (1,) * (len(dims) - position - 1))

    loudness = one(*cuts[0])
    for cut in cuts[1:]:
        loudness = loudness * one(*cut)
    return loudness


def bell_draw(own_key, extent, spread, limit, shards=(), kind=jnp.bfloat16):
    values = jax.random.normal(own_key, extent, jnp.float32) * spread
    if len(shards) > 0:
        values = block_scale(own_key, extent, shards, -0.22, 0.18) * values
    return jnp.clip(values, min=-limit, max=limit).astype(kind)


def setup_inputs(seed: int = 0) -> dict:
    seeds = jax.random.split(jax.random.key(seed), 11)
    return {
        "tokens": bell_draw(seeds[0], (SEQS, SEQ_LEN, D), 1.0, 6.0, ((0, 4), (1, 8))),
        "block_order": draw_block_order(jax.random.fold_in(seeds[10], 71), 0),
        "w_attn": bell_draw(seeds[2], (D, 3 * D), (D // 2) ** -0.5, 0.21875, ((0, 4),)),
        "w_proj": bell_draw(seeds[3], (D, D), (D // 8) ** -0.5, 0.4375, ((0, 4),)),
        "w_fc": bell_draw(seeds[4], (D, FF), D ** -0.5, 0.15625, ((0, 4),)),
        "w_out": bell_draw(seeds[5], (FF, D), (FF // 4) ** -0.5, 0.15625, ((0, 4),)),
        "norm_gains": jnp.clip(1.0 + 0.1 * jax.random.normal(seeds[6], (2, D), jnp.float32), 0.5, 1.5).astype(jnp.bfloat16),
        "biases": bell_draw(seeds[7], (6, D), 0.3, 4.0, ((1, 4),)),
        "fc_bias": bell_draw(seeds[8], (FF,), 0.3, 4.0, ((0, 4),)),
        "cotangent": bell_draw(seeds[9], (SEQS, SEQ_LEN, D), 1.0, 6.0, ((0, 4), (1, 8))),
    }


@jax.custom_vjp
def low(v):
    return lax.optimization_barrier(v.astype(jnp.bfloat16)).astype(jnp.float32)

@jax.custom_vjp
def low_back(v):
    return v

def low_keep(v):
    return (low(v), None)

def low_pass(kept, grad):
    return (grad,)

def back_keep(v):
    return (v, None)

def back_low(kept, grad):
    return (low(grad),)
low.defvjp(low_keep, low_pass)
low_back.defvjp(back_keep, back_low)
epsilon = 1e-05

def layer_norm(token_rows, gain_row, shift_row):
    mean_row = lax.optimization_barrier(jnp.mean(token_rows, axis=-1, keepdims=True))
    centered = token_rows - mean_row
    variance = lax.optimization_barrier(jnp.mean(centered * centered, axis=-1, keepdims=True))
    return centered * lax.rsqrt(variance + epsilon) * gain_row + shift_row

def gelu_tanh(inputs):
    return 0.5 * inputs * (1.0 + jnp.tanh(0.7978845608028654 * (inputs + 0.044715 * inputs * inputs * inputs)))

def matmul(left, right):
    return jnp.dot(left, right, preferred_element_type=jnp.float32, precision=lax.Precision.HIGHEST)

def split_heads(matrix):
    return matrix.reshape(matrix.shape[0], HEADS, HEAD_DIM).transpose(1, 0, 2)

def sequence_layer(token_rows, places, w_attn, w_proj, w_fc, w_out, norm_gains, biases, fc_bias):
    row_count = token_rows.shape[0]
    model_width = token_rows.shape[1]
    score_scale = HEAD_DIM ** (-0.5)
    normed_one = low(layer_norm(token_rows, norm_gains[0], biases[0]))
    qkv_shift = jnp.concatenate([biases[2], jnp.zeros_like(biases[2]), biases[3]])
    joined_rows = low(low_back(matmul(normed_one, w_attn) + qkv_shift))
    queries = joined_rows[:, :model_width]
    keys_rows = joined_rows[:, model_width:2 * model_width]
    values_rows = joined_rows[:, 2 * model_width:]
    allowed = places[:, None] >= places[None, :]

    def one_head(triple):
        query_head, key_head, value_head = triple
        scores = low_back(matmul(query_head, key_head.T) * score_scale)
        scores = jnp.where(allowed, scores, -1e+30)
        row_max = lax.optimization_barrier(jnp.max(scores, axis=1, keepdims=True))
        weights = jnp.exp(scores - row_max)
        probabilities = low(weights / lax.optimization_barrier(jnp.sum(weights, axis=1, keepdims=True)))
        return matmul(probabilities, value_head)
    head_outs = lax.map(jax.checkpoint(one_head), (split_heads(queries), split_heads(keys_rows), split_heads(values_rows)))
    attended = head_outs.transpose(1, 0, 2).reshape(row_count, model_width)
    attended = low(low_back(attended))
    residual_mid = token_rows + low_back(matmul(attended, w_proj) + biases[4])
    normed_two = low(layer_norm(residual_mid, norm_gains[1], biases[1]))
    hidden = low_back(matmul(normed_two, w_fc) + fc_bias)
    active = low(gelu_tanh(hidden))
    return residual_mid + low_back(matmul(active, w_out) + biases[5])

def reference(tokens, block_order, w_attn, w_proj, w_fc, w_out, norm_gains, biases, fc_bias, cotangent):
    block_rows = tokens.shape[1] // block_order.shape[1]
    places = (block_order[:, :, None] * block_rows + jnp.arange(block_rows, dtype=jnp.int32)[None, None, :]).reshape(block_order.shape[0], -1).astype(jnp.int32)
    params = tuple((item.astype(jnp.float32) for item in (w_attn, w_proj, w_fc, w_out, norm_gains, biases, fc_bias)))

    def forward(token_all, *weight_list):

        def per_sequence(pair):
            return jax.checkpoint(sequence_layer)(pair[0], pair[1], *weight_list)
        return lax.map(per_sequence, (token_all, places))
    result, pullback = jax.vjp(forward, tokens.astype(jnp.float32), *params)
    grads = pullback(cotangent.astype(jnp.float32))
    return (result.astype(jnp.bfloat16), grads[0].astype(jnp.bfloat16), grads[1], grads[2], grads[3], grads[4], grads[5], grads[6], grads[7])
```

```python
import functools

import jax
import jax.numpy as jnp
from jax import lax
from jax.experimental import pallas as pl
from jax.experimental.pallas import tpu as pltpu
from jax.sharding import PartitionSpec as P

HEAD_DIM = 64
BLOCK = 128
QROWS = 256
EPS = 1e-05
SCALE = HEAD_DIM ** (-0.5)
F32 = jnp.float32
BF16 = jnp.bfloat16
VMEM_LIMIT = 56 * 1024 * 1024
LAST = (((1,), (1,)), ((), ()))


def dot_last(a, b):
    return lax.dot_general(a, b, LAST, preferred_element_type=F32)


def dot(a, b):
    return jnp.dot(a, b, preferred_element_type=F32)


def qkv_kernel(inv_ref, xa_ref, xb_ref, w_ref, gain_ref, shift_ref, bias_ref, n_ref, o_ref):
    x = jnp.concatenate([xa_ref[...], xb_ref[...]], axis=0).astype(F32)
    mean = jnp.mean(x, axis=1, keepdims=True)
    cen = x - mean
    var = jnp.mean(cen * cen, axis=1, keepdims=True)
    normed = (cen * lax.rsqrt(var + EPS) * gain_ref[...] + shift_ref[...]).astype(BF16)
    n_ref[...] = normed
    for s in range(w_ref.shape[0]):
        o_ref[s] = (dot(normed, w_ref[s]) + bias_ref[s]).astype(BF16)


def qkv_call(inv, x_all, w_slots, gain, shift, bias_slots):
    rows, width = x_all.shape
    slots, _, cols = w_slots.shape
    full = lambda *shape: pl.BlockSpec(shape, lambda i, inv: (0,) * len(shape))
    return pl.pallas_call(
        qkv_kernel,
        grid_spec=pltpu.PrefetchScalarGridSpec(
            num_scalar_prefetch=1,
            grid=(rows // QROWS,),
            in_specs=[
                pl.BlockSpec((BLOCK, width), lambda i, inv: (inv[2 * i], 0)),
                pl.BlockSpec((BLOCK, width), lambda i, inv: (inv[2 * i + 1], 0)),
                full(slots, width, cols),
                full(1, width),
                full(1, width),
                full(slots, 1, cols),
            ],
            out_specs=[
                pl.BlockSpec((QROWS, width), lambda i, inv: (i, 0)),
                pl.BlockSpec((slots, QROWS, cols), lambda i, inv: (0, i, 0)),
            ],
        ),
        out_shape=[
            jax.ShapeDtypeStruct((rows, width), BF16),
            jax.ShapeDtypeStruct((slots, rows, cols), BF16),
        ],
        compiler_params=pltpu.CompilerParams(vmem_limit_bytes=VMEM_LIMIT),
        name="norm_qkv",
    )(inv, x_all, x_all, w_slots, gain, shift, bias_slots)


def causal_scores(k, q_rows, start):
    scores = dot_last(k, q_rows)
    keep = start
    tail = scores[keep:]
    key_id = lax.broadcasted_iota(jnp.int32, tail.shape, 0)
    query_id = lax.broadcasted_iota(jnp.int32, tail.shape, 1)
    tail = jnp.where(key_id <= query_id, tail, -1e30)
    if keep == 0:
        return tail
    return jnp.concatenate([scores[:keep], tail], axis=0)


def soft(scores, v_t):
    top = jnp.max(scores, axis=0, keepdims=True)
    weights = jnp.exp(scores - top)
    total = jnp.sum(weights, axis=0, keepdims=True)
    out = dot(v_t, weights.astype(BF16)) / total
    return out, top + jnp.log(total)


def attn_fwd_kernel(inv_ref, x_ref, o_ref, l_ref):
    rows = x_ref.shape[1]
    hd = HEAD_DIM
    q = x_ref[0, :, :hd] * BF16(SCALE)
    k = x_ref[0, :, hd : 2 * hd]
    v_t = x_ref[0, :, 2 * hd :].T
    for i in range(rows // QROWS):
        lo, hi = i * QROWS, (i + 1) * QROWS
        out, lse = soft(causal_scores(k[:hi], q[lo:hi], lo), v_t[:, :hi])
        l_ref[0, :, lo:hi] = lse
        out = out.astype(BF16)
        for b in range(QROWS // BLOCK):
            o_ref[inv_ref[2 * i + b]] = out[:, b * BLOCK : (b + 1) * BLOCK]


def attn_fwd(inv, qkv, heads):
    rows, cols = qkv.shape[1:]
    blocks = rows // BLOCK
    return pl.pallas_call(
        attn_fwd_kernel,
        grid_spec=pltpu.PrefetchScalarGridSpec(
            num_scalar_prefetch=1,
            grid=(heads,),
            in_specs=[pl.BlockSpec((1, rows, cols), lambda h, inv: (h, 0, 0))],
            out_specs=[
                pl.BlockSpec((blocks, HEAD_DIM, BLOCK), lambda h, inv: (0, h, 0)),
                pl.BlockSpec((1, 1, rows), lambda h, inv: (h, 0, 0)),
            ],
        ),
        out_shape=[
            jax.ShapeDtypeStruct((blocks, heads * HEAD_DIM, BLOCK), BF16),
            jax.ShapeDtypeStruct((heads, 1, rows), F32),
        ],
        compiler_params=pltpu.CompilerParams(vmem_limit_bytes=VMEM_LIMIT),
        name="attn_fwd",
    )(inv, qkv)


def attn_bwd_kernel(inv_ref, x_ref, do_ref, o_ref, l_ref, dx_ref, dk_acc, dv_acc):
    rows = x_ref.shape[1]
    hd = HEAD_DIM
    q = x_ref[0, :, :hd] * BF16(SCALE)
    k = x_ref[0, :, hd : 2 * hd]
    v = x_ref[0, :, 2 * hd :]
    k_t = k.T
    dk_acc[...] = jnp.zeros_like(dk_acc)
    dv_acc[...] = jnp.zeros_like(dv_acc)
    for i in range(rows // QROWS):
        lo, hi = i * QROWS, (i + 1) * QROWS
        ids = [inv_ref[2 * i + b] for b in range(QROWS // BLOCK)]
        do_t = jnp.concatenate([do_ref[b] for b in ids], axis=1)
        o_t = jnp.concatenate([o_ref[b] for b in ids], axis=1)
        inner = jnp.sum(do_t.astype(F32) * o_t.astype(F32), axis=0, keepdims=True)
        probs = jnp.exp(causal_scores(k[:hi], q[lo:hi], lo) - l_ref[0, :, lo:hi])
        dprobs = dot(v[:hi], do_t)
        dscores = (probs * (dprobs - inner)).astype(BF16)
        dv_acc[:hi] += dot_last(probs.astype(BF16), do_t)
        dk_acc[:hi] += dot(dscores, q[lo:hi])
        dq = (dot(k_t[:, :hi], dscores) * SCALE).T
        dx_ref[0, lo:hi, :hd] = dq.astype(BF16)
    dx_ref[0, :, hd : 2 * hd] = dk_acc[...].astype(BF16)
    dx_ref[0, :, 2 * hd :] = dv_acc[...].astype(BF16)


def attn_bwd(inv, qkv, d_out, out, lse, heads):
    rows, cols = qkv.shape[1:]
    blocks = rows // BLOCK
    feat = pl.BlockSpec((blocks, HEAD_DIM, BLOCK), lambda h, inv: (0, h, 0))
    return pl.pallas_call(
        attn_bwd_kernel,
        grid_spec=pltpu.PrefetchScalarGridSpec(
            num_scalar_prefetch=1,
            grid=(heads,),
            in_specs=[
                pl.BlockSpec((1, rows, cols), lambda h, inv: (h, 0, 0)),
                feat,
                feat,
                pl.BlockSpec((1, 1, rows), lambda h, inv: (h, 0, 0)),
            ],
            out_specs=pl.BlockSpec((1, rows, cols), lambda h, inv: (h, 0, 0)),
            scratch_shapes=[pltpu.VMEM((rows, HEAD_DIM), F32)] * 2,
        ),
        out_shape=jax.ShapeDtypeStruct((heads, rows, cols), BF16),
        compiler_params=pltpu.CompilerParams(vmem_limit_bytes=VMEM_LIMIT),
        name="attn_bwd",
    )(inv, qkv, d_out, out, lse)


def own_scores(own_ref, x_ref, k):
    hd = HEAD_DIM
    starts = [pl.multiple_of(own_ref[b] * BLOCK, BLOCK) for b in range(2)]
    q = jnp.concatenate([x_ref[0, pl.ds(s, BLOCK), :] for s in starts], axis=0)[:, :hd]
    q = q * BF16(SCALE)
    scores = dot_last(k, q)
    key_id = lax.broadcasted_iota(jnp.int32, scores.shape, 0)
    lane = lax.broadcasted_iota(jnp.int32, (1, scores.shape[1]), 1)
    place = jnp.where(lane < BLOCK, starts[0] + lane, starts[1] + lane - BLOCK)
    return q, starts, jnp.where(key_id <= place, scores, -1e30)


def rest_fwd_kernel(own_ref, x_ref, o_ref, l_ref):
    hd = HEAD_DIM
    _, _, scores = own_scores(own_ref, x_ref, x_ref[0, :, hd : 2 * hd])
    out, lse = soft(scores, x_ref[0, :, 2 * hd :].T)
    o_ref[0] = out.astype(BF16)
    l_ref[0] = lse


def rest_fwd(own, qkv, base):
    slots, rows, cols = qkv.shape
    rest = slots - base
    return pl.pallas_call(
        rest_fwd_kernel,
        grid_spec=pltpu.PrefetchScalarGridSpec(
            num_scalar_prefetch=1,
            grid=(rest,),
            in_specs=[pl.BlockSpec((1, rows, cols), lambda h, own: (base + h, 0, 0))],
            out_specs=[
                pl.BlockSpec((1, HEAD_DIM, QROWS), lambda h, own: (h, 0, 0)),
                pl.BlockSpec((1, 1, QROWS), lambda h, own: (h, 0, 0)),
            ],
        ),
        out_shape=[
            jax.ShapeDtypeStruct((rest, HEAD_DIM, QROWS), BF16),
            jax.ShapeDtypeStruct((rest, 1, QROWS), F32),
        ],
        compiler_params=pltpu.CompilerParams(vmem_limit_bytes=VMEM_LIMIT),
        name="rest_fwd",
    )(own, qkv)


def rest_bwd_kernel(own_ref, x_ref, do_ref, o_ref, l_ref, dx_ref):
    hd = HEAD_DIM
    k = x_ref[0, :, hd : 2 * hd]
    q, starts, scores = own_scores(own_ref, x_ref, k)
    do_t = do_ref[0]
    inner = jnp.sum(do_t.astype(F32) * o_ref[0].astype(F32), axis=0, keepdims=True)
    probs = jnp.exp(scores - l_ref[0])
    dprobs = dot(x_ref[0, :, 2 * hd :], do_t)
    dscores = (probs * (dprobs - inner)).astype(BF16)
    dx_ref[0, :, 2 * hd :] = dot_last(probs.astype(BF16), do_t).astype(BF16)
    dx_ref[0, :, hd : 2 * hd] = dot(dscores, q).astype(BF16)
    dq = (dot(k.T, dscores) * SCALE).T.astype(BF16)
    dx_ref[0, :, :hd] = jnp.zeros((dx_ref.shape[1], hd), BF16)
    for b, s in enumerate(starts):
        dx_ref[0, pl.ds(s, BLOCK), :hd] = dq[b * BLOCK : (b + 1) * BLOCK]


def rest_bwd(own, qkv, d_out, out, lse, base):
    slots, rows, cols = qkv.shape
    rest = slots - base
    feat = pl.BlockSpec((1, HEAD_DIM, QROWS), lambda h, own: (h, 0, 0))
    return pl.pallas_call(
        rest_bwd_kernel,
        grid_spec=pltpu.PrefetchScalarGridSpec(
            num_scalar_prefetch=1,
            grid=(rest,),
            in_specs=[
                pl.BlockSpec((1, rows, cols), lambda h, own: (base + h, 0, 0)),
                feat,
                feat,
                pl.BlockSpec((1, 1, QROWS), lambda h, own: (h, 0, 0)),
            ],
            out_specs=pl.BlockSpec((1, rows, cols), lambda h, own: (h, 0, 0)),
        ),
        out_shape=jax.ShapeDtypeStruct((rest, rows, cols), BF16),
        compiler_params=pltpu.CompilerParams(vmem_limit_bytes=VMEM_LIMIT),
        name="rest_bwd",
    )(own, qkv, d_out, out, lse)


def assemble_kernel(own_ref, rest_ref, o_ref):
    hd = HEAD_DIM
    width = o_ref.shape[1] // 3
    count = own_ref.shape[0]
    for h in range(width // hd):
        src = own_ref.at[h] if h < count else rest_ref.at[h - count]
        for part in range(3):
            at = part * width + h * hd
            o_ref[:, at : at + hd] = src[:, part * hd : (part + 1) * hd].astype(F32)


def assemble(own, rest, out_cols):
    rows = own.shape[1]
    return pl.pallas_call(
        assemble_kernel,
        out_shape=jax.ShapeDtypeStruct((rows, out_cols), F32),
        compiler_params=pltpu.CompilerParams(vmem_limit_bytes=VMEM_LIMIT),
        name="assemble",
    )(own, rest)


def norm_parts(rows):
    mean = jnp.mean(rows, axis=-1, keepdims=True)
    cen = rows - mean
    rstd = lax.rsqrt(jnp.mean(cen * cen, axis=-1, keepdims=True) + EPS)
    return cen * rstd, rstd


def norm_back(xhat, rstd, gain, grad):
    dxhat = grad * gain
    return rstd * (
        dxhat
        - jnp.mean(dxhat, axis=-1, keepdims=True)
        - xhat * jnp.mean(dxhat * xhat, axis=-1, keepdims=True)
    )


def shards(
    n_ctx,
    n_fsdp,
    tokens,
    block_order,
    w_attn,
    w_proj,
    w_fc,
    w_out,
    norm_gains,
    biases,
    fc_bias,
    cotangent,
):
    hd = HEAD_DIM
    count, width = tokens.shape[1:]
    shard = width // n_fsdp
    heads = width // hd
    base = heads // n_ctx
    rest = heads - base * n_ctx
    slots = base + rest
    own_blocks = count // BLOCK
    c = lax.axis_index("ctx")
    f = lax.axis_index("fsdp")

    order = block_order[0]
    inv = jnp.argsort(order).astype(jnp.int32)
    own = lax.dynamic_slice_in_dim(order, c * own_blocks, own_blocks)

    x_all = lax.all_gather(tokens[0], "ctx", axis=0, tiled=True)

    def head_cols(h):
        return jnp.concatenate(
            [
                lax.dynamic_slice(w_attn, (0, part * width + h * hd), (shard, hd))
                for part in range(3)
            ],
            axis=1,
        )

    slot_heads = [c * base + s for s in range(base)] + [n_ctx * base + r for r in range(rest)]
    w_slots = jnp.stack([head_cols(h) for h in slot_heads])
    w_slots = lax.all_gather(w_slots, "fsdp", axis=1, tiled=True)
    small = lax.all_gather(
        jnp.concatenate([norm_gains, biases], axis=0), "fsdp", axis=1, tiled=True
    ).astype(F32)
    gains, shifts = small[:2], small[2:]
    full_proj = lax.all_gather(w_proj, "fsdp", axis=0, tiled=True)
    fc_cols = lax.all_to_all(w_fc, "fsdp", split_axis=1, concat_axis=0, tiled=True)
    cot = cotangent[0]
    cot_all = lax.all_gather(cot, "fsdp", axis=0, tiled=True)

    zero_bias = jnp.zeros((hd,), F32)
    bias_slots = jnp.stack(
        [
            jnp.concatenate(
                [
                    lax.dynamic_slice_in_dim(shifts[2], h * hd, hd),
                    zero_bias,
                    lax.dynamic_slice_in_dim(shifts[3], h * hd, hd),
                ]
            )[None]
            for h in slot_heads
        ]
    )
    normed_one, qkv = qkv_call(inv, x_all, w_slots, gains[:1], shifts[:1], bias_slots)
    out_own, lse_own = attn_fwd(inv, qkv, base)
    got = lax.all_to_all(out_own, "ctx", split_axis=0, concat_axis=0, tiled=True)
    got = got.reshape(n_ctx, own_blocks, base * hd, BLOCK).transpose(1, 3, 0, 2)
    attended = got.reshape(count, n_ctx * base * hd)
    if rest:
        out_rest, lse_rest = rest_fwd(own, qkv, base)
        attended = jnp.concatenate([attended, out_rest.reshape(rest * hd, count).T], axis=1)

    rows = tokens[0].astype(F32)
    mid = rows + (dot(attended, full_proj) + shifts[4])
    xhat_two, rstd_two = norm_parts(mid)
    normed_two = (xhat_two * gains[1] + shifts[1]).astype(BF16)

    normed_all = lax.all_gather(normed_two, "fsdp", axis=0, tiled=True)
    hidden = dot(normed_all, fc_cols) + fc_bias.astype(F32)
    square = hidden * hidden
    tanh = jnp.tanh(0.7978845608028654 * (hidden + 0.044715 * square * hidden))
    active = (0.5 * hidden * (1.0 + tanh)).astype(BF16)
    slope = 0.5 * (1.0 + tanh) + 0.5 * hidden * (1.0 - tanh * tanh) * 0.7978845608028654 * (
        1.0 + 3.0 * 0.044715 * square
    )
    out_part = dot(active, w_out).astype(BF16)
    out_rows = lax.psum_scatter(out_part, "fsdp", scatter_dimension=0, tiled=True)
    layer_rows = (mid + (out_rows.astype(F32) + shifts[5])).astype(BF16)

    active_grad = dot_last(cot_all, w_out)
    hidden_grad = (active_grad * slope).astype(BF16)
    normed_part = dot_last(hidden_grad, fc_cols).astype(BF16)
    normed_two_grad = lax.psum_scatter(
        normed_part, "fsdp", scatter_dimension=0, tiled=True
    ).astype(F32)
    over_rows = functools.partial(jnp.einsum, "ta,tb->ab", preferred_element_type=F32)
    w_out_part = over_rows(active, cot_all).astype(BF16)
    w_fc_part = over_rows(normed_all, hidden_grad).astype(BF16)
    fc_bias_part = jnp.sum(hidden_grad.astype(F32), axis=0)
    w_fc_part = lax.all_to_all(w_fc_part, "fsdp", split_axis=0, concat_axis=1, tiled=True)
    w_out_grad = lax.psum(w_out_part, "ctx").astype(F32)
    w_fc_grad = lax.psum(w_fc_part, "ctx").astype(F32)

    cot_rows = cot.astype(F32)
    mid_grad = cot_rows + norm_back(xhat_two, rstd_two, gains[1], normed_two_grad)
    mid_low = mid_grad.astype(BF16)
    attended_grad = dot_last(mid_low, full_proj).astype(BF16)
    w_proj_part = over_rows(attended, mid_low).astype(BF16)
    w_proj_part = lax.psum_scatter(w_proj_part, "fsdp", scatter_dimension=0, tiled=True)
    w_proj_grad = lax.psum(w_proj_part, "ctx").astype(F32)

    main = n_ctx * base * hd
    sent = attended_grad[:, :main].reshape(own_blocks, BLOCK, n_ctx, base * hd)
    sent = sent.transpose(2, 0, 3, 1).reshape(n_ctx * own_blocks, base * hd, BLOCK)
    d_out = lax.all_to_all(sent, "ctx", split_axis=0, concat_axis=0, tiled=True)
    dqkv = attn_bwd(inv, qkv, d_out, out_own, lse_own, base)
    if rest:
        d_rest = attended_grad[:, main:].T.reshape(rest, hd, count)
        dqkv = jnp.concatenate(
            [dqkv, rest_bwd(own, qkv, d_rest, out_rest, lse_rest, base)], axis=0
        )
    flat = dqkv.transpose(1, 0, 2).reshape(x_all.shape[0], slots * 3 * hd)
    flat_w = w_slots.transpose(1, 0, 2).reshape(width, slots * 3 * hd)
    one_part = dot_last(flat, flat_w).astype(BF16)
    one_part = one_part.reshape(-1, BLOCK, width)[order].reshape(one_part.shape)
    normed_one_grad = lax.psum_scatter(
        one_part, "ctx", scatter_dimension=0, tiled=True
    ).astype(F32)
    slot_part = jnp.einsum("td,hte->hde", normed_one, dqkv, preferred_element_type=F32)
    slot_part = lax.psum_scatter(
        slot_part.astype(BF16), "fsdp", scatter_dimension=1, tiled=True
    )
    own_cols = lax.all_gather(slot_part[:base], "ctx", axis=0, tiled=True)
    if rest:
        rest_cols = lax.psum(slot_part[base:], "ctx")
    else:
        rest_cols = own_cols
    w_attn_grad = assemble(own_cols, rest_cols, 3 * width)

    xhat_one, rstd_one = norm_parts(rows)
    tokens_grad = (mid_grad + norm_back(xhat_one, rstd_one, gains[0], normed_one_grad)).astype(
        BF16
    )

    sums = jnp.sum(dqkv.astype(F32), axis=1)

    def placed(part):
        cols = sums[:, part * hd : (part + 1) * hd]
        line = lax.dynamic_update_slice_in_dim(
            jnp.zeros((width,), F32), cols[:base].reshape(-1), c * base * hd, 0
        )
        return line + jnp.pad(cols[base:].reshape(-1), (main, 0))

    lines = jnp.stack(
        [
            jnp.sum(normed_one_grad * xhat_one, axis=0),
            jnp.sum(normed_two_grad * xhat_two, axis=0),
            jnp.sum(normed_one_grad, axis=0),
            jnp.sum(normed_two_grad, axis=0),
            placed(0),
            placed(2),
            jnp.sum(mid_low.astype(F32), axis=0),
            jnp.sum(cot_rows, axis=0),
        ]
    )
    lines = lax.psum(lines, ("ctx", "fsdp"))
    lines = lax.dynamic_slice_in_dim(lines, f * shard, shard, 1)
    fc_bias_grad = lax.psum(fc_bias_part, "ctx")
    return (
        layer_rows[None],
        tokens_grad[None],
        w_attn_grad,
        w_proj_grad,
        w_fc_grad,
        w_out_grad,
        lines[:2],
        lines[2:],
        fc_bias_grad,
    )


def solution(mesh):
    rows = P("fsdp", "ctx", None)
    weight = P("fsdp", None)
    vectors = P(None, "fsdp")
    return jax.shard_map(
        functools.partial(shards, mesh.shape["ctx"], mesh.shape["fsdp"]),
        mesh=mesh,
        in_specs=(
            rows, weight, weight, weight, weight, weight, vectors, vectors, P("fsdp"), rows,
        ),
        out_specs=(
            rows, rows, weight, weight, weight, weight, vectors, vectors, P("fsdp"),
        ),
        check_vma=False,
    )
```

```python
import functools

import jax
import jax.numpy as jnp
from jax import lax
from jax.experimental import pallas as pl
from jax.experimental.pallas import tpu as pltpu
from jax.sharding import PartitionSpec as P

HEAD_DIM = 64
BLOCK = 128
QROWS = 256
EPS = 1e-05
SCALE = HEAD_DIM ** (-0.5)
F32 = jnp.float32
BF16 = jnp.bfloat16
VMEM_LIMIT = 56 * 1024 * 1024
LAST = (((1,), (1,)), ((), ()))


def dot_last(a, b):
    return lax.dot_general(a, b, LAST, preferred_element_type=F32)


def dot(a, b):
    return jnp.dot(a, b, preferred_element_type=F32)


def qkv_kernel(inv_ref, xa_ref, xb_ref, w_ref, gain_ref, shift_ref, bias_ref, n_ref, o_ref):
    x = jnp.concatenate([xa_ref[...], xb_ref[...]], axis=0).astype(F32)
    mean = jnp.mean(x, axis=1, keepdims=True)
    cen = x - mean
    var = jnp.mean(cen * cen, axis=1, keepdims=True)
    normed = (cen * lax.rsqrt(var + EPS) * gain_ref[...] + shift_ref[...]).astype(BF16)
    n_ref[...] = normed
    for s in range(w_ref.shape[0]):
        o_ref[s] = (dot(normed, w_ref[s]) + bias_ref[s]).astype(BF16)


def qkv_call(inv, x_all, w_slots, gain, shift, bias_slots):
    rows, width = x_all.shape
    slots, _, cols = w_slots.shape
    full = lambda *shape: pl.BlockSpec(shape, lambda i, inv: (0,) * len(shape))
    return pl.pallas_call(
        qkv_kernel,
        grid_spec=pltpu.PrefetchScalarGridSpec(
            num_scalar_prefetch=1,
            grid=(rows // QROWS,),
            in_specs=[
                pl.BlockSpec((BLOCK, width), lambda i, inv: (inv[2 * i], 0)),
                pl.BlockSpec((BLOCK, width), lambda i, inv: (inv[2 * i + 1], 0)),
                full(slots, width, cols),
                full(1, width),
                full(1, width),
                full(slots, 1, cols),
            ],
            out_specs=[
                pl.BlockSpec((QROWS, width), lambda i, inv: (i, 0)),
                pl.BlockSpec((slots, QROWS, cols), lambda i, inv: (0, i, 0)),
            ],
        ),
        out_shape=[
            jax.ShapeDtypeStruct((rows, width), BF16),
            jax.ShapeDtypeStruct((slots, rows, cols), BF16),
        ],
        compiler_params=pltpu.CompilerParams(vmem_limit_bytes=VMEM_LIMIT),
        name="norm_qkv",
    )(inv, x_all, x_all, w_slots, gain, shift, bias_slots)


def causal_scores(k, q_rows, start):
    scores = dot_last(k, q_rows)
    keep = start
    tail = scores[keep:]
    key_id = lax.broadcasted_iota(jnp.int32, tail.shape, 0)
    query_id = lax.broadcasted_iota(jnp.int32, tail.shape, 1)
    tail = jnp.where(key_id <= query_id, tail, -1e30)
    if keep == 0:
        return tail
    return jnp.concatenate([scores[:keep], tail], axis=0)


def soft(scores, v_t):
    top = jnp.max(scores, axis=0, keepdims=True)
    weights = jnp.exp(scores - top)
    total = jnp.sum(weights, axis=0, keepdims=True)
    out = dot(v_t, weights.astype(BF16)) / total
    return out, top + jnp.log(total)


def attn_fwd_kernel(inv_ref, x_ref, o_ref, l_ref):
    rows = x_ref.shape[1]
    hd = HEAD_DIM
    q = x_ref[0, :, :hd] * BF16(SCALE)
    k = x_ref[0, :, hd : 2 * hd]
    v_t = x_ref[0, :, 2 * hd :].T
    for i in range(rows // QROWS):
        lo, hi = i * QROWS, (i + 1) * QROWS
        out, lse = soft(causal_scores(k[:hi], q[lo:hi], lo), v_t[:, :hi])
        l_ref[0, :, lo:hi] = lse
        out = out.astype(BF16)
        for b in range(QROWS // BLOCK):
            o_ref[inv_ref[2 * i + b]] = out[:, b * BLOCK : (b + 1) * BLOCK]


def attn_fwd(inv, qkv, heads):
    rows, cols = qkv.shape[1:]
    blocks = rows // BLOCK
    return pl.pallas_call(
        attn_fwd_kernel,
        grid_spec=pltpu.PrefetchScalarGridSpec(
            num_scalar_prefetch=1,
            grid=(heads,),
            in_specs=[pl.BlockSpec((1, rows, cols), lambda h, inv: (h, 0, 0))],
            out_specs=[
                pl.BlockSpec((blocks, HEAD_DIM, BLOCK), lambda h, inv: (0, h, 0)),
                pl.BlockSpec((1, 1, rows), lambda h, inv: (h, 0, 0)),
            ],
        ),
        out_shape=[
            jax.ShapeDtypeStruct((blocks, heads * HEAD_DIM, BLOCK), BF16),
            jax.ShapeDtypeStruct((heads, 1, rows), F32),
        ],
        compiler_params=pltpu.CompilerParams(vmem_limit_bytes=VMEM_LIMIT),
        name="attn_fwd",
    )(inv, qkv)


def attn_bwd_kernel(inv_ref, x_ref, do_ref, o_ref, l_ref, dx_ref, dk_acc, dv_acc):
    rows = x_ref.shape[1]
    hd = HEAD_DIM
    q = x_ref[0, :, :hd] * BF16(SCALE)
    k = x_ref[0, :, hd : 2 * hd]
    v = x_ref[0, :, 2 * hd :]
    k_t = k.T
    dk_acc[...] = jnp.zeros_like(dk_acc)
    dv_acc[...] = jnp.zeros_like(dv_acc)
    for i in range(rows // QROWS):
        lo, hi = i * QROWS, (i + 1) * QROWS
        ids = [inv_ref[2 * i + b] for b in range(QROWS // BLOCK)]
        do_t = jnp.concatenate([do_ref[b] for b in ids], axis=1)
        o_t = jnp.concatenate([o_ref[b] for b in ids], axis=1)
        inner = jnp.sum(do_t.astype(F32) * o_t.astype(F32), axis=0, keepdims=True)
        probs = jnp.exp(causal_scores(k[:hi], q[lo:hi], lo) - l_ref[0, :, lo:hi])
        dprobs = dot(v[:hi], do_t)
        dscores = (probs * (dprobs - inner)).astype(BF16)
        dv_acc[:hi] += dot_last(probs.astype(BF16), do_t)
        dk_acc[:hi] += dot(dscores, q[lo:hi])
        dq = (dot(k_t[:, :hi], dscores) * SCALE).T
        dx_ref[0, lo:hi, :hd] = dq.astype(BF16)
    dx_ref[0, :, hd : 2 * hd] = dk_acc[...].astype(BF16)
    dx_ref[0, :, 2 * hd :] = dv_acc[...].astype(BF16)


def attn_bwd(inv, qkv, d_out, out, lse, heads):
    rows, cols = qkv.shape[1:]
    blocks = rows // BLOCK
    feat = pl.BlockSpec((blocks, HEAD_DIM, BLOCK), lambda h, inv: (0, h, 0))
    return pl.pallas_call(
        attn_bwd_kernel,
        grid_spec=pltpu.PrefetchScalarGridSpec(
            num_scalar_prefetch=1,
            grid=(heads,),
            in_specs=[
                pl.BlockSpec((1, rows, cols), lambda h, inv: (h, 0, 0)),
                feat,
                feat,
                pl.BlockSpec((1, 1, rows), lambda h, inv: (h, 0, 0)),
            ],
            out_specs=pl.BlockSpec((1, rows, cols), lambda h, inv: (h, 0, 0)),
            scratch_shapes=[pltpu.VMEM((rows, HEAD_DIM), F32)] * 2,
        ),
        out_shape=jax.ShapeDtypeStruct((heads, rows, cols), BF16),
        compiler_params=pltpu.CompilerParams(vmem_limit_bytes=VMEM_LIMIT),
        name="attn_bwd",
    )(inv, qkv, d_out, out, lse)


def own_scores(own_ref, x_ref, k):
    hd = HEAD_DIM
    starts = [pl.multiple_of(own_ref[b] * BLOCK, BLOCK) for b in range(2)]
    q = jnp.concatenate([x_ref[0, pl.ds(s, BLOCK), :] for s in starts], axis=0)[:, :hd]
    q = q * BF16(SCALE)
    scores = dot_last(k, q)
    key_id = lax.broadcasted_iota(jnp.int32, scores.shape, 0)
    lane = lax.broadcasted_iota(jnp.int32, (1, scores.shape[1]), 1)
    place = jnp.where(lane < BLOCK, starts[0] + lane, starts[1] + lane - BLOCK)
    return q, starts, jnp.where(key_id <= place, scores, -1e30)


def rest_fwd_kernel(own_ref, x_ref, o_ref, l_ref):
    hd = HEAD_DIM
    _, _, scores = own_scores(own_ref, x_ref, x_ref[0, :, hd : 2 * hd])
    out, lse = soft(scores, x_ref[0, :, 2 * hd :].T)
    o_ref[0] = out.astype(BF16)
    l_ref[0] = lse


def rest_fwd(own, qkv, base):
    slots, rows, cols = qkv.shape
    rest = slots - base
    return pl.pallas_call(
        rest_fwd_kernel,
        grid_spec=pltpu.PrefetchScalarGridSpec(
            num_scalar_prefetch=1,
            grid=(rest,),
            in_specs=[pl.BlockSpec((1, rows, cols), lambda h, own: (base + h, 0, 0))],
            out_specs=[
                pl.BlockSpec((1, HEAD_DIM, QROWS), lambda h, own: (h, 0, 0)),
                pl.BlockSpec((1, 1, QROWS), lambda h, own: (h, 0, 0)),
            ],
        ),
        out_shape=[
            jax.ShapeDtypeStruct((rest, HEAD_DIM, QROWS), BF16),
            jax.ShapeDtypeStruct((rest, 1, QROWS), F32),
        ],
        compiler_params=pltpu.CompilerParams(vmem_limit_bytes=VMEM_LIMIT),
        name="rest_fwd",
    )(own, qkv)


def rest_bwd_kernel(own_ref, x_ref, do_ref, o_ref, l_ref, dx_ref):
    hd = HEAD_DIM
    k = x_ref[0, :, hd : 2 * hd]
    q, starts, scores = own_scores(own_ref, x_ref, k)
    do_t = do_ref[0]
    inner = jnp.sum(do_t.astype(F32) * o_ref[0].astype(F32), axis=0, keepdims=True)
    probs = jnp.exp(scores - l_ref[0])
    dprobs = dot(x_ref[0, :, 2 * hd :], do_t)
    dscores = (probs * (dprobs - inner)).astype(BF16)
    dx_ref[0, :, 2 * hd :] = dot_last(probs.astype(BF16), do_t).astype(BF16)
    dx_ref[0, :, hd : 2 * hd] = dot(dscores, q).astype(BF16)
    dq = (dot(k.T, dscores) * SCALE).T.astype(BF16)
    dx_ref[0, :, :hd] = jnp.zeros((dx_ref.shape[1], hd), BF16)
    for b, s in enumerate(starts):
        dx_ref[0, pl.ds(s, BLOCK), :hd] = dq[b * BLOCK : (b + 1) * BLOCK]


def rest_bwd(own, qkv, d_out, out, lse, base):
    slots, rows, cols = qkv.shape
    rest = slots - base
    feat = pl.BlockSpec((1, HEAD_DIM, QROWS), lambda h, own: (h, 0, 0))
    return pl.pallas_call(
        rest_bwd_kernel,
        grid_spec=pltpu.PrefetchScalarGridSpec(
            num_scalar_prefetch=1,
            grid=(rest,),
            in_specs=[
                pl.BlockSpec((1, rows, cols), lambda h, own: (base + h, 0, 0)),
                feat,
                feat,
                pl.BlockSpec((1, 1, QROWS), lambda h, own: (h, 0, 0)),
            ],
            out_specs=pl.BlockSpec((1, rows, cols), lambda h, own: (h, 0, 0)),
        ),
        out_shape=jax.ShapeDtypeStruct((rest, rows, cols), BF16),
        compiler_params=pltpu.CompilerParams(vmem_limit_bytes=VMEM_LIMIT),
        name="rest_bwd",
    )(own, qkv, d_out, out, lse)


def assemble_kernel(own_ref, rest_ref, o_ref):
    hd = HEAD_DIM
    width = o_ref.shape[1] // 3
    count = own_ref.shape[0]
    for h in range(width // hd):
        src = own_ref.at[h] if h < count else rest_ref.at[h - count]
        for part in range(3):
            at = part * width + h * hd
            o_ref[:, at : at + hd] = src[:, part * hd : (part + 1) * hd].astype(F32)


def assemble(own, rest, out_cols):
    rows = own.shape[1]
    return pl.pallas_call(
        assemble_kernel,
        out_shape=jax.ShapeDtypeStruct((rows, out_cols), F32),
        compiler_params=pltpu.CompilerParams(vmem_limit_bytes=VMEM_LIMIT),
        name="assemble",
    )(own, rest)


def norm_parts(rows):
    mean = jnp.mean(rows, axis=-1, keepdims=True)
    cen = rows - mean
    rstd = lax.rsqrt(jnp.mean(cen * cen, axis=-1, keepdims=True) + EPS)
    return cen * rstd, rstd


def norm_back(xhat, rstd, gain, grad):
    dxhat = grad * gain
    return rstd * (
        dxhat
        - jnp.mean(dxhat, axis=-1, keepdims=True)
        - xhat * jnp.mean(dxhat * xhat, axis=-1, keepdims=True)
    )


def swap(value, axis, size, k):
    return lax.ppermute(value, axis, [(i, i ^ k) for i in range(size)])


def shards(
    n_ctx,
    n_fsdp,
    tokens,
    block_order,
    w_attn,
    w_proj,
    w_fc,
    w_out,
    norm_gains,
    biases,
    fc_bias,
    cotangent,
):
    hd = HEAD_DIM
    count, width = tokens.shape[1:]
    shard = width // n_fsdp
    heads = width // hd
    base = heads // n_ctx
    rest = heads - base * n_ctx
    slots = base + rest
    own_blocks = count // BLOCK
    c = lax.axis_index("ctx")
    f = lax.axis_index("fsdp")

    order = block_order[0]
    inv = jnp.argsort(order).astype(jnp.int32)
    own = lax.dynamic_slice_in_dim(order, c * own_blocks, own_blocks)

    x_all = lax.all_gather(tokens[0], "ctx", axis=0, tiled=True)

    def head_cols(h):
        return jnp.concatenate(
            [
                lax.dynamic_slice(w_attn, (0, part * width + h * hd), (shard, hd))
                for part in range(3)
            ],
            axis=1,
        )

    slot_heads = [c * base + s for s in range(base)] + [n_ctx * base + r for r in range(rest)]
    w_slots = jnp.stack([head_cols(h) for h in slot_heads])
    w_slots = lax.all_gather(w_slots, "fsdp", axis=1, tiled=True)
    small = lax.all_gather(
        jnp.concatenate([norm_gains, biases], axis=0), "fsdp", axis=1, tiled=True
    ).astype(F32)
    gains, shifts = small[:2], small[2:]
    full_proj = lax.all_gather(w_proj, "fsdp", axis=0, tiled=True)
    hidden_cols = w_fc.shape[1] // n_fsdp
    fc_parts = jnp.stack(
        [w_fc[:, j * hidden_cols : (j + 1) * hidden_cols] for j in range(n_fsdp)]
    )
    fc_cols = jnp.zeros_like(fc_parts)
    for k in range(n_fsdp):
        piece = lax.dynamic_index_in_dim(fc_parts, f ^ k, keepdims=True)
        if k:
            piece = swap(piece, "fsdp", n_fsdp, k)
        fc_cols = lax.dynamic_update_slice(fc_cols, piece, (f ^ k, 0, 0))
    fc_cols = fc_cols.reshape(width, hidden_cols)
    cot = cotangent[0]

    def from_fsdp(own_rows):
        return jnp.concatenate(
            [own_rows] + [swap(own_rows, "fsdp", n_fsdp, k) for k in range(1, n_fsdp)]
        )

    def to_fsdp(part):
        part = part.reshape(n_fsdp, -1, part.shape[1])
        return sum(
            swap(part[k], "fsdp", n_fsdp, k).astype(F32) if k else part[k].astype(F32)
            for k in range(n_fsdp)
        )

    cot_all = from_fsdp(cot)

    zero_bias = jnp.zeros((hd,), F32)
    bias_slots = jnp.stack(
        [
            jnp.concatenate(
                [
                    lax.dynamic_slice_in_dim(shifts[2], h * hd, hd),
                    zero_bias,
                    lax.dynamic_slice_in_dim(shifts[3], h * hd, hd),
                ]
            )[None]
            for h in slot_heads
        ]
    )
    normed_one, qkv = qkv_call(inv, x_all, w_slots, gains[:1], shifts[:1], bias_slots)
    out_own, lse_own = attn_fwd(inv, qkv, base)
    got = lax.all_to_all(out_own, "ctx", split_axis=0, concat_axis=0, tiled=True)
    got = got.reshape(n_ctx, own_blocks, base * hd, BLOCK).transpose(1, 3, 0, 2)
    attended = got.reshape(count, n_ctx * base * hd)
    if rest:
        out_rest, lse_rest = rest_fwd(own, qkv, base)
        attended = jnp.concatenate([attended, out_rest.reshape(rest * hd, count).T], axis=1)

    rows = tokens[0].astype(F32)
    mid = rows + (dot(attended, full_proj) + shifts[4])
    xhat_two, rstd_two = norm_parts(mid)
    normed_two = (xhat_two * gains[1] + shifts[1]).astype(BF16)

    normed_all = from_fsdp(normed_two)
    hidden = dot(normed_all, fc_cols) + fc_bias.astype(F32)
    square = hidden * hidden
    tanh = jnp.tanh(0.7978845608028654 * (hidden + 0.044715 * square * hidden))
    active = (0.5 * hidden * (1.0 + tanh)).astype(BF16)
    slope = 0.5 * (1.0 + tanh) + 0.5 * hidden * (1.0 - tanh * tanh) * 0.7978845608028654 * (
        1.0 + 3.0 * 0.044715 * square
    )
    out_part = dot(active, w_out).astype(BF16)

    active_grad = dot_last(cot_all, w_out)
    hidden_grad = (active_grad * slope).astype(BF16)
    normed_part = dot_last(hidden_grad, fc_cols).astype(BF16)
    normed_two_grad = to_fsdp(normed_part)
    layer_rows = (mid + (to_fsdp(out_part) + shifts[5])).astype(BF16)
    over_rows = functools.partial(jnp.einsum, "ta,tb->ab", preferred_element_type=F32)
    w_out_part = over_rows(active, cot_all).astype(BF16)
    w_fc_part = over_rows(normed_all, hidden_grad).astype(BF16)
    fc_bias_part = jnp.sum(hidden_grad.astype(F32), axis=0)
    w_fc_part = w_fc_part.reshape(n_fsdp, shard, hidden_cols)
    fc_recv = []
    for k in range(n_fsdp):
        piece = lax.dynamic_index_in_dim(w_fc_part, f ^ k, keepdims=False)
        fc_recv.append(swap(piece, "fsdp", n_fsdp, k) if k else piece)
    w_out_low, w_fc_low = lax.psum((w_out_part, jnp.stack(fc_recv)), "ctx")
    w_out_grad = w_out_low.astype(F32)
    w_fc_grad = jnp.concatenate(
        [lax.dynamic_index_in_dim(w_fc_low, f ^ j, keepdims=False) for j in range(n_fsdp)],
        axis=1,
    ).astype(F32)

    cot_rows = cot.astype(F32)
    mid_grad = cot_rows + norm_back(xhat_two, rstd_two, gains[1], normed_two_grad)
    mid_low = mid_grad.astype(BF16)
    attended_grad = dot_last(mid_low, full_proj).astype(BF16)
    w_proj_part = over_rows(attended, mid_low).astype(BF16)
    w_proj_part = w_proj_part.reshape(n_fsdp, shard, width)
    w_proj_part = sum(
        swap(
            lax.dynamic_index_in_dim(w_proj_part, f ^ k, keepdims=False), "fsdp", n_fsdp, k
        ).astype(F32)
        if k
        else lax.dynamic_index_in_dim(w_proj_part, f, keepdims=False).astype(F32)
        for k in range(n_fsdp)
    ).astype(BF16)

    main = n_ctx * base * hd
    sent = attended_grad[:, :main].reshape(own_blocks, BLOCK, n_ctx, base * hd)
    sent = sent.transpose(2, 0, 3, 1).reshape(n_ctx * own_blocks, base * hd, BLOCK)
    d_out = lax.all_to_all(sent, "ctx", split_axis=0, concat_axis=0, tiled=True)
    dqkv = attn_bwd(inv, qkv, d_out, out_own, lse_own, base)
    if rest:
        d_rest = attended_grad[:, main:].T.reshape(rest, hd, count)
        dqkv = jnp.concatenate(
            [dqkv, rest_bwd(own, qkv, d_rest, out_rest, lse_rest, base)], axis=0
        )
    flat = dqkv.transpose(1, 0, 2).reshape(x_all.shape[0], slots * 3 * hd)
    flat_w = w_slots.transpose(1, 0, 2).reshape(width, slots * 3 * hd)
    one_part = dot_last(flat, flat_w).astype(BF16)
    one_part = one_part.reshape(-1, BLOCK, width)[order].reshape(one_part.shape)
    normed_one_grad = lax.psum_scatter(
        one_part, "ctx", scatter_dimension=0, tiled=True
    ).astype(F32)
    slot_part = jnp.einsum("td,hte->hde", normed_one, dqkv, preferred_element_type=F32)
    slot_part = slot_part.astype(BF16)

    def slot_rows(k):
        return lax.dynamic_slice_in_dim(slot_part, (f ^ k) * shard, shard, 1)

    slot_sum = slot_rows(0).astype(F32)
    for k in range(1, n_fsdp):
        slot_sum += swap(slot_rows(k), "fsdp", n_fsdp, k).astype(F32)
    slot_sum = slot_sum.astype(BF16)
    own_cols = lax.all_gather(slot_sum[:base], "ctx", axis=0, tiled=True)
    w_proj_part, rest_part, _, _ = lax.optimization_barrier(
        (w_proj_part, slot_sum[base:], w_out_low, w_fc_low)
    )
    w_proj_low, rest_cols = lax.psum((w_proj_part, rest_part), "ctx")
    w_proj_grad = w_proj_low.astype(F32)
    if not rest:
        rest_cols = own_cols
    w_attn_grad = assemble(own_cols, rest_cols, 3 * width)

    xhat_one, rstd_one = norm_parts(rows)
    tokens_grad = (mid_grad + norm_back(xhat_one, rstd_one, gains[0], normed_one_grad)).astype(
        BF16
    )

    sums = jnp.sum(dqkv.astype(F32), axis=1)

    def placed(part):
        cols = sums[:, part * hd : (part + 1) * hd]
        line = lax.dynamic_update_slice_in_dim(
            jnp.zeros((width,), F32), cols[:base].reshape(-1), c * base * hd, 0
        )
        return line + jnp.pad(cols[base:].reshape(-1), (main, 0))

    lines = jnp.stack(
        [
            jnp.sum(normed_one_grad * xhat_one, axis=0),
            jnp.sum(normed_two_grad * xhat_two, axis=0),
            jnp.sum(normed_one_grad, axis=0),
            jnp.sum(normed_two_grad, axis=0),
            placed(0),
            placed(2),
            jnp.sum(mid_low.astype(F32), axis=0),
            jnp.sum(cot_rows, axis=0),
        ]
    )
    fc_lines = lax.dynamic_update_slice_in_dim(
        jnp.zeros((n_fsdp, hidden_cols), F32), fc_bias_part[None], f, 0
    )
    count_lines = lines.size
    flat_lines = jnp.concatenate([lines.reshape(-1), fc_lines.reshape(-1)])
    flat_lines = lax.psum(flat_lines, ("ctx", "fsdp"))
    lines = flat_lines[:count_lines].reshape(lines.shape)
    lines = lax.dynamic_slice_in_dim(lines, f * shard, shard, 1)
    fc_bias_grad = lax.dynamic_slice_in_dim(
        flat_lines, count_lines + f * hidden_cols, hidden_cols
    )
    return (
        layer_rows[None],
        tokens_grad[None],
        w_attn_grad,
        w_proj_grad,
        w_fc_grad,
        w_out_grad,
        lines[:2],
        lines[2:],
        fc_bias_grad,
    )


def solution(mesh):
    rows = P("fsdp", "ctx", None)
    weight = P("fsdp", None)
    vectors = P(None, "fsdp")
    return jax.shard_map(
        functools.partial(shards, mesh.shape["ctx"], mesh.shape["fsdp"]),
        mesh=mesh,
        in_specs=(
            rows, weight, weight, weight, weight, weight, vectors, vectors, P("fsdp"), rows,
        ),
        out_specs=(
            rows, rows, weight, weight, weight, weight, vectors, vectors, P("fsdp"),
        ),
        check_vma=False,
    )
```

```python
import functools

import jax
import jax.numpy as jnp
from jax import lax
from jax.experimental import pallas as pl
from jax.experimental.pallas import tpu as pltpu
from jax.sharding import PartitionSpec as P

HEAD_DIM = 64
BLOCK = 128
QROWS = 256
EPS = 1e-05
SCALE = HEAD_DIM ** (-0.5)
F32 = jnp.float32
BF16 = jnp.bfloat16
VMEM_LIMIT = 56 * 1024 * 1024
LAST = (((1,), (1,)), ((), ()))
FIRST = (((0,), (0,)), ((), ()))
MESH = pl.DeviceIdType.MESH
TILE = 256


def dot_last(a, b):
    return lax.dot_general(a, b, LAST, preferred_element_type=F32)


def dot(a, b):
    return jnp.dot(a, b, preferred_element_type=F32)


def dot_first(a, b):
    return lax.dot_general(a, b, FIRST, preferred_element_type=F32)


def flip(place, k, size):
    out = 0
    bit = 1
    while bit < size:
        out = out + (place // bit + k // bit) % 2 * bit
        bit *= 2
    return out

def enter(peers):
    barrier = pltpu.get_barrier_semaphore()
    for peer in peers:
        pl.semaphore_signal(barrier, inc=1, device_id=peer, device_id_type=MESH)
    pl.semaphore_wait(barrier, len(peers))

def send(src, dst, send_sem, recv_sem, peer):
    return pltpu.make_async_remote_copy(
        src_ref=src, dst_ref=dst, send_sem=send_sem, recv_sem=recv_sem,
        device_id=peer, device_id_type=MESH)


def ffn_kernel(n, nt_hbm, cot_hbm, wfc_hbm, wout_hbm, bias_ref,
               gsum_ref, fcb_ref, out_hbm, wout_grad_hbm, wfc_grad_hbm,
               cot_ref, wfc_ref, wout_ref, all_ref, act_ref, hg_ref, ag_ref, part_ref, got_ref, stage_d, stage_h,
               s1, r1, s2, r2, local):
    c = lax.axis_index("ctx")
    f = lax.axis_index("fsdp")
    rows, width = nt_hbm.shape
    enter([(c, flip(f, k, n)) for k in range(1, n)])

    def rows_out(k):
        return send(nt_hbm, all_ref.at[k], s1.at[k], r1.at[k], (c, flip(f, k, n)))

    def grad_back(k):
        return send(part_ref.at[k], got_ref.at[k], s2.at[k], r2.at[k], (c, flip(f, k, n)))

    near = [k for k in range(1, n) if k & (k - 1) == 0]
    far = [k for k in range(1, n) if k not in near]
    for k in near:
        rows_out(k).start()
    loads = [
        pltpu.make_async_copy(nt_hbm, all_ref.at[0], local.at[0]),
        pltpu.make_async_copy(wout_hbm, wout_ref, local.at[1]),
        pltpu.make_async_copy(cot_hbm, cot_ref, local.at[2]),
        pltpu.make_async_copy(wfc_hbm, wfc_ref, local.at[3]),
    ]
    for load in loads:
        load.start()
    fcb_ref[...] = jnp.zeros_like(fcb_ref)
    loads[1].wait()
    loads[2].wait()

    def active_grad(k, carry):
        ag_ref[k] = dot_last(cot_ref[k], wout_ref[...])
        return carry

    lax.fori_loop(0, n, active_grad, 0)
    for k in far:
        rows_out(k).start()
    loads[0].wait()
    loads[3].wait()

    def chunk(k, carry):
        @pl.when(k > 0)
        def _():
            rows_out(k).wait_recv()

        hidden = dot(all_ref[k], wfc_ref[...]) + bias_ref[...]
        square = hidden * hidden
        tanh = jnp.tanh(0.7978845608028654 * (hidden + 0.044715 * square * hidden))
        act_ref[k] = (0.5 * hidden * (1.0 + tanh)).astype(BF16)
        slope = 0.5 * (1.0 + tanh) + 0.5 * hidden * (1.0 - tanh * tanh) * 0.7978845608028654 * (
            1.0 + 3.0 * 0.044715 * square
        )
        grad = (ag_ref[k] * slope).astype(BF16)
        hg_ref[k] = grad
        fcb_ref[...] += jnp.sum(grad.astype(F32), axis=0, keepdims=True)
        part_ref[k] = dot_last(grad, wfc_ref[...]).astype(BF16)

        @pl.when(k > 0)
        def _():
            grad_back(k).start()

        return carry

    lax.fori_loop(0, n, chunk, 0)

    def grads(left_ref, right_ref, dst, stage_ref, base):
        wide = left_ref.shape[2]
        right = right_ref[...].reshape(n * rows, right_ref.shape[2])
        copies = []
        for i, lo in enumerate(range(0, wide, TILE)):
            hi = min(lo + TILE, wide)
            slot = i % 2
            if i >= 2:
                copies[i - 2].wait()
            left = left_ref[:, :, lo:hi].reshape(n * rows, hi - lo)
            stage_ref[slot, : hi - lo] = dot_first(left, right).astype(BF16)
            copies.append(
                pltpu.make_async_copy(
                    stage_ref.at[slot, : hi - lo], dst.at[lo:hi], local.at[base + slot]
                )
            )
            copies[-1].start()
        for copy in copies[-2:]:
            copy.wait()

    grads(act_ref, cot_ref, wout_grad_hbm, stage_d, 4)
    grads(all_ref, hg_ref, wfc_grad_hbm, stage_h, 6)

    def out_copy(k):
        return pltpu.make_async_copy(
            stage_d.at[k % 2, :rows], out_hbm.at[k], local.at[4 + k % 2]
        )

    for k in range(n):
        if k >= 2:
            out_copy(k - 2).wait()
        stage_d[k % 2, :rows] = dot(act_ref[k], wout_ref[...]).astype(BF16)
        out_copy(k).start()

    gsum_ref[...] = part_ref[0].astype(F32)
    for k in near + far:
        grad_back(k).wait_recv()
        gsum_ref[...] += got_ref[k].astype(F32)
    for k in range(1, n):
        rows_out(k).wait_send()
        grad_back(k).wait_send()
    for k in range(max(0, n - 2), n):
        out_copy(k).wait()


def ffn(n, nt, cot, wfc, wout, bias, cid=1):
    m, d = nt.shape
    h = wfc.shape[1]
    vm = pl.BlockSpec(memory_space=pltpu.VMEM)
    anym = pl.BlockSpec(memory_space=pl.ANY)
    return pl.pallas_call(
        functools.partial(ffn_kernel, n),
        in_specs=[anym] * 4 + [vm],
        out_specs=[vm, vm] + [anym] * 3,
        out_shape=[
            jax.ShapeDtypeStruct((m, d), F32),
            jax.ShapeDtypeStruct((1, h), F32),
            jax.ShapeDtypeStruct((n, m, d), BF16),
            jax.ShapeDtypeStruct((h, d), BF16),
            jax.ShapeDtypeStruct((d, h), BF16),
        ],
        scratch_shapes=[
            pltpu.VMEM((n, m, d), BF16),
            pltpu.VMEM((d, h), BF16),
            pltpu.VMEM((h, d), BF16),
            pltpu.VMEM((n, m, d), BF16),
            pltpu.VMEM((n, m, h), BF16),
            pltpu.VMEM((n, m, h), BF16),
            pltpu.VMEM((n, m, h), F32),
            pltpu.VMEM((n, m, d), BF16),
            pltpu.VMEM((n, m, d), BF16),
            pltpu.VMEM((2, max(TILE, m), d), BF16),
            pltpu.VMEM((2, TILE, h), BF16),
        ]
        + [pltpu.SemaphoreType.DMA((n,))] * 4
        + [pltpu.SemaphoreType.DMA((8,))],
        compiler_params=pltpu.CompilerParams(
            collective_id=cid, has_side_effects=True, vmem_limit_bytes=60 * 1024 * 1024
        ),
        name="feed_forward",
    )(nt, cot, wfc, wout, bias)


def lines_kernel(n_ctx, n_fsdp, lead, x_ref, o_ref, got_ref, ss, rs):
    c = lax.axis_index("ctx")
    f = lax.axis_index("fsdp")
    peers = []
    bit = 1
    while bit < n_ctx:
        peers.append((flip(c, bit, n_ctx), f))
        bit *= 2
    ctx_phases = len(peers)
    bit = 1
    while bit < n_fsdp:
        peers.append((c, flip(f, bit, n_fsdp)))
        bit *= 2
    enter(peers)
    o_ref[...] = x_ref[...]
    for i, peer in enumerate(peers):
        rows = x_ref.shape[0] if i < ctx_phases else lead
        copy = send(o_ref.at[:rows], got_ref.at[i, :rows], ss.at[i], rs.at[i], peer)
        copy.start()
        copy.wait()
        o_ref[:rows] += got_ref[i, :rows]


def sum_lines(x, lead, n_ctx, n_fsdp, cid):
    phases = (n_ctx * n_fsdp).bit_length() - 1
    vm = pl.BlockSpec(memory_space=pltpu.VMEM)
    return pl.pallas_call(
        functools.partial(lines_kernel, n_ctx, n_fsdp, lead),
        in_specs=[vm],
        out_specs=vm,
        out_shape=jax.ShapeDtypeStruct(x.shape, F32),
        scratch_shapes=[pltpu.VMEM((phases,) + x.shape, F32)]
        + [pltpu.SemaphoreType.DMA((phases,))] * 2,
        compiler_params=pltpu.CompilerParams(collective_id=cid, has_side_effects=True),
        name="sum_lines",
    )(x)


def qkv_kernel(inv_ref, xa_ref, xb_ref, w_ref, gain_ref, shift_ref, bias_ref, n_ref, o_ref):
    x = jnp.concatenate([xa_ref[...], xb_ref[...]], axis=0).astype(F32)
    mean = jnp.mean(x, axis=1, keepdims=True)
    cen = x - mean
    var = jnp.mean(cen * cen, axis=1, keepdims=True)
    normed = (cen * lax.rsqrt(var + EPS) * gain_ref[...] + shift_ref[...]).astype(BF16)
    n_ref[...] = normed
    for s in range(w_ref.shape[0]):
        o_ref[s] = (dot(normed, w_ref[s]) + bias_ref[s]).astype(BF16)


def qkv_call(inv, x_all, w_slots, gain, shift, bias_slots):
    rows, width = x_all.shape
    slots, _, cols = w_slots.shape
    full = lambda *shape: pl.BlockSpec(shape, lambda i, inv: (0,) * len(shape))
    return pl.pallas_call(
        qkv_kernel,
        grid_spec=pltpu.PrefetchScalarGridSpec(
            num_scalar_prefetch=1,
            grid=(rows // QROWS,),
            in_specs=[
                pl.BlockSpec((BLOCK, width), lambda i, inv: (inv[2 * i], 0)),
                pl.BlockSpec((BLOCK, width), lambda i, inv: (inv[2 * i + 1], 0)),
                full(slots, width, cols),
                full(1, width),
                full(1, width),
                full(slots, 1, cols),
            ],
            out_specs=[
                pl.BlockSpec((QROWS, width), lambda i, inv: (i, 0)),
                pl.BlockSpec((slots, QROWS, cols), lambda i, inv: (0, i, 0)),
            ],
        ),
        out_shape=[
            jax.ShapeDtypeStruct((rows, width), BF16),
            jax.ShapeDtypeStruct((slots, rows, cols), BF16),
        ],
        compiler_params=pltpu.CompilerParams(vmem_limit_bytes=VMEM_LIMIT),
        name="norm_qkv",
    )(inv, x_all, x_all, w_slots, gain, shift, bias_slots)


def causal_scores(k, q_rows, start):
    scores = dot_last(k, q_rows)
    keep = start
    tail = scores[keep:]
    key_id = lax.broadcasted_iota(jnp.int32, tail.shape, 0)
    query_id = lax.broadcasted_iota(jnp.int32, tail.shape, 1)
    tail = jnp.where(key_id <= query_id, tail, -1e30)
    if keep == 0:
        return tail
    return jnp.concatenate([scores[:keep], tail], axis=0)


def soft(scores, v_t):
    top = jnp.max(scores, axis=0, keepdims=True)
    weights = jnp.exp(scores - top)
    total = jnp.sum(weights, axis=0, keepdims=True)
    out = dot(v_t, weights.astype(BF16)) / total
    return out, top + jnp.log(total)


def attn_fwd_kernel(inv_ref, x_ref, o_ref, l_ref):
    rows = x_ref.shape[1]
    hd = HEAD_DIM
    q = x_ref[0, :, :hd] * BF16(SCALE)
    k = x_ref[0, :, hd : 2 * hd]
    v_t = x_ref[0, :, 2 * hd :].T
    for i in range(rows // QROWS):
        lo, hi = i * QROWS, (i + 1) * QROWS
        out, lse = soft(causal_scores(k[:hi], q[lo:hi], lo), v_t[:, :hi])
        l_ref[0, :, lo:hi] = lse
        out = out.astype(BF16)
        for b in range(QROWS // BLOCK):
            o_ref[inv_ref[2 * i + b]] = out[:, b * BLOCK : (b + 1) * BLOCK]


def attn_fwd(inv, qkv, heads):
    rows, cols = qkv.shape[1:]
    blocks = rows // BLOCK
    return pl.pallas_call(
        attn_fwd_kernel,
        grid_spec=pltpu.PrefetchScalarGridSpec(
            num_scalar_prefetch=1,
            grid=(heads,),
            in_specs=[pl.BlockSpec((1, rows, cols), lambda h, inv: (h, 0, 0))],
            out_specs=[
                pl.BlockSpec((blocks, HEAD_DIM, BLOCK), lambda h, inv: (0, h, 0)),
                pl.BlockSpec((1, 1, rows), lambda h, inv: (h, 0, 0)),
            ],
        ),
        out_shape=[
            jax.ShapeDtypeStruct((blocks, heads * HEAD_DIM, BLOCK), BF16),
            jax.ShapeDtypeStruct((heads, 1, rows), F32),
        ],
        compiler_params=pltpu.CompilerParams(vmem_limit_bytes=VMEM_LIMIT),
        name="attn_fwd",
    )(inv, qkv)


def attn_bwd_kernel(inv_ref, x_ref, do_ref, o_ref, l_ref, dx_ref, dk_acc, dv_acc):
    rows = x_ref.shape[1]
    hd = HEAD_DIM
    q = x_ref[0, :, :hd] * BF16(SCALE)
    k = x_ref[0, :, hd : 2 * hd]
    v = x_ref[0, :, 2 * hd :]
    k_t = k.T
    dk_acc[...] = jnp.zeros_like(dk_acc)
    dv_acc[...] = jnp.zeros_like(dv_acc)
    for i in range(rows // QROWS):
        lo, hi = i * QROWS, (i + 1) * QROWS
        ids = [inv_ref[2 * i + b] for b in range(QROWS // BLOCK)]
        do_t = jnp.concatenate([do_ref[b] for b in ids], axis=1)
        o_t = jnp.concatenate([o_ref[b] for b in ids], axis=1)
        inner = jnp.sum(do_t.astype(F32) * o_t.astype(F32), axis=0, keepdims=True)
        probs = jnp.exp(causal_scores(k[:hi], q[lo:hi], lo) - l_ref[0, :, lo:hi])
        dprobs = dot(v[:hi], do_t)
        dscores = (probs * (dprobs - inner)).astype(BF16)
        dv_acc[:hi] += dot_last(probs.astype(BF16), do_t)
        dk_acc[:hi] += dot(dscores, q[lo:hi])
        dq = (dot(k_t[:, :hi], dscores) * SCALE).T
        dx_ref[0, lo:hi, :hd] = dq.astype(BF16)
    dx_ref[0, :, hd : 2 * hd] = dk_acc[...].astype(BF16)
    dx_ref[0, :, 2 * hd :] = dv_acc[...].astype(BF16)


def attn_bwd(inv, qkv, d_out, out, lse, heads):
    rows, cols = qkv.shape[1:]
    blocks = rows // BLOCK
    feat = pl.BlockSpec((blocks, HEAD_DIM, BLOCK), lambda h, inv: (0, h, 0))
    return pl.pallas_call(
        attn_bwd_kernel,
        grid_spec=pltpu.PrefetchScalarGridSpec(
            num_scalar_prefetch=1,
            grid=(heads,),
            in_specs=[
                pl.BlockSpec((1, rows, cols), lambda h, inv: (h, 0, 0)),
                feat,
                feat,
                pl.BlockSpec((1, 1, rows), lambda h, inv: (h, 0, 0)),
            ],
            out_specs=pl.BlockSpec((1, rows, cols), lambda h, inv: (h, 0, 0)),
            scratch_shapes=[pltpu.VMEM((rows, HEAD_DIM), F32)] * 2,
        ),
        out_shape=jax.ShapeDtypeStruct((heads, rows, cols), BF16),
        compiler_params=pltpu.CompilerParams(vmem_limit_bytes=VMEM_LIMIT),
        name="attn_bwd",
    )(inv, qkv, d_out, out, lse)


def own_scores(own_ref, x_ref, k):
    hd = HEAD_DIM
    starts = [pl.multiple_of(own_ref[b] * BLOCK, BLOCK) for b in range(2)]
    q = jnp.concatenate([x_ref[0, pl.ds(s, BLOCK), :] for s in starts], axis=0)[:, :hd]
    q = q * BF16(SCALE)
    scores = dot_last(k, q)
    key_id = lax.broadcasted_iota(jnp.int32, scores.shape, 0)
    lane = lax.broadcasted_iota(jnp.int32, (1, scores.shape[1]), 1)
    place = jnp.where(lane < BLOCK, starts[0] + lane, starts[1] + lane - BLOCK)
    return q, starts, jnp.where(key_id <= place, scores, -1e30)


def rest_fwd_kernel(own_ref, x_ref, o_ref, l_ref):
    hd = HEAD_DIM
    _, _, scores = own_scores(own_ref, x_ref, x_ref[0, :, hd : 2 * hd])
    out, lse = soft(scores, x_ref[0, :, 2 * hd :].T)
    o_ref[0] = out.astype(BF16)
    l_ref[0] = lse


def rest_fwd(own, qkv, base):
    slots, rows, cols = qkv.shape
    rest = slots - base
    return pl.pallas_call(
        rest_fwd_kernel,
        grid_spec=pltpu.PrefetchScalarGridSpec(
            num_scalar_prefetch=1,
            grid=(rest,),
            in_specs=[pl.BlockSpec((1, rows, cols), lambda h, own: (base + h, 0, 0))],
            out_specs=[
                pl.BlockSpec((1, HEAD_DIM, QROWS), lambda h, own: (h, 0, 0)),
                pl.BlockSpec((1, 1, QROWS), lambda h, own: (h, 0, 0)),
            ],
        ),
        out_shape=[
            jax.ShapeDtypeStruct((rest, HEAD_DIM, QROWS), BF16),
            jax.ShapeDtypeStruct((rest, 1, QROWS), F32),
        ],
        compiler_params=pltpu.CompilerParams(vmem_limit_bytes=VMEM_LIMIT),
        name="rest_fwd",
    )(own, qkv)


def rest_bwd_kernel(own_ref, x_ref, do_ref, o_ref, l_ref, dx_ref):
    hd = HEAD_DIM
    k = x_ref[0, :, hd : 2 * hd]
    q, starts, scores = own_scores(own_ref, x_ref, k)
    do_t = do_ref[0]
    inner = jnp.sum(do_t.astype(F32) * o_ref[0].astype(F32), axis=0, keepdims=True)
    probs = jnp.exp(scores - l_ref[0])
    dprobs = dot(x_ref[0, :, 2 * hd :], do_t)
    dscores = (probs * (dprobs - inner)).astype(BF16)
    dx_ref[0, :, 2 * hd :] = dot_last(probs.astype(BF16), do_t).astype(BF16)
    dx_ref[0, :, hd : 2 * hd] = dot(dscores, q).astype(BF16)
    dq = (dot(k.T, dscores) * SCALE).T.astype(BF16)
    dx_ref[0, :, :hd] = jnp.zeros((dx_ref.shape[1], hd), BF16)
    for b, s in enumerate(starts):
        dx_ref[0, pl.ds(s, BLOCK), :hd] = dq[b * BLOCK : (b + 1) * BLOCK]


def rest_bwd(own, qkv, d_out, out, lse, base):
    slots, rows, cols = qkv.shape
    rest = slots - base
    feat = pl.BlockSpec((1, HEAD_DIM, QROWS), lambda h, own: (h, 0, 0))
    return pl.pallas_call(
        rest_bwd_kernel,
        grid_spec=pltpu.PrefetchScalarGridSpec(
            num_scalar_prefetch=1,
            grid=(rest,),
            in_specs=[
                pl.BlockSpec((1, rows, cols), lambda h, own: (base + h, 0, 0)),
                feat,
                feat,
                pl.BlockSpec((1, 1, QROWS), lambda h, own: (h, 0, 0)),
            ],
            out_specs=pl.BlockSpec((1, rows, cols), lambda h, own: (h, 0, 0)),
        ),
        out_shape=jax.ShapeDtypeStruct((rest, rows, cols), BF16),
        compiler_params=pltpu.CompilerParams(vmem_limit_bytes=VMEM_LIMIT),
        name="rest_bwd",
    )(own, qkv, d_out, out, lse)


def assemble_kernel(own_ref, rest_ref, o_ref):
    hd = HEAD_DIM
    width = o_ref.shape[1] // 3
    count = own_ref.shape[0]
    for h in range(width // hd):
        src = own_ref.at[h] if h < count else rest_ref.at[h - count]
        for part in range(3):
            at = part * width + h * hd
            o_ref[:, at : at + hd] = src[:, part * hd : (part + 1) * hd].astype(F32)


def assemble(own, rest, out_cols):
    rows = own.shape[1]
    return pl.pallas_call(
        assemble_kernel,
        out_shape=jax.ShapeDtypeStruct((rows, out_cols), F32),
        compiler_params=pltpu.CompilerParams(vmem_limit_bytes=VMEM_LIMIT),
        name="assemble",
    )(own, rest)


def norm_parts(rows):
    mean = jnp.mean(rows, axis=-1, keepdims=True)
    cen = rows - mean
    rstd = lax.rsqrt(jnp.mean(cen * cen, axis=-1, keepdims=True) + EPS)
    return cen * rstd, rstd


def norm_back(xhat, rstd, gain, grad):
    dxhat = grad * gain
    return rstd * (
        dxhat
        - jnp.mean(dxhat, axis=-1, keepdims=True)
        - xhat * jnp.mean(dxhat * xhat, axis=-1, keepdims=True)
    )


def swap(value, axis, size, k):
    return lax.ppermute(value, axis, [(i, i ^ k) for i in range(size)])


def shards(
    n_ctx,
    n_fsdp,
    tokens,
    block_order,
    w_attn,
    w_proj,
    w_fc,
    w_out,
    norm_gains,
    biases,
    fc_bias,
    cotangent,
):
    hd = HEAD_DIM
    count, width = tokens.shape[1:]
    shard = width // n_fsdp
    heads = width // hd
    base = heads // n_ctx
    rest = heads - base * n_ctx
    slots = base + rest
    own_blocks = count // BLOCK
    c = lax.axis_index("ctx")
    f = lax.axis_index("fsdp")

    order = block_order[0]
    inv = jnp.argsort(order).astype(jnp.int32)
    own = lax.dynamic_slice_in_dim(order, c * own_blocks, own_blocks)

    x_all = lax.all_gather(tokens[0], "ctx", axis=0, tiled=True)

    def head_cols(h):
        return jnp.concatenate(
            [
                lax.dynamic_slice(w_attn, (0, part * width + h * hd), (shard, hd))
                for part in range(3)
            ],
            axis=1,
        )

    slot_heads = [c * base + s for s in range(base)] + [n_ctx * base + r for r in range(rest)]
    w_slots = jnp.stack([head_cols(h) for h in slot_heads])
    w_slots = lax.all_gather(w_slots, "fsdp", axis=1, tiled=True)
    small = lax.all_gather(
        jnp.concatenate([norm_gains, biases], axis=0), "fsdp", axis=1, tiled=True
    ).astype(F32)
    gains, shifts = small[:2], small[2:]
    full_proj = lax.all_gather(w_proj, "fsdp", axis=0, tiled=True)
    hidden_cols = w_fc.shape[1] // n_fsdp
    fc_parts = jnp.stack(
        [w_fc[:, j * hidden_cols : (j + 1) * hidden_cols] for j in range(n_fsdp)]
    )
    fc_cols = jnp.zeros_like(fc_parts)
    for k in range(n_fsdp):
        piece = lax.dynamic_index_in_dim(fc_parts, f ^ k, keepdims=True)
        if k:
            piece = swap(piece, "fsdp", n_fsdp, k)
        fc_cols = lax.dynamic_update_slice(fc_cols, piece, (f ^ k, 0, 0))
    fc_cols = fc_cols.reshape(width, hidden_cols)
    cot = cotangent[0]

    def from_fsdp(own_rows):
        return jnp.concatenate(
            [own_rows] + [swap(own_rows, "fsdp", n_fsdp, k) for k in range(1, n_fsdp)]
        )

    def to_fsdp(part):
        return sum(
            swap(part[k], "fsdp", n_fsdp, k).astype(F32) if k else part[k].astype(F32)
            for k in range(n_fsdp)
        )

    cot_all = from_fsdp(cot)

    zero_bias = jnp.zeros((hd,), F32)
    bias_slots = jnp.stack(
        [
            jnp.concatenate(
                [
                    lax.dynamic_slice_in_dim(shifts[2], h * hd, hd),
                    zero_bias,
                    lax.dynamic_slice_in_dim(shifts[3], h * hd, hd),
                ]
            )[None]
            for h in slot_heads
        ]
    )
    normed_one, qkv = qkv_call(inv, x_all, w_slots, gains[:1], shifts[:1], bias_slots)
    out_own, lse_own = attn_fwd(inv, qkv, base)
    got = lax.all_to_all(out_own, "ctx", split_axis=0, concat_axis=0, tiled=True)
    got = got.reshape(n_ctx, own_blocks, base * hd, BLOCK).transpose(1, 3, 0, 2)
    attended = got.reshape(count, n_ctx * base * hd)
    if rest:
        out_rest, lse_rest = rest_fwd(own, qkv, base)
        attended = jnp.concatenate([attended, out_rest.reshape(rest * hd, count).T], axis=1)

    rows = tokens[0].astype(F32)
    mid = rows + (dot(attended, full_proj) + shifts[4])
    xhat_two, rstd_two = norm_parts(mid)
    normed_two = (xhat_two * gains[1] + shifts[1]).astype(BF16)

    normed_two_grad, fc_bias_part, out_part, w_out_part, w_fc_part = ffn(
        n_fsdp,
        normed_two,
        cot_all.reshape(n_fsdp, count, width),
        fc_cols,
        w_out,
        fc_bias.astype(F32)[None],
    )
    layer_rows = (mid + (to_fsdp(out_part) + shifts[5])).astype(BF16)
    w_fc_part = w_fc_part.reshape(n_fsdp, shard, hidden_cols)
    fc_recv = []
    for k in range(n_fsdp):
        piece = lax.dynamic_index_in_dim(w_fc_part, f ^ k, keepdims=False)
        fc_recv.append(swap(piece, "fsdp", n_fsdp, k) if k else piece)
    w_out_low, w_fc_low = lax.psum((w_out_part, jnp.stack(fc_recv)), "ctx")
    w_out_grad = w_out_low.astype(F32)
    w_fc_grad = jnp.concatenate(
        [lax.dynamic_index_in_dim(w_fc_low, f ^ j, keepdims=False) for j in range(n_fsdp)],
        axis=1,
    ).astype(F32)

    cot_rows = cot.astype(F32)
    mid_grad = cot_rows + norm_back(xhat_two, rstd_two, gains[1], normed_two_grad)
    mid_low = mid_grad.astype(BF16)
    over_rows = functools.partial(jnp.einsum, "ta,tb->ab", preferred_element_type=F32)
    attended_grad = dot_last(mid_low, full_proj).astype(BF16)
    w_proj_part = over_rows(attended, mid_low).astype(BF16)
    w_proj_part = w_proj_part.reshape(n_fsdp, shard, width)
    w_proj_part = sum(
        swap(
            lax.dynamic_index_in_dim(w_proj_part, f ^ k, keepdims=False), "fsdp", n_fsdp, k
        ).astype(F32)
        if k
        else lax.dynamic_index_in_dim(w_proj_part, f, keepdims=False).astype(F32)
        for k in range(n_fsdp)
    ).astype(BF16)

    main = n_ctx * base * hd
    sent = attended_grad[:, :main].reshape(own_blocks, BLOCK, n_ctx, base * hd)
    sent = sent.transpose(2, 0, 3, 1).reshape(n_ctx * own_blocks, base * hd, BLOCK)
    d_out = lax.all_to_all(sent, "ctx", split_axis=0, concat_axis=0, tiled=True)
    dqkv = attn_bwd(inv, qkv, d_out, out_own, lse_own, base)
    if rest:
        d_rest = attended_grad[:, main:].T.reshape(rest, hd, count)
        dqkv = jnp.concatenate(
            [dqkv, rest_bwd(own, qkv, d_rest, out_rest, lse_rest, base)], axis=0
        )
    flat = dqkv.transpose(1, 0, 2).reshape(x_all.shape[0], slots * 3 * hd)
    flat_w = w_slots.transpose(1, 0, 2).reshape(width, slots * 3 * hd)
    one_part = dot_last(flat, flat_w).astype(BF16)
    one_part = one_part.reshape(-1, BLOCK, width)[order].reshape(one_part.shape)
    normed_one_grad = lax.psum_scatter(
        one_part, "ctx", scatter_dimension=0, tiled=True
    ).astype(F32)
    slot_part = jnp.einsum("td,hte->hde", normed_one, dqkv, preferred_element_type=F32)
    slot_part = slot_part.astype(BF16)

    def slot_rows(k):
        return lax.dynamic_slice_in_dim(slot_part, (f ^ k) * shard, shard, 1)

    slot_sum = slot_rows(0).astype(F32)
    for k in range(1, n_fsdp):
        slot_sum += swap(slot_rows(k), "fsdp", n_fsdp, k).astype(F32)
    slot_sum = slot_sum.astype(BF16)
    own_cols = lax.all_gather(slot_sum[:base], "ctx", axis=0, tiled=True)
    w_proj_part, rest_part, _, _ = lax.optimization_barrier(
        (w_proj_part, slot_sum[base:], w_out_low, w_fc_low)
    )
    w_proj_low, rest_cols = lax.psum((w_proj_part, rest_part), "ctx")
    w_proj_grad = w_proj_low.astype(F32)
    if not rest:
        rest_cols = own_cols
    w_attn_grad = assemble(own_cols, rest_cols, 3 * width)

    xhat_one, rstd_one = norm_parts(rows)
    tokens_grad = (mid_grad + norm_back(xhat_one, rstd_one, gains[0], normed_one_grad)).astype(
        BF16
    )

    sums = jnp.sum(dqkv.astype(F32), axis=1)

    def placed(part):
        cols = sums[:, part * hd : (part + 1) * hd]
        line = lax.dynamic_update_slice_in_dim(
            jnp.zeros((width,), F32), cols[:base].reshape(-1), c * base * hd, 0
        )
        return line + jnp.pad(cols[base:].reshape(-1), (main, 0))

    lines = jnp.stack(
        [
            jnp.sum(normed_one_grad * xhat_one, axis=0),
            jnp.sum(normed_two_grad * xhat_two, axis=0),
            jnp.sum(normed_one_grad, axis=0),
            jnp.sum(normed_two_grad, axis=0),
            placed(0),
            placed(2),
            jnp.sum(mid_low.astype(F32), axis=0),
            jnp.sum(cot_rows, axis=0),
        ]
    )
    lead = lines.shape[0]
    tail = jnp.pad(fc_bias_part, ((0, 7), (0, max(0, width - hidden_cols))))
    lines = sum_lines(jnp.concatenate([lines, tail]), lead, n_ctx, n_fsdp, 2)
    fc_bias_grad = lines[lead, :hidden_cols]
    lines = lax.dynamic_slice_in_dim(lines[:lead], f * shard, shard, 1)
    return (
        layer_rows[None],
        tokens_grad[None],
        w_attn_grad,
        w_proj_grad,
        w_fc_grad,
        w_out_grad,
        lines[:2],
        lines[2:],
        fc_bias_grad,
    )


def solution(mesh):
    rows = P("fsdp", "ctx", None)
    weight = P("fsdp", None)
    vectors = P(None, "fsdp")
    return jax.shard_map(
        functools.partial(shards, mesh.shape["ctx"], mesh.shape["fsdp"]),
        mesh=mesh,
        in_specs=(
            rows, weight, weight, weight, weight, weight, vectors, vectors, P("fsdp"), rows,
        ),
        out_specs=(
            rows, rows, weight, weight, weight, weight, vectors, vectors, P("fsdp"),
        ),
        check_vma=False,
    )
```

```python
import functools

import jax
import jax.numpy as jnp
from jax import lax
from jax.experimental import pallas as pl
from jax.experimental.pallas import tpu as pltpu
from jax.sharding import PartitionSpec as P

HEAD_DIM = 64
BLOCK = 128
QROWS = 256
EPS = 1e-05
SCALE = HEAD_DIM ** (-0.5)
F32 = jnp.float32
BF16 = jnp.bfloat16
VMEM_LIMIT = 56 * 1024 * 1024
LAST = (((1,), (1,)), ((), ()))
FIRST = (((0,), (0,)), ((), ()))
MESH = pl.DeviceIdType.MESH
TILE = 256


def dot_last(a, b):
    return lax.dot_general(a, b, LAST, preferred_element_type=F32)


def dot(a, b):
    return jnp.dot(a, b, preferred_element_type=F32)


def dot_first(a, b):
    return lax.dot_general(a, b, FIRST, preferred_element_type=F32)


def flip(place, k, size):
    out = 0
    bit = 1
    while bit < size:
        out = out + (place // bit + k // bit) % 2 * bit
        bit *= 2
    return out

def enter(peers):
    barrier = pltpu.get_barrier_semaphore()
    for peer in peers:
        pl.semaphore_signal(barrier, inc=1, device_id=peer, device_id_type=MESH)
    pl.semaphore_wait(barrier, len(peers))

def send(src, dst, send_sem, recv_sem, peer):
    return pltpu.make_async_remote_copy(
        src_ref=src, dst_ref=dst, send_sem=send_sem, recv_sem=recv_sem,
        device_id=peer, device_id_type=MESH)


def ffn_kernel(n, nt_hbm, cot_hbm, wfc_hbm, wout_hbm, bias_ref,
               gsum_ref, fcb_ref, out_hbm, wout_grad_hbm, wfc_grad_hbm,
               cot_ref, wfc_ref, wout_ref, all_ref, act_ref, hg_ref, ag_ref, part_ref, got_ref, stage_d, stage_h,
               s1, r1, s2, r2, local):
    c = lax.axis_index("ctx")
    f = lax.axis_index("fsdp")
    rows, width = nt_hbm.shape
    enter([(c, flip(f, k, n)) for k in range(1, n)])

    def rows_out(k):
        return send(nt_hbm, all_ref.at[f], s1.at[k], r1.at[k], (c, flip(f, k, n)))

    def grad_back(k):
        other = flip(f, k, n)
        return send(part_ref.at[other], got_ref.at[k], s2.at[k], r2.at[k], (c, other))

    near = [k for k in range(1, n) if k & (k - 1) == 0]
    far = [k for k in range(1, n) if k not in near]
    for k in near:
        rows_out(k).start()
    loads = [
        pltpu.make_async_copy(nt_hbm, all_ref.at[f], local.at[0]),
        pltpu.make_async_copy(wout_hbm, wout_ref, local.at[1]),
        pltpu.make_async_copy(cot_hbm, cot_ref, local.at[2]),
        pltpu.make_async_copy(wfc_hbm, wfc_ref, local.at[3]),
    ]
    for load in loads:
        load.start()
    fcb_ref[...] = jnp.zeros_like(fcb_ref)
    loads[1].wait()
    loads[2].wait()

    def active_grad(k, carry):
        ag_ref[k] = dot_last(cot_ref[k], wout_ref[...])
        return carry

    lax.fori_loop(0, n, active_grad, 0)
    for k in far:
        rows_out(k).start()
    loads[0].wait()
    loads[3].wait()

    def chunk(k, carry):
        src = flip(f, k, n)

        @pl.when(k > 0)
        def _():
            rows_out(k).wait_recv()

        hidden = dot(all_ref[src], wfc_ref[...]) + bias_ref[...]
        square = hidden * hidden
        tanh = jnp.tanh(0.7978845608028654 * (hidden + 0.044715 * square * hidden))
        act_ref[src] = (0.5 * hidden * (1.0 + tanh)).astype(BF16)
        slope = 0.5 * (1.0 + tanh) + 0.5 * hidden * (1.0 - tanh * tanh) * 0.7978845608028654 * (
            1.0 + 3.0 * 0.044715 * square
        )
        grad = (ag_ref[src] * slope).astype(BF16)
        hg_ref[src] = grad
        fcb_ref[...] += jnp.sum(grad.astype(F32), axis=0, keepdims=True)
        part_ref[src] = dot_last(grad, wfc_ref[...]).astype(BF16)

        @pl.when(k > 0)
        def _():
            grad_back(k).start()

        return carry

    lax.fori_loop(0, n, chunk, 0)

    def grads(left_ref, right_ref, dst, stage_ref, base):
        wide = left_ref.shape[2]
        right = right_ref[...].reshape(n * rows, right_ref.shape[2])
        copies = []
        for i, lo in enumerate(range(0, wide, TILE)):
            hi = min(lo + TILE, wide)
            slot = i % 2
            if i >= 2:
                copies[i - 2].wait()
            left = left_ref[:, :, lo:hi].reshape(n * rows, hi - lo)
            stage_ref[slot, : hi - lo] = dot_first(left, right).astype(BF16)
            copies.append(
                pltpu.make_async_copy(
                    stage_ref.at[slot, : hi - lo], dst.at[lo:hi], local.at[base + slot]
                )
            )
            copies[-1].start()
        for copy in copies[-2:]:
            copy.wait()

    grads(act_ref, cot_ref, wout_grad_hbm, stage_d, 4)
    grads(all_ref, hg_ref, wfc_grad_hbm, stage_h, 6)

    def out_copy(k):
        return pltpu.make_async_copy(
            stage_d.at[k % 2, :rows], out_hbm.at[k], local.at[4 + k % 2]
        )

    for k in range(n):
        if k >= 2:
            out_copy(k - 2).wait()
        stage_d[k % 2, :rows] = dot(act_ref[k], wout_ref[...]).astype(BF16)
        out_copy(k).start()

    gsum_ref[...] = part_ref[f].astype(F32)
    for k in near + far:
        grad_back(k).wait_recv()
        gsum_ref[...] += got_ref[k].astype(F32)
    for k in range(1, n):
        rows_out(k).wait_send()
        grad_back(k).wait_send()
    for k in range(max(0, n - 2), n):
        out_copy(k).wait()


def ffn(n, nt, cot, wfc, wout, bias, cid=1):
    m, d = nt.shape
    h = wfc.shape[1]
    vm = pl.BlockSpec(memory_space=pltpu.VMEM)
    anym = pl.BlockSpec(memory_space=pl.ANY)
    return pl.pallas_call(
        functools.partial(ffn_kernel, n),
        in_specs=[anym] * 4 + [vm],
        out_specs=[vm, vm] + [anym] * 3,
        out_shape=[
            jax.ShapeDtypeStruct((m, d), F32),
            jax.ShapeDtypeStruct((1, h), F32),
            jax.ShapeDtypeStruct((n, m, d), BF16),
            jax.ShapeDtypeStruct((h, d), BF16),
            jax.ShapeDtypeStruct((d, h), BF16),
        ],
        scratch_shapes=[
            pltpu.VMEM((n, m, d), BF16),
            pltpu.VMEM((d, h), BF16),
            pltpu.VMEM((h, d), BF16),
            pltpu.VMEM((n, m, d), BF16),
            pltpu.VMEM((n, m, h), BF16),
            pltpu.VMEM((n, m, h), BF16),
            pltpu.VMEM((n, m, h), F32),
            pltpu.VMEM((n, m, d), BF16),
            pltpu.VMEM((n, m, d), BF16),
            pltpu.VMEM((2, max(TILE, m), d), BF16),
            pltpu.VMEM((2, TILE, h), BF16),
        ]
        + [pltpu.SemaphoreType.DMA((n,))] * 4
        + [pltpu.SemaphoreType.DMA((8,))],
        compiler_params=pltpu.CompilerParams(
            collective_id=cid, has_side_effects=True, vmem_limit_bytes=60 * 1024 * 1024
        ),
        name="feed_forward",
    )(nt, cot, wfc, wout, bias)


def lines_kernel(n_ctx, n_fsdp, lead, x_ref, o_ref, got_ref, ss, rs):
    c = lax.axis_index("ctx")
    f = lax.axis_index("fsdp")
    peers = []
    bit = 1
    while bit < n_ctx:
        peers.append((flip(c, bit, n_ctx), f))
        bit *= 2
    ctx_phases = len(peers)
    bit = 1
    while bit < n_fsdp:
        peers.append((c, flip(f, bit, n_fsdp)))
        bit *= 2
    enter(peers)
    o_ref[...] = x_ref[...]
    for i, peer in enumerate(peers):
        rows = x_ref.shape[0] if i < ctx_phases else lead
        copy = send(o_ref.at[:rows], got_ref.at[i, :rows], ss.at[i], rs.at[i], peer)
        copy.start()
        copy.wait()
        o_ref[:rows] += got_ref[i, :rows]


def sum_lines(x, lead, n_ctx, n_fsdp, cid):
    phases = (n_ctx * n_fsdp).bit_length() - 1
    vm = pl.BlockSpec(memory_space=pltpu.VMEM)
    return pl.pallas_call(
        functools.partial(lines_kernel, n_ctx, n_fsdp, lead),
        in_specs=[vm],
        out_specs=vm,
        out_shape=jax.ShapeDtypeStruct(x.shape, F32),
        scratch_shapes=[pltpu.VMEM((phases,) + x.shape, F32)]
        + [pltpu.SemaphoreType.DMA((phases,))] * 2,
        compiler_params=pltpu.CompilerParams(collective_id=cid, has_side_effects=True),
        name="sum_lines",
    )(x)


def start_kernel(
    n_ctx,
    n_fsdp,
    base,
    tok_hbm,
    w_hbm,
    small_ref,
    proj_hbm,
    fc_hbm,
    n_hbm,
    qkv_hbm,
    proj_all,
    fc_all,
    w_ref,
    lines_ref,
    n_ref,
    qkv_ref,
    x_ref,
    wg_ref,
    sg_ref,
    tok_recv,
    right_sem,
    left_sem,
    twin_sem,
    w_send,
    w_recv,
    s_send,
    s_recv,
    proj_send,
    proj_recv,
    fc_send,
    fc_recv,
    local,
):
    c = lax.axis_index("ctx")
    f = lax.axis_index("fsdp")
    chips = n_ctx // 2
    chip, core = c // 2, c % 2
    slots, width, cols = w_ref.shape
    shard = width // n_fsdp
    hd = HEAD_DIM
    enter(
        [(lax.rem(c + i, n_ctx), f) for i in range(1, n_ctx)]
        + [(c, flip(f, k, n_fsdp)) for k in range(1, n_fsdp)]
    )

    def block(at, same):
        return 2 * at + (core if same else 1 - core)

    def hop(step, to_right, from_own):
        origin = block(chip - step if to_right else chip + step, True)
        src = tok_hbm if from_own else x_ref.at[origin]
        sem = (right_sem if to_right else left_sem).at[step]
        peer = (c + 2 if to_right else c - 2, f)
        return send(src, x_ref.at[origin], sem, tok_recv.at[origin], peer)

    def twin(at, from_own):
        origin = block(at, True)
        src = tok_hbm if from_own else x_ref.at[origin]
        return send(
            src, x_ref.at[origin], twin_sem.at[at], tok_recv.at[origin], (block(chip, False), f)
        )

    def w_copy(k):
        return send(w_hbm, wg_ref.at[f], w_send.at[k], w_recv.at[k], (c, flip(f, k, n_fsdp)))

    def s_copy(k):
        return send(small_ref, sg_ref.at[f], s_send.at[k], s_recv.at[k], (c, flip(f, k, n_fsdp)))

    cut = shard // 32 * 16 if shard % 16 == 0 else 0
    shares = ((0, cut), (cut, shard)) if cut else ((0, shard), (0, shard))

    def weight_copy(share, k, onward, which):
        lo, hi = share
        other = flip(f, k, n_fsdp)
        dst = (proj_all, fc_all)[which]
        ss = (proj_send, fc_send)[which]
        rs = (proj_recv, fc_recv)[which]
        if onward:
            part = dst.at[other, lo:hi]
            return send(part, part, ss.at[1, k], rs.at[1, k], (block(chip, False), f))
        src = fc_hbm.at[other, lo:hi] if which else proj_hbm.at[lo:hi]
        return send(src, dst.at[f, lo:hi], ss.at[0, k], rs.at[0, k], (c, other))

    def by_core(act):
        for h in range(2):

            @pl.when(core == h)
            def _(h=h):
                act(shares[h], shares[1 - h])

    def weights_start(mine, theirs):
        for i in range(2):
            for k in range(1, n_fsdp):
                weight_copy(mine, k, False, i).start()

    def weights_onward(mine, theirs):
        for i in range(2):
            for k in range(1, n_fsdp):
                weight_copy(mine, k, False, i).wait_recv()
                if cut:
                    weight_copy(mine, k, True, i).start()

    def weights_done(mine, theirs):
        for i in range(2):
            for k in range(1, n_fsdp):
                if cut:
                    weight_copy(theirs, k, True, i).wait_recv()
                    weight_copy(mine, k, True, i).wait_send()
                weight_copy(mine, k, False, i).wait_send()

    for k in range(1, n_fsdp):
        s_copy(k).start()

    @pl.when(chip < chips - 1)
    def _():
        hop(0, True, True).start()

    @pl.when(chip > 0)
    def _():
        hop(0, False, True).start()

    for k in range(1, n_fsdp):
        w_copy(k).start()
    twin(chip, True).start()
    own_x = pltpu.make_async_copy(tok_hbm, x_ref.at[c], local.at[0])
    own_w = pltpu.make_async_copy(w_hbm, wg_ref.at[f], local.at[1])
    own_proj = pltpu.make_async_copy(proj_hbm, proj_all.at[f], local.at[2])
    own_fc = pltpu.make_async_copy(fc_hbm.at[f], fc_all.at[f], local.at[3])
    for copy in (own_x, own_w, own_proj, own_fc):
        copy.start()
    sg_ref[f] = small_ref[...]
    for k in range(1, n_fsdp):
        s_copy(k).wait_recv()
    for j in range(n_fsdp):
        lines_ref[:, j * shard : (j + 1) * shard] = sg_ref[j]
    main = n_ctx * base * hd
    row_id = lax.broadcasted_iota(jnp.int32, (width, slots * hd), 0)
    col_id = lax.broadcasted_iota(jnp.int32, (width, slots * hd), 1)
    wanted = jnp.where(col_id < base * hd, c * base * hd + col_id, main + col_id - base * hd)
    picked = dot(lines_ref[...].astype(BF16), (row_id == wanted).astype(BF16))
    zero = jnp.zeros((1, hd), F32)
    bias = [
        jnp.concatenate(
            [picked[4:5, s * hd : (s + 1) * hd], zero, picked[5:6, s * hd : (s + 1) * hd]], axis=1
        )
        for s in range(slots)
    ]
    own_w.wait()
    own_x.wait()
    for k in range(1, n_fsdp):
        w_copy(k).wait_recv()
    by_core(weights_start)
    for j in range(n_fsdp):
        w_ref[:, j * shard : (j + 1) * shard, :] = wg_ref[j]

    def results(origin):
        return (
            pltpu.make_async_copy(n_ref, n_hbm.at[origin], local.at[0]),
            pltpu.make_async_copy(qkv_ref, qkv_hbm.at[:, origin], local.at[1]),
        )

    def project(at, same, first=False):
        origin = block(at, same)
        rows = x_ref[origin].astype(F32)
        mean = jnp.mean(rows, axis=1, keepdims=True)
        cen = rows - mean
        var = jnp.mean(cen * cen, axis=1, keepdims=True)
        normed = cen * lax.rsqrt(var + EPS) * lines_ref[0:1] + lines_ref[2:3]
        normed = normed.astype(BF16)

        @pl.when(jnp.logical_not(first))
        def _():
            for copy in results(origin):
                copy.wait()

        n_ref[...] = normed
        for s in range(slots):
            qkv_ref[s] = (dot(normed, w_ref[s]) + bias[s]).astype(BF16)
        for copy in results(origin):
            copy.start()

    def arrived(at, same):
        origin = block(at, same)
        pltpu.make_async_copy(x_ref.at[origin], x_ref.at[origin], tok_recv.at[origin]).wait()

    def step(s, carry):
        @pl.when((s > 0) & (chip - s >= 0))
        def _():
            arrived(chip - s, True)
            twin(chip - s, False).start()

            @pl.when(chip < chips - 1)
            def _():
                hop(s, True, False).start()

        @pl.when((s > 0) & (chip + s < chips))
        def _():
            arrived(chip + s, True)
            twin(chip + s, False).start()

            @pl.when(chip > 0)
            def _():
                hop(s, False, False).start()

        @pl.when(chip - s >= 0)
        def _():
            project(chip - s, True, s == 0)

        @pl.when((s > 0) & (chip + s < chips))
        def _():
            project(chip + s, True)

        @pl.when(chip - s >= 0)
        def _():
            arrived(chip - s, False)
            project(chip - s, False)

        @pl.when((s > 0) & (chip + s < chips))
        def _():
            arrived(chip + s, False)
            project(chip + s, False)

        return carry

    lax.fori_loop(0, chips, step, 0)
    by_core(weights_onward)
    for copy in results(c):
        copy.wait()
    own_proj.wait()
    own_fc.wait()

    for s in range(chips):
        if s < chips - 1:

            @pl.when((chip - s >= 0) & (chip < chips - 1))
            def _():
                hop(s, True, False).wait_send()

            @pl.when((chip + s < chips) & (chip > 0))
            def _():
                hop(s, False, False).wait_send()

        twin(s, False).wait_send()
    for k in range(1, n_fsdp):
        w_copy(k).wait_send()
        s_copy(k).wait_send()
    by_core(weights_done)


def start_call(n_ctx, n_fsdp, base, tok, w_slots, small, w_proj, fc_parts, cid):
    count, width = tok.shape
    slots, shard, cols = w_slots.shape
    vm = pl.BlockSpec(memory_space=pltpu.VMEM)
    anym = pl.BlockSpec(memory_space=pl.ANY)
    dma = pltpu.SemaphoreType.DMA
    return pl.pallas_call(
        functools.partial(start_kernel, n_ctx, n_fsdp, base),
        in_specs=[anym, anym, vm, anym, anym],
        out_specs=[anym, anym, anym, anym, vm, vm],
        out_shape=[
            jax.ShapeDtypeStruct((n_ctx, count, width), BF16),
            jax.ShapeDtypeStruct((slots, n_ctx, count, cols), BF16),
            jax.ShapeDtypeStruct((n_fsdp,) + w_proj.shape, BF16),
            jax.ShapeDtypeStruct(fc_parts.shape, BF16),
            jax.ShapeDtypeStruct((slots, width, cols), BF16),
            jax.ShapeDtypeStruct((small.shape[0], width), F32),
        ],
        scratch_shapes=[
            pltpu.VMEM((count, width), BF16),
            pltpu.VMEM((slots, count, cols), BF16),
            pltpu.VMEM((n_ctx, count, width), BF16),
            pltpu.VMEM((n_fsdp, slots, shard, cols), BF16),
            pltpu.VMEM((n_fsdp,) + small.shape, F32),
            dma((n_ctx,)),
            dma((n_ctx // 2,)),
            dma((n_ctx // 2,)),
            dma((n_ctx // 2,)),
            dma((n_fsdp,)),
            dma((n_fsdp,)),
            dma((n_fsdp,)),
            dma((n_fsdp,)),
            dma((2, n_fsdp)),
            dma((2, n_fsdp)),
            dma((2, n_fsdp)),
            dma((2, n_fsdp)),
            dma((4,)),
        ],
        compiler_params=pltpu.CompilerParams(
            collective_id=cid, has_side_effects=True, vmem_limit_bytes=VMEM_LIMIT
        ),
        name="tokens_qkv",
    )(tok, w_slots, small, w_proj, fc_parts)


def causal_scores(k, q_rows, start):
    scores = dot_last(k, q_rows)
    keep = start
    tail = scores[keep:]
    key_id = lax.broadcasted_iota(jnp.int32, tail.shape, 0)
    query_id = lax.broadcasted_iota(jnp.int32, tail.shape, 1)
    tail = jnp.where(key_id <= query_id, tail, -1e30)
    if keep == 0:
        return tail
    return jnp.concatenate([scores[:keep], tail], axis=0)


def soft(scores, v_t):
    top = jnp.max(scores, axis=0, keepdims=True)
    weights = jnp.exp(scores - top)
    total = jnp.sum(weights, axis=0, keepdims=True)
    out = dot(v_t, weights.astype(BF16)) / total
    return out, top + jnp.log(total)


def causal(inv_ref, x_ref):
    return jnp.concatenate([x_ref[0, inv_ref[i]] for i in range(x_ref.shape[1])], axis=0)


def attn_fwd_kernel(inv_ref, x_ref, o_ref, l_ref):
    rows = l_ref.shape[2]
    hd = HEAD_DIM
    x = causal(inv_ref, x_ref)
    q = x[:, :hd] * BF16(SCALE)
    k = x[:, hd : 2 * hd]
    v_t = x[:, 2 * hd :].T
    for i in range(rows // QROWS):
        lo, hi = i * QROWS, (i + 1) * QROWS
        out, lse = soft(causal_scores(k[:hi], q[lo:hi], lo), v_t[:, :hi])
        l_ref[0, :, lo:hi] = lse
        out = out.astype(BF16)
        for b in range(QROWS // BLOCK):
            o_ref[inv_ref[2 * i + b]] = out[:, b * BLOCK : (b + 1) * BLOCK]


def attn_fwd(inv, qkv, heads):
    blocks, _, cols = qkv.shape[1:]
    rows = blocks * BLOCK
    return pl.pallas_call(
        attn_fwd_kernel,
        grid_spec=pltpu.PrefetchScalarGridSpec(
            num_scalar_prefetch=1,
            grid=(heads,),
            in_specs=[pl.BlockSpec((1, blocks, BLOCK, cols), lambda h, inv: (h, 0, 0, 0))],
            out_specs=[
                pl.BlockSpec((blocks, HEAD_DIM, BLOCK), lambda h, inv: (0, h, 0)),
                pl.BlockSpec((1, 1, rows), lambda h, inv: (h, 0, 0)),
            ],
        ),
        out_shape=[
            jax.ShapeDtypeStruct((blocks, heads * HEAD_DIM, BLOCK), BF16),
            jax.ShapeDtypeStruct((heads, 1, rows), F32),
        ],
        compiler_params=pltpu.CompilerParams(vmem_limit_bytes=VMEM_LIMIT),
        name="attn_fwd",
    )(inv, qkv)


def attn_bwd_kernel(inv_ref, x_ref, do_ref, o_ref, l_ref, dx_ref, dk_acc, dv_acc):
    rows = l_ref.shape[2]
    hd = HEAD_DIM
    x = causal(inv_ref, x_ref)
    q = x[:, :hd] * BF16(SCALE)
    k = x[:, hd : 2 * hd]
    v = x[:, 2 * hd :]
    k_t = k.T
    dk_acc[...] = jnp.zeros_like(dk_acc)
    dv_acc[...] = jnp.zeros_like(dv_acc)
    for i in range(rows // QROWS):
        lo, hi = i * QROWS, (i + 1) * QROWS
        ids = [inv_ref[2 * i + b] for b in range(QROWS // BLOCK)]
        do_t = jnp.concatenate([do_ref[b] for b in ids], axis=1)
        o_t = jnp.concatenate([o_ref[b] for b in ids], axis=1)
        inner = jnp.sum(do_t.astype(F32) * o_t.astype(F32), axis=0, keepdims=True)
        probs = jnp.exp(causal_scores(k[:hi], q[lo:hi], lo) - l_ref[0, :, lo:hi])
        dprobs = dot(v[:hi], do_t)
        dscores = (probs * (dprobs - inner)).astype(BF16)
        dv_acc[:hi] += dot_last(probs.astype(BF16), do_t)
        dk_acc[:hi] += dot(dscores, q[lo:hi])
        dq = (dot(k_t[:, :hi], dscores) * SCALE).T
        for n, b in enumerate(ids):
            dx_ref[0, b, :, :hd] = dq[n * BLOCK : (n + 1) * BLOCK].astype(BF16)
    for i in range(rows // BLOCK):
        lo, hi = i * BLOCK, (i + 1) * BLOCK
        dx_ref[0, inv_ref[i], :, hd : 2 * hd] = dk_acc[lo:hi].astype(BF16)
        dx_ref[0, inv_ref[i], :, 2 * hd :] = dv_acc[lo:hi].astype(BF16)


def attn_bwd(inv, qkv, d_out, out, lse, heads):
    blocks, _, cols = qkv.shape[1:]
    rows = blocks * BLOCK
    whole = pl.BlockSpec((1, blocks, BLOCK, cols), lambda h, inv: (h, 0, 0, 0))
    feat = pl.BlockSpec((blocks, HEAD_DIM, BLOCK), lambda h, inv: (0, h, 0))
    return pl.pallas_call(
        attn_bwd_kernel,
        grid_spec=pltpu.PrefetchScalarGridSpec(
            num_scalar_prefetch=1,
            grid=(heads,),
            in_specs=[
                whole,
                feat,
                feat,
                pl.BlockSpec((1, 1, rows), lambda h, inv: (h, 0, 0)),
            ],
            out_specs=whole,
            scratch_shapes=[pltpu.VMEM((rows, HEAD_DIM), F32)] * 2,
        ),
        out_shape=jax.ShapeDtypeStruct((heads, blocks, BLOCK, cols), BF16),
        compiler_params=pltpu.CompilerParams(vmem_limit_bytes=VMEM_LIMIT),
        name="attn_bwd",
    )(inv, qkv, d_out, out, lse)


def own_scores(order_ref, x_ref, k):
    hd = HEAD_DIM
    blocks = x_ref.shape[1]
    first = order_ref[blocks]
    q = jnp.concatenate([x_ref[0, first], x_ref[0, first + 1]], axis=0)[:, :hd]
    q = q * BF16(SCALE)
    scores = dot_last(k, q)
    row = lax.broadcasted_iota(jnp.int32, (BLOCK, 1), 0)
    key_place = jnp.concatenate([order_ref[b] * BLOCK + row for b in range(blocks)], axis=0)
    lane = lax.broadcasted_iota(jnp.int32, (1, 2 * BLOCK), 1)
    low, high = order_ref[order_ref[blocks]], order_ref[order_ref[blocks] + 1]
    place = jnp.where(lane < BLOCK, low * BLOCK + lane, (high - 1) * BLOCK + lane)
    return q, first, jnp.where(key_place <= place, scores, -1e30)


def rest_fwd_kernel(order_ref, x_ref, o_ref, l_ref):
    hd = HEAD_DIM
    x = x_ref[0].reshape(-1, 3 * hd)
    _, _, scores = own_scores(order_ref, x_ref, x[:, hd : 2 * hd])
    out, lse = soft(scores, x[:, 2 * hd :].T)
    o_ref[0] = out.astype(BF16)
    l_ref[0] = lse


def rest_fwd(order, qkv, base):
    slots, blocks, _, cols = qkv.shape
    rest = slots - base
    return pl.pallas_call(
        rest_fwd_kernel,
        grid_spec=pltpu.PrefetchScalarGridSpec(
            num_scalar_prefetch=1,
            grid=(rest,),
            in_specs=[
                pl.BlockSpec((1, blocks, BLOCK, cols), lambda h, o: (base + h, 0, 0, 0))
            ],
            out_specs=[
                pl.BlockSpec((1, HEAD_DIM, QROWS), lambda h, o: (h, 0, 0)),
                pl.BlockSpec((1, 1, QROWS), lambda h, o: (h, 0, 0)),
            ],
        ),
        out_shape=[
            jax.ShapeDtypeStruct((rest, HEAD_DIM, QROWS), BF16),
            jax.ShapeDtypeStruct((rest, 1, QROWS), F32),
        ],
        compiler_params=pltpu.CompilerParams(vmem_limit_bytes=VMEM_LIMIT),
        name="rest_fwd",
    )(order, qkv)


def rest_bwd_kernel(order_ref, x_ref, do_ref, o_ref, l_ref, dx_ref):
    hd = HEAD_DIM
    x = x_ref[0].reshape(-1, 3 * hd)
    blocks = x_ref.shape[1]
    k = x[:, hd : 2 * hd]
    q, first, scores = own_scores(order_ref, x_ref, k)
    do_t = do_ref[0]
    inner = jnp.sum(do_t.astype(F32) * o_ref[0].astype(F32), axis=0, keepdims=True)
    probs = jnp.exp(scores - l_ref[0])
    dprobs = dot(x[:, 2 * hd :], do_t)
    dscores = (probs * (dprobs - inner)).astype(BF16)
    dv = dot_last(probs.astype(BF16), do_t).astype(BF16)
    dk = dot(dscores, q).astype(BF16)
    dq = (dot(k.T, dscores) * SCALE).T.astype(BF16)
    dx_ref[0, :, :, 2 * hd :] = dv.reshape(blocks, BLOCK, hd)
    dx_ref[0, :, :, hd : 2 * hd] = dk.reshape(blocks, BLOCK, hd)
    dx_ref[0, :, :, :hd] = jnp.zeros((blocks, BLOCK, hd), BF16)
    for b in range(2):
        dx_ref[0, first + b, :, :hd] = dq[b * BLOCK : (b + 1) * BLOCK]


def rest_bwd(order, qkv, d_out, out, lse, base):
    slots, blocks, _, cols = qkv.shape
    rest = slots - base
    feat = pl.BlockSpec((1, HEAD_DIM, QROWS), lambda h, o: (h, 0, 0))
    return pl.pallas_call(
        rest_bwd_kernel,
        grid_spec=pltpu.PrefetchScalarGridSpec(
            num_scalar_prefetch=1,
            grid=(rest,),
            in_specs=[
                pl.BlockSpec((1, blocks, BLOCK, cols), lambda h, o: (base + h, 0, 0, 0)),
                feat,
                feat,
                pl.BlockSpec((1, 1, QROWS), lambda h, o: (h, 0, 0)),
            ],
            out_specs=pl.BlockSpec((1, blocks, BLOCK, cols), lambda h, o: (h, 0, 0, 0)),
        ),
        out_shape=jax.ShapeDtypeStruct((rest, blocks, BLOCK, cols), BF16),
        compiler_params=pltpu.CompilerParams(vmem_limit_bytes=VMEM_LIMIT),
        name="rest_bwd",
    )(order, qkv, d_out, out, lse)


def assemble_kernel(own_ref, rest_ref, o_ref):
    hd = HEAD_DIM
    width = o_ref.shape[1] // 3
    count = own_ref.shape[0]
    for h in range(width // hd):
        src = own_ref.at[h] if h < count else rest_ref.at[h - count]
        for part in range(3):
            at = part * width + h * hd
            o_ref[:, at : at + hd] = src[:, part * hd : (part + 1) * hd].astype(F32)


def assemble(own, rest, out_cols):
    rows = own.shape[1]
    return pl.pallas_call(
        assemble_kernel,
        out_shape=jax.ShapeDtypeStruct((rows, out_cols), F32),
        compiler_params=pltpu.CompilerParams(vmem_limit_bytes=VMEM_LIMIT),
        name="assemble",
    )(own, rest)


def norm_parts(rows):
    mean = jnp.mean(rows, axis=-1, keepdims=True)
    cen = rows - mean
    rstd = lax.rsqrt(jnp.mean(cen * cen, axis=-1, keepdims=True) + EPS)
    return cen * rstd, rstd


def norm_back(xhat, rstd, gain, grad):
    dxhat = grad * gain
    return rstd * (
        dxhat
        - jnp.mean(dxhat, axis=-1, keepdims=True)
        - xhat * jnp.mean(dxhat * xhat, axis=-1, keepdims=True)
    )


def swap(value, axis, size, k):
    return lax.ppermute(value, axis, [(i, i ^ k) for i in range(size)])


def shards(
    n_ctx,
    n_fsdp,
    tokens,
    block_order,
    w_attn,
    w_proj,
    w_fc,
    w_out,
    norm_gains,
    biases,
    fc_bias,
    cotangent,
):
    hd = HEAD_DIM
    count, width = tokens.shape[1:]
    shard = width // n_fsdp
    heads = width // hd
    base = heads // n_ctx
    rest = heads - base * n_ctx
    slots = base + rest
    own_blocks = count // BLOCK
    c = lax.axis_index("ctx")
    f = lax.axis_index("fsdp")

    order = block_order[0]
    inv = jnp.argsort(order).astype(jnp.int32)
    order_own = jnp.concatenate([order, (c * own_blocks)[None]])

    def head_cols(h):
        return jnp.concatenate(
            [
                lax.dynamic_slice(w_attn, (0, part * width + h * hd), (shard, hd))
                for part in range(3)
            ],
            axis=1,
        )

    slot_heads = [c * base + s for s in range(base)] + [n_ctx * base + r for r in range(rest)]
    w_slots = jnp.stack([head_cols(h) for h in slot_heads])
    small = jnp.concatenate([norm_gains, biases], axis=0).astype(F32)
    hidden_cols = w_fc.shape[1] // n_fsdp
    fc_parts = jnp.stack(
        [w_fc[:, j * hidden_cols : (j + 1) * hidden_cols] for j in range(n_fsdp)]
    )
    normed_one, qkv, full_proj, fc_cols, w_slots, small = start_call(
        n_ctx, n_fsdp, base, tokens[0], w_slots, small, w_proj, fc_parts, 3
    )
    full_proj = full_proj.reshape(width, width)
    fc_cols = fc_cols.reshape(width, hidden_cols)
    qkv = qkv.reshape(slots, n_ctx * own_blocks, BLOCK, 3 * hd)
    normed_one = normed_one.reshape(n_ctx * count, width)
    gains, shifts = small[:2], small[2:]
    cot = cotangent[0]

    cot_late, _ = lax.optimization_barrier((cot, small))
    cot_all = lax.all_gather(cot_late, "fsdp", axis=0)

    out_own, lse_own = attn_fwd(inv, qkv, base)
    got = lax.all_to_all(out_own, "ctx", split_axis=0, concat_axis=0, tiled=True)
    got = got.reshape(n_ctx, own_blocks, base * hd, BLOCK).transpose(1, 3, 0, 2)
    attended = got.reshape(count, n_ctx * base * hd)
    if rest:
        out_rest, lse_rest = rest_fwd(order_own, qkv, base)
        attended = jnp.concatenate([attended, out_rest.reshape(rest * hd, count).T], axis=1)

    rows = tokens[0].astype(F32)
    mid = rows + (dot(attended, full_proj) + shifts[4])
    xhat_two, rstd_two = norm_parts(mid)
    normed_two = (xhat_two * gains[1] + shifts[1]).astype(BF16)

    normed_two_grad, fc_bias_part, out_part, w_out_part, w_fc_part = ffn(
        n_fsdp,
        normed_two,
        cot_all,
        fc_cols,
        w_out,
        fc_bias.astype(F32)[None],
    )
    out_rows = lax.psum_scatter(
        out_part.reshape(n_fsdp * count, width), "fsdp", scatter_dimension=0, tiled=True
    )
    layer_rows = (mid + (out_rows.astype(F32) + shifts[5])).astype(BF16)
    w_fc_part = w_fc_part.reshape(n_fsdp, shard, hidden_cols)
    fc_recv = []
    for k in range(n_fsdp):
        piece = lax.dynamic_index_in_dim(w_fc_part, f ^ k, keepdims=False)
        fc_recv.append(swap(piece, "fsdp", n_fsdp, k) if k else piece)
    w_out_low, w_fc_low = lax.psum((w_out_part, jnp.stack(fc_recv)), "ctx")
    w_out_grad = w_out_low.astype(F32)
    w_fc_grad = jnp.concatenate(
        [lax.dynamic_index_in_dim(w_fc_low, f ^ j, keepdims=False) for j in range(n_fsdp)],
        axis=1,
    ).astype(F32)

    cot_rows = cot.astype(F32)
    mid_grad = cot_rows + norm_back(xhat_two, rstd_two, gains[1], normed_two_grad)
    mid_low = mid_grad.astype(BF16)
    over_rows = functools.partial(jnp.einsum, "ta,tb->ab", preferred_element_type=F32)
    attended_grad = dot_last(mid_low, full_proj).astype(BF16)
    w_proj_part = over_rows(attended, mid_low).astype(BF16)
    w_proj_part = w_proj_part.reshape(n_fsdp, shard, width)
    w_proj_part = sum(
        swap(
            lax.dynamic_index_in_dim(w_proj_part, f ^ k, keepdims=False), "fsdp", n_fsdp, k
        ).astype(F32)
        if k
        else lax.dynamic_index_in_dim(w_proj_part, f, keepdims=False).astype(F32)
        for k in range(n_fsdp)
    ).astype(BF16)

    main = n_ctx * base * hd
    sent = attended_grad[:, :main].reshape(own_blocks, BLOCK, n_ctx, base * hd)
    sent = sent.transpose(2, 0, 3, 1).reshape(n_ctx * own_blocks, base * hd, BLOCK)
    d_out = lax.all_to_all(sent, "ctx", split_axis=0, concat_axis=0, tiled=True)
    dqkv = attn_bwd(inv, qkv, d_out, out_own, lse_own, base)
    if rest:
        d_rest = attended_grad[:, main:].T.reshape(rest, hd, count)
        dqkv = jnp.concatenate(
            [dqkv, rest_bwd(order_own, qkv, d_rest, out_rest, lse_rest, base)], axis=0
        )
    dqkv = dqkv.reshape(slots, n_ctx * count, 3 * hd)
    flat = dqkv.transpose(1, 0, 2).reshape(n_ctx * count, slots * 3 * hd)
    flat_w = w_slots.transpose(1, 0, 2).reshape(width, slots * 3 * hd)
    one_part = dot_last(flat, flat_w).astype(BF16)
    normed_one_grad = lax.psum_scatter(
        one_part, "ctx", scatter_dimension=0, tiled=True
    ).astype(F32)
    slot_part = jnp.einsum("td,hte->hde", normed_one, dqkv, preferred_element_type=F32)
    slot_part = slot_part.astype(BF16)

    def slot_rows(k):
        return lax.dynamic_slice_in_dim(slot_part, (f ^ k) * shard, shard, 1)

    slot_sum = slot_rows(0).astype(F32)
    for k in range(1, n_fsdp):
        slot_sum += swap(slot_rows(k), "fsdp", n_fsdp, k).astype(F32)
    slot_sum = slot_sum.astype(BF16)
    own_cols = lax.all_gather(slot_sum[:base], "ctx", axis=0, tiled=True)
    w_proj_part, rest_part, _, _ = lax.optimization_barrier(
        (w_proj_part, slot_sum[base:], w_out_low, w_fc_low)
    )
    w_proj_low, rest_cols = lax.psum((w_proj_part, rest_part), "ctx")
    w_proj_grad = w_proj_low.astype(F32)
    if not rest:
        rest_cols = own_cols
    w_attn_grad = assemble(own_cols, rest_cols, 3 * width)

    xhat_one, rstd_one = norm_parts(rows)
    tokens_grad = (mid_grad + norm_back(xhat_one, rstd_one, gains[0], normed_one_grad)).astype(
        BF16
    )

    sums = jnp.sum(dqkv.astype(F32), axis=1)

    def placed(part):
        cols = sums[:, part * hd : (part + 1) * hd]
        line = lax.dynamic_update_slice_in_dim(
            jnp.zeros((width,), F32), cols[:base].reshape(-1), c * base * hd, 0
        )
        return line + jnp.pad(cols[base:].reshape(-1), (main, 0))

    lines = jnp.stack(
        [
            jnp.sum(normed_one_grad * xhat_one, axis=0),
            jnp.sum(normed_two_grad * xhat_two, axis=0),
            jnp.sum(normed_one_grad, axis=0),
            jnp.sum(normed_two_grad, axis=0),
            placed(0),
            placed(2),
            jnp.sum(mid_low.astype(F32), axis=0),
            jnp.sum(cot_rows, axis=0),
        ]
    )
    lead = lines.shape[0]
    tail = jnp.pad(fc_bias_part, ((0, 7), (0, max(0, width - hidden_cols))))
    lines = sum_lines(jnp.concatenate([lines, tail]), lead, n_ctx, n_fsdp, 2)
    fc_bias_grad = lines[lead, :hidden_cols]
    lines = lax.dynamic_slice_in_dim(lines[:lead], f * shard, shard, 1)
    return (
        layer_rows[None],
        tokens_grad[None],
        w_attn_grad,
        w_proj_grad,
        w_fc_grad,
        w_out_grad,
        lines[:2],
        lines[2:],
        fc_bias_grad,
    )


def solution(mesh):
    rows = P("fsdp", "ctx", None)
    weight = P("fsdp", None)
    vectors = P(None, "fsdp")
    return jax.shard_map(
        functools.partial(shards, mesh.shape["ctx"], mesh.shape["fsdp"]),
        mesh=mesh,
        in_specs=(
            rows, weight, weight, weight, weight, weight, vectors, vectors, P("fsdp"), rows,
        ),
        out_specs=(
            rows, rows, weight, weight, weight, weight, vectors, vectors, P("fsdp"),
        ),
        check_vma=False,
    )
```

```python
import functools

import jax
import jax.numpy as jnp
from jax import lax
from jax.experimental import pallas as pl
from jax.experimental.pallas import tpu as pltpu
from jax.sharding import PartitionSpec as P

HEAD_DIM = 64
BLOCK = 128
QROWS = 256
EPS = 1e-05
SCALE = HEAD_DIM ** (-0.5)
F32 = jnp.float32
BF16 = jnp.bfloat16
VMEM_LIMIT = 56 * 1024 * 1024
LAST = (((1,), (1,)), ((), ()))
FIRST = (((0,), (0,)), ((), ()))
MESH = pl.DeviceIdType.MESH
TILE = 256


def dot_last(a, b):
    return lax.dot_general(a, b, LAST, preferred_element_type=F32)


def dot(a, b):
    return jnp.dot(a, b, preferred_element_type=F32)


def dot_first(a, b):
    return lax.dot_general(a, b, FIRST, preferred_element_type=F32)


def flip(place, k, size):
    out = 0
    bit = 1
    while bit < size:
        out = out + (place // bit + k // bit) % 2 * bit
        bit *= 2
    return out

def enter(peers):
    barrier = pltpu.get_barrier_semaphore()
    for peer in peers:
        pl.semaphore_signal(barrier, inc=1, device_id=peer, device_id_type=MESH)
    pl.semaphore_wait(barrier, len(peers))

def send(src, dst, send_sem, recv_sem, peer):
    return pltpu.make_async_remote_copy(
        src_ref=src, dst_ref=dst, send_sem=send_sem, recv_sem=recv_sem,
        device_id=peer, device_id_type=MESH)


def ffn_kernel(n, nt_hbm, cot_hbm, wfc_hbm, wout_hbm, bias_ref,
               gsum_ref, fcb_ref, out_hbm, wout_grad_hbm, wfc_grad_hbm,
               cot_ref, wfc_ref, wout_ref, all_ref, act_ref, hg_ref, ag_ref, part_ref, got_ref, stage_d, stage_h,
               s1, r1, s2, r2, local):
    c = lax.axis_index("ctx")
    f = lax.axis_index("fsdp")
    rows, width = nt_hbm.shape
    enter([(c, flip(f, k, n)) for k in range(1, n)])

    def rows_out(k):
        return send(nt_hbm, all_ref.at[f], s1.at[k], r1.at[k], (c, flip(f, k, n)))

    def grad_back(k):
        other = flip(f, k, n)
        return send(part_ref.at[other], got_ref.at[k], s2.at[k], r2.at[k], (c, other))

    near = [k for k in range(1, n) if k & (k - 1) == 0]
    far = [k for k in range(1, n) if k not in near]
    for k in near:
        rows_out(k).start()
    loads = [
        pltpu.make_async_copy(nt_hbm, all_ref.at[f], local.at[0]),
        pltpu.make_async_copy(wout_hbm, wout_ref, local.at[1]),
        pltpu.make_async_copy(cot_hbm, cot_ref, local.at[2]),
        pltpu.make_async_copy(wfc_hbm, wfc_ref, local.at[3]),
    ]
    for load in loads:
        load.start()
    fcb_ref[...] = jnp.zeros_like(fcb_ref)
    loads[1].wait()
    loads[2].wait()

    def active_grad(k, carry):
        ag_ref[k] = dot_last(cot_ref[k], wout_ref[...])
        return carry

    lax.fori_loop(0, n, active_grad, 0)
    for k in far:
        rows_out(k).start()
    loads[0].wait()
    loads[3].wait()

    def chunk(k, carry):
        src = flip(f, k, n)

        @pl.when(k > 0)
        def _():
            rows_out(k).wait_recv()

        hidden = dot(all_ref[src], wfc_ref[...]) + bias_ref[...]
        square = hidden * hidden
        tanh = jnp.tanh(0.7978845608028654 * (hidden + 0.044715 * square * hidden))
        act_ref[src] = (0.5 * hidden * (1.0 + tanh)).astype(BF16)
        slope = 0.5 * (1.0 + tanh) + 0.5 * hidden * (1.0 - tanh * tanh) * 0.7978845608028654 * (
            1.0 + 3.0 * 0.044715 * square
        )
        grad = (ag_ref[src] * slope).astype(BF16)
        hg_ref[src] = grad
        fcb_ref[...] += jnp.sum(grad.astype(F32), axis=0, keepdims=True)
        part_ref[src] = dot_last(grad, wfc_ref[...]).astype(BF16)

        @pl.when(k > 0)
        def _():
            grad_back(k).start()

        return carry

    lax.fori_loop(0, n, chunk, 0)

    def grads(left_ref, right_ref, dst, stage_ref, base):
        wide = left_ref.shape[2]
        right = right_ref[...].reshape(n * rows, right_ref.shape[2])
        copies = []
        for i, lo in enumerate(range(0, wide, TILE)):
            hi = min(lo + TILE, wide)
            slot = i % 2
            if i >= 2:
                copies[i - 2].wait()
            left = left_ref[:, :, lo:hi].reshape(n * rows, hi - lo)
            stage_ref[slot, : hi - lo] = dot_first(left, right).astype(BF16)
            copies.append(
                pltpu.make_async_copy(
                    stage_ref.at[slot, : hi - lo], dst.at[lo:hi], local.at[base + slot]
                )
            )
            copies[-1].start()
        for copy in copies[-2:]:
            copy.wait()

    grads(act_ref, cot_ref, wout_grad_hbm, stage_d, 4)
    grads(all_ref, hg_ref, wfc_grad_hbm, stage_h, 6)

    def out_copy(k):
        return pltpu.make_async_copy(
            stage_d.at[k % 2, :rows], out_hbm.at[k], local.at[4 + k % 2]
        )

    for k in range(n):
        if k >= 2:
            out_copy(k - 2).wait()
        stage_d[k % 2, :rows] = dot(act_ref[k], wout_ref[...]).astype(BF16)
        out_copy(k).start()

    gsum_ref[...] = part_ref[f].astype(F32)
    for k in near + far:
        grad_back(k).wait_recv()
        gsum_ref[...] += got_ref[k].astype(F32)
    for k in range(1, n):
        rows_out(k).wait_send()
        grad_back(k).wait_send()
    for k in range(max(0, n - 2), n):
        out_copy(k).wait()


def ffn(n, nt, cot, wfc, wout, bias, cid=1):
    m, d = nt.shape
    h = wfc.shape[1]
    vm = pl.BlockSpec(memory_space=pltpu.VMEM)
    anym = pl.BlockSpec(memory_space=pl.ANY)
    return pl.pallas_call(
        functools.partial(ffn_kernel, n),
        in_specs=[anym] * 4 + [vm],
        out_specs=[vm, vm] + [anym] * 3,
        out_shape=[
            jax.ShapeDtypeStruct((m, d), F32),
            jax.ShapeDtypeStruct((1, h), F32),
            jax.ShapeDtypeStruct((n, m, d), BF16),
            jax.ShapeDtypeStruct((h, d), BF16),
            jax.ShapeDtypeStruct((d, h), BF16),
        ],
        scratch_shapes=[
            pltpu.VMEM((n, m, d), BF16),
            pltpu.VMEM((d, h), BF16),
            pltpu.VMEM((h, d), BF16),
            pltpu.VMEM((n, m, d), BF16),
            pltpu.VMEM((n, m, h), BF16),
            pltpu.VMEM((n, m, h), BF16),
            pltpu.VMEM((n, m, h), F32),
            pltpu.VMEM((n, m, d), BF16),
            pltpu.VMEM((n, m, d), BF16),
            pltpu.VMEM((2, max(TILE, m), d), BF16),
            pltpu.VMEM((2, TILE, h), BF16),
        ]
        + [pltpu.SemaphoreType.DMA((n,))] * 4
        + [pltpu.SemaphoreType.DMA((8,))],
        compiler_params=pltpu.CompilerParams(
            collective_id=cid, has_side_effects=True, vmem_limit_bytes=60 * 1024 * 1024
        ),
        name="feed_forward",
    )(nt, cot, wfc, wout, bias)


def start_kernel(
    n_ctx,
    n_fsdp,
    base,
    tok_hbm,
    w_hbm,
    small_ref,
    proj_hbm,
    fc_hbm,
    n_hbm,
    qkv_hbm,
    proj_all,
    fc_all,
    w_ref,
    lines_ref,
    n_ref,
    qkv_ref,
    x_ref,
    wg_ref,
    sg_ref,
    tok_recv,
    right_sem,
    left_sem,
    twin_sem,
    w_send,
    w_recv,
    s_send,
    s_recv,
    proj_send,
    proj_recv,
    fc_send,
    fc_recv,
    local,
):
    c = lax.axis_index("ctx")
    f = lax.axis_index("fsdp")
    chips = n_ctx // 2
    chip, core = c // 2, c % 2
    slots, width, cols = w_ref.shape
    shard = width // n_fsdp
    hd = HEAD_DIM
    enter(
        [(lax.rem(c + i, n_ctx), f) for i in range(1, n_ctx)]
        + [(c, flip(f, k, n_fsdp)) for k in range(1, n_fsdp)]
    )

    def block(at, same):
        return 2 * at + (core if same else 1 - core)

    def hop(step, to_right, from_own):
        origin = block(chip - step if to_right else chip + step, True)
        src = tok_hbm if from_own else x_ref.at[origin]
        sem = (right_sem if to_right else left_sem).at[step]
        peer = (c + 2 if to_right else c - 2, f)
        return send(src, x_ref.at[origin], sem, tok_recv.at[origin], peer)

    def twin(at, from_own):
        origin = block(at, True)
        src = tok_hbm if from_own else x_ref.at[origin]
        return send(
            src, x_ref.at[origin], twin_sem.at[at], tok_recv.at[origin], (block(chip, False), f)
        )

    def w_copy(k):
        return send(w_hbm, wg_ref.at[f], w_send.at[k], w_recv.at[k], (c, flip(f, k, n_fsdp)))

    def s_copy(k):
        return send(small_ref, sg_ref.at[f], s_send.at[k], s_recv.at[k], (c, flip(f, k, n_fsdp)))

    cut = shard // 32 * 16 if shard % 16 == 0 else 0
    shares = ((0, cut), (cut, shard)) if cut else ((0, shard), (0, shard))

    def weight_copy(share, k, onward, which):
        lo, hi = share
        other = flip(f, k, n_fsdp)
        dst = (proj_all, fc_all)[which]
        ss = (proj_send, fc_send)[which]
        rs = (proj_recv, fc_recv)[which]
        if onward:
            part = dst.at[other, lo:hi]
            return send(part, part, ss.at[1, k], rs.at[1, k], (block(chip, False), f))
        src = fc_hbm.at[other, lo:hi] if which else proj_hbm.at[lo:hi]
        return send(src, dst.at[f, lo:hi], ss.at[0, k], rs.at[0, k], (c, other))

    def by_core(act):
        for h in range(2):

            @pl.when(core == h)
            def _(h=h):
                act(shares[h], shares[1 - h])

    def weights_start(mine, theirs):
        for i in range(2):
            for k in range(1, n_fsdp):
                weight_copy(mine, k, False, i).start()

    def weights_onward(mine, theirs):
        for i in range(2):
            for k in range(1, n_fsdp):
                weight_copy(mine, k, False, i).wait_recv()
                if cut:
                    weight_copy(mine, k, True, i).start()

    def weights_done(mine, theirs):
        for i in range(2):
            for k in range(1, n_fsdp):
                if cut:
                    weight_copy(theirs, k, True, i).wait_recv()
                    weight_copy(mine, k, True, i).wait_send()
                weight_copy(mine, k, False, i).wait_send()

    for k in range(1, n_fsdp):
        s_copy(k).start()

    @pl.when(chip < chips - 1)
    def _():
        hop(0, True, True).start()

    @pl.when(chip > 0)
    def _():
        hop(0, False, True).start()

    for k in range(1, n_fsdp):
        w_copy(k).start()
    twin(chip, True).start()
    own_x = pltpu.make_async_copy(tok_hbm, x_ref.at[c], local.at[0])
    own_w = pltpu.make_async_copy(w_hbm, wg_ref.at[f], local.at[1])
    own_proj = pltpu.make_async_copy(proj_hbm, proj_all.at[f], local.at[2])
    own_fc = pltpu.make_async_copy(fc_hbm.at[f], fc_all.at[f], local.at[3])
    for copy in (own_x, own_w, own_proj, own_fc):
        copy.start()
    sg_ref[f] = small_ref[...]
    for k in range(1, n_fsdp):
        s_copy(k).wait_recv()
    for j in range(n_fsdp):
        lines_ref[:, j * shard : (j + 1) * shard] = sg_ref[j]
    main = n_ctx * base * hd
    row_id = lax.broadcasted_iota(jnp.int32, (width, slots * hd), 0)
    col_id = lax.broadcasted_iota(jnp.int32, (width, slots * hd), 1)
    wanted = jnp.where(col_id < base * hd, c * base * hd + col_id, main + col_id - base * hd)
    picked = dot(lines_ref[...].astype(BF16), (row_id == wanted).astype(BF16))
    zero = jnp.zeros((1, hd), F32)
    bias = [
        jnp.concatenate(
            [picked[4:5, s * hd : (s + 1) * hd], zero, picked[5:6, s * hd : (s + 1) * hd]], axis=1
        )
        for s in range(slots)
    ]
    own_w.wait()
    own_x.wait()
    for k in range(1, n_fsdp):
        w_copy(k).wait_recv()
    by_core(weights_start)
    for j in range(n_fsdp):
        w_ref[:, j * shard : (j + 1) * shard, :] = wg_ref[j]

    def results(origin):
        return (
            pltpu.make_async_copy(n_ref, n_hbm.at[origin], local.at[0]),
            pltpu.make_async_copy(qkv_ref, qkv_hbm.at[:, origin], local.at[1]),
        )

    def project(at, same, first=False):
        origin = block(at, same)
        rows = x_ref[origin].astype(F32)
        mean = jnp.mean(rows, axis=1, keepdims=True)
        cen = rows - mean
        var = jnp.mean(cen * cen, axis=1, keepdims=True)
        normed = cen * lax.rsqrt(var + EPS) * lines_ref[0:1] + lines_ref[2:3]
        normed = normed.astype(BF16)

        @pl.when(jnp.logical_not(first))
        def _():
            for copy in results(origin):
                copy.wait()

        n_ref[...] = normed
        for s in range(slots):
            qkv_ref[s] = (dot(normed, w_ref[s]) + bias[s]).astype(BF16)
        for copy in results(origin):
            copy.start()

    def arrived(at, same):
        origin = block(at, same)
        pltpu.make_async_copy(x_ref.at[origin], x_ref.at[origin], tok_recv.at[origin]).wait()

    def step(s, carry):
        @pl.when((s > 0) & (chip - s >= 0))
        def _():
            arrived(chip - s, True)
            twin(chip - s, False).start()

            @pl.when(chip < chips - 1)
            def _():
                hop(s, True, False).start()

        @pl.when((s > 0) & (chip + s < chips))
        def _():
            arrived(chip + s, True)
            twin(chip + s, False).start()

            @pl.when(chip > 0)
            def _():
                hop(s, False, False).start()

        @pl.when(chip - s >= 0)
        def _():
            project(chip - s, True, s == 0)

        @pl.when((s > 0) & (chip + s < chips))
        def _():
            project(chip + s, True)

        @pl.when(chip - s >= 0)
        def _():
            arrived(chip - s, False)
            project(chip - s, False)

        @pl.when((s > 0) & (chip + s < chips))
        def _():
            arrived(chip + s, False)
            project(chip + s, False)

        return carry

    lax.fori_loop(0, chips, step, 0)
    by_core(weights_onward)
    for copy in results(c):
        copy.wait()
    own_proj.wait()
    own_fc.wait()

    for s in range(chips):
        if s < chips - 1:

            @pl.when((chip - s >= 0) & (chip < chips - 1))
            def _():
                hop(s, True, False).wait_send()

            @pl.when((chip + s < chips) & (chip > 0))
            def _():
                hop(s, False, False).wait_send()

        twin(s, False).wait_send()
    for k in range(1, n_fsdp):
        w_copy(k).wait_send()
        s_copy(k).wait_send()
    by_core(weights_done)


def start_call(n_ctx, n_fsdp, base, tok, w_slots, small, w_proj, fc_parts, cid):
    count, width = tok.shape
    slots, shard, cols = w_slots.shape
    vm = pl.BlockSpec(memory_space=pltpu.VMEM)
    anym = pl.BlockSpec(memory_space=pl.ANY)
    dma = pltpu.SemaphoreType.DMA
    return pl.pallas_call(
        functools.partial(start_kernel, n_ctx, n_fsdp, base),
        in_specs=[anym, anym, vm, anym, anym],
        out_specs=[anym, anym, anym, anym, vm, vm],
        out_shape=[
            jax.ShapeDtypeStruct((n_ctx, count, width), BF16),
            jax.ShapeDtypeStruct((slots, n_ctx, count, cols), BF16),
            jax.ShapeDtypeStruct((n_fsdp,) + w_proj.shape, BF16),
            jax.ShapeDtypeStruct(fc_parts.shape, BF16),
            jax.ShapeDtypeStruct((slots, width, cols), BF16),
            jax.ShapeDtypeStruct((small.shape[0], width), F32),
        ],
        scratch_shapes=[
            pltpu.VMEM((count, width), BF16),
            pltpu.VMEM((slots, count, cols), BF16),
            pltpu.VMEM((n_ctx, count, width), BF16),
            pltpu.VMEM((n_fsdp, slots, shard, cols), BF16),
            pltpu.VMEM((n_fsdp,) + small.shape, F32),
            dma((n_ctx,)),
            dma((n_ctx // 2,)),
            dma((n_ctx // 2,)),
            dma((n_ctx // 2,)),
            dma((n_fsdp,)),
            dma((n_fsdp,)),
            dma((n_fsdp,)),
            dma((n_fsdp,)),
            dma((2, n_fsdp)),
            dma((2, n_fsdp)),
            dma((2, n_fsdp)),
            dma((2, n_fsdp)),
            dma((4,)),
        ],
        compiler_params=pltpu.CompilerParams(
            collective_id=cid, has_side_effects=True, vmem_limit_bytes=VMEM_LIMIT
        ),
        name="tokens_qkv",
    )(tok, w_slots, small, w_proj, fc_parts)


def causal_scores(k, q_rows, start):
    scores = dot_last(k, q_rows)
    keep = start
    tail = scores[keep:]
    key_id = lax.broadcasted_iota(jnp.int32, tail.shape, 0)
    query_id = lax.broadcasted_iota(jnp.int32, tail.shape, 1)
    tail = jnp.where(key_id <= query_id, tail, -1e30)
    if keep == 0:
        return tail
    return jnp.concatenate([scores[:keep], tail], axis=0)


def soft(scores, v_t):
    top = jnp.max(scores, axis=0, keepdims=True)
    weights = jnp.exp(scores - top)
    total = jnp.sum(weights, axis=0, keepdims=True)
    out = dot(v_t, weights.astype(BF16)) / total
    return out, top + jnp.log(total)


def causal(inv_ref, x_ref):
    return jnp.concatenate([x_ref[0, inv_ref[i]] for i in range(x_ref.shape[1])], axis=0)


def attn_fwd_kernel(inv_ref, x_ref, o_ref, l_ref):
    rows = l_ref.shape[2]
    hd = HEAD_DIM
    x = causal(inv_ref, x_ref)
    q = x[:, :hd] * BF16(SCALE)
    k = x[:, hd : 2 * hd]
    v_t = x[:, 2 * hd :].T
    for i in range(rows // QROWS):
        lo, hi = i * QROWS, (i + 1) * QROWS
        out, lse = soft(causal_scores(k[:hi], q[lo:hi], lo), v_t[:, :hi])
        l_ref[0, :, lo:hi] = lse
        out = out.astype(BF16)
        for b in range(QROWS // BLOCK):
            o_ref[inv_ref[2 * i + b]] = out[:, b * BLOCK : (b + 1) * BLOCK]


def attn_fwd(inv, qkv, heads):
    blocks, _, cols = qkv.shape[1:]
    rows = blocks * BLOCK
    return pl.pallas_call(
        attn_fwd_kernel,
        grid_spec=pltpu.PrefetchScalarGridSpec(
            num_scalar_prefetch=1,
            grid=(heads,),
            in_specs=[pl.BlockSpec((1, blocks, BLOCK, cols), lambda h, inv: (h, 0, 0, 0))],
            out_specs=[
                pl.BlockSpec((blocks, HEAD_DIM, BLOCK), lambda h, inv: (0, h, 0)),
                pl.BlockSpec((1, 1, rows), lambda h, inv: (h, 0, 0)),
            ],
        ),
        out_shape=[
            jax.ShapeDtypeStruct((blocks, heads * HEAD_DIM, BLOCK), BF16),
            jax.ShapeDtypeStruct((heads, 1, rows), F32),
        ],
        compiler_params=pltpu.CompilerParams(vmem_limit_bytes=VMEM_LIMIT),
        name="attn_fwd",
    )(inv, qkv)


def attn_bwd_kernel(inv_ref, x_ref, do_ref, o_ref, l_ref, dx_ref, dk_acc, dv_acc):
    rows = l_ref.shape[2]
    hd = HEAD_DIM
    x = causal(inv_ref, x_ref)
    q = x[:, :hd] * BF16(SCALE)
    k = x[:, hd : 2 * hd]
    v = x[:, 2 * hd :]
    k_t = k.T
    dk_acc[...] = jnp.zeros_like(dk_acc)
    dv_acc[...] = jnp.zeros_like(dv_acc)
    for i in range(rows // QROWS):
        lo, hi = i * QROWS, (i + 1) * QROWS
        ids = [inv_ref[2 * i + b] for b in range(QROWS // BLOCK)]
        do_t = jnp.concatenate([do_ref[b] for b in ids], axis=1)
        o_t = jnp.concatenate([o_ref[b] for b in ids], axis=1)
        inner = jnp.sum(do_t.astype(F32) * o_t.astype(F32), axis=0, keepdims=True)
        probs = jnp.exp(causal_scores(k[:hi], q[lo:hi], lo) - l_ref[0, :, lo:hi])
        dprobs = dot(v[:hi], do_t)
        dscores = (probs * (dprobs - inner)).astype(BF16)
        dv_acc[:hi] += dot_last(probs.astype(BF16), do_t)
        dk_acc[:hi] += dot(dscores, q[lo:hi])
        dq = (dot(k_t[:, :hi], dscores) * SCALE).T
        for n, b in enumerate(ids):
            dx_ref[0, b, :, :hd] = dq[n * BLOCK : (n + 1) * BLOCK].astype(BF16)
    for i in range(rows // BLOCK):
        lo, hi = i * BLOCK, (i + 1) * BLOCK
        dx_ref[0, inv_ref[i], :, hd : 2 * hd] = dk_acc[lo:hi].astype(BF16)
        dx_ref[0, inv_ref[i], :, 2 * hd :] = dv_acc[lo:hi].astype(BF16)


def attn_bwd(inv, qkv, d_out, out, lse, heads):
    blocks, _, cols = qkv.shape[1:]
    rows = blocks * BLOCK
    whole = pl.BlockSpec((1, blocks, BLOCK, cols), lambda h, inv: (h, 0, 0, 0))
    feat = pl.BlockSpec((blocks, HEAD_DIM, BLOCK), lambda h, inv: (0, h, 0))
    return pl.pallas_call(
        attn_bwd_kernel,
        grid_spec=pltpu.PrefetchScalarGridSpec(
            num_scalar_prefetch=1,
            grid=(heads,),
            in_specs=[
                whole,
                feat,
                feat,
                pl.BlockSpec((1, 1, rows), lambda h, inv: (h, 0, 0)),
            ],
            out_specs=whole,
            scratch_shapes=[pltpu.VMEM((rows, HEAD_DIM), F32)] * 2,
        ),
        out_shape=jax.ShapeDtypeStruct((heads, blocks, BLOCK, cols), BF16),
        compiler_params=pltpu.CompilerParams(vmem_limit_bytes=VMEM_LIMIT),
        name="attn_bwd",
    )(inv, qkv, d_out, out, lse)


def own_scores(order_ref, x_ref, k):
    hd = HEAD_DIM
    blocks = x_ref.shape[1]
    first = order_ref[blocks]
    q = jnp.concatenate([x_ref[0, first], x_ref[0, first + 1]], axis=0)[:, :hd]
    q = q * BF16(SCALE)
    scores = dot_last(k, q)
    row = lax.broadcasted_iota(jnp.int32, (BLOCK, 1), 0)
    key_place = jnp.concatenate([order_ref[b] * BLOCK + row for b in range(blocks)], axis=0)
    lane = lax.broadcasted_iota(jnp.int32, (1, 2 * BLOCK), 1)
    low, high = order_ref[order_ref[blocks]], order_ref[order_ref[blocks] + 1]
    place = jnp.where(lane < BLOCK, low * BLOCK + lane, (high - 1) * BLOCK + lane)
    return q, first, jnp.where(key_place <= place, scores, -1e30)


def rest_fwd_kernel(order_ref, x_ref, o_ref, l_ref):
    hd = HEAD_DIM
    x = x_ref[0].reshape(-1, 3 * hd)
    _, _, scores = own_scores(order_ref, x_ref, x[:, hd : 2 * hd])
    out, lse = soft(scores, x[:, 2 * hd :].T)
    o_ref[0] = out.astype(BF16)
    l_ref[0] = lse


def rest_fwd(order, qkv, base):
    slots, blocks, _, cols = qkv.shape
    rest = slots - base
    return pl.pallas_call(
        rest_fwd_kernel,
        grid_spec=pltpu.PrefetchScalarGridSpec(
            num_scalar_prefetch=1,
            grid=(rest,),
            in_specs=[
                pl.BlockSpec((1, blocks, BLOCK, cols), lambda h, o: (base + h, 0, 0, 0))
            ],
            out_specs=[
                pl.BlockSpec((1, HEAD_DIM, QROWS), lambda h, o: (h, 0, 0)),
                pl.BlockSpec((1, 1, QROWS), lambda h, o: (h, 0, 0)),
            ],
        ),
        out_shape=[
            jax.ShapeDtypeStruct((rest, HEAD_DIM, QROWS), BF16),
            jax.ShapeDtypeStruct((rest, 1, QROWS), F32),
        ],
        compiler_params=pltpu.CompilerParams(vmem_limit_bytes=VMEM_LIMIT),
        name="rest_fwd",
    )(order, qkv)


def rest_bwd_kernel(order_ref, x_ref, do_ref, o_ref, l_ref, dx_ref):
    hd = HEAD_DIM
    x = x_ref[0].reshape(-1, 3 * hd)
    blocks = x_ref.shape[1]
    k = x[:, hd : 2 * hd]
    q, first, scores = own_scores(order_ref, x_ref, k)
    do_t = do_ref[0]
    inner = jnp.sum(do_t.astype(F32) * o_ref[0].astype(F32), axis=0, keepdims=True)
    probs = jnp.exp(scores - l_ref[0])
    dprobs = dot(x[:, 2 * hd :], do_t)
    dscores = (probs * (dprobs - inner)).astype(BF16)
    dv = dot_last(probs.astype(BF16), do_t).astype(BF16)
    dk = dot(dscores, q).astype(BF16)
    dq = (dot(k.T, dscores) * SCALE).T.astype(BF16)
    dx_ref[0, :, :, 2 * hd :] = dv.reshape(blocks, BLOCK, hd)
    dx_ref[0, :, :, hd : 2 * hd] = dk.reshape(blocks, BLOCK, hd)
    dx_ref[0, :, :, :hd] = jnp.zeros((blocks, BLOCK, hd), BF16)
    for b in range(2):
        dx_ref[0, first + b, :, :hd] = dq[b * BLOCK : (b + 1) * BLOCK]


def rest_bwd(order, qkv, d_out, out, lse, base):
    slots, blocks, _, cols = qkv.shape
    rest = slots - base
    feat = pl.BlockSpec((1, HEAD_DIM, QROWS), lambda h, o: (h, 0, 0))
    return pl.pallas_call(
        rest_bwd_kernel,
        grid_spec=pltpu.PrefetchScalarGridSpec(
            num_scalar_prefetch=1,
            grid=(rest,),
            in_specs=[
                pl.BlockSpec((1, blocks, BLOCK, cols), lambda h, o: (base + h, 0, 0, 0)),
                feat,
                feat,
                pl.BlockSpec((1, 1, QROWS), lambda h, o: (h, 0, 0)),
            ],
            out_specs=pl.BlockSpec((1, blocks, BLOCK, cols), lambda h, o: (h, 0, 0, 0)),
        ),
        out_shape=jax.ShapeDtypeStruct((rest, blocks, BLOCK, cols), BF16),
        compiler_params=pltpu.CompilerParams(vmem_limit_bytes=VMEM_LIMIT),
        name="rest_bwd",
    )(order, qkv, d_out, out, lse)


def far_first(i, chips):
    return (i % 2) * (i // 2) + (1 - i % 2) * (chips - 1 - i // 2)


def line_sum(chip, chips, f, core, part, from_left, from_right, sems, ready=None):
    sent, left_sem, right_sem = sems

    def to_right(d):
        return send(
            part.at[d], from_left.at[d], sent.at[d], left_sem.at[d], (2 * (chip + 1) + core, f)
        )

    def to_left(d):
        return send(
            part.at[d], from_right.at[d], sent.at[d], right_sem.at[d], (2 * (chip - 1) + core, f)
        )

    def add(d, other):
        part[d] = (part[d].astype(F32) + other[d].astype(F32)).astype(BF16)

    def step(t):
        far, near = chips - 1 - t, t

        @pl.when(chip < far)
        def _():
            if ready is not None:
                ready(far)

            @pl.when(chip > 0)
            def _():
                to_right(far).wait_recv()
                add(far, from_left)

            to_right(far).start()

        @pl.when(chip > near)
        def _():
            if ready is not None:
                ready(near)

            @pl.when(chip < chips - 1)
            def _():
                to_left(near).wait_recv()
                add(near, from_right)

            to_left(near).start()

    def finish():
        if ready is not None:
            ready(chip)

        @pl.when(chip > 0)
        def _():
            to_right(chip).wait_recv()
            add(chip, from_left)

        @pl.when(chip < chips - 1)
        def _():
            to_left(chip).wait_recv()
            add(chip, from_right)

    def done():
        for d in range(chips):

            @pl.when(chip < d)
            def _(d=d):
                to_right(d).wait_send()

            @pl.when(chip > d)
            def _(d=d):
                to_left(d).wait_send()

    return step, finish, done


def line_gather(chip, chips, f, core, view, sems):
    right, left, twin_sent, got, twin_got = sems
    twin_id = (2 * chip + 1 - core, f)

    def hop(s, rightward):
        origin = chip - s if rightward else chip + s
        ref = view(origin, core)
        peer = (2 * (chip + 1 if rightward else chip - 1) + core, f)
        return send(ref, ref, (right if rightward else left).at[s], got.at[origin], peer)

    def twin(origin):
        ref = view(origin, core)
        return send(ref, ref, twin_sent.at[origin], twin_got.at[origin], twin_id)

    def arrived(origin):
        ref = view(origin, core)
        send(ref, ref, right.at[0], got.at[origin], twin_id).wait_recv()

    def step(s):
        @pl.when(chip - s >= 0)
        def _():
            if s:
                arrived(chip - s)

            @pl.when(chip < chips - 1)
            def _():
                hop(s, True).start()

            twin(chip - s).start()

        @pl.when(chip + s < chips)
        def _():
            if s:
                arrived(chip + s)

            @pl.when(chip > 0)
            def _():
                hop(s, False).start()

            if s:
                twin(chip + s).start()

    def done():
        for s in range(chips):
            if s < chips - 1:

                @pl.when((chip - s >= 0) & (chip < chips - 1))
                def _(s=s):
                    hop(s, True).wait_send()

                @pl.when((chip + s < chips) & (chip > 0))
                def _(s=s):
                    hop(s, False).wait_send()

            twin(s).wait_send()
            ref = view(s, 1 - core)
            send(ref, ref, twin_sent.at[s], twin_got.at[s], twin_id).wait_recv()

    return step, done


def back_kernel(
    n_ctx,
    n_fsdp,
    own_ref,
    rest_ref,
    w_ref,
    n_ref,
    one_ref,
    cols_ref,
    part,
    twin_out,
    twin_in,
    from_left,
    from_right,
    mine,
    theirs,
    twin_send,
    twin_recv,
    line_send,
    left_recv,
    right_recv,
    cols_send,
    cols_recv,
):
    c = lax.axis_index("ctx")
    f = lax.axis_index("fsdp")
    chips = n_ctx // 2
    chip, core = c // 2, c % 2
    slots, width, cols = w_ref.shape
    count = own_ref.shape[2]
    base = own_ref.shape[0]
    shard = width // n_fsdp
    enter(
        [(lax.rem(c + i, n_ctx), f) for i in range(1, n_ctx)]
        + [(c, flip(f, k, n_fsdp)) for k in range(1, n_fsdp)]
    )

    def grad(s):
        return own_ref.at[s] if s < base else rest_ref.at[s - base]

    def for_block(b):
        total = dot_last(grad(0)[b], w_ref[0])
        for s in range(1, slots):
            total += dot_last(grad(s)[b], w_ref[s])
        return total.astype(BF16)

    def to_twin(d):
        return send(
            twin_out.at[d], twin_in.at[d], twin_send.at[d], twin_recv.at[d], (2 * chip + 1 - core, f)
        )

    def products(i, carry):
        d = far_first(i, chips)
        twin_out[d] = for_block(2 * d + 1 - core)
        to_twin(d).start()
        part[d] = for_block(2 * d + core)
        return carry

    def ready(d):
        to_twin(d).wait_recv()
        part[d] = (part[d].astype(F32) + twin_in[d].astype(F32)).astype(BF16)

    step, finish, done = line_sum(
        chip, chips, f, core, part, from_left, from_right, (line_send, left_recv, right_recv), ready
    )

    def columns(j):
        left = n_ref[:, :, j * shard : (j + 1) * shard].reshape(n_ctx * count, shard)
        for s in range(slots):
            right = grad(s)[...].reshape(n_ctx * count, cols)
            mine[j, s] = dot_first(left, right).astype(BF16)

        @pl.when(f != j)
        def _():
            send(mine.at[j], theirs.at[f], cols_send.at[j], cols_recv.at[f], (c, j)).start()

    lax.fori_loop(0, chips, products, 0)
    for t in range(max(chips - 1, n_fsdp)):
        if t < chips - 1:
            step(t)
        if t < n_fsdp:
            columns(t)
    total = mine[f].astype(F32)
    for k in range(1, n_fsdp):
        other = flip(f, k, n_fsdp)
        send(
            mine.at[other], theirs.at[other], cols_send.at[other], cols_recv.at[other], (c, other)
        ).wait_recv()
        total += theirs[other].astype(F32)
    cols_ref[...] = total.astype(BF16)
    finish()
    one_ref[...] = part[chip].astype(F32)
    done()
    for d in range(chips):
        to_twin(d).wait_send()
    for k in range(1, n_fsdp):
        other = flip(f, k, n_fsdp)
        send(
            mine.at[other], theirs.at[other], cols_send.at[other], cols_recv.at[other], (c, other)
        ).wait_send()


def back_fits(n_ctx, n_fsdp, count, width, slots):
    blocks = (5 * (n_ctx // 2) + n_ctx) * count * width
    heads = slots * 256 * (n_ctx * count + 3 * width)
    return 2 * (blocks + heads) < 50 * 1024 * 1024


def back_call(n_ctx, n_fsdp, own, rest, w_slots, normed, cid):
    slots, width, cols = w_slots.shape
    count = normed.shape[1]
    chips = n_ctx // 2
    shard = width // n_fsdp
    vm = pl.BlockSpec(memory_space=pltpu.VMEM)
    dma = pltpu.SemaphoreType.DMA
    block = pltpu.VMEM((chips, count, width), BF16)
    piece = pltpu.VMEM((n_fsdp, slots, shard, cols), BF16)
    return pl.pallas_call(
        functools.partial(back_kernel, n_ctx, n_fsdp),
        in_specs=[vm] * 4,
        out_specs=[vm] * 2,
        out_shape=[
            jax.ShapeDtypeStruct((count, width), F32),
            jax.ShapeDtypeStruct((slots, shard, cols), BF16),
        ],
        scratch_shapes=[block] * 5
        + [piece] * 2
        + [dma((chips,))] * 5
        + [dma((n_fsdp,))] * 2,
        compiler_params=pltpu.CompilerParams(
            collective_id=cid, has_side_effects=True, vmem_limit_bytes=60 * 1024 * 1024
        ),
        name="qkv_back",
    )(own, rest, w_slots, normed)


def sums_kernel(n_ctx, n_fsdp, lead, *refs):
    (blob_ref, cols_ref, lines_in, blob_all, cols_all, lines_ref, part, from_left, from_right) = (
        refs[:9]
    )
    (lines_got, sum_send, left_recv, right_recv) = refs[9:13]
    blob_sems, cols_sems, (lines_send, lines_recv, local) = refs[13:18], refs[18:23], refs[23:26]
    c = lax.axis_index("ctx")
    f = lax.axis_index("fsdp")
    chips = n_ctx // 2
    chip, core = c // 2, c % 2
    enter(
        [(lax.rem(c + i, n_ctx), f) for i in range(1, n_ctx)]
        + [(c, flip(f, k, n_fsdp)) for k in range(1, n_fsdp)]
    )
    cols_step, cols_done = line_gather(
        chip, chips, f, core, lambda at, h: cols_all.at[2 * at + h], cols_sems
    )
    blob_step, blob_done = line_gather(
        chip, chips, f, core, lambda at, h: blob_all.at[h, at], blob_sems
    )
    sum_step, sum_finish, sum_done = line_sum(
        chip, chips, f, core, part, from_left, from_right, (sum_send, left_recv, right_recv)
    )
    load = pltpu.make_async_copy(cols_ref, cols_all.at[c], local.at[0])
    load.start()
    part[...] = blob_ref[...]
    sum_step(0)
    load.wait()
    cols_step(0)
    peers = [(flip(c, 1 << i, n_ctx), f) for i in range(n_ctx.bit_length() - 1)]
    ctx_phases = len(peers)
    peers += [(c, flip(f, 1 << i, n_fsdp)) for i in range(n_fsdp.bit_length() - 1)]
    lines_ref[...] = lines_in[...]
    for i, peer in enumerate(peers):
        rows = lines_in.shape[0] if i < ctx_phases else lead
        copy = send(
            lines_ref.at[:rows], lines_got.at[i, :rows], lines_send.at[i], lines_recv.at[i], peer
        )
        copy.start()
        copy.wait()
        lines_ref[:rows] += lines_got[i, :rows]
    for t in range(1, chips):
        if t < chips - 1:
            sum_step(t)
        cols_step(t)
    sum_finish()
    keep = pltpu.make_async_copy(part.at[chip], blob_all.at[core, chip], local.at[1])
    keep.start()
    keep.wait()
    for s in range(chips):
        blob_step(s)
    sum_done()
    cols_done()
    blob_done()


def sums_call(n_ctx, n_fsdp, blob, cols, lines, lead, cid):
    chips = n_ctx // 2
    phases = (n_ctx * n_fsdp).bit_length() - 1
    vm = pl.BlockSpec(memory_space=pltpu.VMEM)
    anym = pl.BlockSpec(memory_space=pl.ANY)
    dma = pltpu.SemaphoreType.DMA
    gather_sems = [dma((chips,))] * 5
    return pl.pallas_call(
        functools.partial(sums_kernel, n_ctx, n_fsdp, lead),
        in_specs=[vm, anym, vm],
        out_specs=[vm, vm, vm],
        out_shape=[
            jax.ShapeDtypeStruct((2,) + blob.shape, BF16),
            jax.ShapeDtypeStruct((n_ctx,) + cols.shape, BF16),
            jax.ShapeDtypeStruct(lines.shape, F32),
        ],
        scratch_shapes=[pltpu.VMEM(blob.shape, BF16)] * 3
        + [pltpu.VMEM((phases,) + lines.shape, F32)]
        + [dma((chips,))] * 3
        + gather_sems * 2
        + [dma((phases,))] * 2
        + [dma((2,))],
        compiler_params=pltpu.CompilerParams(
            collective_id=cid, has_side_effects=True, vmem_limit_bytes=60 * 1024 * 1024
        ),
        name="weight_sums",
    )(blob, cols, lines)


def assemble_kernel(own_ref, rest_ref, o_ref):
    hd = HEAD_DIM
    width = o_ref.shape[1] // 3
    count = own_ref.shape[0]
    for h in range(width // hd):
        src = own_ref.at[h] if h < count else rest_ref.at[h - count]
        for part in range(3):
            at = part * width + h * hd
            o_ref[:, at : at + hd] = src[:, part * hd : (part + 1) * hd].astype(F32)


def assemble(own, rest, out_cols):
    rows = own.shape[1]
    return pl.pallas_call(
        assemble_kernel,
        out_shape=jax.ShapeDtypeStruct((rows, out_cols), F32),
        compiler_params=pltpu.CompilerParams(vmem_limit_bytes=VMEM_LIMIT),
        name="assemble",
    )(own, rest)


def norm_parts(rows):
    mean = jnp.mean(rows, axis=-1, keepdims=True)
    cen = rows - mean
    rstd = lax.rsqrt(jnp.mean(cen * cen, axis=-1, keepdims=True) + EPS)
    return cen * rstd, rstd


def norm_back(xhat, rstd, gain, grad):
    dxhat = grad * gain
    return rstd * (
        dxhat
        - jnp.mean(dxhat, axis=-1, keepdims=True)
        - xhat * jnp.mean(dxhat * xhat, axis=-1, keepdims=True)
    )


def swap(value, axis, size, k):
    return lax.ppermute(value, axis, [(i, i ^ k) for i in range(size)])


def shards(
    n_ctx,
    n_fsdp,
    tokens,
    block_order,
    w_attn,
    w_proj,
    w_fc,
    w_out,
    norm_gains,
    biases,
    fc_bias,
    cotangent,
):
    hd = HEAD_DIM
    count, width = tokens.shape[1:]
    shard = width // n_fsdp
    heads = width // hd
    base = heads // n_ctx
    rest = heads - base * n_ctx
    slots = base + rest
    own_blocks = count // BLOCK
    c = lax.axis_index("ctx")
    f = lax.axis_index("fsdp")

    order = block_order[0]
    inv = jnp.argsort(order).astype(jnp.int32)
    order_own = jnp.concatenate([order, (c * own_blocks)[None]])

    def head_cols(h):
        return jnp.concatenate(
            [
                lax.dynamic_slice(w_attn, (0, part * width + h * hd), (shard, hd))
                for part in range(3)
            ],
            axis=1,
        )

    slot_heads = [c * base + s for s in range(base)] + [n_ctx * base + r for r in range(rest)]
    w_slots = jnp.stack([head_cols(h) for h in slot_heads])
    small = jnp.concatenate([norm_gains, biases], axis=0).astype(F32)
    hidden_cols = w_fc.shape[1] // n_fsdp
    fc_parts = jnp.stack(
        [w_fc[:, j * hidden_cols : (j + 1) * hidden_cols] for j in range(n_fsdp)]
    )
    normed_one, qkv, full_proj, fc_cols, w_slots, small = start_call(
        n_ctx, n_fsdp, base, tokens[0], w_slots, small, w_proj, fc_parts, 3
    )
    full_proj = full_proj.reshape(width, width)
    fc_cols = fc_cols.reshape(width, hidden_cols)
    qkv = qkv.reshape(slots, n_ctx * own_blocks, BLOCK, 3 * hd)
    gains, shifts = small[:2], small[2:]
    cot = cotangent[0]

    cot_late, _ = lax.optimization_barrier((cot, small))
    cot_all = lax.all_gather(cot_late, "fsdp", axis=0)

    out_own, lse_own = attn_fwd(inv, qkv, base)
    got = lax.all_to_all(out_own, "ctx", split_axis=0, concat_axis=0, tiled=True)
    got = got.reshape(n_ctx, own_blocks, base * hd, BLOCK).transpose(1, 3, 0, 2)
    attended = got.reshape(count, n_ctx * base * hd)
    if rest:
        out_rest, lse_rest = rest_fwd(order_own, qkv, base)
        attended = jnp.concatenate([attended, out_rest.reshape(rest * hd, count).T], axis=1)

    rows = tokens[0].astype(F32)
    mid = rows + (dot(attended, full_proj) + shifts[4])
    xhat_two, rstd_two = norm_parts(mid)
    normed_two = (xhat_two * gains[1] + shifts[1]).astype(BF16)

    normed_two_grad, fc_bias_part, out_part, w_out_part, w_fc_part = ffn(
        n_fsdp,
        normed_two,
        cot_all,
        fc_cols,
        w_out,
        fc_bias.astype(F32)[None],
    )
    out_rows = lax.psum_scatter(
        out_part.reshape(n_fsdp * count, width), "fsdp", scatter_dimension=0, tiled=True
    )
    layer_rows = (mid + (out_rows.astype(F32) + shifts[5])).astype(BF16)
    w_out_grad = lax.psum(w_out_part, "ctx").astype(F32)

    half = shard // 2
    core = c % 2

    def core_half(part):
        away = lax.dynamic_slice_in_dim(part, (1 - core) * half, half, 1)
        here = lax.dynamic_slice_in_dim(part, core * half, half, 1)
        return (here.astype(F32) + swap(away, "ctx", n_ctx, 1).astype(F32)).astype(BF16)

    def over_fsdp(part):
        out = []
        for k in range(n_fsdp):
            piece = lax.dynamic_index_in_dim(part, f ^ k, keepdims=False)
            out.append(swap(piece, "fsdp", n_fsdp, k) if k else piece)
        return out

    w_fc_half = jnp.stack(over_fsdp(core_half(w_fc_part.reshape(n_fsdp, shard, hidden_cols))))

    cot_rows = cot.astype(F32)
    mid_grad = cot_rows + norm_back(xhat_two, rstd_two, gains[1], normed_two_grad)
    mid_low = mid_grad.astype(BF16)
    over_rows = functools.partial(jnp.einsum, "ta,tb->ab", preferred_element_type=F32)
    attended_grad = dot_last(mid_low, full_proj).astype(BF16)
    w_proj_part = over_rows(attended, mid_low).astype(BF16)
    w_proj_half = sum(
        piece.astype(F32)
        for piece in over_fsdp(core_half(w_proj_part.reshape(n_fsdp, shard, width)))
    ).astype(BF16)

    main = n_ctx * base * hd
    sent = attended_grad[:, :main].reshape(own_blocks, BLOCK, n_ctx, base * hd)
    sent = sent.transpose(2, 0, 3, 1).reshape(n_ctx * own_blocks, base * hd, BLOCK)
    d_out = lax.all_to_all(sent, "ctx", split_axis=0, concat_axis=0, tiled=True)
    d_own = attn_bwd(inv, qkv, d_out, out_own, lse_own, base)
    d_own = d_own.reshape(base, n_ctx, count, 3 * hd)
    if rest:
        d_rest = attended_grad[:, main:].T.reshape(rest, hd, count)
        d_rest = rest_bwd(order_own, qkv, d_rest, out_rest, lse_rest, base)
        d_rest = d_rest.reshape(rest, n_ctx, count, 3 * hd)
        sums = jnp.concatenate(
            [jnp.sum(d.astype(F32), axis=(1, 2)) for d in (d_own, d_rest)], axis=0
        )
    else:
        d_rest = d_own
        sums = jnp.sum(d_own.astype(F32), axis=(1, 2))
    if back_fits(n_ctx, n_fsdp, count, width, slots):
        normed_one_grad, cols_sum = back_call(
            n_ctx, n_fsdp, d_own, d_rest, w_slots, normed_one, 4
        )
    else:
        dqkv = jnp.concatenate([d_own, d_rest])[:slots].reshape(slots, n_ctx * count, 3 * hd)
        one_part = jnp.einsum("hte,hde->td", dqkv, w_slots, preferred_element_type=F32)
        normed_one_grad = lax.psum_scatter(
            one_part.astype(BF16), "ctx", scatter_dimension=0, tiled=True
        ).astype(F32)
        slot_part = jnp.einsum(
            "td,hte->hde",
            normed_one.reshape(n_ctx * count, width),
            dqkv,
            preferred_element_type=F32,
        ).astype(BF16)
        cols_sum = lax.psum_scatter(slot_part, "fsdp", scatter_dimension=1, tiled=True)

    xhat_one, rstd_one = norm_parts(rows)
    tokens_grad = (mid_grad + norm_back(xhat_one, rstd_one, gains[0], normed_one_grad)).astype(
        BF16
    )

    def placed(part):
        cols = sums[:, part * hd : (part + 1) * hd]
        line = lax.dynamic_update_slice_in_dim(
            jnp.zeros((width,), F32), cols[:base].reshape(-1), c * base * hd, 0
        )
        return line + jnp.pad(cols[base:].reshape(-1), (main, 0))

    lines = jnp.stack(
        [
            jnp.sum(normed_one_grad * xhat_one, axis=0),
            jnp.sum(normed_two_grad * xhat_two, axis=0),
            jnp.sum(normed_one_grad, axis=0),
            jnp.sum(normed_two_grad, axis=0),
            placed(0),
            placed(2),
            jnp.sum(mid_low.astype(F32), axis=0),
            jnp.sum(cot_rows, axis=0),
        ]
    )
    lead = lines.shape[0]
    tail = jnp.pad(fc_bias_part, ((0, 7), (0, width - hidden_cols)))
    lines = jnp.concatenate([lines, tail])

    chips = n_ctx // 2
    parts = [w_fc_half.reshape(-1, width), w_proj_half]
    if rest:
        parts.append(core_half(cols_sum[base:]).reshape(-1, width))
    bounds = [0]
    for part in parts:
        bounds.append(bounds[-1] + part.shape[0])
    per_chip = -(-bounds[-1] // (16 * chips)) * 16
    blob = jnp.concatenate(parts)
    blob = jnp.pad(blob, ((0, per_chip * chips - bounds[-1]), (0, 0)))
    blob, own_cols, lines = sums_call(
        n_ctx, n_fsdp, blob.reshape(chips, per_chip, width), cols_sum[:base], lines, lead, 5
    )
    blob = blob.reshape(2, chips * per_chip, width)
    w_fc_low = blob[:, : bounds[1]].reshape(2, n_fsdp, half, hidden_cols)
    w_fc_grad = jnp.concatenate(
        [
            lax.dynamic_index_in_dim(w_fc_low, f ^ j, axis=1, keepdims=False).reshape(
                shard, hidden_cols
            )
            for j in range(n_fsdp)
        ],
        axis=1,
    ).astype(F32)
    w_proj_grad = blob[:, bounds[1] : bounds[2]].reshape(shard, width).astype(F32)
    own_cols = own_cols.reshape(n_ctx * base, shard, 3 * hd)
    if rest:
        rest_cols = blob[:, bounds[2] : bounds[3]].reshape(2, rest, half, 3 * hd)
        rest_cols = rest_cols.transpose(1, 0, 2, 3).reshape(rest, shard, 3 * hd)
    else:
        rest_cols = own_cols
    w_attn_grad = assemble(own_cols, rest_cols, 3 * width)
    fc_bias_grad = lines[lead, :hidden_cols]
    lines = lax.dynamic_slice_in_dim(lines[:lead], f * shard, shard, 1)
    return (
        layer_rows[None],
        tokens_grad[None],
        w_attn_grad,
        w_proj_grad,
        w_fc_grad,
        w_out_grad,
        lines[:2],
        lines[2:],
        fc_bias_grad,
    )


def solution(mesh):
    rows = P("fsdp", "ctx", None)
    weight = P("fsdp", None)
    vectors = P(None, "fsdp")
    return jax.shard_map(
        functools.partial(shards, mesh.shape["ctx"], mesh.shape["fsdp"]),
        mesh=mesh,
        in_specs=(
            rows, weight, weight, weight, weight, weight, vectors, vectors, P("fsdp"), rows,
        ),
        out_specs=(
            rows, rows, weight, weight, weight, weight, vectors, vectors, P("fsdp"),
        ),
        check_vma=False,
    )
```

```python
import functools

import jax
import jax.numpy as jnp
from jax import lax
from jax.experimental import pallas as pl
from jax.experimental.pallas import tpu as pltpu
from jax.sharding import PartitionSpec as P

HEAD_DIM = 64
BLOCK = 128
QROWS = 256
EPS = 1e-05
SCALE = HEAD_DIM ** (-0.5)
F32 = jnp.float32
BF16 = jnp.bfloat16
VMEM_LIMIT = 56 * 1024 * 1024
LAST = (((1,), (1,)), ((), ()))
FIRST = (((0,), (0,)), ((), ()))
MESH = pl.DeviceIdType.MESH
TILE = 256


def dot_last(a, b):
    return lax.dot_general(a, b, LAST, preferred_element_type=F32)


def dot(a, b):
    return jnp.dot(a, b, preferred_element_type=F32)


def dot_first(a, b):
    return lax.dot_general(a, b, FIRST, preferred_element_type=F32)


SHORT = pl.CostEstimate(flops=1, bytes_accessed=1, transcendentals=0)


def flip(place, k, size):
    out = 0
    bit = 1
    while bit < size:
        out = out + (place // bit + k // bit) % 2 * bit
        bit *= 2
    return out

def enter(peers):
    barrier = pltpu.get_barrier_semaphore()
    for peer in peers:
        pl.semaphore_signal(barrier, inc=1, device_id=peer, device_id_type=MESH)
    pl.semaphore_wait(barrier, len(peers))

def send(src, dst, send_sem, recv_sem, peer):
    return pltpu.make_async_remote_copy(
        src_ref=src, dst_ref=dst, send_sem=send_sem, recv_sem=recv_sem,
        device_id=peer, device_id_type=MESH)


def ffn_kernel(n, nt_hbm, cot_hbm, wfc_hbm, wout_hbm, bias_ref,
               gsum_ref, fcb_ref, out_hbm, wout_grad_hbm, wfc_grad_hbm,
               cot_ref, wfc_ref, wout_ref, all_ref, act_ref, hg_ref, ag_ref, part_ref, got_ref, stage_d, stage_h,
               s1, r1, s2, r2, local):
    c = lax.axis_index("ctx")
    f = lax.axis_index("fsdp")
    rows, width = nt_hbm.shape
    enter([(c, flip(f, k, n)) for k in range(1, n)])

    def rows_out(k):
        return send(nt_hbm, all_ref.at[f], s1.at[k], r1.at[k], (c, flip(f, k, n)))

    def grad_back(k):
        other = flip(f, k, n)
        return send(part_ref.at[other], got_ref.at[k], s2.at[k], r2.at[k], (c, other))

    near = [k for k in range(1, n) if k & (k - 1) == 0]
    far = [k for k in range(1, n) if k not in near]
    for k in near:
        rows_out(k).start()
    loads = [
        pltpu.make_async_copy(nt_hbm, all_ref.at[f], local.at[0]),
        pltpu.make_async_copy(wout_hbm, wout_ref, local.at[1]),
        pltpu.make_async_copy(cot_hbm, cot_ref, local.at[2]),
        pltpu.make_async_copy(wfc_hbm, wfc_ref, local.at[3]),
    ]
    for load in loads:
        load.start()
    fcb_ref[...] = jnp.zeros_like(fcb_ref)
    loads[1].wait()
    loads[2].wait()

    def active_grad(k, carry):
        ag_ref[k] = dot_last(cot_ref[k], wout_ref[...])
        return carry

    lax.fori_loop(0, n, active_grad, 0)
    for k in far:
        rows_out(k).start()
    loads[0].wait()
    loads[3].wait()

    def chunk(k, carry):
        src = flip(f, k, n)

        @pl.when(k > 0)
        def _():
            rows_out(k).wait_recv()

        hidden = dot(all_ref[src], wfc_ref[...]) + bias_ref[...]
        square = hidden * hidden
        tanh = jnp.tanh(0.7978845608028654 * (hidden + 0.044715 * square * hidden))
        act_ref[src] = (0.5 * hidden * (1.0 + tanh)).astype(BF16)
        slope = 0.5 * (1.0 + tanh) + 0.5 * hidden * (1.0 - tanh * tanh) * 0.7978845608028654 * (
            1.0 + 3.0 * 0.044715 * square
        )
        grad = (ag_ref[src] * slope).astype(BF16)
        hg_ref[src] = grad
        fcb_ref[...] += jnp.sum(grad.astype(F32), axis=0, keepdims=True)
        part_ref[src] = dot_last(grad, wfc_ref[...]).astype(BF16)

        @pl.when(k > 0)
        def _():
            grad_back(k).start()

        return carry

    lax.fori_loop(0, n, chunk, 0)

    def grads(left_ref, right_ref, dst, stage_ref, base):
        wide = left_ref.shape[2]
        right = right_ref[...].reshape(n * rows, right_ref.shape[2])
        copies = []
        for i, lo in enumerate(range(0, wide, TILE)):
            hi = min(lo + TILE, wide)
            slot = i % 2
            if i >= 2:
                copies[i - 2].wait()
            left = left_ref[:, :, lo:hi].reshape(n * rows, hi - lo)
            stage_ref[slot, : hi - lo] = dot_first(left, right).astype(BF16)
            copies.append(
                pltpu.make_async_copy(
                    stage_ref.at[slot, : hi - lo], dst.at[lo:hi], local.at[base + slot]
                )
            )
            copies[-1].start()
        for copy in copies[-2:]:
            copy.wait()

    grads(act_ref, cot_ref, wout_grad_hbm, stage_d, 4)
    grads(all_ref, hg_ref, wfc_grad_hbm, stage_h, 6)

    def out_copy(k):
        return pltpu.make_async_copy(
            stage_d.at[k % 2, :rows], out_hbm.at[k], local.at[4 + k % 2]
        )

    for k in range(n):
        if k >= 2:
            out_copy(k - 2).wait()
        stage_d[k % 2, :rows] = dot(act_ref[k], wout_ref[...]).astype(BF16)
        out_copy(k).start()

    gsum_ref[...] = part_ref[f].astype(F32)
    for k in near + far:
        grad_back(k).wait_recv()
        gsum_ref[...] += got_ref[k].astype(F32)
    for k in range(1, n):
        rows_out(k).wait_send()
        grad_back(k).wait_send()
    for k in range(max(0, n - 2), n):
        out_copy(k).wait()


def ffn(n, nt, cot, wfc, wout, bias, cid=1):
    m, d = nt.shape
    h = wfc.shape[1]
    vm = pl.BlockSpec(memory_space=pltpu.VMEM)
    anym = pl.BlockSpec(memory_space=pl.ANY)
    return pl.pallas_call(
        functools.partial(ffn_kernel, n),
        in_specs=[anym] * 4 + [vm],
        out_specs=[vm, vm] + [anym] * 3,
        out_shape=[
            jax.ShapeDtypeStruct((m, d), F32),
            jax.ShapeDtypeStruct((1, h), F32),
            jax.ShapeDtypeStruct((n, m, d), BF16),
            jax.ShapeDtypeStruct((h, d), BF16),
            jax.ShapeDtypeStruct((d, h), BF16),
        ],
        scratch_shapes=[
            pltpu.VMEM((n, m, d), BF16),
            pltpu.VMEM((d, h), BF16),
            pltpu.VMEM((h, d), BF16),
            pltpu.VMEM((n, m, d), BF16),
            pltpu.VMEM((n, m, h), BF16),
            pltpu.VMEM((n, m, h), BF16),
            pltpu.VMEM((n, m, h), F32),
            pltpu.VMEM((n, m, d), BF16),
            pltpu.VMEM((n, m, d), BF16),
            pltpu.VMEM((2, max(TILE, m), d), BF16),
            pltpu.VMEM((2, TILE, h), BF16),
        ]
        + [pltpu.SemaphoreType.DMA((n,))] * 4
        + [pltpu.SemaphoreType.DMA((8,))],
        compiler_params=pltpu.CompilerParams(
            collective_id=cid, has_side_effects=True, vmem_limit_bytes=60 * 1024 * 1024
        ),
        cost_estimate=SHORT,
        name="feed_forward",
    )(nt, cot, wfc, wout, bias)


def start_kernel(
    n_ctx,
    n_fsdp,
    base,
    tok_hbm,
    w_hbm,
    small_ref,
    proj_hbm,
    fc_hbm,
    n_hbm,
    qkv_hbm,
    proj_all,
    fc_all,
    w_ref,
    lines_ref,
    n_ref,
    qkv_ref,
    x_ref,
    wg_ref,
    sg_ref,
    tok_recv,
    right_sem,
    left_sem,
    twin_sem,
    w_send,
    w_recv,
    s_send,
    s_recv,
    proj_send,
    proj_recv,
    fc_send,
    fc_recv,
    local,
):
    c = lax.axis_index("ctx")
    f = lax.axis_index("fsdp")
    chips = n_ctx // 2
    chip, core = c // 2, c % 2
    slots, width, cols = w_ref.shape
    shard = width // n_fsdp
    hd = HEAD_DIM
    enter(
        [(lax.rem(c + i, n_ctx), f) for i in range(1, n_ctx)]
        + [(c, flip(f, k, n_fsdp)) for k in range(1, n_fsdp)]
    )

    def block(at, same):
        return 2 * at + (core if same else 1 - core)

    def hop(step, to_right, from_own):
        origin = block(chip - step if to_right else chip + step, True)
        src = tok_hbm if from_own else x_ref.at[origin]
        sem = (right_sem if to_right else left_sem).at[step]
        peer = (c + 2 if to_right else c - 2, f)
        return send(src, x_ref.at[origin], sem, tok_recv.at[origin], peer)

    def twin(at, from_own):
        origin = block(at, True)
        src = tok_hbm if from_own else x_ref.at[origin]
        return send(
            src, x_ref.at[origin], twin_sem.at[at], tok_recv.at[origin], (block(chip, False), f)
        )

    def w_copy(k):
        return send(w_hbm, wg_ref.at[f], w_send.at[k], w_recv.at[k], (c, flip(f, k, n_fsdp)))

    def s_copy(k):
        return send(small_ref, sg_ref.at[f], s_send.at[k], s_recv.at[k], (c, flip(f, k, n_fsdp)))

    cut = shard // 32 * 16 if shard % 16 == 0 else 0
    shares = ((0, cut), (cut, shard)) if cut else ((0, shard), (0, shard))

    def weight_copy(share, k, onward, which):
        lo, hi = share
        other = flip(f, k, n_fsdp)
        dst = (proj_all, fc_all)[which]
        ss = (proj_send, fc_send)[which]
        rs = (proj_recv, fc_recv)[which]
        if onward:
            part = dst.at[other, lo:hi]
            return send(part, part, ss.at[1, k], rs.at[1, k], (block(chip, False), f))
        src = fc_hbm.at[other, lo:hi] if which else proj_hbm.at[lo:hi]
        return send(src, dst.at[f, lo:hi], ss.at[0, k], rs.at[0, k], (c, other))

    def by_core(act):
        for h in range(2):

            @pl.when(core == h)
            def _(h=h):
                act(shares[h], shares[1 - h])

    def weights_start(mine, theirs):
        for i in range(2):
            for k in range(1, n_fsdp):
                weight_copy(mine, k, False, i).start()

    def weights_onward(mine, theirs):
        for i in range(2):
            for k in range(1, n_fsdp):
                weight_copy(mine, k, False, i).wait_recv()
                if cut:
                    weight_copy(mine, k, True, i).start()

    def weights_done(mine, theirs):
        for i in range(2):
            for k in range(1, n_fsdp):
                if cut:
                    weight_copy(theirs, k, True, i).wait_recv()
                    weight_copy(mine, k, True, i).wait_send()
                weight_copy(mine, k, False, i).wait_send()

    for k in range(1, n_fsdp):
        s_copy(k).start()

    @pl.when(chip < chips - 1)
    def _():
        hop(0, True, True).start()

    @pl.when(chip > 0)
    def _():
        hop(0, False, True).start()

    for k in range(1, n_fsdp):
        w_copy(k).start()
    twin(chip, True).start()
    own_x = pltpu.make_async_copy(tok_hbm, x_ref.at[c], local.at[0])
    own_w = pltpu.make_async_copy(w_hbm, wg_ref.at[f], local.at[1])
    own_proj = pltpu.make_async_copy(proj_hbm, proj_all.at[f], local.at[2])
    own_fc = pltpu.make_async_copy(fc_hbm.at[f], fc_all.at[f], local.at[3])
    for copy in (own_x, own_w, own_proj, own_fc):
        copy.start()
    sg_ref[f] = small_ref[...]
    for k in range(1, n_fsdp):
        s_copy(k).wait_recv()
    for j in range(n_fsdp):
        lines_ref[:, j * shard : (j + 1) * shard] = sg_ref[j]
    main = n_ctx * base * hd
    row_id = lax.broadcasted_iota(jnp.int32, (width, slots * hd), 0)
    col_id = lax.broadcasted_iota(jnp.int32, (width, slots * hd), 1)
    wanted = jnp.where(col_id < base * hd, c * base * hd + col_id, main + col_id - base * hd)
    picked = dot(lines_ref[...].astype(BF16), (row_id == wanted).astype(BF16))
    zero = jnp.zeros((1, hd), F32)
    bias = [
        jnp.concatenate(
            [picked[4:5, s * hd : (s + 1) * hd], zero, picked[5:6, s * hd : (s + 1) * hd]], axis=1
        )
        for s in range(slots)
    ]
    own_w.wait()
    own_x.wait()
    for k in range(1, n_fsdp):
        w_copy(k).wait_recv()
    by_core(weights_start)
    for j in range(n_fsdp):
        w_ref[:, j * shard : (j + 1) * shard, :] = wg_ref[j]

    def results(origin):
        return (
            pltpu.make_async_copy(n_ref, n_hbm.at[origin], local.at[0]),
            pltpu.make_async_copy(qkv_ref, qkv_hbm.at[:, origin], local.at[1]),
        )

    def project(at, same, first=False):
        origin = block(at, same)
        rows = x_ref[origin].astype(F32)
        mean = jnp.mean(rows, axis=1, keepdims=True)
        cen = rows - mean
        var = jnp.mean(cen * cen, axis=1, keepdims=True)
        normed = cen * lax.rsqrt(var + EPS) * lines_ref[0:1] + lines_ref[2:3]
        normed = normed.astype(BF16)

        @pl.when(jnp.logical_not(first))
        def _():
            for copy in results(origin):
                copy.wait()

        n_ref[...] = normed
        for s in range(slots):
            qkv_ref[s] = (dot(normed, w_ref[s]) + bias[s]).astype(BF16)
        for copy in results(origin):
            copy.start()

    def arrived(at, same):
        origin = block(at, same)
        pltpu.make_async_copy(x_ref.at[origin], x_ref.at[origin], tok_recv.at[origin]).wait()

    def step(s, carry):
        @pl.when((s > 0) & (chip - s >= 0))
        def _():
            arrived(chip - s, True)
            twin(chip - s, False).start()

            @pl.when(chip < chips - 1)
            def _():
                hop(s, True, False).start()

        @pl.when((s > 0) & (chip + s < chips))
        def _():
            arrived(chip + s, True)
            twin(chip + s, False).start()

            @pl.when(chip > 0)
            def _():
                hop(s, False, False).start()

        @pl.when(chip - s >= 0)
        def _():
            project(chip - s, True, s == 0)

        @pl.when((s > 0) & (chip + s < chips))
        def _():
            project(chip + s, True)

        @pl.when(chip - s >= 0)
        def _():
            arrived(chip - s, False)
            project(chip - s, False)

        @pl.when((s > 0) & (chip + s < chips))
        def _():
            arrived(chip + s, False)
            project(chip + s, False)

        return carry

    lax.fori_loop(0, chips, step, 0)
    by_core(weights_onward)
    for copy in results(c):
        copy.wait()
    own_proj.wait()
    own_fc.wait()

    for s in range(chips):
        if s < chips - 1:

            @pl.when((chip - s >= 0) & (chip < chips - 1))
            def _():
                hop(s, True, False).wait_send()

            @pl.when((chip + s < chips) & (chip > 0))
            def _():
                hop(s, False, False).wait_send()

        twin(s, False).wait_send()
    for k in range(1, n_fsdp):
        w_copy(k).wait_send()
        s_copy(k).wait_send()
    by_core(weights_done)


def start_call(n_ctx, n_fsdp, base, tok, w_slots, small, w_proj, fc_parts, cid):
    count, width = tok.shape
    slots, shard, cols = w_slots.shape
    vm = pl.BlockSpec(memory_space=pltpu.VMEM)
    anym = pl.BlockSpec(memory_space=pl.ANY)
    dma = pltpu.SemaphoreType.DMA
    return pl.pallas_call(
        functools.partial(start_kernel, n_ctx, n_fsdp, base),
        in_specs=[anym, anym, vm, anym, anym],
        out_specs=[anym, anym, anym, anym, vm, vm],
        out_shape=[
            jax.ShapeDtypeStruct((n_ctx, count, width), BF16),
            jax.ShapeDtypeStruct((slots, n_ctx, count, cols), BF16),
            jax.ShapeDtypeStruct((n_fsdp,) + w_proj.shape, BF16),
            jax.ShapeDtypeStruct(fc_parts.shape, BF16),
            jax.ShapeDtypeStruct((slots, width, cols), BF16),
            jax.ShapeDtypeStruct((small.shape[0], width), F32),
        ],
        scratch_shapes=[
            pltpu.VMEM((count, width), BF16),
            pltpu.VMEM((slots, count, cols), BF16),
            pltpu.VMEM((n_ctx, count, width), BF16),
            pltpu.VMEM((n_fsdp, slots, shard, cols), BF16),
            pltpu.VMEM((n_fsdp,) + small.shape, F32),
            dma((n_ctx,)),
            dma((n_ctx // 2,)),
            dma((n_ctx // 2,)),
            dma((n_ctx // 2,)),
            dma((n_fsdp,)),
            dma((n_fsdp,)),
            dma((n_fsdp,)),
            dma((n_fsdp,)),
            dma((2, n_fsdp)),
            dma((2, n_fsdp)),
            dma((2, n_fsdp)),
            dma((2, n_fsdp)),
            dma((4,)),
        ],
        compiler_params=pltpu.CompilerParams(
            collective_id=cid, has_side_effects=True, vmem_limit_bytes=VMEM_LIMIT
        ),
        cost_estimate=SHORT,
        name="tokens_qkv",
    )(tok, w_slots, small, w_proj, fc_parts)


def causal_scores(k, q_rows, start):
    scores = dot_last(k, q_rows)
    keep = start
    tail = scores[keep:]
    key_id = lax.broadcasted_iota(jnp.int32, tail.shape, 0)
    query_id = lax.broadcasted_iota(jnp.int32, tail.shape, 1)
    tail = jnp.where(key_id <= query_id, tail, -1e30)
    if keep == 0:
        return tail
    return jnp.concatenate([scores[:keep], tail], axis=0)


def soft(scores, v_t):
    top = jnp.max(scores, axis=0, keepdims=True)
    weights = jnp.exp(scores - top)
    total = jnp.sum(weights, axis=0, keepdims=True)
    out = dot(v_t, weights.astype(BF16)) / total
    return out, top + jnp.log(total)


def causal(inv_ref, x_ref):
    return jnp.concatenate([x_ref[0, inv_ref[i]] for i in range(x_ref.shape[1])], axis=0)


def attn_fwd_kernel(inv_ref, x_ref, o_ref, l_ref):
    rows = l_ref.shape[2]
    hd = HEAD_DIM
    x = causal(inv_ref, x_ref)
    q = x[:, :hd] * BF16(SCALE)
    k = x[:, hd : 2 * hd]
    v_t = x[:, 2 * hd :].T
    for i in range(rows // QROWS):
        lo, hi = i * QROWS, (i + 1) * QROWS
        out, lse = soft(causal_scores(k[:hi], q[lo:hi], lo), v_t[:, :hi])
        l_ref[0, :, lo:hi] = lse
        out = out.astype(BF16)
        for b in range(QROWS // BLOCK):
            o_ref[inv_ref[2 * i + b]] = out[:, b * BLOCK : (b + 1) * BLOCK]


def attn_fwd(inv, qkv, heads):
    blocks, _, cols = qkv.shape[1:]
    rows = blocks * BLOCK
    return pl.pallas_call(
        attn_fwd_kernel,
        grid_spec=pltpu.PrefetchScalarGridSpec(
            num_scalar_prefetch=1,
            grid=(heads,),
            in_specs=[pl.BlockSpec((1, blocks, BLOCK, cols), lambda h, inv: (h, 0, 0, 0))],
            out_specs=[
                pl.BlockSpec((blocks, HEAD_DIM, BLOCK), lambda h, inv: (0, h, 0)),
                pl.BlockSpec((1, 1, rows), lambda h, inv: (h, 0, 0)),
            ],
        ),
        out_shape=[
            jax.ShapeDtypeStruct((blocks, heads * HEAD_DIM, BLOCK), BF16),
            jax.ShapeDtypeStruct((heads, 1, rows), F32),
        ],
        compiler_params=pltpu.CompilerParams(vmem_limit_bytes=VMEM_LIMIT),
        cost_estimate=SHORT,
        name="attn_fwd",
    )(inv, qkv)


def attn_bwd_kernel(inv_ref, x_ref, do_ref, o_ref, l_ref, dx_ref, dk_acc, dv_acc):
    rows = l_ref.shape[2]
    hd = HEAD_DIM
    x = causal(inv_ref, x_ref)
    q = x[:, :hd] * BF16(SCALE)
    k = x[:, hd : 2 * hd]
    v = x[:, 2 * hd :]
    k_t = k.T
    dk_acc[...] = jnp.zeros_like(dk_acc)
    dv_acc[...] = jnp.zeros_like(dv_acc)
    for i in range(rows // QROWS):
        lo, hi = i * QROWS, (i + 1) * QROWS
        ids = [inv_ref[2 * i + b] for b in range(QROWS // BLOCK)]
        do_t = jnp.concatenate([do_ref[b] for b in ids], axis=1)
        o_t = jnp.concatenate([o_ref[b] for b in ids], axis=1)
        inner = jnp.sum(do_t.astype(F32) * o_t.astype(F32), axis=0, keepdims=True)
        probs = jnp.exp(causal_scores(k[:hi], q[lo:hi], lo) - l_ref[0, :, lo:hi])
        dprobs = dot(v[:hi], do_t)
        dscores = (probs * (dprobs - inner)).astype(BF16)
        dv_acc[:hi] += dot_last(probs.astype(BF16), do_t)
        dk_acc[:hi] += dot(dscores, q[lo:hi])
        dq = (dot(k_t[:, :hi], dscores) * SCALE).T
        for n, b in enumerate(ids):
            dx_ref[0, b, :, :hd] = dq[n * BLOCK : (n + 1) * BLOCK].astype(BF16)
    for i in range(rows // BLOCK):
        lo, hi = i * BLOCK, (i + 1) * BLOCK
        dx_ref[0, inv_ref[i], :, hd : 2 * hd] = dk_acc[lo:hi].astype(BF16)
        dx_ref[0, inv_ref[i], :, 2 * hd :] = dv_acc[lo:hi].astype(BF16)


def attn_bwd(inv, qkv, d_out, out, lse, heads):
    blocks, _, cols = qkv.shape[1:]
    rows = blocks * BLOCK
    whole = pl.BlockSpec((1, blocks, BLOCK, cols), lambda h, inv: (h, 0, 0, 0))
    feat = pl.BlockSpec((blocks, HEAD_DIM, BLOCK), lambda h, inv: (0, h, 0))
    return pl.pallas_call(
        attn_bwd_kernel,
        grid_spec=pltpu.PrefetchScalarGridSpec(
            num_scalar_prefetch=1,
            grid=(heads,),
            in_specs=[
                whole,
                feat,
                feat,
                pl.BlockSpec((1, 1, rows), lambda h, inv: (h, 0, 0)),
            ],
            out_specs=whole,
            scratch_shapes=[pltpu.VMEM((rows, HEAD_DIM), F32)] * 2,
        ),
        out_shape=jax.ShapeDtypeStruct((heads, blocks, BLOCK, cols), BF16),
        compiler_params=pltpu.CompilerParams(vmem_limit_bytes=VMEM_LIMIT),
        cost_estimate=pl.CostEstimate(
            flops=24 * 10**9, bytes_accessed=24 * 10**6, transcendentals=0
        ),
        name="attn_bwd",
    )(inv, qkv, d_out, out, lse)


def own_scores(order_ref, x_ref, k):
    hd = HEAD_DIM
    blocks = x_ref.shape[1]
    first = order_ref[blocks]
    q = jnp.concatenate([x_ref[0, first], x_ref[0, first + 1]], axis=0)[:, :hd]
    q = q * BF16(SCALE)
    scores = dot_last(k, q)
    row = lax.broadcasted_iota(jnp.int32, (BLOCK, 1), 0)
    key_place = jnp.concatenate([order_ref[b] * BLOCK + row for b in range(blocks)], axis=0)
    lane = lax.broadcasted_iota(jnp.int32, (1, 2 * BLOCK), 1)
    low, high = order_ref[order_ref[blocks]], order_ref[order_ref[blocks] + 1]
    place = jnp.where(lane < BLOCK, low * BLOCK + lane, (high - 1) * BLOCK + lane)
    return q, first, jnp.where(key_place <= place, scores, -1e30)


def rest_fwd_kernel(order_ref, x_ref, o_ref, l_ref):
    hd = HEAD_DIM
    x = x_ref[0].reshape(-1, 3 * hd)
    _, _, scores = own_scores(order_ref, x_ref, x[:, hd : 2 * hd])
    out, lse = soft(scores, x[:, 2 * hd :].T)
    o_ref[0] = out.astype(BF16)
    l_ref[0] = lse


def rest_fwd(order, qkv, base):
    slots, blocks, _, cols = qkv.shape
    rest = slots - base
    return pl.pallas_call(
        rest_fwd_kernel,
        grid_spec=pltpu.PrefetchScalarGridSpec(
            num_scalar_prefetch=1,
            grid=(rest,),
            in_specs=[
                pl.BlockSpec((1, blocks, BLOCK, cols), lambda h, o: (base + h, 0, 0, 0))
            ],
            out_specs=[
                pl.BlockSpec((1, HEAD_DIM, QROWS), lambda h, o: (h, 0, 0)),
                pl.BlockSpec((1, 1, QROWS), lambda h, o: (h, 0, 0)),
            ],
        ),
        out_shape=[
            jax.ShapeDtypeStruct((rest, HEAD_DIM, QROWS), BF16),
            jax.ShapeDtypeStruct((rest, 1, QROWS), F32),
        ],
        compiler_params=pltpu.CompilerParams(vmem_limit_bytes=VMEM_LIMIT),
        cost_estimate=SHORT,
        name="rest_fwd",
    )(order, qkv)


def rest_bwd_kernel(order_ref, x_ref, do_ref, o_ref, l_ref, dx_ref):
    hd = HEAD_DIM
    x = x_ref[0].reshape(-1, 3 * hd)
    blocks = x_ref.shape[1]
    k = x[:, hd : 2 * hd]
    q, first, scores = own_scores(order_ref, x_ref, k)
    do_t = do_ref[0]
    inner = jnp.sum(do_t.astype(F32) * o_ref[0].astype(F32), axis=0, keepdims=True)
    probs = jnp.exp(scores - l_ref[0])
    dprobs = dot(x[:, 2 * hd :], do_t)
    dscores = (probs * (dprobs - inner)).astype(BF16)
    dv = dot_last(probs.astype(BF16), do_t).astype(BF16)
    dk = dot(dscores, q).astype(BF16)
    dq = (dot(k.T, dscores) * SCALE).T.astype(BF16)
    dx_ref[0, :, :, 2 * hd :] = dv.reshape(blocks, BLOCK, hd)
    dx_ref[0, :, :, hd : 2 * hd] = dk.reshape(blocks, BLOCK, hd)
    dx_ref[0, :, :, :hd] = jnp.zeros((blocks, BLOCK, hd), BF16)
    for b in range(2):
        dx_ref[0, first + b, :, :hd] = dq[b * BLOCK : (b + 1) * BLOCK]


def rest_bwd(order, qkv, d_out, out, lse, base):
    slots, blocks, _, cols = qkv.shape
    rest = slots - base
    feat = pl.BlockSpec((1, HEAD_DIM, QROWS), lambda h, o: (h, 0, 0))
    return pl.pallas_call(
        rest_bwd_kernel,
        grid_spec=pltpu.PrefetchScalarGridSpec(
            num_scalar_prefetch=1,
            grid=(rest,),
            in_specs=[
                pl.BlockSpec((1, blocks, BLOCK, cols), lambda h, o: (base + h, 0, 0, 0)),
                feat,
                feat,
                pl.BlockSpec((1, 1, QROWS), lambda h, o: (h, 0, 0)),
            ],
            out_specs=pl.BlockSpec((1, blocks, BLOCK, cols), lambda h, o: (h, 0, 0, 0)),
        ),
        out_shape=jax.ShapeDtypeStruct((rest, blocks, BLOCK, cols), BF16),
        compiler_params=pltpu.CompilerParams(vmem_limit_bytes=VMEM_LIMIT),
        cost_estimate=SHORT,
        name="rest_bwd",
    )(order, qkv, d_out, out, lse)


def far_first(i, chips):
    return (i % 2) * (i // 2) + (1 - i % 2) * (chips - 1 - i // 2)


def line_sum(chip, chips, f, core, part, came, sems, ready=None):
    sent, left_sem, right_sem = sems

    def to_right(d):
        return send(
            part.at[d], came.at[d], sent.at[d], left_sem.at[d], (2 * (chip + 1) + core, f)
        )

    def to_left(d):
        place = jnp.where(d == chip - 1, chips, d)
        return send(
            part.at[d], came.at[place], sent.at[d], right_sem.at[d], (2 * (chip - 1) + core, f)
        )

    def from_left(d):
        send(part.at[d], came.at[d], sent.at[d], left_sem.at[d], (2 * chip + core, f)).wait_recv()
        add(d, d)

    def from_right(d, place):
        send(
            part.at[d], came.at[place], sent.at[d], right_sem.at[d], (2 * chip + core, f)
        ).wait_recv()
        add(d, place)

    def add(d, place):
        part[d] = (part[d].astype(F32) + came[place].astype(F32)).astype(BF16)

    def step(t):
        far = chips - 1 - t + chip
        near = t - (chips - 1 - chip)

        @pl.when(chip <= t)
        def _():
            if ready is not None:
                ready(far)

            @pl.when(chip > 0)
            def _():
                from_left(far)

            to_right(far).start()

        @pl.when(near >= 0)
        def _():
            if ready is not None:
                ready(near)

            @pl.when(chip < chips - 1)
            def _():
                from_right(near, near)

            to_left(near).start()

    def finish():
        if ready is not None:
            ready(chip)

        @pl.when(chip > 0)
        def _():
            from_left(chip)

        @pl.when(chip < chips - 1)
        def _():
            from_right(chip, chips)

    def done():
        for d in range(chips):

            @pl.when(chip < d)
            def _(d=d):
                to_right(d).wait_send()

            @pl.when(chip > d)
            def _(d=d):
                to_left(d).wait_send()

    return step, finish, done


def line_gather(chip, chips, f, core, view, sems):
    right, left, twin_sent, got, twin_got = sems
    twin_id = (2 * chip + 1 - core, f)

    def hop(s, rightward):
        origin = chip - s if rightward else chip + s
        ref = view(origin, core)
        peer = (2 * (chip + 1 if rightward else chip - 1) + core, f)
        return send(ref, ref, (right if rightward else left).at[s], got.at[origin], peer)

    def twin(origin):
        ref = view(origin, core)
        return send(ref, ref, twin_sent.at[origin], twin_got.at[origin], twin_id)

    def arrived(origin):
        ref = view(origin, core)
        send(ref, ref, right.at[0], got.at[origin], twin_id).wait_recv()

    def step(s):
        @pl.when(chip - s >= 0)
        def _():
            if s:
                arrived(chip - s)

            @pl.when(chip < chips - 1)
            def _():
                hop(s, True).start()

            twin(chip - s).start()

        @pl.when(chip + s < chips)
        def _():
            if s:
                arrived(chip + s)

            @pl.when(chip > 0)
            def _():
                hop(s, False).start()

            if s:
                twin(chip + s).start()

    def done():
        for s in range(chips):
            if s < chips - 1:

                @pl.when((chip - s >= 0) & (chip < chips - 1))
                def _(s=s):
                    hop(s, True).wait_send()

                @pl.when((chip + s < chips) & (chip > 0))
                def _(s=s):
                    hop(s, False).wait_send()

            twin(s).wait_send()
            ref = view(s, 1 - core)
            send(ref, ref, twin_sent.at[s], twin_got.at[s], twin_id).wait_recv()

    return step, done


def back_kernel(
    n_ctx,
    n_fsdp,
    own_ref,
    rest_ref,
    w_ref,
    n_ref,
    att_ref,
    mid_ref,
    one_ref,
    cols_ref,
    proj_ref,
    part,
    twin_out,
    twin_in,
    came,
    mine,
    theirs,
    proj_part,
    proj_in,
    proj_got,
    twin_send,
    twin_recv,
    line_send,
    left_recv,
    right_recv,
    cols_send,
    cols_recv,
    proj_send,
    proj_recv,
    pair_sem,
):
    c = lax.axis_index("ctx")
    f = lax.axis_index("fsdp")
    chips = n_ctx // 2
    chip, core = c // 2, c % 2
    slots, width, cols = w_ref.shape
    count = own_ref.shape[2]
    base = own_ref.shape[0]
    shard = width // n_fsdp
    half = shard // 2
    twin_id = (2 * chip + 1 - core, f)
    enter(
        [(lax.rem(c + i, n_ctx), f) for i in range(1, n_ctx)]
        + [(c, flip(f, k, n_fsdp)) for k in range(1, n_fsdp)]
    )

    def grad(s):
        return own_ref.at[s] if s < base else rest_ref.at[s - base]

    def for_block(b):
        total = dot_last(grad(0)[b], w_ref[0])
        for s in range(1, slots):
            total += dot_last(grad(s)[b], w_ref[s])
        return total.astype(BF16)

    def to_twin(d, slot):
        return send(twin_out.at[slot], twin_in.at[d], twin_send.at[slot], twin_recv.at[d], twin_id)

    def products(i, carry):
        d = far_first(i, chips)
        slot = i % 2
        product = for_block(2 * d + 1 - core)

        @pl.when(i > 1)
        def _():
            to_twin(d, slot).wait_send()

        twin_out[slot] = product
        to_twin(d, slot).start()
        part[d] = for_block(2 * d + core)
        return carry

    def ready(d):
        to_twin(d, 0).wait_recv()
        part[d] = (part[d].astype(F32) + twin_in[d].astype(F32)).astype(BF16)

    step, finish, done = line_sum(
        chip, chips, f, core, part, came, (line_send, left_recv, right_recv), ready
    )

    def cols_copy(src, dst, at):
        return send(mine.at[src], theirs.at[at], cols_send.at[src], cols_recv.at[at], (c, dst))

    def columns(j):
        left = n_ref[:, :, j * shard : (j + 1) * shard].reshape(n_ctx * count, shard)
        for s in range(slots):
            right = grad(s)[...].reshape(n_ctx * count, cols)
            mine[j, s] = dot_first(left, right).astype(BF16)

        @pl.when(f != j)
        def _():
            cols_copy(j, j, f).start()

    def proj_pair():
        return send(proj_part.at[1 - core], proj_in, pair_sem.at[0], pair_sem.at[1], twin_id)

    def proj_copy(k):
        other = flip(f, k, n_fsdp)
        return send(
            proj_part.at[core, other],
            proj_got.at[f],
            proj_send.at[k],
            proj_recv.at[k],
            (c, other),
        )

    def proj_products(j):
        for h in range(2):
            lo = j * shard + h * half
            proj_part[h, j, :half] = dot_first(att_ref[:, lo : lo + half], mid_ref[...]).astype(BF16)
            if half < proj_part.shape[2]:
                pad = proj_part.shape[2] - half
                proj_part[h, j, half:] = jnp.zeros((pad, width), BF16)

    lax.fori_loop(0, chips, products, 0)
    step(0)
    for j in range(n_fsdp):
        proj_products(j)
    proj_pair().start()
    for t in range(1, max(chips, n_fsdp + 1)):
        if t <= n_fsdp:
            columns(t - 1)
        if t < chips - 1:
            step(t)
    proj_pair().wait()

    def proj_add(j, carry):
        proj_part[core, j] = (
            proj_part[core, j].astype(F32) + proj_in[j].astype(F32)
        ).astype(BF16)
        return carry

    lax.fori_loop(0, n_fsdp, proj_add, 0)
    for k in range(1, n_fsdp):
        proj_copy(k).start()
    total = mine[f].astype(F32)
    for k in range(1, n_fsdp):
        other = flip(f, k, n_fsdp)
        cols_copy(other, other, other).wait_recv()
        total += theirs[other].astype(F32)
    cols_ref[...] = total.astype(BF16)
    finish()
    one_ref[...] = part[chip]
    total = proj_part[core, f].astype(F32)
    for k in range(1, n_fsdp):
        proj_copy(k).wait_recv()
        total += proj_got[flip(f, k, n_fsdp)].astype(F32)
    proj_ref[...] = total.astype(BF16)
    done()
    for slot in range(2):
        to_twin(0, slot).wait_send()
    for k in range(1, n_fsdp):
        other = flip(f, k, n_fsdp)
        cols_copy(other, other, other).wait_send()
        proj_copy(k).wait_send()


def back_fits(n_ctx, n_fsdp, count, width, slots):
    blocks = (5 * (n_ctx // 2) + n_ctx) * count * width
    heads = slots * 256 * (n_ctx * count + 3 * width)
    return 2 * (blocks + heads) < 50 * 1024 * 1024


def back_call(n_ctx, n_fsdp, own, rest, w_slots, normed, attended, mid_low, cid):
    slots, width, cols = w_slots.shape
    count = normed.shape[1]
    chips = n_ctx // 2
    shard = width // n_fsdp
    high = -(-(shard // 2) // 16) * 16
    vm = pl.BlockSpec(memory_space=pltpu.VMEM)
    dma = pltpu.SemaphoreType.DMA
    block = pltpu.VMEM((chips, count, width), BF16)
    piece = pltpu.VMEM((n_fsdp, slots, shard, cols), BF16)
    return pl.pallas_call(
        functools.partial(back_kernel, n_ctx, n_fsdp),
        in_specs=[vm] * 6,
        out_specs=[vm] * 3,
        out_shape=[
            jax.ShapeDtypeStruct((count, width), BF16),
            jax.ShapeDtypeStruct((slots, shard, cols), BF16),
            jax.ShapeDtypeStruct((high, width), BF16),
        ],
        scratch_shapes=[
            block,
            pltpu.VMEM((2, count, width), BF16),
            block,
            pltpu.VMEM((chips + 1, count, width), BF16),
        ]
        + [piece] * 2
        + [
            pltpu.VMEM((2, n_fsdp, high, width), BF16),
            pltpu.VMEM((n_fsdp, high, width), BF16),
            pltpu.VMEM((n_fsdp, high, width), BF16),
        ]
        + [dma((2,))]
        + [dma((chips,))] * 4
        + [dma((n_fsdp,))] * 4
        + [dma((2,))],
        compiler_params=pltpu.CompilerParams(
            collective_id=cid, has_side_effects=True, vmem_limit_bytes=60 * 1024 * 1024
        ),
        cost_estimate=SHORT,
        name="qkv_back",
    )(own, rest, w_slots, normed, attended, mid_low)


def sums_kernel(n_ctx, n_fsdp, lead, *refs):
    (blob_ref, cols_ref, lines_in, blob_all, cols_all, lines_ref, part, came) = refs[:8]
    (lines_got, sum_send, left_recv, right_recv) = refs[8:12]
    blob_sems, cols_sems, (lines_send, lines_recv, local) = refs[12:17], refs[17:22], refs[22:25]
    c = lax.axis_index("ctx")
    f = lax.axis_index("fsdp")
    chips = n_ctx // 2
    chip, core = c // 2, c % 2
    enter(
        [(lax.rem(c + i, n_ctx), f) for i in range(1, n_ctx)]
        + [(c, flip(f, k, n_fsdp)) for k in range(1, n_fsdp)]
    )
    cols_step, cols_done = line_gather(
        chip, chips, f, core, lambda at, h: cols_all.at[2 * at + h], cols_sems
    )
    blob_step, blob_done = line_gather(
        chip, chips, f, core, lambda at, h: blob_all.at[h, at], blob_sems
    )
    sum_step, sum_finish, sum_done = line_sum(
        chip, chips, f, core, part, came, (sum_send, left_recv, right_recv)
    )
    load = pltpu.make_async_copy(cols_ref, cols_all.at[c], local.at[0])
    load.start()
    part[...] = blob_ref[...]
    sum_step(0)
    load.wait()
    cols_step(0)
    peers = [(flip(c, 1 << i, n_ctx), f) for i in range(n_ctx.bit_length() - 1)]
    ctx_phases = len(peers)
    peers += [(c, flip(f, 1 << i, n_fsdp)) for i in range(n_fsdp.bit_length() - 1)]
    lines_ref[...] = lines_in[...]

    def line_copy(i):
        rows = lines_in.shape[0] if i < ctx_phases else lead
        return send(
            lines_ref.at[:rows],
            lines_got.at[i, :rows],
            lines_send.at[i],
            lines_recv.at[i],
            peers[i],
        )

    def line_phase(i):
        if 0 < i <= len(peers):
            rows = lines_in.shape[0] if i <= ctx_phases else lead
            line_copy(i - 1).wait()
            lines_ref[:rows] += lines_got[i - 1, :rows]
        if i < len(peers):
            line_copy(i).start()

    phase = 0
    for t in range(1, chips):
        if t < chips - 1:
            sum_step(t)
        cols_step(t)
        line_phase(phase)
        phase += 1
    sum_finish()
    line_phase(phase)
    phase += 1
    keep = pltpu.make_async_copy(part.at[chip], blob_all.at[core, chip], local.at[1])
    keep.start()
    keep.wait()
    for s in range(chips):
        blob_step(s)
        line_phase(phase)
        phase += 1
    while phase <= len(peers):
        line_phase(phase)
        phase += 1
    sum_done()
    cols_done()
    blob_done()


def sums_call(n_ctx, n_fsdp, blob, cols, lines, lead, cid):
    chips = n_ctx // 2
    phases = (n_ctx * n_fsdp).bit_length() - 1
    vm = pl.BlockSpec(memory_space=pltpu.VMEM)
    anym = pl.BlockSpec(memory_space=pl.ANY)
    dma = pltpu.SemaphoreType.DMA
    gather_sems = [dma((chips,))] * 5
    return pl.pallas_call(
        functools.partial(sums_kernel, n_ctx, n_fsdp, lead),
        in_specs=[vm, anym, vm],
        out_specs=[vm, vm, vm],
        out_shape=[
            jax.ShapeDtypeStruct((2,) + blob.shape, BF16),
            jax.ShapeDtypeStruct((n_ctx,) + cols.shape, BF16),
            jax.ShapeDtypeStruct(lines.shape, F32),
        ],
        scratch_shapes=[pltpu.VMEM(blob.shape, BF16)]
        + [pltpu.VMEM((chips + 1,) + blob.shape[1:], BF16)]
        + [pltpu.VMEM((phases,) + lines.shape, F32)]
        + [dma((chips,))] * 3
        + gather_sems * 2
        + [dma((phases,))] * 2
        + [dma((2,))],
        compiler_params=pltpu.CompilerParams(
            collective_id=cid, has_side_effects=True, vmem_limit_bytes=60 * 1024 * 1024
        ),
        cost_estimate=SHORT,
        name="weight_sums",
    )(blob, cols, lines)


def assemble_kernel(own_ref, rest_ref, o_ref):
    hd = HEAD_DIM
    width = o_ref.shape[1] // 3
    count = own_ref.shape[0]
    for h in range(width // hd):
        src = own_ref.at[h] if h < count else rest_ref.at[h - count]
        for part in range(3):
            at = part * width + h * hd
            o_ref[:, at : at + hd] = src[:, part * hd : (part + 1) * hd].astype(F32)


def assemble(own, rest, out_cols):
    rows = own.shape[1]
    return pl.pallas_call(
        assemble_kernel,
        out_shape=jax.ShapeDtypeStruct((rows, out_cols), F32),
        compiler_params=pltpu.CompilerParams(vmem_limit_bytes=VMEM_LIMIT),
        cost_estimate=SHORT,
        name="assemble",
    )(own, rest)


def norm_parts(rows):
    mean = jnp.mean(rows, axis=-1, keepdims=True)
    cen = rows - mean
    rstd = lax.rsqrt(jnp.mean(cen * cen, axis=-1, keepdims=True) + EPS)
    return cen * rstd, rstd


def norm_back(xhat, rstd, gain, grad):
    dxhat = grad * gain
    return rstd * (
        dxhat
        - jnp.mean(dxhat, axis=-1, keepdims=True)
        - xhat * jnp.mean(dxhat * xhat, axis=-1, keepdims=True)
    )


def swap(value, axis, size, k):
    return lax.ppermute(value, axis, [(i, i ^ k) for i in range(size)])


def shards(
    n_ctx,
    n_fsdp,
    tokens,
    block_order,
    w_attn,
    w_proj,
    w_fc,
    w_out,
    norm_gains,
    biases,
    fc_bias,
    cotangent,
):
    hd = HEAD_DIM
    count, width = tokens.shape[1:]
    shard = width // n_fsdp
    heads = width // hd
    base = heads // n_ctx
    rest = heads - base * n_ctx
    slots = base + rest
    own_blocks = count // BLOCK
    c = lax.axis_index("ctx")
    f = lax.axis_index("fsdp")

    order = block_order[0]
    inv = jnp.argsort(order).astype(jnp.int32)
    order_own = jnp.concatenate([order, (c * own_blocks)[None]])

    def head_cols(h):
        return jnp.concatenate(
            [
                lax.dynamic_slice(w_attn, (0, part * width + h * hd), (shard, hd))
                for part in range(3)
            ],
            axis=1,
        )

    slot_heads = [c * base + s for s in range(base)] + [n_ctx * base + r for r in range(rest)]
    w_slots = jnp.stack([head_cols(h) for h in slot_heads])
    small = jnp.concatenate([norm_gains, biases], axis=0).astype(F32)
    hidden_cols = w_fc.shape[1] // n_fsdp
    fc_parts = jnp.stack(
        [w_fc[:, j * hidden_cols : (j + 1) * hidden_cols] for j in range(n_fsdp)]
    )
    normed_one, qkv, full_proj, fc_cols, w_slots, small = start_call(
        n_ctx, n_fsdp, base, tokens[0], w_slots, small, w_proj, fc_parts, 3
    )
    full_proj = full_proj.reshape(width, width)
    fc_cols = fc_cols.reshape(width, hidden_cols)
    qkv = qkv.reshape(slots, n_ctx * own_blocks, BLOCK, 3 * hd)
    gains, shifts = small[:2], small[2:]
    cot = cotangent[0]

    cot_late, _ = lax.optimization_barrier((cot, small))
    cot_all = lax.all_gather(cot_late, "fsdp", axis=0)

    out_own, lse_own = attn_fwd(inv, qkv, base)
    got = lax.all_to_all(out_own, "ctx", split_axis=0, concat_axis=0, tiled=True)
    got = got.reshape(n_ctx, own_blocks, base * hd, BLOCK).transpose(1, 3, 0, 2)
    attended = got.reshape(count, n_ctx * base * hd)
    if rest:
        out_rest, lse_rest = rest_fwd(order_own, qkv, base)
        attended = jnp.concatenate([attended, out_rest.reshape(rest * hd, count).T], axis=1)

    rows = tokens[0].astype(F32)
    mid = rows + (dot(attended, full_proj) + shifts[4])
    xhat_two, rstd_two = norm_parts(mid)
    normed_two = (xhat_two * gains[1] + shifts[1]).astype(BF16)

    normed_two_grad, fc_bias_part, out_part, w_out_part, w_fc_part = ffn(
        n_fsdp,
        normed_two,
        cot_all,
        fc_cols,
        w_out,
        fc_bias.astype(F32)[None],
    )
    out_rows = lax.psum_scatter(
        out_part.reshape(n_fsdp * count, width), "fsdp", scatter_dimension=0, tiled=True
    )
    w_out_low = lax.psum(w_out_part, "ctx")

    cot_rows = cot.astype(F32)
    mid_grad = cot_rows + norm_back(xhat_two, rstd_two, gains[1], normed_two_grad)
    mid_low = mid_grad.astype(BF16)
    over_rows = functools.partial(jnp.einsum, "ta,tb->ab", preferred_element_type=F32)
    attended_grad = dot_last(mid_low, full_proj).astype(BF16)
    half = shard // 2
    core = c % 2

    def core_half(part):
        away = lax.dynamic_slice_in_dim(part, (1 - core) * half, half, 1)
        here = lax.dynamic_slice_in_dim(part, core * half, half, 1)
        return (here.astype(F32) + swap(away, "ctx", n_ctx, 1).astype(F32)).astype(BF16)

    def over_fsdp(part):
        out = []
        for k in range(n_fsdp):
            piece = lax.dynamic_index_in_dim(part, f ^ k, keepdims=False)
            out.append(swap(piece, "fsdp", n_fsdp, k) if k else piece)
        return out

    w_fc_part, _ = lax.optimization_barrier((w_fc_part, attended_grad))
    w_fc_mid = core_half(w_fc_part.reshape(n_fsdp, shard, hidden_cols))

    main = n_ctx * base * hd
    sent = attended_grad[:, :main].reshape(own_blocks, BLOCK, n_ctx, base * hd)
    sent = sent.transpose(2, 0, 3, 1).reshape(n_ctx * own_blocks, base * hd, BLOCK)
    d_out = lax.all_to_all(sent, "ctx", split_axis=0, concat_axis=0, tiled=True)
    d_out, w_fc_mid = lax.optimization_barrier((d_out, w_fc_mid))
    w_fc_half = jnp.stack(over_fsdp(w_fc_mid))
    d_own = attn_bwd(inv, qkv, d_out, out_own, lse_own, base)
    d_own = d_own.reshape(base, n_ctx, count, 3 * hd)
    if rest:
        d_rest = attended_grad[:, main:].T.reshape(rest, hd, count)
        d_rest = rest_bwd(order_own, qkv, d_rest, out_rest, lse_rest, base)
        d_rest = d_rest.reshape(rest, n_ctx, count, 3 * hd)
        sums = jnp.concatenate(
            [jnp.sum(d.astype(F32), axis=(1, 2)) for d in (d_own, d_rest)], axis=0
        )
    else:
        d_rest = d_own
        sums = jnp.sum(d_own.astype(F32), axis=(1, 2))
    if back_fits(n_ctx, n_fsdp, count, width, slots):
        d_own, w_fc_half = lax.optimization_barrier((d_own, w_fc_half))
        normed_one_grad, cols_sum, w_proj_half = back_call(
            n_ctx, n_fsdp, d_own, d_rest, w_slots, normed_one, attended, mid_low, 4
        )
        w_proj_half = w_proj_half[:half]
        normed_one_grad = normed_one_grad.astype(F32)
    else:
        dqkv = jnp.concatenate([d_own, d_rest])[:slots].reshape(slots, n_ctx * count, 3 * hd)
        one_part = jnp.einsum("hte,hde->td", dqkv, w_slots, preferred_element_type=F32)
        normed_one_grad = lax.psum_scatter(
            one_part.astype(BF16), "ctx", scatter_dimension=0, tiled=True
        ).astype(F32)
        slot_part = jnp.einsum(
            "td,hte->hde",
            normed_one.reshape(n_ctx * count, width),
            dqkv,
            preferred_element_type=F32,
        ).astype(BF16)
        cols_sum = lax.psum_scatter(slot_part, "fsdp", scatter_dimension=1, tiled=True)
        w_proj_part = over_rows(attended, mid_low).astype(BF16)
        w_proj_half = sum(
            piece.astype(F32)
            for piece in over_fsdp(core_half(w_proj_part.reshape(n_fsdp, shard, width)))
        ).astype(BF16)

    w_out_low, _ = lax.optimization_barrier((w_out_low, cols_sum))
    w_out_grad = w_out_low.astype(F32)
    xhat_one, rstd_one = norm_parts(rows)
    tokens_grad = (mid_grad + norm_back(xhat_one, rstd_one, gains[0], normed_one_grad)).astype(
        BF16
    )

    def placed(part):
        cols = sums[:, part * hd : (part + 1) * hd]
        line = lax.dynamic_update_slice_in_dim(
            jnp.zeros((width,), F32), cols[:base].reshape(-1), c * base * hd, 0
        )
        return line + jnp.pad(cols[base:].reshape(-1), (main, 0))

    lines = jnp.stack(
        [
            jnp.sum(normed_one_grad * xhat_one, axis=0),
            jnp.sum(normed_two_grad * xhat_two, axis=0),
            jnp.sum(normed_one_grad, axis=0),
            jnp.sum(normed_two_grad, axis=0),
            placed(0),
            placed(2),
            jnp.sum(mid_low.astype(F32), axis=0),
            jnp.sum(cot_rows, axis=0),
        ]
    )
    lead = lines.shape[0]
    tail = jnp.pad(fc_bias_part, ((0, 7), (0, width - hidden_cols)))
    lines = jnp.concatenate([lines, tail])

    chips = n_ctx // 2
    parts = [w_fc_half.reshape(-1, width), w_proj_half]
    if rest:
        parts.append(core_half(cols_sum[base:]).reshape(-1, width))
    bounds = [0]
    for part in parts:
        bounds.append(bounds[-1] + part.shape[0])
    per_chip = -(-bounds[-1] // (16 * chips)) * 16
    blob = jnp.concatenate(parts)
    blob = jnp.pad(blob, ((0, per_chip * chips - bounds[-1]), (0, 0)))
    blob, own_cols, lines = sums_call(
        n_ctx, n_fsdp, blob.reshape(chips, per_chip, width), cols_sum[:base], lines, lead, 5
    )
    out_rows, lines = lax.optimization_barrier((out_rows, lines))
    layer_rows = (mid + (out_rows.astype(F32) + shifts[5])).astype(BF16)
    blob = blob.reshape(2, chips * per_chip, width)
    w_fc_low = blob[:, : bounds[1]].reshape(2, n_fsdp, half, hidden_cols)
    w_fc_grad = jnp.concatenate(
        [
            lax.dynamic_index_in_dim(w_fc_low, f ^ j, axis=1, keepdims=False).reshape(
                shard, hidden_cols
            )
            for j in range(n_fsdp)
        ],
        axis=1,
    ).astype(F32)
    w_proj_grad = blob[:, bounds[1] : bounds[2]].reshape(shard, width).astype(F32)
    own_cols = own_cols.reshape(n_ctx * base, shard, 3 * hd)
    if rest:
        rest_cols = blob[:, bounds[2] : bounds[3]].reshape(2, rest, half, 3 * hd)
        rest_cols = rest_cols.transpose(1, 0, 2, 3).reshape(rest, shard, 3 * hd)
    else:
        rest_cols = own_cols
    w_attn_grad = assemble(own_cols, rest_cols, 3 * width)
    fc_bias_grad = lines[lead, :hidden_cols]
    lines = lax.dynamic_slice_in_dim(lines[:lead], f * shard, shard, 1)
    return (
        layer_rows[None],
        tokens_grad[None],
        w_attn_grad,
        w_proj_grad,
        w_fc_grad,
        w_out_grad,
        lines[:2],
        lines[2:],
        fc_bias_grad,
    )


def solution(mesh):
    rows = P("fsdp", "ctx", None)
    weight = P("fsdp", None)
    vectors = P(None, "fsdp")
    return jax.shard_map(
        functools.partial(shards, mesh.shape["ctx"], mesh.shape["fsdp"]),
        mesh=mesh,
        in_specs=(
            rows, weight, weight, weight, weight, weight, vectors, vectors, P("fsdp"), rows,
        ),
        out_specs=(
            rows, rows, weight, weight, weight, weight, vectors, vectors, P("fsdp"),
        ),
        check_vma=False,
    )
```

```python
import functools

import jax
import jax.numpy as jnp
from jax import lax
from jax.experimental import pallas as pl
from jax.experimental.pallas import tpu as pltpu
from jax.sharding import PartitionSpec as P

HEAD_DIM = 64
BLOCK = 128
QROWS = 256
EPS = 1e-05
SCALE = HEAD_DIM ** (-0.5)
F32 = jnp.float32
BF16 = jnp.bfloat16
VMEM_LIMIT = 56 * 1024 * 1024
LAST = (((1,), (1,)), ((), ()))
FIRST = (((0,), (0,)), ((), ()))
MESH = pl.DeviceIdType.MESH
TILE = 256


def dot_last(a, b):
    return lax.dot_general(a, b, LAST, preferred_element_type=F32)


def dot(a, b):
    return jnp.dot(a, b, preferred_element_type=F32)


def dot_first(a, b):
    return lax.dot_general(a, b, FIRST, preferred_element_type=F32)


SHORT = pl.CostEstimate(flops=1, bytes_accessed=1, transcendentals=0)


def flip(place, k, size):
    out = 0
    bit = 1
    while bit < size:
        out = out + (place // bit + k // bit) % 2 * bit
        bit *= 2
    return out

def enter(peers):
    barrier = pltpu.get_barrier_semaphore()
    for peer in peers:
        pl.semaphore_signal(barrier, inc=1, device_id=peer, device_id_type=MESH)
    pl.semaphore_wait(barrier, len(peers))

def send(src, dst, send_sem, recv_sem, peer):
    return pltpu.make_async_remote_copy(
        src_ref=src, dst_ref=dst, send_sem=send_sem, recv_sem=recv_sem,
        device_id=peer, device_id_type=MESH)


def ffn_kernel(n, nt_hbm, cot_hbm, wfc_hbm, wout_hbm, bias_ref,
               gsum_ref, fcb_ref, out_hbm, wout_grad_hbm, wfc_grad_hbm,
               cot_ref, wfc_ref, wout_ref, all_ref, act_ref, hg_ref, ag_ref, part_ref, got_ref, stage_d, stage_h,
               s1, r1, s2, r2, local):
    c = lax.axis_index("ctx")
    f = lax.axis_index("fsdp")
    rows, width = nt_hbm.shape
    enter([(c, flip(f, k, n)) for k in range(1, n)])

    def rows_out(k):
        return send(nt_hbm, all_ref.at[f], s1.at[k], r1.at[k], (c, flip(f, k, n)))

    def grad_back(k):
        other = flip(f, k, n)
        return send(part_ref.at[other], got_ref.at[k], s2.at[k], r2.at[k], (c, other))

    near = [k for k in range(1, n) if k & (k - 1) == 0]
    far = [k for k in range(1, n) if k not in near]
    for k in near:
        rows_out(k).start()
    loads = [
        pltpu.make_async_copy(nt_hbm, all_ref.at[f], local.at[0]),
        pltpu.make_async_copy(wout_hbm, wout_ref, local.at[1]),
        pltpu.make_async_copy(cot_hbm, cot_ref, local.at[2]),
        pltpu.make_async_copy(wfc_hbm, wfc_ref, local.at[3]),
    ]
    for load in loads:
        load.start()
    fcb_ref[...] = jnp.zeros_like(fcb_ref)
    loads[1].wait()
    loads[2].wait()

    def active_grad(k, carry):
        ag_ref[k] = dot_last(cot_ref[k], wout_ref[...])
        return carry

    lax.fori_loop(0, n, active_grad, 0)
    for k in far:
        rows_out(k).start()
    loads[0].wait()
    loads[3].wait()

    def chunk(k, carry):
        src = flip(f, k, n)

        @pl.when(k > 0)
        def _():
            rows_out(k).wait_recv()

        hidden = dot(all_ref[src], wfc_ref[...]) + bias_ref[...]
        square = hidden * hidden
        tanh = jnp.tanh(0.7978845608028654 * (hidden + 0.044715 * square * hidden))
        act_ref[src] = (0.5 * hidden * (1.0 + tanh)).astype(BF16)
        slope = 0.5 * (1.0 + tanh) + 0.5 * hidden * (1.0 - tanh * tanh) * 0.7978845608028654 * (
            1.0 + 3.0 * 0.044715 * square
        )
        grad = (ag_ref[src] * slope).astype(BF16)
        hg_ref[src] = grad
        fcb_ref[...] += jnp.sum(grad.astype(F32), axis=0, keepdims=True)
        part_ref[src] = dot_last(grad, wfc_ref[...]).astype(BF16)

        @pl.when(k > 0)
        def _():
            grad_back(k).start()

        return carry

    lax.fori_loop(0, n, chunk, 0)

    def grads(left_ref, right_ref, dst, stage_ref, base):
        wide = left_ref.shape[2]
        right = right_ref[...].reshape(n * rows, right_ref.shape[2])
        copies = []
        for i, lo in enumerate(range(0, wide, TILE)):
            hi = min(lo + TILE, wide)
            slot = i % 2
            if i >= 2:
                copies[i - 2].wait()
            left = left_ref[:, :, lo:hi].reshape(n * rows, hi - lo)
            stage_ref[slot, : hi - lo] = dot_first(left, right).astype(BF16)
            copies.append(
                pltpu.make_async_copy(
                    stage_ref.at[slot, : hi - lo], dst.at[lo:hi], local.at[base + slot]
                )
            )
            copies[-1].start()
        for copy in copies[-2:]:
            copy.wait()

    grads(act_ref, cot_ref, wout_grad_hbm, stage_d, 4)
    grads(all_ref, hg_ref, wfc_grad_hbm, stage_h, 6)

    def out_copy(k):
        return pltpu.make_async_copy(
            stage_d.at[k % 2, :rows], out_hbm.at[k], local.at[4 + k % 2]
        )

    for k in range(n):
        if k >= 2:
            out_copy(k - 2).wait()
        stage_d[k % 2, :rows] = dot(act_ref[k], wout_ref[...]).astype(BF16)
        out_copy(k).start()

    gsum_ref[...] = part_ref[f].astype(F32)
    for k in near + far:
        grad_back(k).wait_recv()
        gsum_ref[...] += got_ref[k].astype(F32)
    for k in range(1, n):
        rows_out(k).wait_send()
        grad_back(k).wait_send()
    for k in range(max(0, n - 2), n):
        out_copy(k).wait()


def ffn(n, nt, cot, wfc, wout, bias, cid=1):
    m, d = nt.shape
    h = wfc.shape[1]
    vm = pl.BlockSpec(memory_space=pltpu.VMEM)
    anym = pl.BlockSpec(memory_space=pl.ANY)
    return pl.pallas_call(
        functools.partial(ffn_kernel, n),
        in_specs=[anym] * 4 + [vm],
        out_specs=[vm, vm] + [anym] * 3,
        out_shape=[
            jax.ShapeDtypeStruct((m, d), F32),
            jax.ShapeDtypeStruct((1, h), F32),
            jax.ShapeDtypeStruct((n, m, d), BF16),
            jax.ShapeDtypeStruct((h, d), BF16),
            jax.ShapeDtypeStruct((d, h), BF16),
        ],
        scratch_shapes=[
            pltpu.VMEM((n, m, d), BF16),
            pltpu.VMEM((d, h), BF16),
            pltpu.VMEM((h, d), BF16),
            pltpu.VMEM((n, m, d), BF16),
            pltpu.VMEM((n, m, h), BF16),
            pltpu.VMEM((n, m, h), BF16),
            pltpu.VMEM((n, m, h), F32),
            pltpu.VMEM((n, m, d), BF16),
            pltpu.VMEM((n, m, d), BF16),
            pltpu.VMEM((2, max(TILE, m), d), BF16),
            pltpu.VMEM((2, TILE, h), BF16),
        ]
        + [pltpu.SemaphoreType.DMA((n,))] * 4
        + [pltpu.SemaphoreType.DMA((8,))],
        compiler_params=pltpu.CompilerParams(
            collective_id=cid, has_side_effects=True, vmem_limit_bytes=60 * 1024 * 1024
        ),
        cost_estimate=SHORT,
        name="feed_forward",
    )(nt, cot, wfc, wout, bias)


def start_kernel(
    n_ctx,
    n_fsdp,
    base,
    tok_hbm,
    w_hbm,
    small_ref,
    proj_hbm,
    fc_hbm,
    n_hbm,
    qkv_hbm,
    proj_all,
    fc_all,
    w_ref,
    lines_ref,
    n_ref,
    qkv_ref,
    x_ref,
    wg_ref,
    sg_ref,
    tok_recv,
    right_sem,
    left_sem,
    twin_sem,
    w_send,
    w_recv,
    s_send,
    s_recv,
    proj_send,
    proj_recv,
    fc_send,
    fc_recv,
    local,
):
    c = lax.axis_index("ctx")
    f = lax.axis_index("fsdp")
    chips = n_ctx // 2
    chip, core = c // 2, c % 2
    slots, width, cols = w_ref.shape
    shard = width // n_fsdp
    hd = HEAD_DIM
    enter(
        [(lax.rem(c + i, n_ctx), f) for i in range(1, n_ctx)]
        + [(c, flip(f, k, n_fsdp)) for k in range(1, n_fsdp)]
    )

    def block(at, same):
        return 2 * at + (core if same else 1 - core)

    def hop(step, to_right, from_own):
        origin = block(chip - step if to_right else chip + step, True)
        src = tok_hbm if from_own else x_ref.at[origin]
        sem = (right_sem if to_right else left_sem).at[step]
        peer = (c + 2 if to_right else c - 2, f)
        return send(src, x_ref.at[origin], sem, tok_recv.at[origin], peer)

    def twin(at, from_own):
        origin = block(at, True)
        src = tok_hbm if from_own else x_ref.at[origin]
        return send(
            src, x_ref.at[origin], twin_sem.at[at], tok_recv.at[origin], (block(chip, False), f)
        )

    def w_copy(k):
        return send(w_hbm, wg_ref.at[f], w_send.at[k], w_recv.at[k], (c, flip(f, k, n_fsdp)))

    def s_copy(k):
        return send(small_ref, sg_ref.at[f], s_send.at[k], s_recv.at[k], (c, flip(f, k, n_fsdp)))

    cut = shard // 32 * 16 if shard % 16 == 0 else 0
    shares = ((0, cut), (cut, shard)) if cut else ((0, shard), (0, shard))

    def weight_copy(share, k, onward, which):
        lo, hi = share
        other = flip(f, k, n_fsdp)
        dst = (proj_all, fc_all)[which]
        ss = (proj_send, fc_send)[which]
        rs = (proj_recv, fc_recv)[which]
        if onward:
            part = dst.at[other, lo:hi]
            return send(part, part, ss.at[1, k], rs.at[1, k], (block(chip, False), f))
        src = fc_hbm.at[other, lo:hi] if which else proj_hbm.at[lo:hi]
        return send(src, dst.at[f, lo:hi], ss.at[0, k], rs.at[0, k], (c, other))

    def by_core(act):
        for h in range(2):

            @pl.when(core == h)
            def _(h=h):
                act(shares[h], shares[1 - h])

    def weights_start(mine, theirs):
        for i in range(2):
            for k in range(1, n_fsdp):
                weight_copy(mine, k, False, i).start()

    def weights_onward(mine, theirs):
        for i in range(2):
            for k in range(1, n_fsdp):
                weight_copy(mine, k, False, i).wait_recv()
                if cut:
                    weight_copy(mine, k, True, i).start()

    def weights_done(mine, theirs):
        for i in range(2):
            for k in range(1, n_fsdp):
                if cut:
                    weight_copy(theirs, k, True, i).wait_recv()
                    weight_copy(mine, k, True, i).wait_send()
                weight_copy(mine, k, False, i).wait_send()

    for k in range(1, n_fsdp):
        s_copy(k).start()

    @pl.when(chip < chips - 1)
    def _():
        hop(0, True, True).start()

    @pl.when(chip > 0)
    def _():
        hop(0, False, True).start()

    for k in range(1, n_fsdp):
        w_copy(k).start()
    twin(chip, True).start()
    own_x = pltpu.make_async_copy(tok_hbm, x_ref.at[c], local.at[0])
    own_w = pltpu.make_async_copy(w_hbm, wg_ref.at[f], local.at[1])
    own_proj = pltpu.make_async_copy(proj_hbm, proj_all.at[f], local.at[2])
    own_fc = pltpu.make_async_copy(fc_hbm.at[f], fc_all.at[f], local.at[3])
    for copy in (own_x, own_w, own_proj, own_fc):
        copy.start()
    sg_ref[f] = small_ref[...]
    for k in range(1, n_fsdp):
        s_copy(k).wait_recv()
    for j in range(n_fsdp):
        lines_ref[:, j * shard : (j + 1) * shard] = sg_ref[j]
    main = n_ctx * base * hd
    row_id = lax.broadcasted_iota(jnp.int32, (width, slots * hd), 0)
    col_id = lax.broadcasted_iota(jnp.int32, (width, slots * hd), 1)
    wanted = jnp.where(col_id < base * hd, c * base * hd + col_id, main + col_id - base * hd)
    picked = dot(lines_ref[...].astype(BF16), (row_id == wanted).astype(BF16))
    zero = jnp.zeros((1, hd), F32)
    bias = [
        jnp.concatenate(
            [picked[4:5, s * hd : (s + 1) * hd], zero, picked[5:6, s * hd : (s + 1) * hd]], axis=1
        )
        for s in range(slots)
    ]
    own_w.wait()
    own_x.wait()
    for k in range(1, n_fsdp):
        w_copy(k).wait_recv()
    by_core(weights_start)
    for j in range(n_fsdp):
        w_ref[:, j * shard : (j + 1) * shard, :] = wg_ref[j]

    def results(origin):
        return (
            pltpu.make_async_copy(n_ref, n_hbm.at[origin], local.at[0]),
            pltpu.make_async_copy(qkv_ref, qkv_hbm.at[:, origin], local.at[1]),
        )

    def project(at, same, first=False):
        origin = block(at, same)
        rows = x_ref[origin].astype(F32)
        mean = jnp.mean(rows, axis=1, keepdims=True)
        cen = rows - mean
        var = jnp.mean(cen * cen, axis=1, keepdims=True)
        normed = cen * lax.rsqrt(var + EPS) * lines_ref[0:1] + lines_ref[2:3]
        normed = normed.astype(BF16)

        @pl.when(jnp.logical_not(first))
        def _():
            for copy in results(origin):
                copy.wait()

        n_ref[...] = normed
        for s in range(slots):
            qkv_ref[s] = (dot(normed, w_ref[s]) + bias[s]).astype(BF16)
        for copy in results(origin):
            copy.start()

    def arrived(at, same):
        origin = block(at, same)
        pltpu.make_async_copy(x_ref.at[origin], x_ref.at[origin], tok_recv.at[origin]).wait()

    def step(s, carry):
        @pl.when((s > 0) & (chip - s >= 0))
        def _():
            arrived(chip - s, True)
            twin(chip - s, False).start()

            @pl.when(chip < chips - 1)
            def _():
                hop(s, True, False).start()

        @pl.when((s > 0) & (chip + s < chips))
        def _():
            arrived(chip + s, True)
            twin(chip + s, False).start()

            @pl.when(chip > 0)
            def _():
                hop(s, False, False).start()

        @pl.when(chip - s >= 0)
        def _():
            project(chip - s, True, s == 0)

        @pl.when((s > 0) & (chip + s < chips))
        def _():
            project(chip + s, True)

        @pl.when(chip - s >= 0)
        def _():
            arrived(chip - s, False)
            project(chip - s, False)

        @pl.when((s > 0) & (chip + s < chips))
        def _():
            arrived(chip + s, False)
            project(chip + s, False)

        return carry

    lax.fori_loop(0, chips, step, 0)
    by_core(weights_onward)
    for copy in results(c):
        copy.wait()
    own_proj.wait()
    own_fc.wait()

    for s in range(chips):
        if s < chips - 1:

            @pl.when((chip - s >= 0) & (chip < chips - 1))
            def _():
                hop(s, True, False).wait_send()

            @pl.when((chip + s < chips) & (chip > 0))
            def _():
                hop(s, False, False).wait_send()

        twin(s, False).wait_send()
    for k in range(1, n_fsdp):
        w_copy(k).wait_send()
        s_copy(k).wait_send()
    by_core(weights_done)


def start_call(n_ctx, n_fsdp, base, tok, w_slots, small, w_proj, fc_parts, cid):
    count, width = tok.shape
    slots, shard, cols = w_slots.shape
    vm = pl.BlockSpec(memory_space=pltpu.VMEM)
    anym = pl.BlockSpec(memory_space=pl.ANY)
    dma = pltpu.SemaphoreType.DMA
    return pl.pallas_call(
        functools.partial(start_kernel, n_ctx, n_fsdp, base),
        in_specs=[anym, anym, vm, anym, anym],
        out_specs=[anym, anym, anym, anym, vm, vm],
        out_shape=[
            jax.ShapeDtypeStruct((n_ctx, count, width), BF16),
            jax.ShapeDtypeStruct((slots, n_ctx, count, cols), BF16),
            jax.ShapeDtypeStruct((n_fsdp,) + w_proj.shape, BF16),
            jax.ShapeDtypeStruct(fc_parts.shape, BF16),
            jax.ShapeDtypeStruct((slots, width, cols), BF16),
            jax.ShapeDtypeStruct((small.shape[0], width), F32),
        ],
        scratch_shapes=[
            pltpu.VMEM((count, width), BF16),
            pltpu.VMEM((slots, count, cols), BF16),
            pltpu.VMEM((n_ctx, count, width), BF16),
            pltpu.VMEM((n_fsdp, slots, shard, cols), BF16),
            pltpu.VMEM((n_fsdp,) + small.shape, F32),
            dma((n_ctx,)),
            dma((n_ctx // 2,)),
            dma((n_ctx // 2,)),
            dma((n_ctx // 2,)),
            dma((n_fsdp,)),
            dma((n_fsdp,)),
            dma((n_fsdp,)),
            dma((n_fsdp,)),
            dma((2, n_fsdp)),
            dma((2, n_fsdp)),
            dma((2, n_fsdp)),
            dma((2, n_fsdp)),
            dma((4,)),
        ],
        compiler_params=pltpu.CompilerParams(
            collective_id=cid, has_side_effects=True, vmem_limit_bytes=VMEM_LIMIT
        ),
        cost_estimate=SHORT,
        name="tokens_qkv",
    )(tok, w_slots, small, w_proj, fc_parts)


def causal_scores(k, q_rows, start):
    scores = dot_last(k, q_rows)
    keep = start
    tail = scores[keep:]
    key_id = lax.broadcasted_iota(jnp.int32, tail.shape, 0)
    query_id = lax.broadcasted_iota(jnp.int32, tail.shape, 1)
    tail = jnp.where(key_id <= query_id, tail, -1e30)
    if keep == 0:
        return tail
    return jnp.concatenate([scores[:keep], tail], axis=0)


def soft(scores, v_t):
    top = jnp.max(scores, axis=0, keepdims=True)
    weights = jnp.exp(scores - top)
    total = jnp.sum(weights, axis=0, keepdims=True)
    out = dot(v_t, weights.astype(BF16)) / total
    return out, top + jnp.log(total)


def causal(inv_ref, x_ref):
    return jnp.concatenate([x_ref[0, inv_ref[i]] for i in range(x_ref.shape[1])], axis=0)


def attn_fwd_kernel(inv_ref, x_ref, o_ref, l_ref):
    rows = l_ref.shape[2]
    hd = HEAD_DIM
    x = causal(inv_ref, x_ref)
    q = x[:, :hd] * BF16(SCALE)
    k = x[:, hd : 2 * hd]
    v_t = x[:, 2 * hd :].T
    for i in range(rows // QROWS):
        lo, hi = i * QROWS, (i + 1) * QROWS
        out, lse = soft(causal_scores(k[:hi], q[lo:hi], lo), v_t[:, :hi])
        l_ref[0, :, lo:hi] = lse
        out = out.astype(BF16)
        for b in range(QROWS // BLOCK):
            o_ref[inv_ref[2 * i + b]] = out[:, b * BLOCK : (b + 1) * BLOCK]


def attn_fwd(inv, qkv, heads):
    blocks, _, cols = qkv.shape[1:]
    rows = blocks * BLOCK
    return pl.pallas_call(
        attn_fwd_kernel,
        grid_spec=pltpu.PrefetchScalarGridSpec(
            num_scalar_prefetch=1,
            grid=(heads,),
            in_specs=[pl.BlockSpec((1, blocks, BLOCK, cols), lambda h, inv: (h, 0, 0, 0))],
            out_specs=[
                pl.BlockSpec((blocks, HEAD_DIM, BLOCK), lambda h, inv: (0, h, 0)),
                pl.BlockSpec((1, 1, rows), lambda h, inv: (h, 0, 0)),
            ],
        ),
        out_shape=[
            jax.ShapeDtypeStruct((blocks, heads * HEAD_DIM, BLOCK), BF16),
            jax.ShapeDtypeStruct((heads, 1, rows), F32),
        ],
        compiler_params=pltpu.CompilerParams(vmem_limit_bytes=VMEM_LIMIT),
        cost_estimate=SHORT,
        name="attn_fwd",
    )(inv, qkv)


def attn_bwd_kernel(inv_ref, x_ref, do_ref, o_ref, l_ref, dx_ref, dk_acc, dv_acc):
    rows = l_ref.shape[2]
    hd = HEAD_DIM
    x = causal(inv_ref, x_ref)
    q = x[:, :hd] * BF16(SCALE)
    k = x[:, hd : 2 * hd]
    v = x[:, 2 * hd :]
    k_t = k.T
    dk_acc[...] = jnp.zeros_like(dk_acc)
    dv_acc[...] = jnp.zeros_like(dv_acc)
    for i in range(rows // QROWS):
        lo, hi = i * QROWS, (i + 1) * QROWS
        ids = [inv_ref[2 * i + b] for b in range(QROWS // BLOCK)]
        do_t = jnp.concatenate([do_ref[b] for b in ids], axis=1)
        o_t = jnp.concatenate([o_ref[b] for b in ids], axis=1)
        inner = jnp.sum(do_t.astype(F32) * o_t.astype(F32), axis=0, keepdims=True)
        probs = jnp.exp(causal_scores(k[:hi], q[lo:hi], lo) - l_ref[0, :, lo:hi])
        dprobs = dot(v[:hi], do_t)
        dscores = (probs * (dprobs - inner)).astype(BF16)
        dv_acc[:hi] += dot_last(probs.astype(BF16), do_t)
        dk_acc[:hi] += dot(dscores, q[lo:hi])
        dq = (dot(k_t[:, :hi], dscores) * SCALE).T
        for n, b in enumerate(ids):
            dx_ref[0, b, :, :hd] = dq[n * BLOCK : (n + 1) * BLOCK].astype(BF16)
    for i in range(rows // BLOCK):
        lo, hi = i * BLOCK, (i + 1) * BLOCK
        dx_ref[0, inv_ref[i], :, hd : 2 * hd] = dk_acc[lo:hi].astype(BF16)
        dx_ref[0, inv_ref[i], :, 2 * hd :] = dv_acc[lo:hi].astype(BF16)


def attn_bwd(inv, qkv, d_out, out, lse, heads):
    blocks, _, cols = qkv.shape[1:]
    rows = blocks * BLOCK
    whole = pl.BlockSpec((1, blocks, BLOCK, cols), lambda h, inv: (h, 0, 0, 0))
    feat = pl.BlockSpec((blocks, HEAD_DIM, BLOCK), lambda h, inv: (0, h, 0))
    return pl.pallas_call(
        attn_bwd_kernel,
        grid_spec=pltpu.PrefetchScalarGridSpec(
            num_scalar_prefetch=1,
            grid=(heads,),
            in_specs=[
                whole,
                feat,
                feat,
                pl.BlockSpec((1, 1, rows), lambda h, inv: (h, 0, 0)),
            ],
            out_specs=whole,
            scratch_shapes=[pltpu.VMEM((rows, HEAD_DIM), F32)] * 2,
        ),
        out_shape=jax.ShapeDtypeStruct((heads, blocks, BLOCK, cols), BF16),
        compiler_params=pltpu.CompilerParams(vmem_limit_bytes=VMEM_LIMIT),
        cost_estimate=pl.CostEstimate(
            flops=24 * 10**9, bytes_accessed=24 * 10**6, transcendentals=0
        ),
        name="attn_bwd",
    )(inv, qkv, d_out, out, lse)


def own_scores(order_ref, x_ref, k):
    hd = HEAD_DIM
    blocks = x_ref.shape[1]
    first = order_ref[blocks]
    q = jnp.concatenate([x_ref[0, first], x_ref[0, first + 1]], axis=0)[:, :hd]
    q = q * BF16(SCALE)
    scores = dot_last(k, q)
    row = lax.broadcasted_iota(jnp.int32, (BLOCK, 1), 0)
    key_place = jnp.concatenate([order_ref[b] * BLOCK + row for b in range(blocks)], axis=0)
    lane = lax.broadcasted_iota(jnp.int32, (1, 2 * BLOCK), 1)
    low, high = order_ref[order_ref[blocks]], order_ref[order_ref[blocks] + 1]
    place = jnp.where(lane < BLOCK, low * BLOCK + lane, (high - 1) * BLOCK + lane)
    return q, first, jnp.where(key_place <= place, scores, -1e30)


def rest_fwd_kernel(order_ref, x_ref, o_ref, l_ref):
    hd = HEAD_DIM
    x = x_ref[0].reshape(-1, 3 * hd)
    _, _, scores = own_scores(order_ref, x_ref, x[:, hd : 2 * hd])
    out, lse = soft(scores, x[:, 2 * hd :].T)
    o_ref[0] = out.astype(BF16)
    l_ref[0] = lse


def rest_fwd(order, qkv, base):
    slots, blocks, _, cols = qkv.shape
    rest = slots - base
    return pl.pallas_call(
        rest_fwd_kernel,
        grid_spec=pltpu.PrefetchScalarGridSpec(
            num_scalar_prefetch=1,
            grid=(rest,),
            in_specs=[
                pl.BlockSpec((1, blocks, BLOCK, cols), lambda h, o: (base + h, 0, 0, 0))
            ],
            out_specs=[
                pl.BlockSpec((1, HEAD_DIM, QROWS), lambda h, o: (h, 0, 0)),
                pl.BlockSpec((1, 1, QROWS), lambda h, o: (h, 0, 0)),
            ],
        ),
        out_shape=[
            jax.ShapeDtypeStruct((rest, HEAD_DIM, QROWS), BF16),
            jax.ShapeDtypeStruct((rest, 1, QROWS), F32),
        ],
        compiler_params=pltpu.CompilerParams(vmem_limit_bytes=VMEM_LIMIT),
        cost_estimate=SHORT,
        name="rest_fwd",
    )(order, qkv)


def rest_bwd_kernel(order_ref, x_ref, do_ref, o_ref, l_ref, dx_ref):
    hd = HEAD_DIM
    x = x_ref[0].reshape(-1, 3 * hd)
    blocks = x_ref.shape[1]
    k = x[:, hd : 2 * hd]
    q, first, scores = own_scores(order_ref, x_ref, k)
    do_t = do_ref[0]
    inner = jnp.sum(do_t.astype(F32) * o_ref[0].astype(F32), axis=0, keepdims=True)
    probs = jnp.exp(scores - l_ref[0])
    dprobs = dot(x[:, 2 * hd :], do_t)
    dscores = (probs * (dprobs - inner)).astype(BF16)
    dv = dot_last(probs.astype(BF16), do_t).astype(BF16)
    dk = dot(dscores, q).astype(BF16)
    dq = (dot(k.T, dscores) * SCALE).T.astype(BF16)
    dx_ref[0, :, :, 2 * hd :] = dv.reshape(blocks, BLOCK, hd)
    dx_ref[0, :, :, hd : 2 * hd] = dk.reshape(blocks, BLOCK, hd)
    dx_ref[0, :, :, :hd] = jnp.zeros((blocks, BLOCK, hd), BF16)
    for b in range(2):
        dx_ref[0, first + b, :, :hd] = dq[b * BLOCK : (b + 1) * BLOCK]


def rest_bwd(order, qkv, d_out, out, lse, base):
    slots, blocks, _, cols = qkv.shape
    rest = slots - base
    feat = pl.BlockSpec((1, HEAD_DIM, QROWS), lambda h, o: (h, 0, 0))
    return pl.pallas_call(
        rest_bwd_kernel,
        grid_spec=pltpu.PrefetchScalarGridSpec(
            num_scalar_prefetch=1,
            grid=(rest,),
            in_specs=[
                pl.BlockSpec((1, blocks, BLOCK, cols), lambda h, o: (base + h, 0, 0, 0)),
                feat,
                feat,
                pl.BlockSpec((1, 1, QROWS), lambda h, o: (h, 0, 0)),
            ],
            out_specs=pl.BlockSpec((1, blocks, BLOCK, cols), lambda h, o: (h, 0, 0, 0)),
        ),
        out_shape=jax.ShapeDtypeStruct((rest, blocks, BLOCK, cols), BF16),
        compiler_params=pltpu.CompilerParams(vmem_limit_bytes=VMEM_LIMIT),
        cost_estimate=SHORT,
        name="rest_bwd",
    )(order, qkv, d_out, out, lse)


def far_first(i, chips):
    return (i % 2) * (i // 2) + (1 - i % 2) * (chips - 1 - i // 2)


def line_sum(chip, chips, f, core, part, came, sems, ready=None):
    sent, left_sem, right_sem = sems

    def to_right(d):
        return send(
            part.at[d], came.at[d], sent.at[d], left_sem.at[d], (2 * (chip + 1) + core, f)
        )

    def to_left(d):
        place = jnp.where(d == chip - 1, chips, d)
        return send(
            part.at[d], came.at[place], sent.at[d], right_sem.at[d], (2 * (chip - 1) + core, f)
        )

    def from_left(d):
        send(part.at[d], came.at[d], sent.at[d], left_sem.at[d], (2 * chip + core, f)).wait_recv()
        add(d, d)

    def from_right(d, place):
        send(
            part.at[d], came.at[place], sent.at[d], right_sem.at[d], (2 * chip + core, f)
        ).wait_recv()
        add(d, place)

    def add(d, place):
        part[d] = (part[d].astype(F32) + came[place].astype(F32)).astype(BF16)

    def step(t):
        far = chips - 1 - t + chip
        near = t - (chips - 1 - chip)

        @pl.when(chip <= t)
        def _():
            if ready is not None:
                ready(far)

            @pl.when(chip > 0)
            def _():
                from_left(far)

            to_right(far).start()

        @pl.when(near >= 0)
        def _():
            if ready is not None:
                ready(near)

            @pl.when(chip < chips - 1)
            def _():
                from_right(near, near)

            to_left(near).start()

    def finish():
        if ready is not None:
            ready(chip)

        @pl.when(chip > 0)
        def _():
            from_left(chip)

        @pl.when(chip < chips - 1)
        def _():
            from_right(chip, chips)

    def done():
        for d in range(chips):

            @pl.when(chip < d)
            def _(d=d):
                to_right(d).wait_send()

            @pl.when(chip > d)
            def _(d=d):
                to_left(d).wait_send()

    return step, finish, done


def line_gather(chip, chips, f, core, view, sems):
    right, left, twin_sent, got, twin_got = sems
    twin_id = (2 * chip + 1 - core, f)

    def hop(s, rightward):
        origin = chip - s if rightward else chip + s
        ref = view(origin, core)
        peer = (2 * (chip + 1 if rightward else chip - 1) + core, f)
        return send(ref, ref, (right if rightward else left).at[s], got.at[origin], peer)

    def twin(origin):
        ref = view(origin, core)
        return send(ref, ref, twin_sent.at[origin], twin_got.at[origin], twin_id)

    def arrived(origin):
        ref = view(origin, core)
        send(ref, ref, right.at[0], got.at[origin], twin_id).wait_recv()

    def step(s):
        @pl.when(chip - s >= 0)
        def _():
            if s:
                arrived(chip - s)

            @pl.when(chip < chips - 1)
            def _():
                hop(s, True).start()

            twin(chip - s).start()

        @pl.when(chip + s < chips)
        def _():
            if s:
                arrived(chip + s)

            @pl.when(chip > 0)
            def _():
                hop(s, False).start()

            if s:
                twin(chip + s).start()

    def done():
        for s in range(chips):
            if s < chips - 1:

                @pl.when((chip - s >= 0) & (chip < chips - 1))
                def _(s=s):
                    hop(s, True).wait_send()

                @pl.when((chip + s < chips) & (chip > 0))
                def _(s=s):
                    hop(s, False).wait_send()

            twin(s).wait_send()
            ref = view(s, 1 - core)
            send(ref, ref, twin_sent.at[s], twin_got.at[s], twin_id).wait_recv()

    return step, done


def back_kernel(
    n_ctx,
    n_fsdp,
    own_ref,
    rest_ref,
    w_ref,
    n_ref,
    one_ref,
    cols_ref,
    part,
    twin_out,
    twin_in,
    came,
    mine,
    theirs,
    twin_send,
    twin_recv,
    line_send,
    left_recv,
    right_recv,
    cols_send,
    cols_recv,
):
    c = lax.axis_index("ctx")
    f = lax.axis_index("fsdp")
    chips = n_ctx // 2
    chip, core = c // 2, c % 2
    slots, width, cols = w_ref.shape
    count = own_ref.shape[2]
    base = own_ref.shape[0]
    shard = width // n_fsdp
    twin_id = (2 * chip + 1 - core, f)
    enter(
        [(lax.rem(c + i, n_ctx), f) for i in range(1, n_ctx)]
        + [(c, flip(f, k, n_fsdp)) for k in range(1, n_fsdp)]
    )

    def grad(s):
        return own_ref.at[s] if s < base else rest_ref.at[s - base]

    def for_block(b):
        total = dot_last(grad(0)[b], w_ref[0])
        for s in range(1, slots):
            total += dot_last(grad(s)[b], w_ref[s])
        return total.astype(BF16)

    def to_twin(d, slot):
        return send(twin_out.at[slot], twin_in.at[d], twin_send.at[slot], twin_recv.at[d], twin_id)

    def products(i, carry):
        d = far_first(i, chips)
        slot = i % 2
        product = for_block(2 * d + 1 - core)

        @pl.when(i > 1)
        def _():
            to_twin(d, slot).wait_send()

        twin_out[slot] = product
        to_twin(d, slot).start()
        part[d] = for_block(2 * d + core)
        return carry

    def ready(d):
        to_twin(d, 0).wait_recv()
        part[d] = (part[d].astype(F32) + twin_in[d].astype(F32)).astype(BF16)

    step, finish, done = line_sum(
        chip, chips, f, core, part, came, (line_send, left_recv, right_recv), ready
    )

    def cols_copy(src, dst, at):
        return send(mine.at[src], theirs.at[at], cols_send.at[src], cols_recv.at[at], (c, dst))

    def columns(j):
        left = n_ref[:, :, j * shard : (j + 1) * shard].reshape(n_ctx * count, shard)
        for s in range(slots):
            right = grad(s)[...].reshape(n_ctx * count, cols)
            mine[j, s] = dot_first(left, right).astype(BF16)

    lax.fori_loop(0, 2, products, 0)
    step(0)
    for j in range(n_fsdp):
        columns(j)
    for k in range(1, n_fsdp):
        other = flip(f, k, n_fsdp)
        cols_copy(other, other, f).start()
    lax.fori_loop(2, chips, products, 0)
    if chips > 2:
        step(1)
    for t in range(2, chips - 1):
        step(t)
    total = mine[f].astype(F32)
    for k in range(1, n_fsdp):
        other = flip(f, k, n_fsdp)
        cols_copy(other, other, other).wait_recv()
        total += theirs[other].astype(F32)
    cols_ref[...] = total.astype(BF16)
    finish()
    one_ref[...] = part[chip]
    done()
    for slot in range(2):
        to_twin(0, slot).wait_send()
    for k in range(1, n_fsdp):
        other = flip(f, k, n_fsdp)
        cols_copy(other, other, other).wait_send()


def back_fits(n_ctx, n_fsdp, count, width, slots):
    blocks = (5 * (n_ctx // 2) + n_ctx) * count * width
    heads = slots * 256 * (n_ctx * count + 3 * width)
    return 2 * (blocks + heads) < 50 * 1024 * 1024


def back_call(n_ctx, n_fsdp, own, rest, w_slots, normed, cid):
    slots, width, cols = w_slots.shape
    count = normed.shape[1]
    chips = n_ctx // 2
    shard = width // n_fsdp
    vm = pl.BlockSpec(memory_space=pltpu.VMEM)
    dma = pltpu.SemaphoreType.DMA
    block = pltpu.VMEM((chips, count, width), BF16)
    piece = pltpu.VMEM((n_fsdp, slots, shard, cols), BF16)
    return pl.pallas_call(
        functools.partial(back_kernel, n_ctx, n_fsdp),
        in_specs=[vm] * 4,
        out_specs=[vm] * 2,
        out_shape=[
            jax.ShapeDtypeStruct((count, width), BF16),
            jax.ShapeDtypeStruct((slots, shard, cols), BF16),
        ],
        scratch_shapes=[
            block,
            pltpu.VMEM((2, count, width), BF16),
            block,
            pltpu.VMEM((chips + 1, count, width), BF16),
        ]
        + [piece] * 2
        + [dma((2,))]
        + [dma((chips,))] * 4
        + [dma((n_fsdp,))] * 2,
        compiler_params=pltpu.CompilerParams(
            collective_id=cid, has_side_effects=True, vmem_limit_bytes=60 * 1024 * 1024
        ),
        cost_estimate=SHORT,
        name="qkv_back",
    )(own, rest, w_slots, normed)


def sums_kernel(n_ctx, n_fsdp, lead, *refs):
    rows_ref, cols_ref, att_ref, mid_ref, lines_in = refs[:5]
    outs, cols_all, lines_ref = refs[5:7], refs[7], refs[8]
    parts, cames = refs[9:11], refs[11:13]
    proj_part, proj_in, proj_got, lines_got = refs[13:17]
    lines_send, lines_recv, local, proj_send, proj_recv, pair_sem = refs[17:23]
    cols_sems = refs[23:28]
    sems = [(refs[28 + 8 * i : 31 + 8 * i], refs[31 + 8 * i : 36 + 8 * i]) for i in range(2)]
    c = lax.axis_index("ctx")
    f = lax.axis_index("fsdp")
    chips = n_ctx // 2
    chip, core = c // 2, c % 2
    width = att_ref.shape[1]
    shard = width // n_fsdp
    half = shard // 2
    high = proj_in.shape[1]
    twin_id = (2 * chip + 1 - core, f)
    enter(
        [(lax.rem(c + i, n_ctx), f) for i in range(1, n_ctx)]
        + [(c, flip(f, k, n_fsdp)) for k in range(1, n_fsdp)]
    )

    def line_ops(i):
        sum_sems, gather_sems = sems[i]
        gather = line_gather(chip, chips, f, core, lambda at, h: outs[i].at[h, at], gather_sems)
        return line_sum(chip, chips, f, core, parts[i], cames[i], sum_sems) + gather

    def proj_pair():
        return send(proj_part.at[1 - core], proj_in, pair_sem.at[0], pair_sem.at[1], twin_id)

    def proj_copy(k):
        other = flip(f, k, n_fsdp)
        return send(
            proj_part.at[core, other],
            proj_got.at[f],
            proj_send.at[k],
            proj_recv.at[k],
            (c, other),
        )

    def proj_products(j):
        for h in range(2):
            lo = j * shard + h * half
            proj_part[h, j, :half] = dot_first(att_ref[:, lo : lo + half], mid_ref[...]).astype(BF16)
            if half < high:
                proj_part[h, j, half:] = jnp.zeros((high - half, width), BF16)

    def proj_add(j, carry):
        proj_part[core, j] = (
            proj_part[core, j].astype(F32) + proj_in[j].astype(F32)
        ).astype(BF16)
        return carry

    def proj_total():
        total = proj_part[core, f].astype(F32)
        for k in range(1, n_fsdp):
            proj_copy(k).wait_recv()
            total += proj_got[flip(f, k, n_fsdp)].astype(F32)
        total = total.astype(BF16)
        step = parts[1].shape[1]
        for p in range(chips):
            lo, hi = min(p * step, high), min((p + 1) * step, high)
            if hi > lo:
                parts[1][p, : hi - lo] = total[lo:hi]
            if hi - lo < step:
                parts[1][p, hi - lo :] = jnp.zeros((step - hi + lo, width), BF16)

    peers = [(flip(c, 1 << i, n_ctx), f) for i in range(n_ctx.bit_length() - 1)]
    ctx_phases = len(peers)
    peers += [(c, flip(f, 1 << i, n_fsdp)) for i in range(n_fsdp.bit_length() - 1)]

    def line_copy(i):
        rows = lines_in.shape[0] if i < ctx_phases else lead
        return send(
            lines_ref.at[:rows],
            lines_got.at[i, :rows],
            lines_send.at[i],
            lines_recv.at[i],
            peers[i],
        )

    def line_phase(i):
        if 0 < i <= len(peers):
            rows = lines_in.shape[0] if i <= ctx_phases else lead
            line_copy(i - 1).wait()
            lines_ref[:rows] += lines_got[i - 1, :rows]
        if i < len(peers):
            line_copy(i).start()

    def settle(finish, i):
        finish()
        keep = pltpu.make_async_copy(parts[i].at[chip], outs[i].at[core, chip], local.at[0])
        keep.start()
        keep.wait()

    sum_a, finish_a, sums_a, gather_a, gathers_a = line_ops(0)
    sum_b, finish_b, sums_b, gather_b, gathers_b = line_ops(1)
    cols_step, cols_done = line_gather(
        chip, chips, f, core, lambda at, h: cols_all.at[2 * at + h], cols_sems
    )
    load = pltpu.make_async_copy(cols_ref, cols_all.at[c], local.at[1])
    load.start()
    parts[0][...] = rows_ref[...]
    sum_a(0)
    load.wait()
    cols_step(0)
    lines_ref[...] = lines_in[...]
    for j in range(n_fsdp):
        proj_products(j)
    proj_pair().start()
    for t in range(1, chips - 1):
        sum_a(t)
        cols_step(t)
        if t == 1:
            proj_pair().wait()
            lax.fori_loop(0, n_fsdp, proj_add, 0)
            for k in range(1, n_fsdp):
                proj_copy(k).start()
    settle(finish_a, 0)
    gather_a(0)
    cols_step(chips - 1)
    proj_total()
    phase = 0
    for s in range(1, chips):
        sum_b(s - 1)
        gather_a(s)
        line_phase(phase)
        phase += 1
    settle(finish_b, 1)
    for s in range(chips):
        gather_b(s)
        line_phase(phase)
        phase += 1
    while phase <= len(peers):
        line_phase(phase)
        phase += 1
    for done in (sums_a, sums_b, cols_done, gathers_a, gathers_b):
        done()
    for k in range(1, n_fsdp):
        proj_copy(k).wait_send()


def sums_call(n_ctx, n_fsdp, rows, cols, attended, mid_low, lines, lead, cid):
    chips = n_ctx // 2
    count, width = attended.shape
    high = -(-(width // n_fsdp // 2) // 16) * 16
    shapes = [rows.shape, (chips, -(-high // (16 * chips)) * 16, width)]
    phases = (n_ctx * n_fsdp).bit_length() - 1
    vm = pl.BlockSpec(memory_space=pltpu.VMEM)
    anym = pl.BlockSpec(memory_space=pl.ANY)
    dma = pltpu.SemaphoreType.DMA
    return pl.pallas_call(
        functools.partial(sums_kernel, n_ctx, n_fsdp, lead),
        in_specs=[vm, anym, vm, vm, vm],
        out_specs=[vm, vm, anym, vm],
        out_shape=[jax.ShapeDtypeStruct((2,) + shape, BF16) for shape in shapes]
        + [jax.ShapeDtypeStruct((n_ctx,) + cols.shape, BF16)]
        + [jax.ShapeDtypeStruct(lines.shape, F32)],
        scratch_shapes=[pltpu.VMEM(shape, BF16) for shape in shapes]
        + [pltpu.VMEM((chips + 1,) + shape[1:], BF16) for shape in shapes]
        + [
            pltpu.VMEM((2, n_fsdp, high, width), BF16),
            pltpu.VMEM((n_fsdp, high, width), BF16),
            pltpu.VMEM((n_fsdp, high, width), BF16),
            pltpu.VMEM((phases,) + lines.shape, F32),
            dma((phases,)),
            dma((phases,)),
            dma((2,)),
            dma((n_fsdp,)),
            dma((n_fsdp,)),
            dma((2,)),
        ]
        + [dma((chips,))] * (5 + 2 * 8),
        compiler_params=pltpu.CompilerParams(
            collective_id=cid, has_side_effects=True, vmem_limit_bytes=56 * 1024 * 1024
        ),
        cost_estimate=SHORT,
        name="weight_sums",
    )(rows, cols, attended, mid_low, lines)


def assemble_kernel(
    n_fsdp,
    own_ref,
    rest_ref,
    rows_ref,
    third_ref,
    out_ref,
    attn_hbm,
    fc_hbm,
    proj_hbm,
    wout_hbm,
    *scratch,
):
    attn_ref, fc_ref, proj_ref, wout_ref, sem = scratch
    hd = HEAD_DIM
    shard, hidden = fc_ref.shape[0], fc_ref.shape[1] // n_fsdp
    half = shard // 2
    width = proj_ref.shape[1]
    count = own_ref.shape[0]
    copies = [
        pltpu.make_async_copy(src, dst, sem.at[i])
        for i, (src, dst) in enumerate(
            ((wout_ref, wout_hbm), (fc_ref, fc_hbm), (proj_ref, proj_hbm), (attn_ref, attn_hbm))
        )
    ]
    wout_ref[...] = out_ref[...].astype(F32)
    copies[0].start()
    for h in range(2):
        for j in range(n_fsdp):
            lo, hi = j * half, (j + 1) * half
            fc_ref[h * half : (h + 1) * half, j * hidden : (j + 1) * hidden] = rows_ref[
                h, lo:hi
            ].astype(F32)
    copies[1].start()
    for h in range(2):
        proj_ref[h * half : (h + 1) * half] = third_ref[h, :half].astype(F32)
    copies[2].start()
    for h in range(width // hd):
        src = own_ref.at[h] if h < count else rest_ref.at[h - count]
        for part in range(3):
            at = part * width + h * hd
            attn_ref[:, at : at + hd] = src[:, part * hd : (part + 1) * hd].astype(F32)
    copies[3].start()
    for copy in copies:
        copy.wait()


def assemble(n_fsdp, own, rest, rows, third, out_low, hidden):
    shard = own.shape[1]
    width = rows.shape[2]
    vm = pl.BlockSpec(memory_space=pltpu.VMEM)
    anym = pl.BlockSpec(memory_space=pl.ANY)
    shapes = [(shard, 3 * width), (shard, n_fsdp * hidden), (shard, width), out_low.shape]
    return pl.pallas_call(
        functools.partial(assemble_kernel, n_fsdp),
        in_specs=[vm] * 5,
        out_specs=[anym] * 4,
        out_shape=[jax.ShapeDtypeStruct(shape, F32) for shape in shapes],
        scratch_shapes=[pltpu.VMEM(shape, F32) for shape in shapes]
        + [pltpu.SemaphoreType.DMA((4,))],
        compiler_params=pltpu.CompilerParams(vmem_limit_bytes=60 * 1024 * 1024),
        cost_estimate=SHORT,
        name="assemble",
    )(own, rest, rows, third, out_low)


def norm_parts(rows):
    mean = jnp.mean(rows, axis=-1, keepdims=True)
    cen = rows - mean
    rstd = lax.rsqrt(jnp.mean(cen * cen, axis=-1, keepdims=True) + EPS)
    return cen * rstd, rstd


def norm_back(xhat, rstd, gain, grad):
    dxhat = grad * gain
    return rstd * (
        dxhat
        - jnp.mean(dxhat, axis=-1, keepdims=True)
        - xhat * jnp.mean(dxhat * xhat, axis=-1, keepdims=True)
    )


def swap(value, axis, size, k):
    return lax.ppermute(value, axis, [(i, i ^ k) for i in range(size)])


def shards(
    n_ctx,
    n_fsdp,
    tokens,
    block_order,
    w_attn,
    w_proj,
    w_fc,
    w_out,
    norm_gains,
    biases,
    fc_bias,
    cotangent,
):
    hd = HEAD_DIM
    count, width = tokens.shape[1:]
    shard = width // n_fsdp
    heads = width // hd
    base = heads // n_ctx
    rest = heads - base * n_ctx
    slots = base + rest
    own_blocks = count // BLOCK
    c = lax.axis_index("ctx")
    f = lax.axis_index("fsdp")

    order = block_order[0]
    inv = jnp.argsort(order).astype(jnp.int32)
    order_own = jnp.concatenate([order, (c * own_blocks)[None]])

    def head_cols(h):
        return jnp.concatenate(
            [
                lax.dynamic_slice(w_attn, (0, part * width + h * hd), (shard, hd))
                for part in range(3)
            ],
            axis=1,
        )

    slot_heads = [c * base + s for s in range(base)] + [n_ctx * base + r for r in range(rest)]
    w_slots = jnp.stack([head_cols(h) for h in slot_heads])
    small = jnp.concatenate([norm_gains, biases], axis=0).astype(F32)
    hidden_cols = w_fc.shape[1] // n_fsdp
    fc_parts = jnp.stack(
        [w_fc[:, j * hidden_cols : (j + 1) * hidden_cols] for j in range(n_fsdp)]
    )
    normed_one, qkv, full_proj, fc_cols, w_slots, small = start_call(
        n_ctx, n_fsdp, base, tokens[0], w_slots, small, w_proj, fc_parts, 3
    )
    full_proj = full_proj.reshape(width, width)
    fc_cols = fc_cols.reshape(width, hidden_cols)
    qkv = qkv.reshape(slots, n_ctx * own_blocks, BLOCK, 3 * hd)
    gains, shifts = small[:2], small[2:]
    cot = cotangent[0]

    cot_late, _ = lax.optimization_barrier((cot, small))
    cot_all = lax.all_gather(cot_late, "fsdp", axis=0)

    out_own, lse_own = attn_fwd(inv, qkv, base)
    got = lax.all_to_all(out_own, "ctx", split_axis=0, concat_axis=0, tiled=True)
    got = got.reshape(n_ctx, own_blocks, base * hd, BLOCK).transpose(1, 3, 0, 2)
    attended = got.reshape(count, n_ctx * base * hd)
    if rest:
        out_rest, lse_rest = rest_fwd(order_own, qkv, base)
        attended = jnp.concatenate([attended, out_rest.reshape(rest * hd, count).T], axis=1)

    rows = tokens[0].astype(F32)
    mid = rows + (dot(attended, full_proj) + shifts[4])
    xhat_two, rstd_two = norm_parts(mid)
    normed_two = (xhat_two * gains[1] + shifts[1]).astype(BF16)

    normed_two_grad, fc_bias_part, out_part, w_out_part, w_fc_part = ffn(
        n_fsdp,
        normed_two,
        cot_all,
        fc_cols,
        w_out,
        fc_bias.astype(F32)[None],
    )
    out_rows = lax.psum_scatter(
        out_part.reshape(n_fsdp * count, width), "fsdp", scatter_dimension=0, tiled=True
    )
    w_out_low = lax.psum(w_out_part, "ctx")

    cot_rows = cot.astype(F32)
    mid_grad = cot_rows + norm_back(xhat_two, rstd_two, gains[1], normed_two_grad)
    mid_low = mid_grad.astype(BF16)
    attended_grad = dot_last(mid_low, full_proj).astype(BF16)
    half = shard // 2
    core = c % 2

    def core_half(part):
        away = lax.dynamic_slice_in_dim(part, (1 - core) * half, half, 1)
        here = lax.dynamic_slice_in_dim(part, core * half, half, 1)
        return (here.astype(F32) + swap(away, "ctx", n_ctx, 1).astype(F32)).astype(BF16)

    def over_fsdp(part):
        out = []
        for k in range(n_fsdp):
            piece = lax.dynamic_index_in_dim(part, f ^ k, keepdims=False)
            out.append(swap(piece, "fsdp", n_fsdp, k) if k else piece)
        return out

    w_fc_part, _ = lax.optimization_barrier((w_fc_part, attended_grad))
    w_fc_mid = core_half(w_fc_part.reshape(n_fsdp, shard, hidden_cols))

    main = n_ctx * base * hd
    sent = attended_grad[:, :main].reshape(own_blocks, BLOCK, n_ctx, base * hd)
    sent = sent.transpose(2, 0, 3, 1).reshape(n_ctx * own_blocks, base * hd, BLOCK)
    d_out = lax.all_to_all(sent, "ctx", split_axis=0, concat_axis=0, tiled=True)
    d_out, w_fc_mid = lax.optimization_barrier((d_out, w_fc_mid))
    w_fc_half = jnp.zeros((n_fsdp, half, hidden_cols), BF16)
    for k, piece in enumerate(over_fsdp(w_fc_mid)):
        w_fc_half = lax.dynamic_update_slice(w_fc_half, piece[None], (f ^ k, 0, 0))
    d_own = attn_bwd(inv, qkv, d_out, out_own, lse_own, base)
    d_own = d_own.reshape(base, n_ctx, count, 3 * hd)
    if rest:
        d_rest = attended_grad[:, main:].T.reshape(rest, hd, count)
        d_rest = rest_bwd(order_own, qkv, d_rest, out_rest, lse_rest, base)
        d_rest = d_rest.reshape(rest, n_ctx, count, 3 * hd)
        sums = jnp.concatenate(
            [jnp.sum(d.astype(F32), axis=(1, 2)) for d in (d_own, d_rest)], axis=0
        )
    else:
        d_rest = d_own
        sums = jnp.sum(d_own.astype(F32), axis=(1, 2))
    if back_fits(n_ctx, n_fsdp, count, width, slots):
        d_own, w_fc_half = lax.optimization_barrier((d_own, w_fc_half))
        normed_one_grad, cols_sum = back_call(
            n_ctx, n_fsdp, d_own, d_rest, w_slots, normed_one, 4
        )
        normed_one_grad = normed_one_grad.astype(F32)
    else:
        dqkv = jnp.concatenate([d_own, d_rest])[:slots].reshape(slots, n_ctx * count, 3 * hd)
        one_part = jnp.einsum("hte,hde->td", dqkv, w_slots, preferred_element_type=F32)
        normed_one_grad = lax.psum_scatter(
            one_part.astype(BF16), "ctx", scatter_dimension=0, tiled=True
        ).astype(F32)
        slot_part = jnp.einsum(
            "td,hte->hde",
            normed_one.reshape(n_ctx * count, width),
            dqkv,
            preferred_element_type=F32,
        ).astype(BF16)
        cols_sum = lax.psum_scatter(slot_part, "fsdp", scatter_dimension=1, tiled=True)

    w_out_low, _ = lax.optimization_barrier((w_out_low, normed_one_grad))
    xhat_one, rstd_one = norm_parts(rows)
    tokens_grad = (mid_grad + norm_back(xhat_one, rstd_one, gains[0], normed_one_grad)).astype(
        BF16
    )

    def placed(part):
        cols = sums[:, part * hd : (part + 1) * hd]
        line = lax.dynamic_update_slice_in_dim(
            jnp.zeros((width,), F32), cols[:base].reshape(-1), c * base * hd, 0
        )
        return line + jnp.pad(cols[base:].reshape(-1), (main, 0))

    lines = jnp.stack(
        [
            jnp.sum(normed_one_grad * xhat_one, axis=0),
            jnp.sum(normed_two_grad * xhat_two, axis=0),
            jnp.sum(normed_one_grad, axis=0),
            jnp.sum(normed_two_grad, axis=0),
            placed(0),
            placed(2),
            jnp.sum(mid_low.astype(F32), axis=0),
            jnp.sum(cot_rows, axis=0),
        ]
    )
    lead = lines.shape[0]
    tail = jnp.pad(fc_bias_part, ((0, 7), (0, width - hidden_cols)))
    lines = jnp.concatenate([lines, tail])

    chips = n_ctx // 2
    parts = [w_fc_half.reshape(-1, width)]
    if rest:
        parts.append(core_half(cols_sum[base:]).reshape(-1, width))
    bounds = [0]
    for part in parts:
        bounds.append(bounds[-1] + part.shape[0])
    per_chip = -(-bounds[-1] // (16 * chips)) * 16
    rows_all = jnp.concatenate(parts)
    rows_all = jnp.pad(rows_all, ((0, per_chip * chips - bounds[-1]), (0, 0)))
    rows_all = rows_all.reshape(chips, per_chip, width)
    rows_all, third, own_cols, lines = sums_call(
        n_ctx, n_fsdp, rows_all, cols_sum[:base], attended, mid_low, lines, lead, 5
    )
    out_rows, lines = lax.optimization_barrier((out_rows, lines))
    layer_rows = (mid + (out_rows.astype(F32) + shifts[5])).astype(BF16)
    rows_all, third = rows_all.reshape(2, -1, width), third.reshape(2, -1, width)
    own_cols = own_cols.reshape(n_ctx * base, shard, 3 * hd)
    if rest:
        rest_cols = rows_all[:, bounds[1] : bounds[2]].reshape(2, rest, half, 3 * hd)
        rest_cols = rest_cols.transpose(1, 0, 2, 3).reshape(rest, shard, 3 * hd)
    else:
        rest_cols = own_cols
    if hidden_cols == width:
        w_attn_grad, w_fc_grad, w_proj_grad, w_out_grad = assemble(
            n_fsdp, own_cols, rest_cols, rows_all, third, w_out_low, hidden_cols
        )
    else:
        w_fc_low = rows_all[:, : bounds[1]].reshape(2, n_fsdp, half, hidden_cols)
        w_fc_grad = w_fc_low.transpose(0, 2, 1, 3).reshape(shard, n_fsdp * hidden_cols)
        w_fc_grad = w_fc_grad.astype(F32)
        w_proj_grad = third[:, :half].reshape(shard, width).astype(F32)
        cols = jnp.concatenate([own_cols, rest_cols])[: width // hd]
        cols = cols.reshape(width // hd, shard, 3, hd).transpose(1, 2, 0, 3)
        w_attn_grad = cols.reshape(shard, 3 * width).astype(F32)
        w_out_grad = w_out_low.astype(F32)
    fc_bias_grad = lines[lead, :hidden_cols]
    lines = lax.dynamic_slice_in_dim(lines[:lead], f * shard, shard, 1)
    return (
        layer_rows[None],
        tokens_grad[None],
        w_attn_grad,
        w_proj_grad,
        w_fc_grad,
        w_out_grad,
        lines[:2],
        lines[2:],
        fc_bias_grad,
    )


def solution(mesh):
    rows = P("fsdp", "ctx", None)
    weight = P("fsdp", None)
    vectors = P(None, "fsdp")
    return jax.shard_map(
        functools.partial(shards, mesh.shape["ctx"], mesh.shape["fsdp"]),
        mesh=mesh,
        in_specs=(
            rows, weight, weight, weight, weight, weight, vectors, vectors, P("fsdp"), rows,
        ),
        out_specs=(
            rows, rows, weight, weight, weight, weight, vectors, vectors, P("fsdp"),
        ),
        check_vma=False,
    )
```

```python
import functools

import jax
import jax.numpy as jnp
from jax import lax
from jax.experimental import pallas as pl
from jax.experimental.pallas import tpu as pltpu
from jax.sharding import PartitionSpec as P

HEAD_DIM = 64
BLOCK = 128
QROWS = 256
EPS = 1e-05
SCALE = HEAD_DIM ** (-0.5)
F32 = jnp.float32
BF16 = jnp.bfloat16
VMEM_LIMIT = 56 * 1024 * 1024
LAST = (((1,), (1,)), ((), ()))
FIRST = (((0,), (0,)), ((), ()))
MESH = pl.DeviceIdType.MESH
TILE = 256


def dot_last(a, b):
    return lax.dot_general(a, b, LAST, preferred_element_type=F32)


def dot(a, b):
    return jnp.dot(a, b, preferred_element_type=F32)


def dot_first(a, b):
    return lax.dot_general(a, b, FIRST, preferred_element_type=F32)


SHORT = pl.CostEstimate(flops=1, bytes_accessed=1, transcendentals=0)


def flip(place, k, size):
    out = 0
    bit = 1
    while bit < size:
        out = out + (place // bit + k // bit) % 2 * bit
        bit *= 2
    return out

def enter(peers):
    barrier = pltpu.get_barrier_semaphore()
    for peer in peers:
        pl.semaphore_signal(barrier, inc=1, device_id=peer, device_id_type=MESH)
    pl.semaphore_wait(barrier, len(peers))

def send(src, dst, send_sem, recv_sem, peer):
    return pltpu.make_async_remote_copy(
        src_ref=src, dst_ref=dst, send_sem=send_sem, recv_sem=recv_sem,
        device_id=peer, device_id_type=MESH)


def ffn_kernel(n, nt_hbm, cot_hbm, wfc_hbm, wout_hbm, bias_ref,
               gsum_ref, fcb_ref, out_hbm, wout_grad_hbm, wfc_grad_hbm,
               cot_ref, wfc_ref, wout_ref, all_ref, act_ref, hg_ref, ag_ref, part_ref, got_ref, stage_d, stage_h,
               s1, r1, s2, r2, local):
    c = lax.axis_index("ctx")
    f = lax.axis_index("fsdp")
    rows, width = nt_hbm.shape
    enter([(c, flip(f, k, n)) for k in range(1, n)])

    def rows_out(k):
        return send(nt_hbm, all_ref.at[f], s1.at[k], r1.at[k], (c, flip(f, k, n)))

    def grad_back(k):
        other = flip(f, k, n)
        return send(part_ref.at[other], got_ref.at[k], s2.at[k], r2.at[k], (c, other))

    near = [k for k in range(1, n) if k & (k - 1) == 0]
    far = [k for k in range(1, n) if k not in near]
    for k in near:
        rows_out(k).start()
    loads = [
        pltpu.make_async_copy(nt_hbm, all_ref.at[f], local.at[0]),
        pltpu.make_async_copy(wout_hbm, wout_ref, local.at[1]),
        pltpu.make_async_copy(cot_hbm, cot_ref, local.at[2]),
        pltpu.make_async_copy(wfc_hbm, wfc_ref, local.at[3]),
    ]
    for load in loads:
        load.start()
    fcb_ref[...] = jnp.zeros_like(fcb_ref)
    loads[1].wait()
    loads[2].wait()

    def active_grad(k, carry):
        ag_ref[k] = dot_last(cot_ref[k], wout_ref[...])
        return carry

    lax.fori_loop(0, n, active_grad, 0)
    for k in far:
        rows_out(k).start()
    loads[0].wait()
    loads[3].wait()

    def chunk(k, carry):
        src = flip(f, k, n)

        @pl.when(k > 0)
        def _():
            rows_out(k).wait_recv()

        hidden = dot(all_ref[src], wfc_ref[...]) + bias_ref[...]
        square = hidden * hidden
        tanh = jnp.tanh(0.7978845608028654 * (hidden + 0.044715 * square * hidden))
        act_ref[src] = (0.5 * hidden * (1.0 + tanh)).astype(BF16)
        slope = 0.5 * (1.0 + tanh) + 0.5 * hidden * (1.0 - tanh * tanh) * 0.7978845608028654 * (
            1.0 + 3.0 * 0.044715 * square
        )
        grad = (ag_ref[src] * slope).astype(BF16)
        hg_ref[src] = grad
        fcb_ref[...] += jnp.sum(grad.astype(F32), axis=0, keepdims=True)
        part_ref[src] = dot_last(grad, wfc_ref[...]).astype(BF16)

        @pl.when(k > 0)
        def _():
            grad_back(k).start()

        return carry

    lax.fori_loop(0, n, chunk, 0)

    def grads(left_ref, right_ref, dst, stage_ref, base):
        wide = left_ref.shape[2]
        right = right_ref[...].reshape(n * rows, right_ref.shape[2])
        copies = []
        for i, lo in enumerate(range(0, wide, TILE)):
            hi = min(lo + TILE, wide)
            slot = i % 2
            if i >= 2:
                copies[i - 2].wait()
            left = left_ref[:, :, lo:hi].reshape(n * rows, hi - lo)
            stage_ref[slot, : hi - lo] = dot_first(left, right).astype(BF16)
            copies.append(
                pltpu.make_async_copy(
                    stage_ref.at[slot, : hi - lo], dst.at[lo:hi], local.at[base + slot]
                )
            )
            copies[-1].start()
        for copy in copies[-2:]:
            copy.wait()

    grads(act_ref, cot_ref, wout_grad_hbm, stage_d, 4)
    grads(all_ref, hg_ref, wfc_grad_hbm, stage_h, 6)

    def out_copy(k):
        return pltpu.make_async_copy(
            stage_d.at[k % 2, :rows], out_hbm.at[k], local.at[4 + k % 2]
        )

    for k in range(n):
        if k >= 2:
            out_copy(k - 2).wait()
        stage_d[k % 2, :rows] = dot(act_ref[k], wout_ref[...]).astype(BF16)
        out_copy(k).start()

    gsum_ref[...] = part_ref[f].astype(F32)
    for k in near + far:
        grad_back(k).wait_recv()
        gsum_ref[...] += got_ref[k].astype(F32)
    for k in range(1, n):
        rows_out(k).wait_send()
        grad_back(k).wait_send()
    for k in range(max(0, n - 2), n):
        out_copy(k).wait()


def ffn(n, nt, cot, wfc, wout, bias, cid=1):
    m, d = nt.shape
    h = wfc.shape[1]
    vm = pl.BlockSpec(memory_space=pltpu.VMEM)
    anym = pl.BlockSpec(memory_space=pl.ANY)
    return pl.pallas_call(
        functools.partial(ffn_kernel, n),
        in_specs=[anym] * 4 + [vm],
        out_specs=[vm, vm] + [anym] * 3,
        out_shape=[
            jax.ShapeDtypeStruct((m, d), F32),
            jax.ShapeDtypeStruct((1, h), F32),
            jax.ShapeDtypeStruct((n, m, d), BF16),
            jax.ShapeDtypeStruct((h, d), BF16),
            jax.ShapeDtypeStruct((d, h), BF16),
        ],
        scratch_shapes=[
            pltpu.VMEM((n, m, d), BF16),
            pltpu.VMEM((d, h), BF16),
            pltpu.VMEM((h, d), BF16),
            pltpu.VMEM((n, m, d), BF16),
            pltpu.VMEM((n, m, h), BF16),
            pltpu.VMEM((n, m, h), BF16),
            pltpu.VMEM((n, m, h), F32),
            pltpu.VMEM((n, m, d), BF16),
            pltpu.VMEM((n, m, d), BF16),
            pltpu.VMEM((2, max(TILE, m), d), BF16),
            pltpu.VMEM((2, TILE, h), BF16),
        ]
        + [pltpu.SemaphoreType.DMA((n,))] * 4
        + [pltpu.SemaphoreType.DMA((8,))],
        compiler_params=pltpu.CompilerParams(
            collective_id=cid, has_side_effects=True, vmem_limit_bytes=60 * 1024 * 1024
        ),
        cost_estimate=SHORT,
        name="feed_forward",
    )(nt, cot, wfc, wout, bias)


def weight_shares(c, f, core, n_fsdp, shard, source, dst, ss, rs):
    cut = shard // 32 * 16 if shard % 16 == 0 else 0
    shares = ((0, cut), (cut, shard)) if cut else ((0, shard), (0, shard))
    twin_id = (c + 1 - 2 * core, f)

    def copy(share, k, onward):
        lo, hi = share
        other = flip(f, k, n_fsdp)
        if onward:
            part = dst.at[other, lo:hi]
            return send(part, part, ss.at[1, k], rs.at[1, k], twin_id)
        return send(source(k).at[lo:hi], dst.at[f, lo:hi], ss.at[0, k], rs.at[0, k], (c, other))

    def by_core(act):
        for h in range(2):

            @pl.when(core == h)
            def _(h=h):
                for k in range(1, n_fsdp):
                    act(shares[h], shares[1 - h], k)

    def start(mine, theirs, k):
        copy(mine, k, False).start()

    def onward(mine, theirs, k):
        copy(mine, k, False).wait_recv()
        if cut:
            copy(mine, k, True).start()

    def done(mine, theirs, k):
        if cut:
            copy(theirs, k, True).wait_recv()
            copy(mine, k, True).wait_send()
        copy(mine, k, False).wait_send()

    return tuple(functools.partial(by_core, act) for act in (start, onward, done))


def start_kernel(
    n_ctx,
    n_fsdp,
    base,
    tok_hbm,
    w_hbm,
    small_ref,
    proj_hbm,
    fc_hbm,
    n_hbm,
    qkv_hbm,
    proj_all,
    fc_parts,
    w_ref,
    lines_ref,
    n_ref,
    qkv_ref,
    fc_ref,
    fc_cut,
    x_ref,
    wg_ref,
    sg_ref,
    tok_recv,
    right_sem,
    left_sem,
    twin_sem,
    w_send,
    w_recv,
    s_send,
    s_recv,
    proj_send,
    proj_recv,
    local,
):
    c = lax.axis_index("ctx")
    f = lax.axis_index("fsdp")
    chips = n_ctx // 2
    chip, core = c // 2, c % 2
    slots, width, cols = w_ref.shape
    shard = width // n_fsdp
    hd = HEAD_DIM
    enter(
        [(lax.rem(c + i, n_ctx), f) for i in range(1, n_ctx)]
        + [(c, flip(f, k, n_fsdp)) for k in range(1, n_fsdp)]
    )

    def block(at, same):
        return 2 * at + (core if same else 1 - core)

    def hop(step, to_right, from_own):
        origin = block(chip - step if to_right else chip + step, True)
        src = tok_hbm if from_own else x_ref.at[origin]
        sem = (right_sem if to_right else left_sem).at[step]
        peer = (c + 2 if to_right else c - 2, f)
        return send(src, x_ref.at[origin], sem, tok_recv.at[origin], peer)

    def twin(at, from_own):
        origin = block(at, True)
        src = tok_hbm if from_own else x_ref.at[origin]
        return send(
            src, x_ref.at[origin], twin_sem.at[at], tok_recv.at[origin], (block(chip, False), f)
        )

    def w_copy(k):
        return send(w_hbm, wg_ref.at[f], w_send.at[k], w_recv.at[k], (c, flip(f, k, n_fsdp)))

    def s_copy(k):
        return send(small_ref, sg_ref.at[f], s_send.at[k], s_recv.at[k], (c, flip(f, k, n_fsdp)))

    weights_start, weights_onward, weights_done = weight_shares(
        c, f, core, n_fsdp, shard, lambda k: proj_hbm, proj_all, proj_send, proj_recv
    )

    for k in range(1, n_fsdp):
        s_copy(k).start()

    @pl.when(chip < chips - 1)
    def _():
        hop(0, True, True).start()

    @pl.when(chip > 0)
    def _():
        hop(0, False, True).start()

    for k in range(1, n_fsdp):
        w_copy(k).start()
    twin(chip, True).start()
    own_x = pltpu.make_async_copy(tok_hbm, x_ref.at[c], local.at[0])
    own_w = pltpu.make_async_copy(w_hbm, wg_ref.at[f], local.at[1])
    own_proj = pltpu.make_async_copy(proj_hbm, proj_all.at[f], local.at[2])
    load_fc = pltpu.make_async_copy(fc_hbm, fc_ref, local.at[3])
    for copy in (own_x, own_w, own_proj, load_fc):
        copy.start()
    sg_ref[f] = small_ref[...]
    for k in range(1, n_fsdp):
        s_copy(k).wait_recv()
    for j in range(n_fsdp):
        lines_ref[:, j * shard : (j + 1) * shard] = sg_ref[j]
    main = n_ctx * base * hd
    row_id = lax.broadcasted_iota(jnp.int32, (width, slots * hd), 0)
    col_id = lax.broadcasted_iota(jnp.int32, (width, slots * hd), 1)
    wanted = jnp.where(col_id < base * hd, c * base * hd + col_id, main + col_id - base * hd)
    picked = dot(lines_ref[...].astype(BF16), (row_id == wanted).astype(BF16))
    zero = jnp.zeros((1, hd), F32)
    bias = [
        jnp.concatenate(
            [picked[4:5, s * hd : (s + 1) * hd], zero, picked[5:6, s * hd : (s + 1) * hd]], axis=1
        )
        for s in range(slots)
    ]
    own_w.wait()
    own_x.wait()
    for k in range(1, n_fsdp):
        w_copy(k).wait_recv()
    weights_start()
    for j in range(n_fsdp):
        w_ref[:, j * shard : (j + 1) * shard, :] = wg_ref[j]

    load_fc.wait()
    hidden = fc_cut.shape[2]
    cuts = []
    for j in range(n_fsdp):
        if j >= 2:
            cuts[j - 2].wait()
        fc_cut[j % 2] = fc_ref[:, j * hidden : (j + 1) * hidden]
        cuts.append(pltpu.make_async_copy(fc_cut.at[j % 2], fc_parts.at[j], local.at[4 + j % 2]))
        cuts[-1].start()

    def results(origin):
        return (
            pltpu.make_async_copy(n_ref, n_hbm.at[origin], local.at[0]),
            pltpu.make_async_copy(qkv_ref, qkv_hbm.at[:, origin], local.at[1]),
        )

    def project(at, same, first=False):
        origin = block(at, same)
        rows = x_ref[origin].astype(F32)
        mean = jnp.mean(rows, axis=1, keepdims=True)
        cen = rows - mean
        var = jnp.mean(cen * cen, axis=1, keepdims=True)
        normed = cen * lax.rsqrt(var + EPS) * lines_ref[0:1] + lines_ref[2:3]
        normed = normed.astype(BF16)

        @pl.when(jnp.logical_not(first))
        def _():
            for copy in results(origin):
                copy.wait()

        n_ref[...] = normed
        for s in range(slots):
            qkv_ref[s] = (dot(normed, w_ref[s]) + bias[s]).astype(BF16)
        for copy in results(origin):
            copy.start()

    def arrived(at, same):
        origin = block(at, same)
        pltpu.make_async_copy(x_ref.at[origin], x_ref.at[origin], tok_recv.at[origin]).wait()

    def step(s, carry):
        @pl.when((s > 0) & (chip - s >= 0))
        def _():
            arrived(chip - s, True)
            twin(chip - s, False).start()

            @pl.when(chip < chips - 1)
            def _():
                hop(s, True, False).start()

        @pl.when((s > 0) & (chip + s < chips))
        def _():
            arrived(chip + s, True)
            twin(chip + s, False).start()

            @pl.when(chip > 0)
            def _():
                hop(s, False, False).start()

        @pl.when(chip - s >= 0)
        def _():
            project(chip - s, True, s == 0)

        @pl.when((s > 0) & (chip + s < chips))
        def _():
            project(chip + s, True)

        @pl.when(chip - s >= 0)
        def _():
            arrived(chip - s, False)
            project(chip - s, False)

        @pl.when((s > 0) & (chip + s < chips))
        def _():
            arrived(chip + s, False)
            project(chip + s, False)

        return carry

    lax.fori_loop(0, chips, step, 0)
    weights_onward()
    for copy in results(c):
        copy.wait()
    own_proj.wait()
    for cut in cuts[-2:]:
        cut.wait()

    for s in range(chips):
        if s < chips - 1:

            @pl.when((chip - s >= 0) & (chip < chips - 1))
            def _():
                hop(s, True, False).wait_send()

            @pl.when((chip + s < chips) & (chip > 0))
            def _():
                hop(s, False, False).wait_send()

        twin(s, False).wait_send()
    for k in range(1, n_fsdp):
        w_copy(k).wait_send()
        s_copy(k).wait_send()
    weights_done()


def start_call(n_ctx, n_fsdp, base, tok, w_slots, small, w_proj, w_fc, cid):
    count, width = tok.shape
    slots, shard, cols = w_slots.shape
    hidden = w_fc.shape[1] // n_fsdp
    vm = pl.BlockSpec(memory_space=pltpu.VMEM)
    anym = pl.BlockSpec(memory_space=pl.ANY)
    dma = pltpu.SemaphoreType.DMA
    return pl.pallas_call(
        functools.partial(start_kernel, n_ctx, n_fsdp, base),
        in_specs=[anym, anym, vm, anym, anym],
        out_specs=[anym, anym, anym, anym, vm, vm],
        out_shape=[
            jax.ShapeDtypeStruct((n_ctx, count, width), BF16),
            jax.ShapeDtypeStruct((slots, n_ctx, count, cols), BF16),
            jax.ShapeDtypeStruct((n_fsdp,) + w_proj.shape, BF16),
            jax.ShapeDtypeStruct((n_fsdp, shard, hidden), BF16),
            jax.ShapeDtypeStruct((slots, width, cols), BF16),
            jax.ShapeDtypeStruct((small.shape[0], width), F32),
        ],
        scratch_shapes=[
            pltpu.VMEM((count, width), BF16),
            pltpu.VMEM((slots, count, cols), BF16),
            pltpu.VMEM(w_fc.shape, BF16),
            pltpu.VMEM((2, shard, hidden), BF16),
            pltpu.VMEM((n_ctx, count, width), BF16),
            pltpu.VMEM((n_fsdp, slots, shard, cols), BF16),
            pltpu.VMEM((n_fsdp,) + small.shape, F32),
            dma((n_ctx,)),
            dma((n_ctx // 2,)),
            dma((n_ctx // 2,)),
            dma((n_ctx // 2,)),
            dma((n_fsdp,)),
            dma((n_fsdp,)),
            dma((n_fsdp,)),
            dma((n_fsdp,)),
            dma((2, n_fsdp)),
            dma((2, n_fsdp)),
            dma((6,)),
        ],
        compiler_params=pltpu.CompilerParams(
            collective_id=cid, has_side_effects=True, vmem_limit_bytes=VMEM_LIMIT
        ),
        cost_estimate=SHORT,
        name="tokens_qkv",
    )(tok, w_slots, small, w_proj, w_fc)


def causal_scores(k, q_rows, start):
    scores = dot_last(k, q_rows)
    keep = start
    tail = scores[keep:]
    key_id = lax.broadcasted_iota(jnp.int32, tail.shape, 0)
    query_id = lax.broadcasted_iota(jnp.int32, tail.shape, 1)
    tail = jnp.where(key_id <= query_id, tail, -1e30)
    if keep == 0:
        return tail
    return jnp.concatenate([scores[:keep], tail], axis=0)


def soft(scores, v_t):
    top = jnp.max(scores, axis=0, keepdims=True)
    weights = jnp.exp(scores - top)
    total = jnp.sum(weights, axis=0, keepdims=True)
    out = dot(v_t, weights.astype(BF16)) / total
    return out, top + jnp.log(total)


def causal(inv_ref, x_ref):
    return jnp.concatenate([x_ref[0, inv_ref[i]] for i in range(x_ref.shape[1])], axis=0)


def attn_fwd_kernel(inv_ref, x_ref, o_ref, l_ref):
    rows = l_ref.shape[2]
    hd = HEAD_DIM
    x = causal(inv_ref, x_ref)
    q = x[:, :hd] * BF16(SCALE)
    k = x[:, hd : 2 * hd]
    v_t = x[:, 2 * hd :].T
    for i in range(rows // QROWS):
        lo, hi = i * QROWS, (i + 1) * QROWS
        out, lse = soft(causal_scores(k[:hi], q[lo:hi], lo), v_t[:, :hi])
        l_ref[0, :, lo:hi] = lse
        out = out.astype(BF16)
        for b in range(QROWS // BLOCK):
            o_ref[inv_ref[2 * i + b]] = out[:, b * BLOCK : (b + 1) * BLOCK]


def attn_fwd(inv, qkv, heads):
    blocks, _, cols = qkv.shape[1:]
    rows = blocks * BLOCK
    return pl.pallas_call(
        attn_fwd_kernel,
        grid_spec=pltpu.PrefetchScalarGridSpec(
            num_scalar_prefetch=1,
            grid=(heads,),
            in_specs=[pl.BlockSpec((1, blocks, BLOCK, cols), lambda h, inv: (h, 0, 0, 0))],
            out_specs=[
                pl.BlockSpec((blocks, HEAD_DIM, BLOCK), lambda h, inv: (0, h, 0)),
                pl.BlockSpec((1, 1, rows), lambda h, inv: (h, 0, 0)),
            ],
        ),
        out_shape=[
            jax.ShapeDtypeStruct((blocks, heads * HEAD_DIM, BLOCK), BF16),
            jax.ShapeDtypeStruct((heads, 1, rows), F32),
        ],
        compiler_params=pltpu.CompilerParams(vmem_limit_bytes=VMEM_LIMIT),
        cost_estimate=SHORT,
        name="attn_fwd",
    )(inv, qkv)


def attn_bwd_kernel(inv_ref, x_ref, do_ref, o_ref, l_ref, dx_ref, dk_acc, dv_acc):
    rows = l_ref.shape[2]
    hd = HEAD_DIM
    x = causal(inv_ref, x_ref)
    q = x[:, :hd] * BF16(SCALE)
    k = x[:, hd : 2 * hd]
    v = x[:, 2 * hd :]
    k_t = k.T
    dk_acc[...] = jnp.zeros_like(dk_acc)
    dv_acc[...] = jnp.zeros_like(dv_acc)
    for i in range(rows // QROWS):
        lo, hi = i * QROWS, (i + 1) * QROWS
        ids = [inv_ref[2 * i + b] for b in range(QROWS // BLOCK)]
        do_t = jnp.concatenate([do_ref[b] for b in ids], axis=1)
        o_t = jnp.concatenate([o_ref[b] for b in ids], axis=1)
        inner = jnp.sum(do_t.astype(F32) * o_t.astype(F32), axis=0, keepdims=True)
        probs = jnp.exp(causal_scores(k[:hi], q[lo:hi], lo) - l_ref[0, :, lo:hi])
        dprobs = dot(v[:hi], do_t)
        dscores = (probs * (dprobs - inner)).astype(BF16)
        dv_acc[:hi] += dot_last(probs.astype(BF16), do_t)
        dk_acc[:hi] += dot(dscores, q[lo:hi])
        dq = (dot(k_t[:, :hi], dscores) * SCALE).T
        for n, b in enumerate(ids):
            dx_ref[0, b, :, :hd] = dq[n * BLOCK : (n + 1) * BLOCK].astype(BF16)
    for i in range(rows // BLOCK):
        lo, hi = i * BLOCK, (i + 1) * BLOCK
        dx_ref[0, inv_ref[i], :, hd : 2 * hd] = dk_acc[lo:hi].astype(BF16)
        dx_ref[0, inv_ref[i], :, 2 * hd :] = dv_acc[lo:hi].astype(BF16)


def attn_bwd(inv, qkv, d_out, out, lse, heads):
    blocks, _, cols = qkv.shape[1:]
    rows = blocks * BLOCK
    whole = pl.BlockSpec((1, blocks, BLOCK, cols), lambda h, inv: (h, 0, 0, 0))
    feat = pl.BlockSpec((blocks, HEAD_DIM, BLOCK), lambda h, inv: (0, h, 0))
    return pl.pallas_call(
        attn_bwd_kernel,
        grid_spec=pltpu.PrefetchScalarGridSpec(
            num_scalar_prefetch=1,
            grid=(heads,),
            in_specs=[
                whole,
                feat,
                feat,
                pl.BlockSpec((1, 1, rows), lambda h, inv: (h, 0, 0)),
            ],
            out_specs=whole,
            scratch_shapes=[pltpu.VMEM((rows, HEAD_DIM), F32)] * 2,
        ),
        out_shape=jax.ShapeDtypeStruct((heads, blocks, BLOCK, cols), BF16),
        compiler_params=pltpu.CompilerParams(vmem_limit_bytes=VMEM_LIMIT),
        cost_estimate=pl.CostEstimate(
            flops=24 * 10**9, bytes_accessed=24 * 10**6, transcendentals=0
        ),
        name="attn_bwd",
    )(inv, qkv, d_out, out, lse)


def own_scores(order_ref, x_ref, k):
    hd = HEAD_DIM
    blocks = x_ref.shape[1]
    first = order_ref[blocks]
    q = jnp.concatenate([x_ref[0, first], x_ref[0, first + 1]], axis=0)[:, :hd]
    q = q * BF16(SCALE)
    scores = dot_last(k, q)
    row = lax.broadcasted_iota(jnp.int32, (BLOCK, 1), 0)
    key_place = jnp.concatenate([order_ref[b] * BLOCK + row for b in range(blocks)], axis=0)
    lane = lax.broadcasted_iota(jnp.int32, (1, 2 * BLOCK), 1)
    low, high = order_ref[order_ref[blocks]], order_ref[order_ref[blocks] + 1]
    place = jnp.where(lane < BLOCK, low * BLOCK + lane, (high - 1) * BLOCK + lane)
    return q, first, jnp.where(key_place <= place, scores, -1e30)


def rest_fwd_kernel(order_ref, x_ref, o_ref, l_ref):
    hd = HEAD_DIM
    x = x_ref[0].reshape(-1, 3 * hd)
    _, _, scores = own_scores(order_ref, x_ref, x[:, hd : 2 * hd])
    out, lse = soft(scores, x[:, 2 * hd :].T)
    o_ref[0] = out.astype(BF16)
    l_ref[0] = lse


def rest_fwd(order, qkv, base):
    slots, blocks, _, cols = qkv.shape
    rest = slots - base
    return pl.pallas_call(
        rest_fwd_kernel,
        grid_spec=pltpu.PrefetchScalarGridSpec(
            num_scalar_prefetch=1,
            grid=(rest,),
            in_specs=[
                pl.BlockSpec((1, blocks, BLOCK, cols), lambda h, o: (base + h, 0, 0, 0))
            ],
            out_specs=[
                pl.BlockSpec((1, HEAD_DIM, QROWS), lambda h, o: (h, 0, 0)),
                pl.BlockSpec((1, 1, QROWS), lambda h, o: (h, 0, 0)),
            ],
        ),
        out_shape=[
            jax.ShapeDtypeStruct((rest, HEAD_DIM, QROWS), BF16),
            jax.ShapeDtypeStruct((rest, 1, QROWS), F32),
        ],
        compiler_params=pltpu.CompilerParams(vmem_limit_bytes=VMEM_LIMIT),
        cost_estimate=SHORT,
        name="rest_fwd",
    )(order, qkv)


def rest_bwd_kernel(order_ref, x_ref, do_ref, o_ref, l_ref, dx_ref):
    hd = HEAD_DIM
    x = x_ref[0].reshape(-1, 3 * hd)
    blocks = x_ref.shape[1]
    k = x[:, hd : 2 * hd]
    q, first, scores = own_scores(order_ref, x_ref, k)
    do_t = do_ref[0]
    inner = jnp.sum(do_t.astype(F32) * o_ref[0].astype(F32), axis=0, keepdims=True)
    probs = jnp.exp(scores - l_ref[0])
    dprobs = dot(x[:, 2 * hd :], do_t)
    dscores = (probs * (dprobs - inner)).astype(BF16)
    dv = dot_last(probs.astype(BF16), do_t).astype(BF16)
    dk = dot(dscores, q).astype(BF16)
    dq = (dot(k.T, dscores) * SCALE).T.astype(BF16)
    dx_ref[0, :, :, 2 * hd :] = dv.reshape(blocks, BLOCK, hd)
    dx_ref[0, :, :, hd : 2 * hd] = dk.reshape(blocks, BLOCK, hd)
    dx_ref[0, :, :, :hd] = jnp.zeros((blocks, BLOCK, hd), BF16)
    for b in range(2):
        dx_ref[0, first + b, :, :hd] = dq[b * BLOCK : (b + 1) * BLOCK]


def rest_bwd(order, qkv, d_out, out, lse, base):
    slots, blocks, _, cols = qkv.shape
    rest = slots - base
    feat = pl.BlockSpec((1, HEAD_DIM, QROWS), lambda h, o: (h, 0, 0))
    return pl.pallas_call(
        rest_bwd_kernel,
        grid_spec=pltpu.PrefetchScalarGridSpec(
            num_scalar_prefetch=1,
            grid=(rest,),
            in_specs=[
                pl.BlockSpec((1, blocks, BLOCK, cols), lambda h, o: (base + h, 0, 0, 0)),
                feat,
                feat,
                pl.BlockSpec((1, 1, QROWS), lambda h, o: (h, 0, 0)),
            ],
            out_specs=pl.BlockSpec((1, blocks, BLOCK, cols), lambda h, o: (h, 0, 0, 0)),
        ),
        out_shape=jax.ShapeDtypeStruct((rest, blocks, BLOCK, cols), BF16),
        compiler_params=pltpu.CompilerParams(vmem_limit_bytes=VMEM_LIMIT),
        cost_estimate=SHORT,
        name="rest_bwd",
    )(order, qkv, d_out, out, lse)


def mix_kernel(
    n_ctx,
    n_fsdp,
    out_hbm,
    rest_ref,
    tok_ref,
    proj_ref,
    lines_ref,
    fc_parts,
    att_ref,
    mid_ref,
    n_ref,
    fc_all,
    got_ref,
    out_send,
    out_recv,
    fc_send,
    fc_recv,
    local,
):
    c = lax.axis_index("ctx")
    f = lax.axis_index("fsdp")
    core = c % 2
    width = tok_ref.shape[1]
    shard = width // n_fsdp
    blocks, feats = got_ref.shape[1], got_ref.shape[2]
    enter(
        [(lax.rem(c + i, n_ctx), f) for i in range(1, n_ctx)]
        + [(c, flip(f, k, n_fsdp)) for k in range(1, n_fsdp)]
    )

    def out_copy(i):
        to = lax.rem(c + i, n_ctx)
        return send(
            out_hbm.at[pl.ds(to * blocks, blocks)],
            got_ref.at[c],
            out_send.at[i],
            out_recv.at[i],
            (to, f),
        )

    for i in range(n_ctx - 1, 0, -1):
        out_copy(i).start()
    weights_start, weights_onward, weights_done = weight_shares(
        c,
        f,
        core,
        n_fsdp,
        shard,
        lambda k: fc_parts.at[flip(f, k, n_fsdp)],
        fc_all,
        fc_send,
        fc_recv,
    )
    weights_start()
    own = pltpu.make_async_copy(
        out_hbm.at[pl.ds(c * blocks, blocks)], got_ref.at[c], local.at[0]
    )
    own_fc = pltpu.make_async_copy(fc_parts.at[f], fc_all.at[f], local.at[1])
    own.start()
    own_fc.start()
    main = n_ctx * feats
    if main < width:
        att_ref[:, main:] = rest_ref[...].reshape(width - main, -1).T
    own.wait()
    for i in range(1, n_ctx):
        out_copy(i).wait_recv()
    for src in range(n_ctx):
        block = jnp.concatenate([got_ref[src, b] for b in range(blocks)], axis=1)
        att_ref[:, src * feats : (src + 1) * feats] = block.T
    mid = tok_ref[...].astype(F32) + (dot(att_ref[...], proj_ref[...]) + lines_ref[6:7])
    mid_ref[...] = mid
    cen = mid - jnp.mean(mid, axis=1, keepdims=True)
    var = jnp.mean(cen * cen, axis=1, keepdims=True)
    n_ref[...] = (cen * lax.rsqrt(var + EPS) * lines_ref[1:2] + lines_ref[3:4]).astype(BF16)
    weights_onward()
    own_fc.wait()
    for i in range(1, n_ctx):
        out_copy(i).wait_send()
    weights_done()


def mix_call(n_ctx, n_fsdp, out_own, out_rest, tok, proj, lines, fc_parts, cid):
    count, width = tok.shape
    vm = pl.BlockSpec(memory_space=pltpu.VMEM)
    anym = pl.BlockSpec(memory_space=pl.ANY)
    dma = pltpu.SemaphoreType.DMA
    return pl.pallas_call(
        functools.partial(mix_kernel, n_ctx, n_fsdp),
        in_specs=[anym, vm, vm, vm, vm, anym],
        out_specs=[vm, vm, vm, anym],
        out_shape=[
            jax.ShapeDtypeStruct((count, width), BF16),
            jax.ShapeDtypeStruct((count, width), F32),
            jax.ShapeDtypeStruct((count, width), BF16),
            jax.ShapeDtypeStruct(fc_parts.shape, BF16),
        ],
        scratch_shapes=[
            pltpu.VMEM((n_ctx, out_own.shape[0] // n_ctx) + out_own.shape[1:], BF16),
            dma((n_ctx,)),
            dma((n_ctx,)),
            dma((2, n_fsdp)),
            dma((2, n_fsdp)),
            dma((2,)),
        ],
        compiler_params=pltpu.CompilerParams(
            collective_id=cid, has_side_effects=True, vmem_limit_bytes=VMEM_LIMIT
        ),
        cost_estimate=SHORT,
        name="mix_rows",
    )(out_own, out_rest, tok, proj, lines, fc_parts)


def far_first(i, chips):
    return (i % 2) * (i // 2) + (1 - i % 2) * (chips - 1 - i // 2)


def line_sum(chip, chips, f, core, part, came, sems, ready=None):
    sent, left_sem, right_sem = sems

    def to_right(d):
        return send(
            part.at[d], came.at[d], sent.at[d], left_sem.at[d], (2 * (chip + 1) + core, f)
        )

    def to_left(d):
        place = jnp.where(d == chip - 1, chips, d)
        return send(
            part.at[d], came.at[place], sent.at[d], right_sem.at[d], (2 * (chip - 1) + core, f)
        )

    def from_left(d):
        send(part.at[d], came.at[d], sent.at[d], left_sem.at[d], (2 * chip + core, f)).wait_recv()
        add(d, d)

    def from_right(d, place):
        send(
            part.at[d], came.at[place], sent.at[d], right_sem.at[d], (2 * chip + core, f)
        ).wait_recv()
        add(d, place)

    def add(d, place):
        part[d] = (part[d].astype(F32) + came[place].astype(F32)).astype(BF16)

    def step(t):
        far = chips - 1 - t + chip
        near = t - (chips - 1 - chip)

        @pl.when(chip <= t)
        def _():
            if ready is not None:
                ready(far)

            @pl.when(chip > 0)
            def _():
                from_left(far)

            to_right(far).start()

        @pl.when(near >= 0)
        def _():
            if ready is not None:
                ready(near)

            @pl.when(chip < chips - 1)
            def _():
                from_right(near, near)

            to_left(near).start()

    def finish():
        if ready is not None:
            ready(chip)

        @pl.when(chip > 0)
        def _():
            from_left(chip)

        @pl.when(chip < chips - 1)
        def _():
            from_right(chip, chips)

    def done():
        for d in range(chips):

            @pl.when(chip < d)
            def _(d=d):
                to_right(d).wait_send()

            @pl.when(chip > d)
            def _(d=d):
                to_left(d).wait_send()

    return step, finish, done


def line_gather(chip, chips, f, core, view, sems):
    right, left, twin_sent, got, twin_got = sems
    twin_id = (2 * chip + 1 - core, f)

    def hop(s, rightward):
        origin = chip - s if rightward else chip + s
        ref = view(origin, core)
        peer = (2 * (chip + 1 if rightward else chip - 1) + core, f)
        return send(ref, ref, (right if rightward else left).at[s], got.at[origin], peer)

    def twin(origin):
        ref = view(origin, core)
        return send(ref, ref, twin_sent.at[origin], twin_got.at[origin], twin_id)

    def arrived(origin):
        ref = view(origin, core)
        send(ref, ref, right.at[0], got.at[origin], twin_id).wait_recv()

    def step(s):
        @pl.when(chip - s >= 0)
        def _():
            if s:
                arrived(chip - s)

            @pl.when(chip < chips - 1)
            def _():
                hop(s, True).start()

            twin(chip - s).start()

        @pl.when(chip + s < chips)
        def _():
            if s:
                arrived(chip + s)

            @pl.when(chip > 0)
            def _():
                hop(s, False).start()

            if s:
                twin(chip + s).start()

    def done():
        for s in range(chips):
            if s < chips - 1:

                @pl.when((chip - s >= 0) & (chip < chips - 1))
                def _(s=s):
                    hop(s, True).wait_send()

                @pl.when((chip + s < chips) & (chip > 0))
                def _(s=s):
                    hop(s, False).wait_send()

            twin(s).wait_send()
            ref = view(s, 1 - core)
            send(ref, ref, twin_sent.at[s], twin_got.at[s], twin_id).wait_recv()

    return step, done


def back_kernel(
    n_ctx,
    n_fsdp,
    own_ref,
    rest_ref,
    w_ref,
    n_ref,
    one_ref,
    cols_ref,
    part,
    twin_out,
    twin_in,
    came,
    mine,
    theirs,
    twin_send,
    twin_recv,
    line_send,
    left_recv,
    right_recv,
    cols_send,
    cols_recv,
):
    c = lax.axis_index("ctx")
    f = lax.axis_index("fsdp")
    chips = n_ctx // 2
    chip, core = c // 2, c % 2
    slots, width, cols = w_ref.shape
    count = own_ref.shape[2]
    base = own_ref.shape[0]
    shard = width // n_fsdp
    twin_id = (2 * chip + 1 - core, f)
    enter(
        [(lax.rem(c + i, n_ctx), f) for i in range(1, n_ctx)]
        + [(c, flip(f, k, n_fsdp)) for k in range(1, n_fsdp)]
    )

    def grad(s):
        return own_ref.at[s] if s < base else rest_ref.at[s - base]

    def for_block(b):
        total = dot_last(grad(0)[b], w_ref[0])
        for s in range(1, slots):
            total += dot_last(grad(s)[b], w_ref[s])
        return total.astype(BF16)

    def to_twin(d, slot):
        return send(twin_out.at[slot], twin_in.at[d], twin_send.at[slot], twin_recv.at[d], twin_id)

    def products(i, carry):
        d = far_first(i, chips)
        slot = i % 2
        product = for_block(2 * d + 1 - core)

        @pl.when(i > 1)
        def _():
            to_twin(d, slot).wait_send()

        twin_out[slot] = product
        to_twin(d, slot).start()
        part[d] = for_block(2 * d + core)
        return carry

    def ready(d):
        to_twin(d, 0).wait_recv()
        part[d] = (part[d].astype(F32) + twin_in[d].astype(F32)).astype(BF16)

    step, finish, done = line_sum(
        chip, chips, f, core, part, came, (line_send, left_recv, right_recv), ready
    )

    def cols_copy(src, dst, at):
        return send(mine.at[src], theirs.at[at], cols_send.at[src], cols_recv.at[at], (c, dst))

    def columns(j):
        left = n_ref[:, :, j * shard : (j + 1) * shard].reshape(n_ctx * count, shard)
        for s in range(slots):
            right = grad(s)[...].reshape(n_ctx * count, cols)
            mine[j, s] = dot_first(left, right).astype(BF16)

    lax.fori_loop(0, 2, products, 0)
    step(0)
    for j in range(n_fsdp):
        columns(j)
    for k in range(1, n_fsdp):
        other = flip(f, k, n_fsdp)
        cols_copy(other, other, f).start()
    lax.fori_loop(2, chips, products, 0)
    if chips > 2:
        step(1)
    for t in range(2, chips - 1):
        step(t)
    total = mine[f].astype(F32)
    for k in range(1, n_fsdp):
        other = flip(f, k, n_fsdp)
        cols_copy(other, other, other).wait_recv()
        total += theirs[other].astype(F32)
    cols_ref[...] = total.astype(BF16)
    finish()
    one_ref[...] = part[chip]
    done()
    for slot in range(2):
        to_twin(0, slot).wait_send()
    for k in range(1, n_fsdp):
        other = flip(f, k, n_fsdp)
        cols_copy(other, other, other).wait_send()


def back_fits(n_ctx, n_fsdp, count, width, slots):
    blocks = (5 * (n_ctx // 2) + n_ctx) * count * width
    heads = slots * 256 * (n_ctx * count + 3 * width)
    return 2 * (blocks + heads) < 50 * 1024 * 1024


def back_call(n_ctx, n_fsdp, own, rest, w_slots, normed, cid):
    slots, width, cols = w_slots.shape
    count = normed.shape[1]
    chips = n_ctx // 2
    shard = width // n_fsdp
    vm = pl.BlockSpec(memory_space=pltpu.VMEM)
    dma = pltpu.SemaphoreType.DMA
    block = pltpu.VMEM((chips, count, width), BF16)
    piece = pltpu.VMEM((n_fsdp, slots, shard, cols), BF16)
    return pl.pallas_call(
        functools.partial(back_kernel, n_ctx, n_fsdp),
        in_specs=[vm] * 4,
        out_specs=[vm] * 2,
        out_shape=[
            jax.ShapeDtypeStruct((count, width), BF16),
            jax.ShapeDtypeStruct((slots, shard, cols), BF16),
        ],
        scratch_shapes=[
            block,
            pltpu.VMEM((2, count, width), BF16),
            block,
            pltpu.VMEM((chips + 1, count, width), BF16),
        ]
        + [piece] * 2
        + [dma((2,))]
        + [dma((chips,))] * 4
        + [dma((n_fsdp,))] * 2,
        compiler_params=pltpu.CompilerParams(
            collective_id=cid, has_side_effects=True, vmem_limit_bytes=60 * 1024 * 1024
        ),
        cost_estimate=SHORT,
        name="qkv_back",
    )(own, rest, w_slots, normed)


def sums_kernel(n_ctx, n_fsdp, lead, *refs):
    rows_ref, cols_ref, att_ref, mid_ref, lines_in = refs[:5]
    outs, cols_all, lines_ref = refs[5:7], refs[7], refs[8]
    parts, cames = refs[9:11], refs[11:13]
    proj_part, proj_in, proj_got, lines_got = refs[13:17]
    lines_send, lines_recv, local, proj_send, proj_recv, pair_sem = refs[17:23]
    cols_sems = refs[23:28]
    sems = [(refs[28 + 8 * i : 31 + 8 * i], refs[31 + 8 * i : 36 + 8 * i]) for i in range(2)]
    c = lax.axis_index("ctx")
    f = lax.axis_index("fsdp")
    chips = n_ctx // 2
    chip, core = c // 2, c % 2
    width = att_ref.shape[1]
    shard = width // n_fsdp
    half = shard // 2
    high = proj_in.shape[1]
    twin_id = (2 * chip + 1 - core, f)
    enter(
        [(lax.rem(c + i, n_ctx), f) for i in range(1, n_ctx)]
        + [(c, flip(f, k, n_fsdp)) for k in range(1, n_fsdp)]
    )

    def line_ops(i):
        sum_sems, gather_sems = sems[i]
        gather = line_gather(chip, chips, f, core, lambda at, h: outs[i].at[h, at], gather_sems)
        return line_sum(chip, chips, f, core, parts[i], cames[i], sum_sems) + gather

    def proj_pair():
        return send(proj_part.at[1 - core], proj_in, pair_sem.at[0], pair_sem.at[1], twin_id)

    def proj_copy(k):
        other = flip(f, k, n_fsdp)
        return send(
            proj_part.at[core, other],
            proj_got.at[f],
            proj_send.at[k],
            proj_recv.at[k],
            (c, other),
        )

    def proj_products(j):
        for h in range(2):
            lo = j * shard + h * half
            proj_part[h, j, :half] = dot_first(att_ref[:, lo : lo + half], mid_ref[...]).astype(BF16)
            if half < high:
                proj_part[h, j, half:] = jnp.zeros((high - half, width), BF16)

    def proj_add(j, carry):
        proj_part[core, j] = (
            proj_part[core, j].astype(F32) + proj_in[j].astype(F32)
        ).astype(BF16)
        return carry

    def proj_total():
        total = proj_part[core, f].astype(F32)
        for k in range(1, n_fsdp):
            proj_copy(k).wait_recv()
            total += proj_got[flip(f, k, n_fsdp)].astype(F32)
        total = total.astype(BF16)
        step = parts[1].shape[1]
        for p in range(chips):
            lo, hi = min(p * step, high), min((p + 1) * step, high)
            if hi > lo:
                parts[1][p, : hi - lo] = total[lo:hi]
            if hi - lo < step:
                parts[1][p, hi - lo :] = jnp.zeros((step - hi + lo, width), BF16)

    peers = [(flip(c, 1 << i, n_ctx), f) for i in range(n_ctx.bit_length() - 1)]
    ctx_phases = len(peers)
    peers += [(c, flip(f, 1 << i, n_fsdp)) for i in range(n_fsdp.bit_length() - 1)]

    def line_copy(i):
        rows = lines_in.shape[0] if i < ctx_phases else lead
        return send(
            lines_ref.at[:rows],
            lines_got.at[i, :rows],
            lines_send.at[i],
            lines_recv.at[i],
            peers[i],
        )

    def line_phase(i):
        if 0 < i <= len(peers):
            rows = lines_in.shape[0] if i <= ctx_phases else lead
            line_copy(i - 1).wait()
            lines_ref[:rows] += lines_got[i - 1, :rows]
        if i < len(peers):
            line_copy(i).start()

    def settle(finish, i):
        finish()
        keep = pltpu.make_async_copy(parts[i].at[chip], outs[i].at[core, chip], local.at[0])
        keep.start()
        keep.wait()

    sum_a, finish_a, sums_a, gather_a, gathers_a = line_ops(0)
    sum_b, finish_b, sums_b, gather_b, gathers_b = line_ops(1)
    cols_step, cols_done = line_gather(
        chip, chips, f, core, lambda at, h: cols_all.at[2 * at + h], cols_sems
    )
    load = pltpu.make_async_copy(cols_ref, cols_all.at[c], local.at[1])
    load.start()
    parts[0][...] = rows_ref[...]
    sum_a(0)
    load.wait()
    cols_step(0)
    lines_ref[...] = lines_in[...]
    for j in range(n_fsdp):
        proj_products(j)
    proj_pair().start()
    for t in range(1, chips - 1):
        sum_a(t)
        cols_step(t)
        if t == 1:
            proj_pair().wait()
            lax.fori_loop(0, n_fsdp, proj_add, 0)
            for k in range(1, n_fsdp):
                proj_copy(k).start()
    settle(finish_a, 0)
    gather_a(0)
    cols_step(chips - 1)
    proj_total()
    phase = 0
    for s in range(1, chips):
        sum_b(s - 1)
        gather_a(s)
        line_phase(phase)
        phase += 1
    settle(finish_b, 1)
    for s in range(chips):
        gather_b(s)
        line_phase(phase)
        phase += 1
    while phase <= len(peers):
        line_phase(phase)
        phase += 1
    for done in (sums_a, sums_b, cols_done, gathers_a, gathers_b):
        done()
    for k in range(1, n_fsdp):
        proj_copy(k).wait_send()


def sums_call(n_ctx, n_fsdp, rows, cols, attended, mid_low, lines, lead, cid):
    chips = n_ctx // 2
    count, width = attended.shape
    high = -(-(width // n_fsdp // 2) // 16) * 16
    shapes = [rows.shape, (chips, -(-high // (16 * chips)) * 16, width)]
    phases = (n_ctx * n_fsdp).bit_length() - 1
    vm = pl.BlockSpec(memory_space=pltpu.VMEM)
    anym = pl.BlockSpec(memory_space=pl.ANY)
    dma = pltpu.SemaphoreType.DMA
    return pl.pallas_call(
        functools.partial(sums_kernel, n_ctx, n_fsdp, lead),
        in_specs=[vm, anym, vm, vm, vm],
        out_specs=[vm, vm, anym, vm],
        out_shape=[jax.ShapeDtypeStruct((2,) + shape, BF16) for shape in shapes]
        + [jax.ShapeDtypeStruct((n_ctx,) + cols.shape, BF16)]
        + [jax.ShapeDtypeStruct(lines.shape, F32)],
        scratch_shapes=[pltpu.VMEM(shape, BF16) for shape in shapes]
        + [pltpu.VMEM((chips + 1,) + shape[1:], BF16) for shape in shapes]
        + [
            pltpu.VMEM((2, n_fsdp, high, width), BF16),
            pltpu.VMEM((n_fsdp, high, width), BF16),
            pltpu.VMEM((n_fsdp, high, width), BF16),
            pltpu.VMEM((phases,) + lines.shape, F32),
            dma((phases,)),
            dma((phases,)),
            dma((2,)),
            dma((n_fsdp,)),
            dma((n_fsdp,)),
            dma((2,)),
        ]
        + [dma((chips,))] * (5 + 2 * 8),
        compiler_params=pltpu.CompilerParams(
            collective_id=cid, has_side_effects=True, vmem_limit_bytes=56 * 1024 * 1024
        ),
        cost_estimate=SHORT,
        name="weight_sums",
    )(rows, cols, attended, mid_low, lines)


def assemble_kernel(
    n_fsdp,
    own_ref,
    rest_ref,
    rows_ref,
    third_ref,
    out_ref,
    attn_hbm,
    fc_hbm,
    proj_hbm,
    wout_hbm,
    *scratch,
):
    attn_ref, fc_ref, proj_ref, wout_ref, low_ref, sem = scratch
    load = pltpu.make_async_copy(out_ref, low_ref, sem.at[4])
    load.start()
    hd = HEAD_DIM
    shard, hidden = fc_ref.shape[0], fc_ref.shape[1] // n_fsdp
    half = shard // 2
    width = proj_ref.shape[1]
    count = own_ref.shape[0]
    copies = [
        pltpu.make_async_copy(src, dst, sem.at[i])
        for i, (src, dst) in enumerate(
            ((wout_ref, wout_hbm), (fc_ref, fc_hbm), (proj_ref, proj_hbm), (attn_ref, attn_hbm))
        )
    ]
    for h in range(2):
        for j in range(n_fsdp):
            lo, hi = j * half, (j + 1) * half
            fc_ref[h * half : (h + 1) * half, j * hidden : (j + 1) * hidden] = rows_ref[
                h, lo:hi
            ].astype(F32)
    copies[1].start()
    for h in range(2):
        proj_ref[h * half : (h + 1) * half] = third_ref[h, :half].astype(F32)
    copies[2].start()
    for h in range(width // hd):
        src = own_ref.at[h] if h < count else rest_ref.at[h - count]
        for part in range(3):
            at = part * width + h * hd
            attn_ref[:, at : at + hd] = src[:, part * hd : (part + 1) * hd].astype(F32)
    copies[3].start()
    load.wait()
    wout_ref[...] = low_ref[...].astype(F32)
    copies[0].start()
    for copy in copies:
        copy.wait()


def assemble(n_fsdp, own, rest, rows, third, out_low, hidden):
    shard = own.shape[1]
    width = rows.shape[2]
    vm = pl.BlockSpec(memory_space=pltpu.VMEM)
    anym = pl.BlockSpec(memory_space=pl.ANY)
    shapes = [(shard, 3 * width), (shard, n_fsdp * hidden), (shard, width), out_low.shape]
    return pl.pallas_call(
        functools.partial(assemble_kernel, n_fsdp),
        in_specs=[vm] * 4 + [anym],
        out_specs=[anym] * 4,
        out_shape=[jax.ShapeDtypeStruct(shape, F32) for shape in shapes],
        scratch_shapes=[pltpu.VMEM(shape, F32) for shape in shapes]
        + [pltpu.VMEM(out_low.shape, BF16), pltpu.SemaphoreType.DMA((5,))],
        compiler_params=pltpu.CompilerParams(vmem_limit_bytes=60 * 1024 * 1024),
        cost_estimate=SHORT,
        name="assemble",
    )(own, rest, rows, third, out_low)


def norm_parts(rows):
    mean = jnp.mean(rows, axis=-1, keepdims=True)
    cen = rows - mean
    rstd = lax.rsqrt(jnp.mean(cen * cen, axis=-1, keepdims=True) + EPS)
    return cen * rstd, rstd


def norm_back(xhat, rstd, gain, grad):
    dxhat = grad * gain
    return rstd * (
        dxhat
        - jnp.mean(dxhat, axis=-1, keepdims=True)
        - xhat * jnp.mean(dxhat * xhat, axis=-1, keepdims=True)
    )


def swap(value, axis, size, k):
    return lax.ppermute(value, axis, [(i, i ^ k) for i in range(size)])


def shards(
    n_ctx,
    n_fsdp,
    tokens,
    block_order,
    w_attn,
    w_proj,
    w_fc,
    w_out,
    norm_gains,
    biases,
    fc_bias,
    cotangent,
):
    hd = HEAD_DIM
    count, width = tokens.shape[1:]
    shard = width // n_fsdp
    heads = width // hd
    base = heads // n_ctx
    rest = heads - base * n_ctx
    slots = base + rest
    own_blocks = count // BLOCK
    c = lax.axis_index("ctx")
    f = lax.axis_index("fsdp")

    order = block_order[0]
    inv = jnp.argsort(order).astype(jnp.int32)
    order_own = jnp.concatenate([order, (c * own_blocks)[None]])

    def head_cols(h):
        return jnp.concatenate(
            [
                lax.dynamic_slice(w_attn, (0, part * width + h * hd), (shard, hd))
                for part in range(3)
            ],
            axis=1,
        )

    slot_heads = [c * base + s for s in range(base)] + [n_ctx * base + r for r in range(rest)]
    w_slots = jnp.stack([head_cols(h) for h in slot_heads])
    small = jnp.concatenate([norm_gains, biases], axis=0).astype(F32)
    hidden_cols = w_fc.shape[1] // n_fsdp
    normed_one, qkv, full_proj, fc_parts, w_slots, small = start_call(
        n_ctx, n_fsdp, base, tokens[0], w_slots, small, w_proj, w_fc, 3
    )
    full_proj = full_proj.reshape(width, width)
    qkv = qkv.reshape(slots, n_ctx * own_blocks, BLOCK, 3 * hd)
    gains, shifts = small[:2], small[2:]
    cot = cotangent[0]

    cot_late, _ = lax.optimization_barrier((cot, small))
    cot_all = lax.all_gather(cot_late, "fsdp", axis=0)

    out_own, lse_own = attn_fwd(inv, qkv, base)
    if rest:
        out_rest, lse_rest = rest_fwd(order_own, qkv, base)
    else:
        out_rest = out_own
    attended, mid, normed_two, fc_cols = mix_call(
        n_ctx, n_fsdp, out_own, out_rest, tokens[0], full_proj, small, fc_parts, 6
    )
    fc_cols = fc_cols.reshape(width, hidden_cols)
    rows = tokens[0].astype(F32)
    xhat_two, rstd_two = norm_parts(mid)

    normed_two_grad, fc_bias_part, out_part, w_out_part, w_fc_part = ffn(
        n_fsdp,
        normed_two,
        cot_all,
        fc_cols,
        w_out,
        fc_bias.astype(F32)[None],
    )
    out_rows = lax.psum_scatter(
        out_part.reshape(n_fsdp * count, width), "fsdp", scatter_dimension=0, tiled=True
    )
    w_out_low = lax.psum(w_out_part, "ctx")

    cot_rows = cot.astype(F32)
    mid_grad = cot_rows + norm_back(xhat_two, rstd_two, gains[1], normed_two_grad)
    mid_low = mid_grad.astype(BF16)
    attended_grad = dot_last(mid_low, full_proj).astype(BF16)
    half = shard // 2
    core = c % 2

    def core_half(part):
        away = lax.dynamic_slice_in_dim(part, (1 - core) * half, half, 1)
        here = lax.dynamic_slice_in_dim(part, core * half, half, 1)
        return (here.astype(F32) + swap(away, "ctx", n_ctx, 1).astype(F32)).astype(BF16)

    def over_fsdp(part):
        out = []
        for k in range(n_fsdp):
            piece = lax.dynamic_index_in_dim(part, f ^ k, keepdims=False)
            out.append(swap(piece, "fsdp", n_fsdp, k) if k else piece)
        return out

    w_fc_part, _ = lax.optimization_barrier((w_fc_part, attended_grad))
    w_fc_mid = core_half(w_fc_part.reshape(n_fsdp, shard, hidden_cols))

    main = n_ctx * base * hd
    sent = attended_grad[:, :main].reshape(own_blocks, BLOCK, n_ctx, base * hd)
    sent = sent.transpose(2, 0, 3, 1).reshape(n_ctx * own_blocks, base * hd, BLOCK)
    d_out = lax.all_to_all(sent, "ctx", split_axis=0, concat_axis=0, tiled=True)
    d_out, w_fc_mid = lax.optimization_barrier((d_out, w_fc_mid))
    w_fc_half = jnp.zeros((n_fsdp, half, hidden_cols), BF16)
    for k, piece in enumerate(over_fsdp(w_fc_mid)):
        w_fc_half = lax.dynamic_update_slice(w_fc_half, piece[None], (f ^ k, 0, 0))
    d_own = attn_bwd(inv, qkv, d_out, out_own, lse_own, base)
    d_own = d_own.reshape(base, n_ctx, count, 3 * hd)
    if rest:
        d_rest = attended_grad[:, main:].T.reshape(rest, hd, count)
        d_rest = rest_bwd(order_own, qkv, d_rest, out_rest, lse_rest, base)
        d_rest = d_rest.reshape(rest, n_ctx, count, 3 * hd)
        sums = jnp.concatenate(
            [jnp.sum(d.astype(F32), axis=(1, 2)) for d in (d_own, d_rest)], axis=0
        )
    else:
        d_rest = d_own
        sums = jnp.sum(d_own.astype(F32), axis=(1, 2))
    if back_fits(n_ctx, n_fsdp, count, width, slots):
        d_own, w_fc_half = lax.optimization_barrier((d_own, w_fc_half))
        normed_one_grad, cols_sum = back_call(
            n_ctx, n_fsdp, d_own, d_rest, w_slots, normed_one, 4
        )
        normed_one_grad = normed_one_grad.astype(F32)
    else:
        dqkv = jnp.concatenate([d_own, d_rest])[:slots].reshape(slots, n_ctx * count, 3 * hd)
        one_part = jnp.einsum("hte,hde->td", dqkv, w_slots, preferred_element_type=F32)
        normed_one_grad = lax.psum_scatter(
            one_part.astype(BF16), "ctx", scatter_dimension=0, tiled=True
        ).astype(F32)
        slot_part = jnp.einsum(
            "td,hte->hde",
            normed_one.reshape(n_ctx * count, width),
            dqkv,
            preferred_element_type=F32,
        ).astype(BF16)
        cols_sum = lax.psum_scatter(slot_part, "fsdp", scatter_dimension=1, tiled=True)

    xhat_one, rstd_one = norm_parts(rows)
    tokens_grad = (mid_grad + norm_back(xhat_one, rstd_one, gains[0], normed_one_grad)).astype(
        BF16
    )

    def placed(part):
        cols = sums[:, part * hd : (part + 1) * hd]
        line = lax.dynamic_update_slice_in_dim(
            jnp.zeros((width,), F32), cols[:base].reshape(-1), c * base * hd, 0
        )
        return line + jnp.pad(cols[base:].reshape(-1), (main, 0))

    lines = jnp.stack(
        [
            jnp.sum(normed_one_grad * xhat_one, axis=0),
            jnp.sum(normed_two_grad * xhat_two, axis=0),
            jnp.sum(normed_one_grad, axis=0),
            jnp.sum(normed_two_grad, axis=0),
            placed(0),
            placed(2),
            jnp.sum(mid_low.astype(F32), axis=0),
            jnp.sum(cot_rows, axis=0),
        ]
    )
    lead = lines.shape[0]
    tail = jnp.pad(fc_bias_part, ((0, 7), (0, width - hidden_cols)))
    lines = jnp.concatenate([lines, tail])

    chips = n_ctx // 2
    parts = [w_fc_half.reshape(-1, width)]
    if rest:
        parts.append(core_half(cols_sum[base:]).reshape(-1, width))
    bounds = [0]
    for part in parts:
        bounds.append(bounds[-1] + part.shape[0])
    per_chip = -(-bounds[-1] // (16 * chips)) * 16
    rows_all = jnp.concatenate(parts)
    rows_all = jnp.pad(rows_all, ((0, per_chip * chips - bounds[-1]), (0, 0)))
    rows_all = rows_all.reshape(chips, per_chip, width)
    rows_all, third, own_cols, lines = sums_call(
        n_ctx, n_fsdp, rows_all, cols_sum[:base], attended, mid_low, lines, lead, 5
    )
    out_rows, w_out_low, lines = lax.optimization_barrier((out_rows, w_out_low, lines))
    layer_rows = (mid + (out_rows.astype(F32) + shifts[5])).astype(BF16)
    rows_all, third = rows_all.reshape(2, -1, width), third.reshape(2, -1, width)
    own_cols = own_cols.reshape(n_ctx * base, shard, 3 * hd)
    if rest:
        rest_cols = rows_all[:, bounds[1] : bounds[2]].reshape(2, rest, half, 3 * hd)
        rest_cols = rest_cols.transpose(1, 0, 2, 3).reshape(rest, shard, 3 * hd)
    else:
        rest_cols = own_cols
    if hidden_cols == width:
        w_attn_grad, w_fc_grad, w_proj_grad, w_out_grad = assemble(
            n_fsdp, own_cols, rest_cols, rows_all, third, w_out_low, hidden_cols
        )
    else:
        w_fc_low = rows_all[:, : bounds[1]].reshape(2, n_fsdp, half, hidden_cols)
        w_fc_grad = w_fc_low.transpose(0, 2, 1, 3).reshape(shard, n_fsdp * hidden_cols)
        w_fc_grad = w_fc_grad.astype(F32)
        w_proj_grad = third[:, :half].reshape(shard, width).astype(F32)
        cols = jnp.concatenate([own_cols, rest_cols])[: width // hd]
        cols = cols.reshape(width // hd, shard, 3, hd).transpose(1, 2, 0, 3)
        w_attn_grad = cols.reshape(shard, 3 * width).astype(F32)
        w_out_grad = w_out_low.astype(F32)
    fc_bias_grad = lines[lead, :hidden_cols]
    lines = lax.dynamic_slice_in_dim(lines[:lead], f * shard, shard, 1)
    return (
        layer_rows[None],
        tokens_grad[None],
        w_attn_grad,
        w_proj_grad,
        w_fc_grad,
        w_out_grad,
        lines[:2],
        lines[2:],
        fc_bias_grad,
    )


def solution(mesh):
    rows = P("fsdp", "ctx", None)
    weight = P("fsdp", None)
    vectors = P(None, "fsdp")
    return jax.shard_map(
        functools.partial(shards, mesh.shape["ctx"], mesh.shape["fsdp"]),
        mesh=mesh,
        in_specs=(
            rows, weight, weight, weight, weight, weight, vectors, vectors, P("fsdp"), rows,
        ),
        out_specs=(
            rows, rows, weight, weight, weight, weight, vectors, vectors, P("fsdp"),
        ),
        check_vma=False,
    )
```

```python
import functools

import jax
import jax.numpy as jnp
from jax import lax
from jax.experimental import pallas as pl
from jax.experimental.pallas import tpu as pltpu
from jax.sharding import PartitionSpec as P

HEAD_DIM = 64
BLOCK = 128
QROWS = 256
EPS = 1e-05
SCALE = HEAD_DIM ** (-0.5)
F32 = jnp.float32
BF16 = jnp.bfloat16
VMEM_LIMIT = 56 * 1024 * 1024
LAST = (((1,), (1,)), ((), ()))
FIRST = (((0,), (0,)), ((), ()))
MESH = pl.DeviceIdType.MESH
TILE = 256


def dot_last(a, b):
    return lax.dot_general(a, b, LAST, preferred_element_type=F32)


def dot(a, b):
    return jnp.dot(a, b, preferred_element_type=F32)


def dot_first(a, b):
    return lax.dot_general(a, b, FIRST, preferred_element_type=F32)


SHORT = pl.CostEstimate(flops=1, bytes_accessed=1, transcendentals=0)


def norm_parts(rows):
    mean = jnp.mean(rows, axis=-1, keepdims=True)
    cen = rows - mean
    rstd = lax.rsqrt(jnp.mean(cen * cen, axis=-1, keepdims=True) + EPS)
    return cen * rstd, rstd


def norm_back(xhat, rstd, gain, grad):
    dxhat = grad * gain
    return rstd * (
        dxhat
        - jnp.mean(dxhat, axis=-1, keepdims=True)
        - xhat * jnp.mean(dxhat * xhat, axis=-1, keepdims=True)
    )


def flip(place, k, size):
    out = 0
    bit = 1
    while bit < size:
        out = out + (place // bit + k // bit) % 2 * bit
        bit *= 2
    return out

def half_high(shard):
    return -(-(shard // 2) // 16) * 16


def enter(peers):
    barrier = pltpu.get_barrier_semaphore()
    for peer in peers:
        pl.semaphore_signal(barrier, inc=1, device_id=peer, device_id_type=MESH)
    pl.semaphore_wait(barrier, len(peers))

def send(src, dst, send_sem, recv_sem, peer):
    return pltpu.make_async_remote_copy(
        src_ref=src, dst_ref=dst, send_sem=send_sem, recv_sem=recv_sem,
        device_id=peer, device_id_type=MESH)


def ffn_kernel(n, nt_hbm, cot_hbm, wfc_hbm, wout_hbm, bias_ref,
               gsum_ref, fcb_ref, out_hbm, wout_grad_hbm, wfc_grad_hbm,
               cot_ref, wfc_ref, wout_ref, all_ref, act_ref, hg_ref, ag_ref, part_ref, got_ref, stage_d, stage_h,
               s1, r1, s2, r2, local):
    c = lax.axis_index("ctx")
    f = lax.axis_index("fsdp")
    rows, width = nt_hbm.shape
    enter([(c, flip(f, k, n)) for k in range(1, n)])

    def rows_out(k):
        return send(nt_hbm, all_ref.at[f], s1.at[k], r1.at[k], (c, flip(f, k, n)))

    def grad_back(k):
        other = flip(f, k, n)
        return send(part_ref.at[other], got_ref.at[k], s2.at[k], r2.at[k], (c, other))

    near = [k for k in range(1, n) if k & (k - 1) == 0]
    far = [k for k in range(1, n) if k not in near]
    for k in near:
        rows_out(k).start()
    loads = [
        pltpu.make_async_copy(nt_hbm, all_ref.at[f], local.at[0]),
        pltpu.make_async_copy(wout_hbm, wout_ref, local.at[1]),
        pltpu.make_async_copy(cot_hbm, cot_ref, local.at[2]),
        pltpu.make_async_copy(wfc_hbm, wfc_ref, local.at[3]),
    ]
    for load in loads:
        load.start()
    fcb_ref[...] = jnp.zeros_like(fcb_ref)
    loads[1].wait()
    loads[2].wait()

    def active_grad(k, carry):
        ag_ref[k] = dot_last(cot_ref[k], wout_ref[...])
        return carry

    lax.fori_loop(0, n, active_grad, 0)
    for k in far:
        rows_out(k).start()
    loads[0].wait()
    loads[3].wait()

    def chunk(k, carry):
        src = flip(f, k, n)

        @pl.when(k > 0)
        def _():
            rows_out(k).wait_recv()

        hidden = dot(all_ref[src], wfc_ref[...]) + bias_ref[...]
        square = hidden * hidden
        tanh = jnp.tanh(0.7978845608028654 * (hidden + 0.044715 * square * hidden))
        act_ref[src] = (0.5 * hidden * (1.0 + tanh)).astype(BF16)
        slope = 0.5 * (1.0 + tanh) + 0.5 * hidden * (1.0 - tanh * tanh) * 0.7978845608028654 * (
            1.0 + 3.0 * 0.044715 * square
        )
        grad = (ag_ref[src] * slope).astype(BF16)
        hg_ref[src] = grad
        fcb_ref[...] += jnp.sum(grad.astype(F32), axis=0, keepdims=True)
        part_ref[src] = dot_last(grad, wfc_ref[...]).astype(BF16)

        @pl.when(k > 0)
        def _():
            grad_back(k).start()

        return carry

    lax.fori_loop(0, n, chunk, 0)

    def grads(left_ref, right_ref, tiles, stage_ref, base):
        right = right_ref[...].reshape(n * rows, right_ref.shape[2])
        copies = []
        for i, (lo, size, sent, dst) in enumerate(tiles):
            slot = i % 2
            if i >= 2:
                copies[i - 2].wait()
            left = left_ref[:, :, lo : lo + size].reshape(n * rows, size)
            stage_ref[slot, :size] = dot_first(left, right).astype(BF16)
            copies.append(
                pltpu.make_async_copy(stage_ref.at[slot, :sent], dst, local.at[base + slot])
            )
            copies[-1].start()
        for copy in copies[-2:]:
            copy.wait()

    half, high = width // n // 2, wfc_grad_hbm.shape[2]
    if half < high:
        stage_h[:, half:high] = jnp.zeros((2, high - half, stage_h.shape[2]), BF16)
    wide = act_ref.shape[2]
    sizes = [(lo, min(TILE, wide - lo)) for lo in range(0, wide, TILE)]
    grads(
        act_ref,
        cot_ref,
        [(lo, size, size, wout_grad_hbm.at[lo : lo + size]) for lo, size in sizes],
        stage_d,
        4,
    )
    grads(
        all_ref,
        hg_ref,
        [
            ((2 * j + h) * half, half, high, wfc_grad_hbm.at[h, j])
            for j in range(n)
            for h in range(2)
        ],
        stage_h,
        6,
    )

    def out_copy(k):
        return pltpu.make_async_copy(
            stage_d.at[k % 2, :rows], out_hbm.at[k], local.at[4 + k % 2]
        )

    for k in range(n):
        if k >= 2:
            out_copy(k - 2).wait()
        stage_d[k % 2, :rows] = dot(act_ref[k], wout_ref[...]).astype(BF16)
        out_copy(k).start()

    gsum_ref[...] = part_ref[f].astype(F32)
    for k in near + far:
        grad_back(k).wait_recv()
        gsum_ref[...] += got_ref[k].astype(F32)
    for k in range(1, n):
        rows_out(k).wait_send()
        grad_back(k).wait_send()
    for k in range(max(0, n - 2), n):
        out_copy(k).wait()


def ffn(n, nt, cot, wfc, wout, bias, cid=1):
    m, d = nt.shape
    h = wfc.shape[1]
    vm = pl.BlockSpec(memory_space=pltpu.VMEM)
    anym = pl.BlockSpec(memory_space=pl.ANY)
    return pl.pallas_call(
        functools.partial(ffn_kernel, n),
        in_specs=[anym] * 4 + [vm],
        out_specs=[vm, vm] + [anym] * 3,
        out_shape=[
            jax.ShapeDtypeStruct((m, d), F32),
            jax.ShapeDtypeStruct((1, h), F32),
            jax.ShapeDtypeStruct((n, m, d), BF16),
            jax.ShapeDtypeStruct((h, d), BF16),
            jax.ShapeDtypeStruct((2, n, half_high(d // n), h), BF16),
        ],
        scratch_shapes=[
            pltpu.VMEM((n, m, d), BF16),
            pltpu.VMEM((d, h), BF16),
            pltpu.VMEM((h, d), BF16),
            pltpu.VMEM((n, m, d), BF16),
            pltpu.VMEM((n, m, h), BF16),
            pltpu.VMEM((n, m, h), BF16),
            pltpu.VMEM((n, m, h), F32),
            pltpu.VMEM((n, m, d), BF16),
            pltpu.VMEM((n, m, d), BF16),
            pltpu.VMEM((2, max(TILE, m), d), BF16),
            pltpu.VMEM((2, half_high(d // n), h), BF16),
        ]
        + [pltpu.SemaphoreType.DMA((n,))] * 4
        + [pltpu.SemaphoreType.DMA((8,))],
        compiler_params=pltpu.CompilerParams(
            collective_id=cid, has_side_effects=True, vmem_limit_bytes=60 * 1024 * 1024
        ),
        cost_estimate=SHORT,
        name="feed_forward",
    )(nt, cot, wfc, wout, bias)


def weight_shares(c, f, core, n_fsdp, shard, source, dst, ss, rs):
    cut = shard // 32 * 16 if shard % 16 == 0 else 0
    shares = ((0, cut), (cut, shard)) if cut else ((0, shard), (0, shard))
    twin_id = (c + 1 - 2 * core, f)

    def copy(share, k, onward):
        lo, hi = share
        other = flip(f, k, n_fsdp)
        if onward:
            part = dst.at[other, lo:hi]
            return send(part, part, ss.at[1, k], rs.at[1, k], twin_id)
        return send(source(k).at[lo:hi], dst.at[f, lo:hi], ss.at[0, k], rs.at[0, k], (c, other))

    def by_core(act):
        for h in range(2):

            @pl.when(core == h)
            def _(h=h):
                for k in range(1, n_fsdp):
                    act(shares[h], shares[1 - h], k)

    def start(mine, theirs, k):
        copy(mine, k, False).start()

    def onward(mine, theirs, k):
        copy(mine, k, False).wait_recv()
        if cut:
            copy(mine, k, True).start()

    def done(mine, theirs, k):
        if cut:
            copy(theirs, k, True).wait_recv()
            copy(mine, k, True).wait_send()
        copy(mine, k, False).wait_send()

    return tuple(functools.partial(by_core, act) for act in (start, onward, done))


def start_kernel(
    n_ctx,
    n_fsdp,
    base,
    tok_hbm,
    w_hbm,
    small_ref,
    proj_hbm,
    fc_hbm,
    n_hbm,
    qkv_hbm,
    proj_all,
    fc_parts,
    w_ref,
    lines_ref,
    n_ref,
    qkv_ref,
    fc_ref,
    fc_cut,
    x_ref,
    wg_ref,
    sg_ref,
    tok_recv,
    right_sem,
    left_sem,
    twin_sem,
    w_send,
    w_recv,
    s_send,
    s_recv,
    proj_send,
    proj_recv,
    local,
):
    c = lax.axis_index("ctx")
    f = lax.axis_index("fsdp")
    chips = n_ctx // 2
    chip, core = c // 2, c % 2
    slots, width, cols = w_ref.shape
    shard = width // n_fsdp
    hd = HEAD_DIM
    enter(
        [(lax.rem(c + i, n_ctx), f) for i in range(1, n_ctx)]
        + [(c, flip(f, k, n_fsdp)) for k in range(1, n_fsdp)]
    )

    def block(at, same):
        return 2 * at + (core if same else 1 - core)

    def hop(step, to_right, from_own):
        origin = block(chip - step if to_right else chip + step, True)
        src = tok_hbm if from_own else x_ref.at[origin]
        sem = (right_sem if to_right else left_sem).at[step]
        peer = (c + 2 if to_right else c - 2, f)
        return send(src, x_ref.at[origin], sem, tok_recv.at[origin], peer)

    def twin(at, from_own):
        origin = block(at, True)
        src = tok_hbm if from_own else x_ref.at[origin]
        return send(
            src, x_ref.at[origin], twin_sem.at[at], tok_recv.at[origin], (block(chip, False), f)
        )

    def w_copy(k):
        return send(w_hbm, wg_ref.at[f], w_send.at[k], w_recv.at[k], (c, flip(f, k, n_fsdp)))

    def s_copy(k):
        return send(small_ref, sg_ref.at[f], s_send.at[k], s_recv.at[k], (c, flip(f, k, n_fsdp)))

    weights_start, weights_onward, weights_done = weight_shares(
        c, f, core, n_fsdp, shard, lambda k: proj_hbm, proj_all, proj_send, proj_recv
    )

    for k in range(1, n_fsdp):
        s_copy(k).start()

    @pl.when(chip < chips - 1)
    def _():
        hop(0, True, True).start()

    @pl.when(chip > 0)
    def _():
        hop(0, False, True).start()

    for k in range(1, n_fsdp):
        w_copy(k).start()
    twin(chip, True).start()
    own_x = pltpu.make_async_copy(tok_hbm, x_ref.at[c], local.at[0])
    own_w = pltpu.make_async_copy(w_hbm, wg_ref.at[f], local.at[1])
    own_proj = pltpu.make_async_copy(proj_hbm, proj_all.at[f], local.at[2])
    load_fc = pltpu.make_async_copy(fc_hbm, fc_ref, local.at[3])
    for copy in (own_x, own_w, own_proj, load_fc):
        copy.start()
    sg_ref[f] = small_ref[...]
    for k in range(1, n_fsdp):
        s_copy(k).wait_recv()
    for j in range(n_fsdp):
        lines_ref[:, j * shard : (j + 1) * shard] = sg_ref[j]
    main = n_ctx * base * hd
    row_id = lax.broadcasted_iota(jnp.int32, (width, slots * hd), 0)
    col_id = lax.broadcasted_iota(jnp.int32, (width, slots * hd), 1)
    wanted = jnp.where(col_id < base * hd, c * base * hd + col_id, main + col_id - base * hd)
    picked = dot(lines_ref[...].astype(BF16), (row_id == wanted).astype(BF16))
    zero = jnp.zeros((1, hd), F32)
    bias = [
        jnp.concatenate(
            [picked[4:5, s * hd : (s + 1) * hd], zero, picked[5:6, s * hd : (s + 1) * hd]], axis=1
        )
        for s in range(slots)
    ]
    own_w.wait()
    own_x.wait()
    for k in range(1, n_fsdp):
        w_copy(k).wait_recv()
    weights_start()
    for j in range(n_fsdp):
        w_ref[:, j * shard : (j + 1) * shard, :] = wg_ref[j]

    load_fc.wait()
    hidden = fc_cut.shape[2]
    cuts = []
    for j in range(n_fsdp):
        if j >= 2:
            cuts[j - 2].wait()
        fc_cut[j % 2] = fc_ref[:, j * hidden : (j + 1) * hidden]
        cuts.append(pltpu.make_async_copy(fc_cut.at[j % 2], fc_parts.at[j], local.at[4 + j % 2]))
        cuts[-1].start()

    def results(origin):
        return (
            pltpu.make_async_copy(n_ref, n_hbm.at[origin], local.at[0]),
            pltpu.make_async_copy(qkv_ref, qkv_hbm.at[:, origin], local.at[1]),
        )

    def project(at, same, first=False):
        origin = block(at, same)
        rows = x_ref[origin].astype(F32)
        mean = jnp.mean(rows, axis=1, keepdims=True)
        cen = rows - mean
        var = jnp.mean(cen * cen, axis=1, keepdims=True)
        normed = cen * lax.rsqrt(var + EPS) * lines_ref[0:1] + lines_ref[2:3]
        normed = normed.astype(BF16)

        @pl.when(jnp.logical_not(first))
        def _():
            for copy in results(origin):
                copy.wait()

        n_ref[...] = normed
        for s in range(slots):
            qkv_ref[s] = (dot(normed, w_ref[s]) + bias[s]).astype(BF16)
        for copy in results(origin):
            copy.start()

    def arrived(at, same):
        origin = block(at, same)
        pltpu.make_async_copy(x_ref.at[origin], x_ref.at[origin], tok_recv.at[origin]).wait()

    def step(s, carry):
        @pl.when((s > 0) & (chip - s >= 0))
        def _():
            arrived(chip - s, True)
            twin(chip - s, False).start()

            @pl.when(chip < chips - 1)
            def _():
                hop(s, True, False).start()

        @pl.when((s > 0) & (chip + s < chips))
        def _():
            arrived(chip + s, True)
            twin(chip + s, False).start()

            @pl.when(chip > 0)
            def _():
                hop(s, False, False).start()

        @pl.when(chip - s >= 0)
        def _():
            project(chip - s, True, s == 0)

        @pl.when((s > 0) & (chip + s < chips))
        def _():
            project(chip + s, True)

        @pl.when(chip - s >= 0)
        def _():
            arrived(chip - s, False)
            project(chip - s, False)

        @pl.when((s > 0) & (chip + s < chips))
        def _():
            arrived(chip + s, False)
            project(chip + s, False)

        return carry

    lax.fori_loop(0, chips, step, 0)
    weights_onward()
    for copy in results(c):
        copy.wait()
    own_proj.wait()
    for cut in cuts[-2:]:
        cut.wait()

    for s in range(chips):
        if s < chips - 1:

            @pl.when((chip - s >= 0) & (chip < chips - 1))
            def _():
                hop(s, True, False).wait_send()

            @pl.when((chip + s < chips) & (chip > 0))
            def _():
                hop(s, False, False).wait_send()

        twin(s, False).wait_send()
    for k in range(1, n_fsdp):
        w_copy(k).wait_send()
        s_copy(k).wait_send()
    weights_done()


def start_call(n_ctx, n_fsdp, base, tok, w_slots, small, w_proj, w_fc, cid):
    count, width = tok.shape
    slots, shard, cols = w_slots.shape
    hidden = w_fc.shape[1] // n_fsdp
    vm = pl.BlockSpec(memory_space=pltpu.VMEM)
    anym = pl.BlockSpec(memory_space=pl.ANY)
    dma = pltpu.SemaphoreType.DMA
    return pl.pallas_call(
        functools.partial(start_kernel, n_ctx, n_fsdp, base),
        in_specs=[anym, anym, vm, anym, anym],
        out_specs=[anym, anym, anym, anym, vm, vm],
        out_shape=[
            jax.ShapeDtypeStruct((n_ctx, count, width), BF16),
            jax.ShapeDtypeStruct((slots, n_ctx, count, cols), BF16),
            jax.ShapeDtypeStruct((n_fsdp,) + w_proj.shape, BF16),
            jax.ShapeDtypeStruct((n_fsdp, shard, hidden), BF16),
            jax.ShapeDtypeStruct((slots, width, cols), BF16),
            jax.ShapeDtypeStruct((small.shape[0], width), F32),
        ],
        scratch_shapes=[
            pltpu.VMEM((count, width), BF16),
            pltpu.VMEM((slots, count, cols), BF16),
            pltpu.VMEM(w_fc.shape, BF16),
            pltpu.VMEM((2, shard, hidden), BF16),
            pltpu.VMEM((n_ctx, count, width), BF16),
            pltpu.VMEM((n_fsdp, slots, shard, cols), BF16),
            pltpu.VMEM((n_fsdp,) + small.shape, F32),
            dma((n_ctx,)),
            dma((n_ctx // 2,)),
            dma((n_ctx // 2,)),
            dma((n_ctx // 2,)),
            dma((n_fsdp,)),
            dma((n_fsdp,)),
            dma((n_fsdp,)),
            dma((n_fsdp,)),
            dma((2, n_fsdp)),
            dma((2, n_fsdp)),
            dma((6,)),
        ],
        compiler_params=pltpu.CompilerParams(
            collective_id=cid, has_side_effects=True, vmem_limit_bytes=VMEM_LIMIT
        ),
        cost_estimate=SHORT,
        name="tokens_qkv",
    )(tok, w_slots, small, w_proj, w_fc)


def causal_scores(k, q_rows, start):
    scores = dot_last(k, q_rows)
    keep = start
    tail = scores[keep:]
    key_id = lax.broadcasted_iota(jnp.int32, tail.shape, 0)
    query_id = lax.broadcasted_iota(jnp.int32, tail.shape, 1)
    tail = jnp.where(key_id <= query_id, tail, -1e30)
    if keep == 0:
        return tail
    return jnp.concatenate([scores[:keep], tail], axis=0)


def soft(scores, v_t):
    top = jnp.max(scores, axis=0, keepdims=True)
    weights = jnp.exp(scores - top)
    total = jnp.sum(weights, axis=0, keepdims=True)
    out = dot(v_t, weights.astype(BF16)) / total
    return out, top + jnp.log(total)


def causal(inv_ref, x_ref):
    return jnp.concatenate([x_ref[0, inv_ref[i]] for i in range(x_ref.shape[1])], axis=0)


def attn_fwd_kernel(inv_ref, x_ref, o_ref, l_ref):
    rows = l_ref.shape[2]
    hd = HEAD_DIM
    x = causal(inv_ref, x_ref)
    q = x[:, :hd] * BF16(SCALE)
    k = x[:, hd : 2 * hd]
    v_t = x[:, 2 * hd :].T
    for i in range(rows // QROWS):
        lo, hi = i * QROWS, (i + 1) * QROWS
        out, lse = soft(causal_scores(k[:hi], q[lo:hi], lo), v_t[:, :hi])
        l_ref[0, :, lo:hi] = lse
        out = out.astype(BF16)
        for b in range(QROWS // BLOCK):
            o_ref[inv_ref[2 * i + b]] = out[:, b * BLOCK : (b + 1) * BLOCK]


def attn_fwd(inv, qkv, heads):
    blocks, _, cols = qkv.shape[1:]
    rows = blocks * BLOCK
    return pl.pallas_call(
        attn_fwd_kernel,
        grid_spec=pltpu.PrefetchScalarGridSpec(
            num_scalar_prefetch=1,
            grid=(heads,),
            in_specs=[pl.BlockSpec((1, blocks, BLOCK, cols), lambda h, inv: (h, 0, 0, 0))],
            out_specs=[
                pl.BlockSpec((blocks, HEAD_DIM, BLOCK), lambda h, inv: (0, h, 0)),
                pl.BlockSpec((1, 1, rows), lambda h, inv: (h, 0, 0)),
            ],
        ),
        out_shape=[
            jax.ShapeDtypeStruct((blocks, heads * HEAD_DIM, BLOCK), BF16),
            jax.ShapeDtypeStruct((heads, 1, rows), F32),
        ],
        compiler_params=pltpu.CompilerParams(vmem_limit_bytes=VMEM_LIMIT),
        cost_estimate=SHORT,
        name="attn_fwd",
    )(inv, qkv)


def attn_bwd_kernel(inv_ref, x_ref, do_ref, o_ref, l_ref, dx_ref, dk_acc, dv_acc):
    rows = l_ref.shape[2]
    hd = HEAD_DIM
    x = causal(inv_ref, x_ref)
    q = x[:, :hd] * BF16(SCALE)
    k = x[:, hd : 2 * hd]
    v = x[:, 2 * hd :]
    k_t = k.T
    dk_acc[...] = jnp.zeros_like(dk_acc)
    dv_acc[...] = jnp.zeros_like(dv_acc)
    for i in range(rows // QROWS):
        lo, hi = i * QROWS, (i + 1) * QROWS
        ids = [inv_ref[2 * i + b] for b in range(QROWS // BLOCK)]
        do_t = jnp.concatenate([do_ref[b] for b in ids], axis=1)
        o_t = jnp.concatenate([o_ref[b] for b in ids], axis=1)
        inner = jnp.sum(do_t.astype(F32) * o_t.astype(F32), axis=0, keepdims=True)
        probs = jnp.exp(causal_scores(k[:hi], q[lo:hi], lo) - l_ref[0, :, lo:hi])
        dprobs = dot(v[:hi], do_t)
        dscores = (probs * (dprobs - inner)).astype(BF16)
        dv_acc[:hi] += dot_last(probs.astype(BF16), do_t)
        dk_acc[:hi] += dot(dscores, q[lo:hi])
        dq = (dot(k_t[:, :hi], dscores) * SCALE).T
        for n, b in enumerate(ids):
            dx_ref[0, b, :, :hd] = dq[n * BLOCK : (n + 1) * BLOCK].astype(BF16)
    for i in range(rows // BLOCK):
        lo, hi = i * BLOCK, (i + 1) * BLOCK
        dx_ref[0, inv_ref[i], :, hd : 2 * hd] = dk_acc[lo:hi].astype(BF16)
        dx_ref[0, inv_ref[i], :, 2 * hd :] = dv_acc[lo:hi].astype(BF16)


def attn_bwd(inv, qkv, d_out, out, lse, heads):
    blocks, _, cols = qkv.shape[1:]
    rows = blocks * BLOCK
    whole = pl.BlockSpec((1, blocks, BLOCK, cols), lambda h, inv: (h, 0, 0, 0))
    feat = pl.BlockSpec((blocks, HEAD_DIM, BLOCK), lambda h, inv: (0, h, 0))
    return pl.pallas_call(
        attn_bwd_kernel,
        grid_spec=pltpu.PrefetchScalarGridSpec(
            num_scalar_prefetch=1,
            grid=(heads,),
            in_specs=[
                whole,
                feat,
                feat,
                pl.BlockSpec((1, 1, rows), lambda h, inv: (h, 0, 0)),
            ],
            out_specs=whole,
            scratch_shapes=[pltpu.VMEM((rows, HEAD_DIM), F32)] * 2,
        ),
        out_shape=jax.ShapeDtypeStruct((heads, blocks, BLOCK, cols), BF16),
        compiler_params=pltpu.CompilerParams(vmem_limit_bytes=VMEM_LIMIT),
        cost_estimate=pl.CostEstimate(
            flops=24 * 10**9, bytes_accessed=24 * 10**6, transcendentals=0
        ),
        name="attn_bwd",
    )(inv, qkv, d_out, out, lse)


def own_scores(order_ref, x_ref, k):
    hd = HEAD_DIM
    blocks = x_ref.shape[1]
    first = order_ref[blocks]
    q = jnp.concatenate([x_ref[0, first], x_ref[0, first + 1]], axis=0)[:, :hd]
    q = q * BF16(SCALE)
    scores = dot_last(k, q)
    row = lax.broadcasted_iota(jnp.int32, (BLOCK, 1), 0)
    key_place = jnp.concatenate([order_ref[b] * BLOCK + row for b in range(blocks)], axis=0)
    lane = lax.broadcasted_iota(jnp.int32, (1, 2 * BLOCK), 1)
    low, high = order_ref[order_ref[blocks]], order_ref[order_ref[blocks] + 1]
    place = jnp.where(lane < BLOCK, low * BLOCK + lane, (high - 1) * BLOCK + lane)
    return q, first, jnp.where(key_place <= place, scores, -1e30)


def rest_fwd_kernel(order_ref, x_ref, o_ref, l_ref):
    hd = HEAD_DIM
    x = x_ref[0].reshape(-1, 3 * hd)
    _, _, scores = own_scores(order_ref, x_ref, x[:, hd : 2 * hd])
    out, lse = soft(scores, x[:, 2 * hd :].T)
    o_ref[0] = out.astype(BF16)
    l_ref[0] = lse


def rest_fwd(order, qkv, base):
    slots, blocks, _, cols = qkv.shape
    rest = slots - base
    return pl.pallas_call(
        rest_fwd_kernel,
        grid_spec=pltpu.PrefetchScalarGridSpec(
            num_scalar_prefetch=1,
            grid=(rest,),
            in_specs=[
                pl.BlockSpec((1, blocks, BLOCK, cols), lambda h, o: (base + h, 0, 0, 0))
            ],
            out_specs=[
                pl.BlockSpec((1, HEAD_DIM, QROWS), lambda h, o: (h, 0, 0)),
                pl.BlockSpec((1, 1, QROWS), lambda h, o: (h, 0, 0)),
            ],
        ),
        out_shape=[
            jax.ShapeDtypeStruct((rest, HEAD_DIM, QROWS), BF16),
            jax.ShapeDtypeStruct((rest, 1, QROWS), F32),
        ],
        compiler_params=pltpu.CompilerParams(vmem_limit_bytes=VMEM_LIMIT),
        cost_estimate=SHORT,
        name="rest_fwd",
    )(order, qkv)


def rest_bwd_kernel(order_ref, x_ref, do_ref, o_ref, l_ref, dx_ref):
    hd = HEAD_DIM
    x = x_ref[0].reshape(-1, 3 * hd)
    blocks = x_ref.shape[1]
    k = x[:, hd : 2 * hd]
    q, first, scores = own_scores(order_ref, x_ref, k)
    do_t = do_ref[0]
    inner = jnp.sum(do_t.astype(F32) * o_ref[0].astype(F32), axis=0, keepdims=True)
    probs = jnp.exp(scores - l_ref[0])
    dprobs = dot(x[:, 2 * hd :], do_t)
    dscores = (probs * (dprobs - inner)).astype(BF16)
    dv = dot_last(probs.astype(BF16), do_t).astype(BF16)
    dk = dot(dscores, q).astype(BF16)
    dq = (dot(k.T, dscores) * SCALE).T.astype(BF16)
    dx_ref[0, :, :, 2 * hd :] = dv.reshape(blocks, BLOCK, hd)
    dx_ref[0, :, :, hd : 2 * hd] = dk.reshape(blocks, BLOCK, hd)
    dx_ref[0, :, :, :hd] = jnp.zeros((blocks, BLOCK, hd), BF16)
    for b in range(2):
        dx_ref[0, first + b, :, :hd] = dq[b * BLOCK : (b + 1) * BLOCK]


def rest_bwd(order, qkv, d_out, out, lse, base):
    slots, blocks, _, cols = qkv.shape
    rest = slots - base
    feat = pl.BlockSpec((1, HEAD_DIM, QROWS), lambda h, o: (h, 0, 0))
    return pl.pallas_call(
        rest_bwd_kernel,
        grid_spec=pltpu.PrefetchScalarGridSpec(
            num_scalar_prefetch=1,
            grid=(rest,),
            in_specs=[
                pl.BlockSpec((1, blocks, BLOCK, cols), lambda h, o: (base + h, 0, 0, 0)),
                feat,
                feat,
                pl.BlockSpec((1, 1, QROWS), lambda h, o: (h, 0, 0)),
            ],
            out_specs=pl.BlockSpec((1, blocks, BLOCK, cols), lambda h, o: (h, 0, 0, 0)),
        ),
        out_shape=jax.ShapeDtypeStruct((rest, blocks, BLOCK, cols), BF16),
        compiler_params=pltpu.CompilerParams(vmem_limit_bytes=VMEM_LIMIT),
        cost_estimate=SHORT,
        name="rest_bwd",
    )(order, qkv, d_out, out, lse)


def mix_kernel(
    n_ctx,
    n_fsdp,
    out_hbm,
    rest_ref,
    tok_ref,
    proj_ref,
    lines_ref,
    fc_parts,
    att_ref,
    mid_ref,
    n_ref,
    fc_all,
    got_ref,
    out_send,
    out_recv,
    fc_send,
    fc_recv,
    local,
):
    c = lax.axis_index("ctx")
    f = lax.axis_index("fsdp")
    core = c % 2
    width = tok_ref.shape[1]
    shard = width // n_fsdp
    blocks, feats = got_ref.shape[1], got_ref.shape[2]
    enter(
        [(lax.rem(c + i, n_ctx), f) for i in range(1, n_ctx)]
        + [(c, flip(f, k, n_fsdp)) for k in range(1, n_fsdp)]
    )

    def out_copy(i):
        to = lax.rem(c + i, n_ctx)
        return send(
            out_hbm.at[pl.ds(to * blocks, blocks)],
            got_ref.at[c],
            out_send.at[i],
            out_recv.at[i],
            (to, f),
        )

    for i in range(n_ctx - 1, 0, -1):
        out_copy(i).start()
    weights_start, weights_onward, weights_done = weight_shares(
        c,
        f,
        core,
        n_fsdp,
        shard,
        lambda k: fc_parts.at[flip(f, k, n_fsdp)],
        fc_all,
        fc_send,
        fc_recv,
    )
    weights_start()
    own = pltpu.make_async_copy(
        out_hbm.at[pl.ds(c * blocks, blocks)], got_ref.at[c], local.at[0]
    )
    own_fc = pltpu.make_async_copy(fc_parts.at[f], fc_all.at[f], local.at[1])
    own.start()
    own_fc.start()
    main = n_ctx * feats
    if main < width:
        att_ref[:, main:] = rest_ref[...].reshape(width - main, -1).T
    own.wait()
    for i in range(1, n_ctx):
        out_copy(i).wait_recv()
    for src in range(n_ctx):
        block = jnp.concatenate([got_ref[src, b] for b in range(blocks)], axis=1)
        att_ref[:, src * feats : (src + 1) * feats] = block.T
    mid = tok_ref[...].astype(F32) + (dot(att_ref[...], proj_ref[...]) + lines_ref[6:7])
    mid_ref[...] = mid
    cen = mid - jnp.mean(mid, axis=1, keepdims=True)
    var = jnp.mean(cen * cen, axis=1, keepdims=True)
    n_ref[...] = (cen * lax.rsqrt(var + EPS) * lines_ref[1:2] + lines_ref[3:4]).astype(BF16)
    weights_onward()
    own_fc.wait()
    for i in range(1, n_ctx):
        out_copy(i).wait_send()
    weights_done()


def mix_call(n_ctx, n_fsdp, out_own, out_rest, tok, proj, lines, fc_parts, cid):
    count, width = tok.shape
    vm = pl.BlockSpec(memory_space=pltpu.VMEM)
    anym = pl.BlockSpec(memory_space=pl.ANY)
    dma = pltpu.SemaphoreType.DMA
    return pl.pallas_call(
        functools.partial(mix_kernel, n_ctx, n_fsdp),
        in_specs=[anym, vm, vm, vm, vm, anym],
        out_specs=[vm, vm, vm, anym],
        out_shape=[
            jax.ShapeDtypeStruct((count, width), BF16),
            jax.ShapeDtypeStruct((count, width), F32),
            jax.ShapeDtypeStruct((count, width), BF16),
            jax.ShapeDtypeStruct(fc_parts.shape, BF16),
        ],
        scratch_shapes=[
            pltpu.VMEM((n_ctx, out_own.shape[0] // n_ctx) + out_own.shape[1:], BF16),
            dma((n_ctx,)),
            dma((n_ctx,)),
            dma((2, n_fsdp)),
            dma((2, n_fsdp)),
            dma((2,)),
        ],
        compiler_params=pltpu.CompilerParams(
            collective_id=cid, has_side_effects=True, vmem_limit_bytes=VMEM_LIMIT
        ),
        cost_estimate=SHORT,
        name="mix_rows",
    )(out_own, out_rest, tok, proj, lines, fc_parts)


def turn_kernel(
    n_ctx,
    gsum_ref,
    cot_ref,
    mid_ref,
    proj_ref,
    lines_ref,
    fc_hbm,
    grad_ref,
    low_ref,
    sums_ref,
    rest_ref,
    fc_ref,
    got_hbm,
    out_ref,
    pair_in,
    out_send,
    out_recv,
    pair_sem,
    local,
):
    c = lax.axis_index("ctx")
    f = lax.axis_index("fsdp")
    core = c % 2
    width = mid_ref.shape[1]
    blocks, feats = out_ref.shape[0] // n_ctx, out_ref.shape[1]
    enter([(lax.rem(c + i, n_ctx), f) for i in range(1, n_ctx)])
    pair = send(fc_hbm.at[1 - core], pair_in, pair_sem.at[0], pair_sem.at[1], (c + 1 - 2 * core, f))
    pair.start()
    own_fc = pltpu.make_async_copy(fc_hbm.at[core], fc_ref, local.at[0])
    own_fc.start()

    xhat, rstd = norm_parts(mid_ref[...])
    grad = gsum_ref[...]
    cot = cot_ref[...].astype(F32)
    mid_grad = cot + norm_back(xhat, rstd, lines_ref[1:2], grad)
    grad_ref[...] = mid_grad
    low = mid_grad.astype(BF16)
    low_ref[...] = low
    att_t = dot_last(low, proj_ref[...]).astype(BF16).T
    for to in range(n_ctx):
        for b in range(blocks):
            out_ref[to * blocks + b] = att_t[
                to * feats : (to + 1) * feats, b * BLOCK : (b + 1) * BLOCK
            ]

    def out_copy(i):
        to = lax.rem(c + i, n_ctx)
        return send(
            out_ref.at[pl.ds(to * blocks, blocks)],
            got_hbm.at[pl.ds(c * blocks, blocks)],
            out_send.at[i],
            out_recv.at[i],
            (to, f),
        )

    for i in range(n_ctx - 1, 0, -1):
        out_copy(i).start()
    own = pltpu.make_async_copy(
        out_ref.at[pl.ds(c * blocks, blocks)], got_hbm.at[pl.ds(c * blocks, blocks)], local.at[1]
    )
    own.start()
    main = n_ctx * feats
    if main < width:
        rest_ref[...] = att_t[main:].reshape(rest_ref.shape)
    else:
        rest_ref[...] = jnp.zeros(rest_ref.shape, BF16)
    for r, line in enumerate((grad * xhat, grad, low.astype(F32), cot)):
        sums_ref[r : r + 1] = jnp.sum(line, axis=0, keepdims=True)
    sums_ref[4:] = jnp.zeros((4, width), F32)
    own_fc.wait()
    pair.wait()

    def add(j, carry):
        fc_ref[j] = (fc_ref[j].astype(F32) + pair_in[j].astype(F32)).astype(BF16)
        return carry

    lax.fori_loop(0, fc_ref.shape[0], add, 0)
    own.wait()
    for i in range(1, n_ctx):
        out_copy(i).wait()


def turn_call(n_ctx, base, gsum, cot, mid, proj, lines, fc_part, cid):
    count, width = mid.shape
    heads = width // HEAD_DIM
    rest = max(heads - base * n_ctx, 1)
    out = (n_ctx * count // BLOCK, base * HEAD_DIM, BLOCK)
    vm = pl.BlockSpec(memory_space=pltpu.VMEM)
    anym = pl.BlockSpec(memory_space=pl.ANY)
    dma = pltpu.SemaphoreType.DMA
    return pl.pallas_call(
        functools.partial(turn_kernel, n_ctx),
        in_specs=[vm] * 5 + [anym],
        out_specs=[vm] * 5 + [anym],
        out_shape=[
            jax.ShapeDtypeStruct((count, width), F32),
            jax.ShapeDtypeStruct((count, width), BF16),
            jax.ShapeDtypeStruct((8, width), F32),
            jax.ShapeDtypeStruct((rest, HEAD_DIM, count), BF16),
            jax.ShapeDtypeStruct(fc_part.shape[1:], BF16),
            jax.ShapeDtypeStruct(out, BF16),
        ],
        scratch_shapes=[
            pltpu.VMEM(out, BF16),
            pltpu.VMEM(fc_part.shape[1:], BF16),
            dma((n_ctx,)),
            dma((n_ctx,)),
            dma((2,)),
            dma((2,)),
        ],
        compiler_params=pltpu.CompilerParams(
            collective_id=cid, has_side_effects=True, vmem_limit_bytes=VMEM_LIMIT
        ),
        cost_estimate=SHORT,
        name="turn_rows",
    )(gsum, cot, mid, proj, lines, fc_part)


def far_first(i, chips):
    return (i % 2) * (i // 2) + (1 - i % 2) * (chips - 1 - i // 2)


def line_sum(chip, chips, f, core, part, came, sems, ready=None):
    sent, left_sem, right_sem = sems

    def to_right(d):
        return send(
            part.at[d], came.at[d], sent.at[d], left_sem.at[d], (2 * (chip + 1) + core, f)
        )

    def to_left(d):
        place = jnp.where(d == chip - 1, chips, d)
        return send(
            part.at[d], came.at[place], sent.at[d], right_sem.at[d], (2 * (chip - 1) + core, f)
        )

    def from_left(d):
        send(part.at[d], came.at[d], sent.at[d], left_sem.at[d], (2 * chip + core, f)).wait_recv()
        add(d, d)

    def from_right(d, place):
        send(
            part.at[d], came.at[place], sent.at[d], right_sem.at[d], (2 * chip + core, f)
        ).wait_recv()
        add(d, place)

    def add(d, place):
        part[d] = (part[d].astype(F32) + came[place].astype(F32)).astype(BF16)

    def step(t):
        far = chips - 1 - t + chip
        near = t - (chips - 1 - chip)

        @pl.when(chip <= t)
        def _():
            if ready is not None:
                ready(far)

            @pl.when(chip > 0)
            def _():
                from_left(far)

            to_right(far).start()

        @pl.when(near >= 0)
        def _():
            if ready is not None:
                ready(near)

            @pl.when(chip < chips - 1)
            def _():
                from_right(near, near)

            to_left(near).start()

    def finish():
        if ready is not None:
            ready(chip)

        @pl.when(chip > 0)
        def _():
            from_left(chip)

        @pl.when(chip < chips - 1)
        def _():
            from_right(chip, chips)

    def done():
        for d in range(chips):

            @pl.when(chip < d)
            def _(d=d):
                to_right(d).wait_send()

            @pl.when(chip > d)
            def _(d=d):
                to_left(d).wait_send()

    return step, finish, done


def line_gather(chip, chips, f, core, view, sems):
    right, left, twin_sent, got, twin_got = sems
    twin_id = (2 * chip + 1 - core, f)

    def hop(s, rightward):
        origin = chip - s if rightward else chip + s
        ref = view(origin, core)
        peer = (2 * (chip + 1 if rightward else chip - 1) + core, f)
        return send(ref, ref, (right if rightward else left).at[s], got.at[origin], peer)

    def twin(origin):
        ref = view(origin, core)
        return send(ref, ref, twin_sent.at[origin], twin_got.at[origin], twin_id)

    def arrived(origin):
        ref = view(origin, core)
        send(ref, ref, right.at[0], got.at[origin], twin_id).wait_recv()

    def step(s):
        @pl.when(chip - s >= 0)
        def _():
            if s:
                arrived(chip - s)

            @pl.when(chip < chips - 1)
            def _():
                hop(s, True).start()

            twin(chip - s).start()

        @pl.when(chip + s < chips)
        def _():
            if s:
                arrived(chip + s)

            @pl.when(chip > 0)
            def _():
                hop(s, False).start()

            if s:
                twin(chip + s).start()

    def done():
        for s in range(chips):
            if s < chips - 1:

                @pl.when((chip - s >= 0) & (chip < chips - 1))
                def _(s=s):
                    hop(s, True).wait_send()

                @pl.when((chip + s < chips) & (chip > 0))
                def _(s=s):
                    hop(s, False).wait_send()

            twin(s).wait_send()
            ref = view(s, 1 - core)
            send(ref, ref, twin_sent.at[s], twin_got.at[s], twin_id).wait_recv()

    return step, done


def back_kernel(
    n_ctx,
    n_fsdp,
    own_ref,
    rest_ref,
    w_ref,
    n_ref,
    fc_hbm,
    one_ref,
    cols_ref,
    fc_all,
    part,
    twin_out,
    twin_in,
    came,
    mine,
    theirs,
    twin_send,
    twin_recv,
    line_send,
    left_recv,
    right_recv,
    cols_send,
    cols_recv,
    fc_send,
    fc_recv,
    local,
):
    c = lax.axis_index("ctx")
    f = lax.axis_index("fsdp")
    chips = n_ctx // 2
    chip, core = c // 2, c % 2
    slots, width, cols = w_ref.shape
    count = own_ref.shape[2]
    base = own_ref.shape[0]
    shard = width // n_fsdp
    twin_id = (2 * chip + 1 - core, f)
    enter(
        [(lax.rem(c + i, n_ctx), f) for i in range(1, n_ctx)]
        + [(c, flip(f, k, n_fsdp)) for k in range(1, n_fsdp)]
    )

    def grad(s):
        return own_ref.at[s] if s < base else rest_ref.at[s - base]

    def for_block(b):
        total = dot_last(grad(0)[b], w_ref[0])
        for s in range(1, slots):
            total += dot_last(grad(s)[b], w_ref[s])
        return total.astype(BF16)

    def to_twin(d, slot):
        return send(twin_out.at[slot], twin_in.at[d], twin_send.at[slot], twin_recv.at[d], twin_id)

    def products(i, carry):
        d = far_first(i, chips)
        slot = i % 2
        product = for_block(2 * d + 1 - core)

        @pl.when(i > 1)
        def _():
            to_twin(d, slot).wait_send()

        twin_out[slot] = product
        to_twin(d, slot).start()
        part[d] = for_block(2 * d + core)
        return carry

    def ready(d):
        to_twin(d, 0).wait_recv()
        part[d] = (part[d].astype(F32) + twin_in[d].astype(F32)).astype(BF16)

    step, finish, done = line_sum(
        chip, chips, f, core, part, came, (line_send, left_recv, right_recv), ready
    )

    def cols_copy(src, dst, at):
        return send(mine.at[src], theirs.at[at], cols_send.at[src], cols_recv.at[at], (c, dst))

    def columns(j):
        left = n_ref[:, :, j * shard : (j + 1) * shard].reshape(n_ctx * count, shard)
        for s in range(slots):
            right = grad(s)[...].reshape(n_ctx * count, cols)
            mine[j, s] = dot_first(left, right).astype(BF16)

    def fc_copy(k):
        other = flip(f, k, n_fsdp)
        return send(fc_hbm.at[other], fc_all.at[f], fc_send.at[k], fc_recv.at[k], (c, other))

    lax.fori_loop(0, 2, products, 0)
    step(0)
    for j in range(n_fsdp):
        columns(j)
    for k in range(1, n_fsdp):
        other = flip(f, k, n_fsdp)
        cols_copy(other, other, f).start()
    for k in range(1, n_fsdp):
        fc_copy(k).start()
    own_fc = pltpu.make_async_copy(fc_hbm.at[f], fc_all.at[f], local)
    own_fc.start()
    lax.fori_loop(2, chips, products, 0)
    if chips > 2:
        step(1)
    for t in range(2, chips - 1):
        step(t)
    total = mine[f].astype(F32)
    for k in range(1, n_fsdp):
        other = flip(f, k, n_fsdp)
        cols_copy(other, other, other).wait_recv()
        total += theirs[other].astype(F32)
    cols_ref[...] = total.astype(BF16)
    finish()
    one_ref[...] = part[chip]
    own_fc.wait()
    for k in range(1, n_fsdp):
        fc_copy(k).wait()
    done()
    for slot in range(2):
        to_twin(0, slot).wait_send()
    for k in range(1, n_fsdp):
        other = flip(f, k, n_fsdp)
        cols_copy(other, other, other).wait_send()


def back_fits(n_ctx, n_fsdp, count, width, slots):
    blocks = (5 * (n_ctx // 2) + n_ctx) * count * width
    heads = slots * 256 * (n_ctx * count + 3 * width)
    return 2 * (blocks + heads) < 50 * 1024 * 1024


def back_call(n_ctx, n_fsdp, own, rest, w_slots, normed, fc_mine, cid):
    slots, width, cols = w_slots.shape
    count = normed.shape[1]
    chips = n_ctx // 2
    shard = width // n_fsdp
    vm = pl.BlockSpec(memory_space=pltpu.VMEM)
    anym = pl.BlockSpec(memory_space=pl.ANY)
    dma = pltpu.SemaphoreType.DMA
    block = pltpu.VMEM((chips, count, width), BF16)
    piece = pltpu.VMEM((n_fsdp, slots, shard, cols), BF16)
    return pl.pallas_call(
        functools.partial(back_kernel, n_ctx, n_fsdp),
        in_specs=[vm] * 4 + [anym],
        out_specs=[vm] * 2 + [anym],
        out_shape=[
            jax.ShapeDtypeStruct((count, width), BF16),
            jax.ShapeDtypeStruct((slots, shard, cols), BF16),
            jax.ShapeDtypeStruct(fc_mine.shape, BF16),
        ],
        scratch_shapes=[
            block,
            pltpu.VMEM((2, count, width), BF16),
            block,
            pltpu.VMEM((chips + 1, count, width), BF16),
        ]
        + [piece] * 2
        + [dma((2,))]
        + [dma((chips,))] * 4
        + [dma((n_fsdp,))] * 4
        + [dma(())],
        compiler_params=pltpu.CompilerParams(
            collective_id=cid, has_side_effects=True, vmem_limit_bytes=60 * 1024 * 1024
        ),
        cost_estimate=SHORT,
        name="qkv_back",
    )(own, rest, w_slots, normed, fc_mine)


def sums_kernel(n_ctx, n_fsdp, lead, *refs):
    rows_ref, cols_ref, extra_ref, att_ref, mid_ref, lines_in = refs[:6]
    outs, cols_all, lines_ref = refs[6:9], refs[9], refs[10]
    parts, cames = refs[11:14], refs[14:17]
    proj_part, proj_in, proj_got, lines_got = refs[17:21]
    lines_send, lines_recv, local, proj_send, proj_recv, pair_sem = refs[21:27]
    cols_sems = refs[27:32]
    sems = [(refs[32 + 8 * i : 35 + 8 * i], refs[35 + 8 * i : 40 + 8 * i]) for i in range(3)]
    c = lax.axis_index("ctx")
    f = lax.axis_index("fsdp")
    chips = n_ctx // 2
    chip, core = c // 2, c % 2
    width = att_ref.shape[1]
    shard = width // n_fsdp
    half = shard // 2
    high = proj_in.shape[1]
    twin_id = (2 * chip + 1 - core, f)
    enter(
        [(lax.rem(c + i, n_ctx), f) for i in range(1, n_ctx)]
        + [(c, flip(f, k, n_fsdp)) for k in range(1, n_fsdp)]
    )

    def line_ops(i):
        sum_sems, gather_sems = sems[i]
        gather = line_gather(chip, chips, f, core, lambda at, h: outs[i].at[h, at], gather_sems)
        return line_sum(chip, chips, f, core, parts[i], cames[i], sum_sems) + gather

    def proj_pair():
        return send(proj_part.at[1 - core], proj_in, pair_sem.at[0], pair_sem.at[1], twin_id)

    def proj_copy(k):
        other = flip(f, k, n_fsdp)
        return send(
            proj_part.at[core, other],
            proj_got.at[f],
            proj_send.at[k],
            proj_recv.at[k],
            (c, other),
        )

    def proj_products(j):
        for h in range(2):
            lo = j * shard + h * half
            proj_part[h, j, :half] = dot_first(att_ref[:, lo : lo + half], mid_ref[...]).astype(BF16)
            if half < high:
                proj_part[h, j, half:] = jnp.zeros((high - half, width), BF16)

    def proj_add(j, carry):
        proj_part[core, j] = (
            proj_part[core, j].astype(F32) + proj_in[j].astype(F32)
        ).astype(BF16)
        return carry

    def proj_total():
        total = proj_part[core, f].astype(F32)
        for k in range(1, n_fsdp):
            proj_copy(k).wait_recv()
            total += proj_got[flip(f, k, n_fsdp)].astype(F32)
        total = jnp.concatenate([total.astype(BF16), extra_ref[...]], axis=0)
        step, rows = parts[2].shape[1], total.shape[0]
        for p in range(chips):
            lo, hi = min(p * step, rows), min((p + 1) * step, rows)
            if hi > lo:
                parts[2][p, : hi - lo] = total[lo:hi]
            if hi - lo < step:
                parts[2][p, hi - lo :] = jnp.zeros((step - hi + lo, width), BF16)

    peers = [(flip(c, 1 << i, n_ctx), f) for i in range(n_ctx.bit_length() - 1)]
    ctx_phases = len(peers)
    peers += [(c, flip(f, 1 << i, n_fsdp)) for i in range(n_fsdp.bit_length() - 1)]

    def line_copy(i):
        rows = lines_in.shape[0] if i < ctx_phases else lead
        return send(
            lines_ref.at[:rows],
            lines_got.at[i, :rows],
            lines_send.at[i],
            lines_recv.at[i],
            peers[i],
        )

    def line_phase(i):
        if 0 < i <= len(peers):
            rows = lines_in.shape[0] if i <= ctx_phases else lead
            line_copy(i - 1).wait()
            lines_ref[:rows] += lines_got[i - 1, :rows]
        if i < len(peers):
            line_copy(i).start()

    def settle(finish, i):
        finish()
        keep = pltpu.make_async_copy(parts[i].at[chip], outs[i].at[core, chip], local.at[0])
        keep.start()
        keep.wait()

    sum_a, finish_a, sums_a, gather_a, gathers_a = line_ops(0)
    sum_b, finish_b, sums_b, gather_b, gathers_b = line_ops(1)
    sum_p, finish_p, sums_p, gather_p, gathers_p = line_ops(2)
    cols_step, cols_done = line_gather(
        chip, chips, f, core, lambda at, h: cols_all.at[2 * at + h], cols_sems
    )
    load = pltpu.make_async_copy(cols_ref, cols_all.at[c], local.at[1])
    load.start()
    cut = parts[0].shape[1]
    parts[0][...] = rows_ref[:, :cut]
    load.wait()
    cols_step(0)
    sum_a(0)
    parts[1][...] = rows_ref[:, cut:]
    lines_ref[...] = lines_in[...]
    for j in range(n_fsdp):
        proj_products(j)
    proj_pair().start()
    for t in range(1, chips - 1):
        cols_step(t)
        sum_a(t)
        if t == 1:
            proj_pair().wait()
            lax.fori_loop(0, n_fsdp, proj_add, 0)
            for k in range(1, n_fsdp):
                proj_copy(k).start()
    sum_b(0)
    cols_step(chips - 1)
    settle(finish_a, 0)
    gather_a(0)
    phase = 0
    for s in range(1, chips - 1):
        sum_b(s)
        gather_a(s)
        line_phase(phase)
        phase += 1
    settle(finish_b, 1)
    gather_b(0)
    gather_a(chips - 1)
    proj_total()
    for s in range(1, chips):
        sum_p(s - 1)
        gather_b(s)
        line_phase(phase)
        phase += 1
    settle(finish_p, 2)
    for s in range(chips):
        gather_p(s)
        line_phase(phase)
        phase += 1
    while phase <= len(peers):
        line_phase(phase)
        phase += 1
    for done in (sums_a, sums_b, sums_p, cols_done, gathers_a, gathers_b, gathers_p):
        done()
    for k in range(1, n_fsdp):
        proj_copy(k).wait_send()


def sums_call(n_ctx, n_fsdp, rows, cols, extra, attended, mid_low, lines, lead, cid):
    chips = n_ctx // 2
    count, width = attended.shape
    high = half_high(width // n_fsdp)
    per_chip = rows.shape[1]
    cut = -(-per_chip // 32) * 16
    third = -(-(high + extra.shape[0]) // (16 * chips)) * 16
    shapes = [(chips, size, width) for size in (cut, per_chip - cut, third)]
    phases = (n_ctx * n_fsdp).bit_length() - 1
    vm = pl.BlockSpec(memory_space=pltpu.VMEM)
    anym = pl.BlockSpec(memory_space=pl.ANY)
    dma = pltpu.SemaphoreType.DMA
    return pl.pallas_call(
        functools.partial(sums_kernel, n_ctx, n_fsdp, lead),
        in_specs=[vm, anym, vm, vm, vm, vm],
        out_specs=[vm, vm, vm, anym, vm],
        out_shape=[jax.ShapeDtypeStruct((2,) + shape, BF16) for shape in shapes]
        + [jax.ShapeDtypeStruct((n_ctx,) + cols.shape, BF16)]
        + [jax.ShapeDtypeStruct(lines.shape, F32)],
        scratch_shapes=[pltpu.VMEM(shape, BF16) for shape in shapes]
        + [pltpu.VMEM((chips + 1,) + shape[1:], BF16) for shape in shapes]
        + [
            pltpu.VMEM((2, n_fsdp, high, width), BF16),
            pltpu.VMEM((n_fsdp, high, width), BF16),
            pltpu.VMEM((n_fsdp, high, width), BF16),
            pltpu.VMEM((phases,) + lines.shape, F32),
            dma((phases,)),
            dma((phases,)),
            dma((2,)),
            dma((n_fsdp,)),
            dma((n_fsdp,)),
            dma((2,)),
        ]
        + [dma((chips,))] * (5 + 3 * 8),
        compiler_params=pltpu.CompilerParams(
            collective_id=cid, has_side_effects=True, vmem_limit_bytes=56 * 1024 * 1024
        ),
        cost_estimate=SHORT,
        name="weight_sums",
    )(rows, cols, extra, attended, mid_low, lines)


def assemble_kernel(
    n_fsdp,
    own_ref,
    rest_ref,
    first_ref,
    second_ref,
    third_ref,
    out_ref,
    attn_hbm,
    fc_hbm,
    proj_hbm,
    wout_hbm,
    *scratch,
):
    attn_ref, fc_ref, proj_ref, wout_ref, low_ref, sem = scratch
    load = pltpu.make_async_copy(out_ref, low_ref, sem.at[4])
    load.start()
    hd = HEAD_DIM
    shard, hidden = fc_ref.shape[0], fc_ref.shape[1] // n_fsdp
    half = shard // 2
    width = proj_ref.shape[1]
    count = own_ref.shape[0]
    copies = [
        pltpu.make_async_copy(src, dst, sem.at[i])
        for i, (src, dst) in enumerate(
            ((wout_ref, wout_hbm), (fc_ref, fc_hbm), (proj_ref, proj_hbm), (attn_ref, attn_hbm))
        )
    ]
    for h in range(2):
        for j in range(n_fsdp):
            cut = min(first_ref.shape[2], half)
            at = slice(j * hidden, (j + 1) * hidden)
            fc_ref[h * half : h * half + cut, at] = first_ref[h, j, :cut].astype(F32)
            if cut < half:
                rows = second_ref[h, j, : half - cut].astype(F32)
                fc_ref[h * half + cut : (h + 1) * half, at] = rows
    copies[1].start()
    for h in range(2):
        proj_ref[h * half : (h + 1) * half] = third_ref[h, :half].astype(F32)
    copies[2].start()
    for h in range(width // hd):
        src = own_ref.at[h] if h < count else rest_ref.at[h - count]
        for part in range(3):
            at = part * width + h * hd
            attn_ref[:, at : at + hd] = src[:, part * hd : (part + 1) * hd].astype(F32)
    copies[3].start()
    load.wait()
    wout_ref[...] = low_ref[...].astype(F32)
    copies[0].start()
    for copy in copies:
        copy.wait()


def assemble(n_fsdp, own, rest, first, second, third, out_low, hidden):
    shard = own.shape[1]
    width = first.shape[3]
    vm = pl.BlockSpec(memory_space=pltpu.VMEM)
    anym = pl.BlockSpec(memory_space=pl.ANY)
    shapes = [(shard, 3 * width), (shard, n_fsdp * hidden), (shard, width), out_low.shape]
    return pl.pallas_call(
        functools.partial(assemble_kernel, n_fsdp),
        in_specs=[vm] * 5 + [anym],
        out_specs=[anym] * 4,
        out_shape=[jax.ShapeDtypeStruct(shape, F32) for shape in shapes],
        scratch_shapes=[pltpu.VMEM(shape, F32) for shape in shapes]
        + [pltpu.VMEM(out_low.shape, BF16), pltpu.SemaphoreType.DMA((5,))],
        compiler_params=pltpu.CompilerParams(vmem_limit_bytes=60 * 1024 * 1024),
        cost_estimate=SHORT,
        name="assemble",
    )(own, rest, first, second, third, out_low)


def swap(value, axis, size, k):
    return lax.ppermute(value, axis, [(i, i ^ k) for i in range(size)])


def shards(
    n_ctx,
    n_fsdp,
    tokens,
    block_order,
    w_attn,
    w_proj,
    w_fc,
    w_out,
    norm_gains,
    biases,
    fc_bias,
    cotangent,
):
    hd = HEAD_DIM
    count, width = tokens.shape[1:]
    shard = width // n_fsdp
    heads = width // hd
    base = heads // n_ctx
    rest = heads - base * n_ctx
    slots = base + rest
    own_blocks = count // BLOCK
    c = lax.axis_index("ctx")
    f = lax.axis_index("fsdp")

    order = block_order[0]
    inv = jnp.argsort(order).astype(jnp.int32)
    order_own = jnp.concatenate([order, (c * own_blocks)[None]])

    def head_cols(h):
        return jnp.concatenate(
            [
                lax.dynamic_slice(w_attn, (0, part * width + h * hd), (shard, hd))
                for part in range(3)
            ],
            axis=1,
        )

    slot_heads = [c * base + s for s in range(base)] + [n_ctx * base + r for r in range(rest)]
    w_slots = jnp.stack([head_cols(h) for h in slot_heads])
    small = jnp.concatenate([norm_gains, biases], axis=0).astype(F32)
    hidden_cols = w_fc.shape[1] // n_fsdp
    normed_one, qkv, full_proj, fc_parts, w_slots, small = start_call(
        n_ctx, n_fsdp, base, tokens[0], w_slots, small, w_proj, w_fc, 3
    )
    full_proj = full_proj.reshape(width, width)
    qkv = qkv.reshape(slots, n_ctx * own_blocks, BLOCK, 3 * hd)
    gains, shifts = small[:2], small[2:]
    cot = cotangent[0]

    cot_late, _ = lax.optimization_barrier((cot, small))
    cot_all = lax.all_gather(cot_late, "fsdp", axis=0)

    out_own, lse_own = attn_fwd(inv, qkv, base)
    if rest:
        out_rest, lse_rest = rest_fwd(order_own, qkv, base)
    else:
        out_rest = out_own
    attended, mid, normed_two, fc_cols = mix_call(
        n_ctx, n_fsdp, out_own, out_rest, tokens[0], full_proj, small, fc_parts, 6
    )
    fc_cols = fc_cols.reshape(width, hidden_cols)
    rows = tokens[0].astype(F32)

    normed_two_grad, fc_bias_part, out_part, w_out_part, w_fc_part = ffn(
        n_fsdp,
        normed_two,
        cot_all,
        fc_cols,
        w_out,
        fc_bias.astype(F32)[None],
    )
    out_rows = lax.psum_scatter(
        out_part.reshape(n_fsdp * count, width), "fsdp", scatter_dimension=0, tiled=True
    )
    w_out_low = lax.psum(w_out_part, "ctx")

    half, high = shard // 2, half_high(shard)
    core = c % 2
    main = n_ctx * base * hd
    mid_grad, mid_low, turn_sums, d_rest, fc_mine, d_out = turn_call(
        n_ctx, base, normed_two_grad, cot, mid, full_proj, small, w_fc_part, 7
    )

    d_own = attn_bwd(inv, qkv, d_out, out_own, lse_own, base)
    d_own = d_own.reshape(base, n_ctx, count, 3 * hd)
    if rest:
        d_rest = rest_bwd(order_own, qkv, d_rest, out_rest, lse_rest, base)
        d_rest = d_rest.reshape(rest, n_ctx, count, 3 * hd)
        sums = jnp.concatenate(
            [jnp.sum(d.astype(F32), axis=(1, 2)) for d in (d_own, d_rest)], axis=0
        )
    else:
        d_rest = d_own
        sums = jnp.sum(d_own.astype(F32), axis=(1, 2))
    if back_fits(n_ctx, n_fsdp, count, width, slots):
        normed_one_grad, cols_sum, fc_rows = back_call(
            n_ctx, n_fsdp, d_own, d_rest, w_slots, normed_one, fc_mine, 4
        )
        normed_one_grad = normed_one_grad.astype(F32)
    else:
        dqkv = jnp.concatenate([d_own, d_rest])[:slots].reshape(slots, n_ctx * count, 3 * hd)
        one_part = jnp.einsum("hte,hde->td", dqkv, w_slots, preferred_element_type=F32)
        normed_one_grad = lax.psum_scatter(
            one_part.astype(BF16), "ctx", scatter_dimension=0, tiled=True
        ).astype(F32)
        slot_part = jnp.einsum(
            "td,hte->hde",
            normed_one.reshape(n_ctx * count, width),
            dqkv,
            preferred_element_type=F32,
        ).astype(BF16)
        cols_sum = lax.psum_scatter(slot_part, "fsdp", scatter_dimension=1, tiled=True)
        fc_rows = lax.all_to_all(fc_mine, "fsdp", split_axis=0, concat_axis=0, tiled=True)

    xhat_one, rstd_one = norm_parts(rows)
    tokens_grad = (mid_grad + norm_back(xhat_one, rstd_one, gains[0], normed_one_grad)).astype(
        BF16
    )

    def placed(part):
        cols = sums[:, part * hd : (part + 1) * hd]
        line = lax.dynamic_update_slice_in_dim(
            jnp.zeros((width,), F32), cols[:base].reshape(-1), c * base * hd, 0
        )
        return line + jnp.pad(cols[base:].reshape(-1), (main, 0))

    lines = jnp.stack(
        [
            jnp.sum(normed_one_grad * xhat_one, axis=0),
            turn_sums[0],
            jnp.sum(normed_one_grad, axis=0),
            turn_sums[1],
            placed(0),
            placed(2),
            turn_sums[2],
            turn_sums[3],
        ]
    )
    lead = lines.shape[0]
    tail = jnp.pad(fc_bias_part, ((0, 7), (0, width - hidden_cols)))
    lines = jnp.concatenate([lines, tail])

    chips = n_ctx // 2
    fc_rows = fc_rows.reshape(-1, width)
    per_chip = -(-fc_rows.shape[0] // (16 * chips)) * 16
    fc_rows = jnp.pad(fc_rows, ((0, per_chip * chips - fc_rows.shape[0]), (0, 0)))
    fc_rows = fc_rows.reshape(chips, per_chip, width)
    extra = jnp.zeros((16, width), BF16)
    if rest:
        away = lax.dynamic_slice_in_dim(cols_sum[base:], (1 - core) * half, half, 1)
        here = lax.dynamic_slice_in_dim(cols_sum[base:], core * half, half, 1)
        extra = here.astype(F32) + swap(away, "ctx", n_ctx, 1).astype(F32)
        extra = extra.astype(BF16).reshape(-1, width)
        extra_rows = extra.shape[0]
        extra = jnp.pad(extra, ((0, -extra_rows % 16), (0, 0)))
    first, second, third, own_cols, lines = sums_call(
        n_ctx, n_fsdp, fc_rows, cols_sum[:base], extra, attended, mid_low, lines, lead, 5
    )
    out_rows, w_out_low, lines = lax.optimization_barrier((out_rows, w_out_low, lines))
    layer_rows = (mid + (out_rows.astype(F32) + shifts[5])).astype(BF16)
    third = third.reshape(2, -1, width)
    own_cols = own_cols.reshape(n_ctx * base, shard, 3 * hd)
    if rest:
        rest_cols = third[:, high : high + extra_rows].reshape(2, rest, half, 3 * hd)
        rest_cols = rest_cols.transpose(1, 0, 2, 3).reshape(rest, shard, 3 * hd)
    else:
        rest_cols = own_cols
    if hidden_cols == width and chips == n_fsdp:
        w_attn_grad, w_fc_grad, w_proj_grad, w_out_grad = assemble(
            n_fsdp, own_cols, rest_cols, first, second, third, w_out_low, hidden_cols
        )
    else:
        w_fc_low = jnp.concatenate([first, second], axis=2).reshape(2, -1, width)
        w_fc_low = w_fc_low[:, : n_fsdp * high * hidden_cols // width]
        w_fc_low = w_fc_low.reshape(2, n_fsdp, high, hidden_cols)[:, :, :half]
        w_fc_grad = w_fc_low.transpose(0, 2, 1, 3).reshape(shard, n_fsdp * hidden_cols)
        w_fc_grad = w_fc_grad.astype(F32)
        w_proj_grad = third[:, :half].reshape(shard, width).astype(F32)
        cols = jnp.concatenate([own_cols, rest_cols])[: width // hd]
        cols = cols.reshape(width // hd, shard, 3, hd).transpose(1, 2, 0, 3)
        w_attn_grad = cols.reshape(shard, 3 * width).astype(F32)
        w_out_grad = w_out_low.astype(F32)
    fc_bias_grad = lines[lead, :hidden_cols]
    lines = lax.dynamic_slice_in_dim(lines[:lead], f * shard, shard, 1)
    return (
        layer_rows[None],
        tokens_grad[None],
        w_attn_grad,
        w_proj_grad,
        w_fc_grad,
        w_out_grad,
        lines[:2],
        lines[2:],
        fc_bias_grad,
    )


def solution(mesh):
    rows = P("fsdp", "ctx", None)
    weight = P("fsdp", None)
    vectors = P(None, "fsdp")
    return jax.shard_map(
        functools.partial(shards, mesh.shape["ctx"], mesh.shape["fsdp"]),
        mesh=mesh,
        in_specs=(
            rows, weight, weight, weight, weight, weight, vectors, vectors, P("fsdp"), rows,
        ),
        out_specs=(
            rows, rows, weight, weight, weight, weight, vectors, vectors, P("fsdp"),
        ),
        check_vma=False,
    )
```

```python
import functools

import jax
import jax.numpy as jnp
from jax import lax
from jax.experimental import pallas as pl
from jax.experimental.pallas import tpu as pltpu
from jax.sharding import PartitionSpec as P

HEAD_DIM = 64
BLOCK = 128
QROWS = 256
EPS = 1e-05
SCALE = HEAD_DIM ** (-0.5)
F32 = jnp.float32
BF16 = jnp.bfloat16
VMEM_LIMIT = 56 * 1024 * 1024
LAST = (((1,), (1,)), ((), ()))
FIRST = (((0,), (0,)), ((), ()))
MESH = pl.DeviceIdType.MESH
TILE = 256


def dot_last(a, b):
    return lax.dot_general(a, b, LAST, preferred_element_type=F32)


def dot(a, b):
    return jnp.dot(a, b, preferred_element_type=F32)


def dot_first(a, b):
    return lax.dot_general(a, b, FIRST, preferred_element_type=F32)


SHORT = pl.CostEstimate(flops=1, bytes_accessed=1, transcendentals=0)


def norm_parts(rows):
    mean = jnp.mean(rows, axis=-1, keepdims=True)
    cen = rows - mean
    rstd = lax.rsqrt(jnp.mean(cen * cen, axis=-1, keepdims=True) + EPS)
    return cen * rstd, rstd


def norm_back(xhat, rstd, gain, grad):
    dxhat = grad * gain
    return rstd * (
        dxhat
        - jnp.mean(dxhat, axis=-1, keepdims=True)
        - xhat * jnp.mean(dxhat * xhat, axis=-1, keepdims=True)
    )


def flip(place, k, size):
    out = 0
    bit = 1
    while bit < size:
        out = out + (place // bit + k // bit) % 2 * bit
        bit *= 2
    return out

def half_high(shard):
    return -(-(shard // 2) // 16) * 16


def enter(peers):
    barrier = pltpu.get_barrier_semaphore()
    for peer in peers:
        pl.semaphore_signal(barrier, inc=1, device_id=peer, device_id_type=MESH)
    pl.semaphore_wait(barrier, len(peers))

def send(src, dst, send_sem, recv_sem, peer):
    return pltpu.make_async_remote_copy(
        src_ref=src, dst_ref=dst, send_sem=send_sem, recv_sem=recv_sem,
        device_id=peer, device_id_type=MESH)


def ffn_kernel(n, nt_hbm, cot_hbm, wfc_hbm, wout_hbm, bias_ref,
               gsum_ref, fcb_ref, out_hbm, wout_grad_hbm, wfc_grad_hbm,
               cot_ref, wfc_ref, wout_ref, all_ref, act_ref, hg_ref, ag_ref, part_ref, got_ref, stage_d, stage_h,
               s1, r1, s2, r2, local):
    c = lax.axis_index("ctx")
    f = lax.axis_index("fsdp")
    rows, width = nt_hbm.shape
    enter([(c, flip(f, k, n)) for k in range(1, n)])

    def rows_out(k):
        return send(nt_hbm, all_ref.at[f], s1.at[k], r1.at[k], (c, flip(f, k, n)))

    def grad_back(k):
        other = flip(f, k, n)
        return send(part_ref.at[other], got_ref.at[k], s2.at[k], r2.at[k], (c, other))

    near = [k for k in range(1, n) if k & (k - 1) == 0]
    far = [k for k in range(1, n) if k not in near]
    for k in near:
        rows_out(k).start()
    loads = [
        pltpu.make_async_copy(nt_hbm, all_ref.at[f], local.at[0]),
        pltpu.make_async_copy(wout_hbm, wout_ref, local.at[1]),
        pltpu.make_async_copy(cot_hbm, cot_ref, local.at[2]),
        pltpu.make_async_copy(wfc_hbm, wfc_ref, local.at[3]),
    ]
    for load in loads:
        load.start()
    fcb_ref[...] = jnp.zeros_like(fcb_ref)
    loads[1].wait()
    loads[2].wait()

    def active_grad(k, carry):
        ag_ref[k] = dot_last(cot_ref[k], wout_ref[...])
        return carry

    lax.fori_loop(0, n, active_grad, 0)
    for k in far:
        rows_out(k).start()
    loads[0].wait()
    loads[3].wait()

    def chunk(k, carry):
        src = flip(f, k, n)

        @pl.when(k > 0)
        def _():
            rows_out(k).wait_recv()

        hidden = dot(all_ref[src], wfc_ref[...]) + bias_ref[...]
        square = hidden * hidden
        tanh = jnp.tanh(0.7978845608028654 * (hidden + 0.044715 * square * hidden))
        act_ref[src] = (0.5 * hidden * (1.0 + tanh)).astype(BF16)
        slope = 0.5 * (1.0 + tanh) + 0.5 * hidden * (1.0 - tanh * tanh) * 0.7978845608028654 * (
            1.0 + 3.0 * 0.044715 * square
        )
        grad = (ag_ref[src] * slope).astype(BF16)
        hg_ref[src] = grad
        fcb_ref[...] += jnp.sum(grad.astype(F32), axis=0, keepdims=True)
        part_ref[src] = dot_last(grad, wfc_ref[...]).astype(BF16)

        @pl.when(k > 0)
        def _():
            grad_back(k).start()

        return carry

    lax.fori_loop(0, n, chunk, 0)

    def grads(left_ref, right_ref, tiles, stage_ref, base):
        right = right_ref[...].reshape(n * rows, right_ref.shape[2])
        copies = []
        for i, (lo, size, sent, dst) in enumerate(tiles):
            slot = i % 2
            if i >= 2:
                copies[i - 2].wait()
            left = left_ref[:, :, lo : lo + size].reshape(n * rows, size)
            stage_ref[slot, :size] = dot_first(left, right).astype(BF16)
            copies.append(
                pltpu.make_async_copy(stage_ref.at[slot, :sent], dst, local.at[base + slot])
            )
            copies[-1].start()
        for copy in copies[-2:]:
            copy.wait()

    half, high = width // n // 2, wfc_grad_hbm.shape[2]
    if half < high:
        stage_h[:, half:high] = jnp.zeros((2, high - half, stage_h.shape[2]), BF16)
    wide = act_ref.shape[2]
    sizes = [(lo, min(TILE, wide - lo)) for lo in range(0, wide, TILE)]
    grads(
        act_ref,
        cot_ref,
        [(lo, size, size, wout_grad_hbm.at[lo : lo + size]) for lo, size in sizes],
        stage_d,
        4,
    )
    grads(
        all_ref,
        hg_ref,
        [
            ((2 * j + h) * half, half, high, wfc_grad_hbm.at[h, j])
            for j in range(n)
            for h in range(2)
        ],
        stage_h,
        6,
    )

    def out_copy(k):
        return pltpu.make_async_copy(
            stage_d.at[k % 2, :rows], out_hbm.at[k], local.at[4 + k % 2]
        )

    for k in range(n):
        if k >= 2:
            out_copy(k - 2).wait()
        stage_d[k % 2, :rows] = dot(act_ref[k], wout_ref[...]).astype(BF16)
        out_copy(k).start()

    gsum_ref[...] = part_ref[f].astype(F32)
    for k in near + far:
        grad_back(k).wait_recv()
        gsum_ref[...] += got_ref[k].astype(F32)
    for k in range(1, n):
        rows_out(k).wait_send()
        grad_back(k).wait_send()
    for k in range(max(0, n - 2), n):
        out_copy(k).wait()


def ffn(n, nt, cot, wfc, wout, bias, cid=1):
    m, d = nt.shape
    h = wfc.shape[1]
    vm = pl.BlockSpec(memory_space=pltpu.VMEM)
    anym = pl.BlockSpec(memory_space=pl.ANY)
    return pl.pallas_call(
        functools.partial(ffn_kernel, n),
        in_specs=[anym] * 4 + [vm],
        out_specs=[vm, vm] + [anym] * 3,
        out_shape=[
            jax.ShapeDtypeStruct((m, d), F32),
            jax.ShapeDtypeStruct((1, h), F32),
            jax.ShapeDtypeStruct((n, m, d), BF16),
            jax.ShapeDtypeStruct((h, d), BF16),
            jax.ShapeDtypeStruct((2, n, half_high(d // n), h), BF16),
        ],
        scratch_shapes=[
            pltpu.VMEM((n, m, d), BF16),
            pltpu.VMEM((d, h), BF16),
            pltpu.VMEM((h, d), BF16),
            pltpu.VMEM((n, m, d), BF16),
            pltpu.VMEM((n, m, h), BF16),
            pltpu.VMEM((n, m, h), BF16),
            pltpu.VMEM((n, m, h), F32),
            pltpu.VMEM((n, m, d), BF16),
            pltpu.VMEM((n, m, d), BF16),
            pltpu.VMEM((2, max(TILE, m), d), BF16),
            pltpu.VMEM((2, half_high(d // n), h), BF16),
        ]
        + [pltpu.SemaphoreType.DMA((n,))] * 4
        + [pltpu.SemaphoreType.DMA((8,))],
        compiler_params=pltpu.CompilerParams(
            collective_id=cid, has_side_effects=True, vmem_limit_bytes=60 * 1024 * 1024
        ),
        cost_estimate=SHORT,
        name="feed_forward",
    )(nt, cot, wfc, wout, bias)


def weight_shares(c, f, core, n_fsdp, shard, source, dst, ss, rs):
    cut = shard // 32 * 16 if shard % 16 == 0 else 0
    shares = ((0, cut), (cut, shard)) if cut else ((0, shard), (0, shard))
    twin_id = (c + 1 - 2 * core, f)

    def copy(share, k, onward):
        lo, hi = share
        other = flip(f, k, n_fsdp)
        if onward:
            part = dst.at[other, lo:hi]
            return send(part, part, ss.at[1, k], rs.at[1, k], twin_id)
        return send(source(k).at[lo:hi], dst.at[f, lo:hi], ss.at[0, k], rs.at[0, k], (c, other))

    def by_core(act):
        for h in range(2):

            @pl.when(core == h)
            def _(h=h):
                for k in range(1, n_fsdp):
                    act(shares[h], shares[1 - h], k)

    def start(mine, theirs, k):
        copy(mine, k, False).start()

    def onward(mine, theirs, k):
        copy(mine, k, False).wait_recv()
        if cut:
            copy(mine, k, True).start()

    def done(mine, theirs, k):
        if cut:
            copy(theirs, k, True).wait_recv()
            copy(mine, k, True).wait_send()
        copy(mine, k, False).wait_send()

    return tuple(functools.partial(by_core, act) for act in (start, onward, done))


def start_kernel(
    n_ctx,
    n_fsdp,
    base,
    tok_hbm,
    w_hbm,
    small_ref,
    proj_hbm,
    fc_hbm,
    n_hbm,
    qkv_hbm,
    proj_all,
    fc_parts,
    w_ref,
    lines_ref,
    n_ref,
    qkv_ref,
    fc_ref,
    fc_cut,
    x_ref,
    wg_ref,
    sg_ref,
    tok_recv,
    right_sem,
    left_sem,
    twin_sem,
    w_send,
    w_recv,
    s_send,
    s_recv,
    proj_send,
    proj_recv,
    local,
):
    c = lax.axis_index("ctx")
    f = lax.axis_index("fsdp")
    chips = n_ctx // 2
    chip, core = c // 2, c % 2
    slots, width, cols = w_ref.shape
    shard = width // n_fsdp
    hd = HEAD_DIM
    enter(
        [(lax.rem(c + i, n_ctx), f) for i in range(1, n_ctx)]
        + [(c, flip(f, k, n_fsdp)) for k in range(1, n_fsdp)]
    )

    def block(at, same):
        return 2 * at + (core if same else 1 - core)

    cut = x_ref.shape[1] // 2

    def part(ref, h):
        return ref.at[pl.ds(h * cut, cut)]

    def hop(step, to_right, from_own, h):
        origin = block(chip - step if to_right else chip + step, True)
        src = tok_hbm if from_own else x_ref.at[origin]
        sem = (right_sem if to_right else left_sem).at[step, h]
        peer = (c + 2 if to_right else c - 2, f)
        dst = part(x_ref.at[origin], h)
        return send(part(src, h), dst, sem, tok_recv.at[origin, h], peer)

    def twin(at, from_own, h):
        origin = block(at, True)
        src = tok_hbm if from_own else x_ref.at[origin]
        dst = part(x_ref.at[origin], h)
        return send(
            part(src, h),
            dst,
            twin_sem.at[at, h],
            tok_recv.at[origin, h],
            (block(chip, False), f),
        )

    def w_copy(k):
        return send(w_hbm, wg_ref.at[f], w_send.at[k], w_recv.at[k], (c, flip(f, k, n_fsdp)))

    def s_copy(k):
        return send(small_ref, sg_ref.at[f], s_send.at[k], s_recv.at[k], (c, flip(f, k, n_fsdp)))

    weights_start, weights_onward, weights_done = weight_shares(
        c, f, core, n_fsdp, shard, lambda k: proj_hbm, proj_all, proj_send, proj_recv
    )

    for k in range(1, n_fsdp):
        s_copy(k).start()

    for h in range(2):

        @pl.when(chip < chips - 1)
        def _(h=h):
            hop(0, True, True, h).start()

        @pl.when(chip > 0)
        def _(h=h):
            hop(0, False, True, h).start()

    for k in range(1, n_fsdp):
        w_copy(k).start()
    for h in range(2):
        twin(chip, True, h).start()
    own_x = pltpu.make_async_copy(tok_hbm, x_ref.at[c], local.at[0])
    own_w = pltpu.make_async_copy(w_hbm, wg_ref.at[f], local.at[1])
    own_proj = pltpu.make_async_copy(proj_hbm, proj_all.at[f], local.at[2])
    load_fc = pltpu.make_async_copy(fc_hbm, fc_ref, local.at[3])
    for copy in (own_x, own_w, own_proj, load_fc):
        copy.start()
    sg_ref[f] = small_ref[...]
    for k in range(1, n_fsdp):
        s_copy(k).wait_recv()
    for j in range(n_fsdp):
        lines_ref[:, j * shard : (j + 1) * shard] = sg_ref[j]
    main = n_ctx * base * hd
    row_id = lax.broadcasted_iota(jnp.int32, (width, slots * hd), 0)
    col_id = lax.broadcasted_iota(jnp.int32, (width, slots * hd), 1)
    wanted = jnp.where(col_id < base * hd, c * base * hd + col_id, main + col_id - base * hd)
    picked = dot(lines_ref[...].astype(BF16), (row_id == wanted).astype(BF16))
    zero = jnp.zeros((1, hd), F32)
    bias = [
        jnp.concatenate(
            [picked[4:5, s * hd : (s + 1) * hd], zero, picked[5:6, s * hd : (s + 1) * hd]], axis=1
        )
        for s in range(slots)
    ]
    own_w.wait()
    own_x.wait()
    for k in range(1, n_fsdp):
        w_copy(k).wait_recv()
    weights_start()
    for j in range(n_fsdp):
        w_ref[:, j * shard : (j + 1) * shard, :] = wg_ref[j]

    load_fc.wait()
    hidden = fc_cut.shape[2]
    cuts = []
    for j in range(n_fsdp):
        if j >= 2:
            cuts[j - 2].wait()
        fc_cut[j % 2] = fc_ref[:, j * hidden : (j + 1) * hidden]
        cuts.append(pltpu.make_async_copy(fc_cut.at[j % 2], fc_parts.at[j], local.at[4 + j % 2]))
        cuts[-1].start()

    def results(origin):
        return (
            pltpu.make_async_copy(n_ref, n_hbm.at[origin], local.at[0]),
            pltpu.make_async_copy(qkv_ref, qkv_hbm.at[:, origin], local.at[1]),
        )

    def project(at, same, first=False):
        origin = block(at, same)
        rows = x_ref[origin].astype(F32)
        mean = jnp.mean(rows, axis=1, keepdims=True)
        cen = rows - mean
        var = jnp.mean(cen * cen, axis=1, keepdims=True)
        normed = cen * lax.rsqrt(var + EPS) * lines_ref[0:1] + lines_ref[2:3]
        normed = normed.astype(BF16)

        @pl.when(jnp.logical_not(first))
        def _():
            for copy in results(origin):
                copy.wait()

        n_ref[...] = normed
        for s in range(slots):
            qkv_ref[s] = (dot(normed, w_ref[s]) + bias[s]).astype(BF16)
        for copy in results(origin):
            copy.start()

    def arrived(at, same, h):
        origin = block(at, same)
        ref = part(x_ref.at[origin], h)
        pltpu.make_async_copy(ref, ref, tok_recv.at[origin, h]).wait()

    def step(s, carry):
        for h in range(2):

            @pl.when((s > 0) & (chip - s >= 0))
            def _(h=h):
                arrived(chip - s, True, h)

                @pl.when(chip < chips - 1)
                def _():
                    hop(s, True, False, h).start()

                twin(chip - s, False, h).start()

            @pl.when((s > 0) & (chip + s < chips))
            def _(h=h):
                arrived(chip + s, True, h)

                @pl.when(chip > 0)
                def _():
                    hop(s, False, False, h).start()

                twin(chip + s, False, h).start()

        @pl.when(s == chips - 1)
        def _():
            weights_onward()

        @pl.when(chip - s >= 0)
        def _():
            project(chip - s, True, s == 0)

        @pl.when((s > 0) & (chip + s < chips))
        def _():
            project(chip + s, True)

        @pl.when(chip - s >= 0)
        def _():
            for h in range(2):
                arrived(chip - s, False, h)
            project(chip - s, False)

        @pl.when((s > 0) & (chip + s < chips))
        def _():
            for h in range(2):
                arrived(chip + s, False, h)
            project(chip + s, False)

        return carry

    lax.fori_loop(0, chips, step, 0)
    for copy in results(c):
        copy.wait()
    own_proj.wait()
    for copy in cuts[-2:]:
        copy.wait()

    for s in range(chips):
        for h in range(2):
            if s < chips - 1:

                @pl.when((chip - s >= 0) & (chip < chips - 1))
                def _(s=s, h=h):
                    hop(s, True, False, h).wait_send()

                @pl.when((chip + s < chips) & (chip > 0))
                def _(s=s, h=h):
                    hop(s, False, False, h).wait_send()

            twin(s, False, h).wait_send()
    for k in range(1, n_fsdp):
        w_copy(k).wait_send()
        s_copy(k).wait_send()
    weights_done()


def start_call(n_ctx, n_fsdp, base, tok, w_slots, small, w_proj, w_fc, cid):
    count, width = tok.shape
    slots, shard, cols = w_slots.shape
    hidden = w_fc.shape[1] // n_fsdp
    vm = pl.BlockSpec(memory_space=pltpu.VMEM)
    anym = pl.BlockSpec(memory_space=pl.ANY)
    dma = pltpu.SemaphoreType.DMA
    return pl.pallas_call(
        functools.partial(start_kernel, n_ctx, n_fsdp, base),
        in_specs=[anym, anym, vm, anym, anym],
        out_specs=[anym, anym, anym, anym, vm, vm],
        out_shape=[
            jax.ShapeDtypeStruct((n_ctx, count, width), BF16),
            jax.ShapeDtypeStruct((slots, n_ctx, count, cols), BF16),
            jax.ShapeDtypeStruct((n_fsdp,) + w_proj.shape, BF16),
            jax.ShapeDtypeStruct((n_fsdp, shard, hidden), BF16),
            jax.ShapeDtypeStruct((slots, width, cols), BF16),
            jax.ShapeDtypeStruct((small.shape[0], width), F32),
        ],
        scratch_shapes=[
            pltpu.VMEM((count, width), BF16),
            pltpu.VMEM((slots, count, cols), BF16),
            pltpu.VMEM(w_fc.shape, BF16),
            pltpu.VMEM((2, shard, hidden), BF16),
            pltpu.VMEM((n_ctx, count, width), BF16),
            pltpu.VMEM((n_fsdp, slots, shard, cols), BF16),
            pltpu.VMEM((n_fsdp,) + small.shape, F32),
            dma((n_ctx, 2)),
            dma((n_ctx // 2, 2)),
            dma((n_ctx // 2, 2)),
            dma((n_ctx // 2, 2)),
            dma((n_fsdp,)),
            dma((n_fsdp,)),
            dma((n_fsdp,)),
            dma((n_fsdp,)),
            dma((2, n_fsdp)),
            dma((2, n_fsdp)),
            dma((6,)),
        ],
        compiler_params=pltpu.CompilerParams(
            collective_id=cid, has_side_effects=True, vmem_limit_bytes=VMEM_LIMIT
        ),
        cost_estimate=SHORT,
        name="tokens_qkv",
    )(tok, w_slots, small, w_proj, w_fc)


def causal_scores(k, q_rows, start):
    scores = dot_last(k, q_rows)
    keep = start
    tail = scores[keep:]
    key_id = lax.broadcasted_iota(jnp.int32, tail.shape, 0)
    query_id = lax.broadcasted_iota(jnp.int32, tail.shape, 1)
    tail = jnp.where(key_id <= query_id, tail, -1e30)
    if keep == 0:
        return tail
    return jnp.concatenate([scores[:keep], tail], axis=0)


def soft(scores, v_t):
    top = jnp.max(scores, axis=0, keepdims=True)
    weights = jnp.exp(scores - top)
    total = jnp.sum(weights, axis=0, keepdims=True)
    out = dot(v_t, weights.astype(BF16)) / total
    return out, top + jnp.log(total)


def causal(inv_ref, x_ref):
    return jnp.concatenate([x_ref[0, inv_ref[i]] for i in range(x_ref.shape[1])], axis=0)


def attn_fwd_kernel(inv_ref, x_ref, o_ref, l_ref):
    rows = l_ref.shape[2]
    hd = HEAD_DIM
    x = causal(inv_ref, x_ref)
    q = x[:, :hd] * BF16(SCALE)
    k = x[:, hd : 2 * hd]
    v_t = x[:, 2 * hd :].T
    for i in range(rows // QROWS):
        lo, hi = i * QROWS, (i + 1) * QROWS
        out, lse = soft(causal_scores(k[:hi], q[lo:hi], lo), v_t[:, :hi])
        l_ref[0, :, lo:hi] = lse
        out = out.astype(BF16)
        for b in range(QROWS // BLOCK):
            o_ref[inv_ref[2 * i + b]] = out[:, b * BLOCK : (b + 1) * BLOCK]


def attn_fwd(inv, qkv, heads):
    blocks, _, cols = qkv.shape[1:]
    rows = blocks * BLOCK
    return pl.pallas_call(
        attn_fwd_kernel,
        grid_spec=pltpu.PrefetchScalarGridSpec(
            num_scalar_prefetch=1,
            grid=(heads,),
            in_specs=[pl.BlockSpec((1, blocks, BLOCK, cols), lambda h, inv: (h, 0, 0, 0))],
            out_specs=[
                pl.BlockSpec((blocks, HEAD_DIM, BLOCK), lambda h, inv: (0, h, 0)),
                pl.BlockSpec((1, 1, rows), lambda h, inv: (h, 0, 0)),
            ],
        ),
        out_shape=[
            jax.ShapeDtypeStruct((blocks, heads * HEAD_DIM, BLOCK), BF16),
            jax.ShapeDtypeStruct((heads, 1, rows), F32),
        ],
        compiler_params=pltpu.CompilerParams(vmem_limit_bytes=VMEM_LIMIT),
        cost_estimate=SHORT,
        name="attn_fwd",
    )(inv, qkv)


def attn_bwd_kernel(inv_ref, x_ref, do_ref, o_ref, l_ref, dx_ref, dk_acc, dv_acc):
    rows = l_ref.shape[2]
    hd = HEAD_DIM
    x = causal(inv_ref, x_ref)
    q = x[:, :hd] * BF16(SCALE)
    k = x[:, hd : 2 * hd]
    v = x[:, 2 * hd :]
    k_t = k.T
    dk_acc[...] = jnp.zeros_like(dk_acc)
    dv_acc[...] = jnp.zeros_like(dv_acc)
    for i in range(rows // QROWS):
        lo, hi = i * QROWS, (i + 1) * QROWS
        ids = [inv_ref[2 * i + b] for b in range(QROWS // BLOCK)]
        do_t = jnp.concatenate([do_ref[b] for b in ids], axis=1)
        o_t = jnp.concatenate([o_ref[b] for b in ids], axis=1)
        inner = jnp.sum(do_t.astype(F32) * o_t.astype(F32), axis=0, keepdims=True)
        probs = jnp.exp(causal_scores(k[:hi], q[lo:hi], lo) - l_ref[0, :, lo:hi])
        dprobs = dot(v[:hi], do_t)
        dscores = (probs * (dprobs - inner)).astype(BF16)
        dv_acc[:hi] += dot_last(probs.astype(BF16), do_t)
        dk_acc[:hi] += dot(dscores, q[lo:hi])
        dq = (dot(k_t[:, :hi], dscores) * SCALE).T
        for n, b in enumerate(ids):
            dx_ref[0, b, :, :hd] = dq[n * BLOCK : (n + 1) * BLOCK].astype(BF16)
    for i in range(rows // BLOCK):
        lo, hi = i * BLOCK, (i + 1) * BLOCK
        dx_ref[0, inv_ref[i], :, hd : 2 * hd] = dk_acc[lo:hi].astype(BF16)
        dx_ref[0, inv_ref[i], :, 2 * hd :] = dv_acc[lo:hi].astype(BF16)


def attn_bwd(inv, qkv, d_out, out, lse, heads):
    blocks, _, cols = qkv.shape[1:]
    rows = blocks * BLOCK
    whole = pl.BlockSpec((1, blocks, BLOCK, cols), lambda h, inv: (h, 0, 0, 0))
    feat = pl.BlockSpec((blocks, HEAD_DIM, BLOCK), lambda h, inv: (0, h, 0))
    return pl.pallas_call(
        attn_bwd_kernel,
        grid_spec=pltpu.PrefetchScalarGridSpec(
            num_scalar_prefetch=1,
            grid=(heads,),
            in_specs=[
                whole,
                feat,
                feat,
                pl.BlockSpec((1, 1, rows), lambda h, inv: (h, 0, 0)),
            ],
            out_specs=whole,
            scratch_shapes=[pltpu.VMEM((rows, HEAD_DIM), F32)] * 2,
        ),
        out_shape=jax.ShapeDtypeStruct((heads, blocks, BLOCK, cols), BF16),
        compiler_params=pltpu.CompilerParams(vmem_limit_bytes=VMEM_LIMIT),
        cost_estimate=pl.CostEstimate(
            flops=24 * 10**9, bytes_accessed=24 * 10**6, transcendentals=0
        ),
        name="attn_bwd",
    )(inv, qkv, d_out, out, lse)


def own_scores(order_ref, x_ref, k):
    hd = HEAD_DIM
    blocks = x_ref.shape[1]
    first = order_ref[blocks]
    q = jnp.concatenate([x_ref[0, first], x_ref[0, first + 1]], axis=0)[:, :hd]
    q = q * BF16(SCALE)
    scores = dot_last(k, q)
    row = lax.broadcasted_iota(jnp.int32, (BLOCK, 1), 0)
    key_place = jnp.concatenate([order_ref[b] * BLOCK + row for b in range(blocks)], axis=0)
    lane = lax.broadcasted_iota(jnp.int32, (1, 2 * BLOCK), 1)
    low, high = order_ref[order_ref[blocks]], order_ref[order_ref[blocks] + 1]
    place = jnp.where(lane < BLOCK, low * BLOCK + lane, (high - 1) * BLOCK + lane)
    return q, first, jnp.where(key_place <= place, scores, -1e30)


def rest_fwd_kernel(order_ref, x_ref, o_ref, l_ref):
    hd = HEAD_DIM
    x = x_ref[0].reshape(-1, 3 * hd)
    _, _, scores = own_scores(order_ref, x_ref, x[:, hd : 2 * hd])
    out, lse = soft(scores, x[:, 2 * hd :].T)
    o_ref[0] = out.astype(BF16)
    l_ref[0] = lse


def rest_fwd(order, qkv, base):
    slots, blocks, _, cols = qkv.shape
    rest = slots - base
    return pl.pallas_call(
        rest_fwd_kernel,
        grid_spec=pltpu.PrefetchScalarGridSpec(
            num_scalar_prefetch=1,
            grid=(rest,),
            in_specs=[
                pl.BlockSpec((1, blocks, BLOCK, cols), lambda h, o: (base + h, 0, 0, 0))
            ],
            out_specs=[
                pl.BlockSpec((1, HEAD_DIM, QROWS), lambda h, o: (h, 0, 0)),
                pl.BlockSpec((1, 1, QROWS), lambda h, o: (h, 0, 0)),
            ],
        ),
        out_shape=[
            jax.ShapeDtypeStruct((rest, HEAD_DIM, QROWS), BF16),
            jax.ShapeDtypeStruct((rest, 1, QROWS), F32),
        ],
        compiler_params=pltpu.CompilerParams(vmem_limit_bytes=VMEM_LIMIT),
        cost_estimate=SHORT,
        name="rest_fwd",
    )(order, qkv)


def rest_bwd_kernel(order_ref, x_ref, do_ref, o_ref, l_ref, dx_ref):
    hd = HEAD_DIM
    x = x_ref[0].reshape(-1, 3 * hd)
    blocks = x_ref.shape[1]
    k = x[:, hd : 2 * hd]
    q, first, scores = own_scores(order_ref, x_ref, k)
    do_t = do_ref[0]
    inner = jnp.sum(do_t.astype(F32) * o_ref[0].astype(F32), axis=0, keepdims=True)
    probs = jnp.exp(scores - l_ref[0])
    dprobs = dot(x[:, 2 * hd :], do_t)
    dscores = (probs * (dprobs - inner)).astype(BF16)
    dv = dot_last(probs.astype(BF16), do_t).astype(BF16)
    dk = dot(dscores, q).astype(BF16)
    dq = (dot(k.T, dscores) * SCALE).T.astype(BF16)
    dx_ref[0, :, :, 2 * hd :] = dv.reshape(blocks, BLOCK, hd)
    dx_ref[0, :, :, hd : 2 * hd] = dk.reshape(blocks, BLOCK, hd)
    dx_ref[0, :, :, :hd] = jnp.zeros((blocks, BLOCK, hd), BF16)
    for b in range(2):
        dx_ref[0, first + b, :, :hd] = dq[b * BLOCK : (b + 1) * BLOCK]


def rest_bwd(order, qkv, d_out, out, lse, base):
    slots, blocks, _, cols = qkv.shape
    rest = slots - base
    feat = pl.BlockSpec((1, HEAD_DIM, QROWS), lambda h, o: (h, 0, 0))
    return pl.pallas_call(
        rest_bwd_kernel,
        grid_spec=pltpu.PrefetchScalarGridSpec(
            num_scalar_prefetch=1,
            grid=(rest,),
            in_specs=[
                pl.BlockSpec((1, blocks, BLOCK, cols), lambda h, o: (base + h, 0, 0, 0)),
                feat,
                feat,
                pl.BlockSpec((1, 1, QROWS), lambda h, o: (h, 0, 0)),
            ],
            out_specs=pl.BlockSpec((1, blocks, BLOCK, cols), lambda h, o: (h, 0, 0, 0)),
        ),
        out_shape=jax.ShapeDtypeStruct((rest, blocks, BLOCK, cols), BF16),
        compiler_params=pltpu.CompilerParams(vmem_limit_bytes=VMEM_LIMIT),
        cost_estimate=SHORT,
        name="rest_bwd",
    )(order, qkv, d_out, out, lse)


def mix_kernel(
    n_ctx,
    n_fsdp,
    out_hbm,
    rest_ref,
    tok_ref,
    proj_ref,
    lines_ref,
    fc_parts,
    att_ref,
    mid_ref,
    n_ref,
    fc_all,
    got_ref,
    out_send,
    out_recv,
    fc_send,
    fc_recv,
    local,
):
    c = lax.axis_index("ctx")
    f = lax.axis_index("fsdp")
    core = c % 2
    width = tok_ref.shape[1]
    shard = width // n_fsdp
    blocks, feats = got_ref.shape[1], got_ref.shape[2]
    enter(
        [(lax.rem(c + i, n_ctx), f) for i in range(1, n_ctx)]
        + [(c, flip(f, k, n_fsdp)) for k in range(1, n_fsdp)]
    )

    def out_copy(i):
        to = lax.rem(c + i, n_ctx)
        return send(
            out_hbm.at[pl.ds(to * blocks, blocks)],
            got_ref.at[c],
            out_send.at[i],
            out_recv.at[i],
            (to, f),
        )

    for i in range(n_ctx - 1, 0, -1):
        out_copy(i).start()
    weights_start, weights_onward, weights_done = weight_shares(
        c,
        f,
        core,
        n_fsdp,
        shard,
        lambda k: fc_parts.at[flip(f, k, n_fsdp)],
        fc_all,
        fc_send,
        fc_recv,
    )
    weights_start()
    own = pltpu.make_async_copy(
        out_hbm.at[pl.ds(c * blocks, blocks)], got_ref.at[c], local.at[0]
    )
    own_fc = pltpu.make_async_copy(fc_parts.at[f], fc_all.at[f], local.at[1])
    own.start()
    own_fc.start()
    main = n_ctx * feats
    if main < width:
        att_ref[:, main:] = rest_ref[...].reshape(width - main, -1).T
    own.wait()
    for i in range(1, n_ctx):
        out_copy(i).wait_recv()
    for src in range(n_ctx):
        block = jnp.concatenate([got_ref[src, b] for b in range(blocks)], axis=1)
        att_ref[:, src * feats : (src + 1) * feats] = block.T
    mid = tok_ref[...].astype(F32) + (dot(att_ref[...], proj_ref[...]) + lines_ref[6:7])
    mid_ref[...] = mid
    cen = mid - jnp.mean(mid, axis=1, keepdims=True)
    var = jnp.mean(cen * cen, axis=1, keepdims=True)
    n_ref[...] = (cen * lax.rsqrt(var + EPS) * lines_ref[1:2] + lines_ref[3:4]).astype(BF16)
    weights_onward()
    own_fc.wait()
    for i in range(1, n_ctx):
        out_copy(i).wait_send()
    weights_done()


def mix_call(n_ctx, n_fsdp, out_own, out_rest, tok, proj, lines, fc_parts, cid):
    count, width = tok.shape
    vm = pl.BlockSpec(memory_space=pltpu.VMEM)
    anym = pl.BlockSpec(memory_space=pl.ANY)
    dma = pltpu.SemaphoreType.DMA
    return pl.pallas_call(
        functools.partial(mix_kernel, n_ctx, n_fsdp),
        in_specs=[anym, vm, vm, vm, vm, anym],
        out_specs=[vm, vm, vm, anym],
        out_shape=[
            jax.ShapeDtypeStruct((count, width), BF16),
            jax.ShapeDtypeStruct((count, width), F32),
            jax.ShapeDtypeStruct((count, width), BF16),
            jax.ShapeDtypeStruct(fc_parts.shape, BF16),
        ],
        scratch_shapes=[
            pltpu.VMEM((n_ctx, out_own.shape[0] // n_ctx) + out_own.shape[1:], BF16),
            dma((n_ctx,)),
            dma((n_ctx,)),
            dma((2, n_fsdp)),
            dma((2, n_fsdp)),
            dma((2,)),
        ],
        compiler_params=pltpu.CompilerParams(
            collective_id=cid, has_side_effects=True, vmem_limit_bytes=VMEM_LIMIT
        ),
        cost_estimate=SHORT,
        name="mix_rows",
    )(out_own, out_rest, tok, proj, lines, fc_parts)


def turn_kernel(
    n_ctx,
    gsum_ref,
    cot_ref,
    mid_ref,
    proj_ref,
    lines_ref,
    fc_hbm,
    grad_ref,
    low_ref,
    sums_ref,
    rest_ref,
    fc_ref,
    got_hbm,
    out_ref,
    pair_in,
    out_send,
    out_recv,
    pair_sem,
    local,
):
    c = lax.axis_index("ctx")
    f = lax.axis_index("fsdp")
    core = c % 2
    width = mid_ref.shape[1]
    blocks, feats = out_ref.shape[0] // n_ctx, out_ref.shape[1]
    enter([(lax.rem(c + i, n_ctx), f) for i in range(1, n_ctx)])
    pair = send(fc_hbm.at[1 - core], pair_in, pair_sem.at[0], pair_sem.at[1], (c + 1 - 2 * core, f))
    pair.start()
    own_fc = pltpu.make_async_copy(fc_hbm.at[core], fc_ref, local.at[0])
    own_fc.start()

    xhat, rstd = norm_parts(mid_ref[...])
    grad = gsum_ref[...]
    cot = cot_ref[...].astype(F32)
    mid_grad = cot + norm_back(xhat, rstd, lines_ref[1:2], grad)
    grad_ref[...] = mid_grad
    low = mid_grad.astype(BF16)
    low_ref[...] = low
    att_t = dot_last(low, proj_ref[...]).astype(BF16).T
    for to in range(n_ctx):
        for b in range(blocks):
            out_ref[to * blocks + b] = att_t[
                to * feats : (to + 1) * feats, b * BLOCK : (b + 1) * BLOCK
            ]

    def out_copy(i):
        to = lax.rem(c + i, n_ctx)
        return send(
            out_ref.at[pl.ds(to * blocks, blocks)],
            got_hbm.at[pl.ds(c * blocks, blocks)],
            out_send.at[i],
            out_recv.at[i],
            (to, f),
        )

    for i in range(n_ctx - 1, 0, -1):
        out_copy(i).start()
    own = pltpu.make_async_copy(
        out_ref.at[pl.ds(c * blocks, blocks)], got_hbm.at[pl.ds(c * blocks, blocks)], local.at[1]
    )
    own.start()
    main = n_ctx * feats
    if main < width:
        rest_ref[...] = att_t[main:].reshape(rest_ref.shape)
    else:
        rest_ref[...] = jnp.zeros(rest_ref.shape, BF16)
    for r, line in enumerate((grad * xhat, grad, low.astype(F32), cot)):
        sums_ref[r : r + 1] = jnp.sum(line, axis=0, keepdims=True)
    sums_ref[4:] = jnp.zeros((4, width), F32)
    own_fc.wait()
    pair.wait()

    def add(j, carry):
        fc_ref[j] = (fc_ref[j].astype(F32) + pair_in[j].astype(F32)).astype(BF16)
        return carry

    lax.fori_loop(0, fc_ref.shape[0], add, 0)
    own.wait()
    for i in range(1, n_ctx):
        out_copy(i).wait()


def turn_call(n_ctx, base, gsum, cot, mid, proj, lines, fc_part, cid):
    count, width = mid.shape
    heads = width // HEAD_DIM
    rest = max(heads - base * n_ctx, 1)
    out = (n_ctx * count // BLOCK, base * HEAD_DIM, BLOCK)
    vm = pl.BlockSpec(memory_space=pltpu.VMEM)
    anym = pl.BlockSpec(memory_space=pl.ANY)
    dma = pltpu.SemaphoreType.DMA
    return pl.pallas_call(
        functools.partial(turn_kernel, n_ctx),
        in_specs=[vm] * 5 + [anym],
        out_specs=[vm] * 5 + [anym],
        out_shape=[
            jax.ShapeDtypeStruct((count, width), F32),
            jax.ShapeDtypeStruct((count, width), BF16),
            jax.ShapeDtypeStruct((8, width), F32),
            jax.ShapeDtypeStruct((rest, HEAD_DIM, count), BF16),
            jax.ShapeDtypeStruct(fc_part.shape[1:], BF16),
            jax.ShapeDtypeStruct(out, BF16),
        ],
        scratch_shapes=[
            pltpu.VMEM(out, BF16),
            pltpu.VMEM(fc_part.shape[1:], BF16),
            dma((n_ctx,)),
            dma((n_ctx,)),
            dma((2,)),
            dma((2,)),
        ],
        compiler_params=pltpu.CompilerParams(
            collective_id=cid, has_side_effects=True, vmem_limit_bytes=VMEM_LIMIT
        ),
        cost_estimate=SHORT,
        name="turn_rows",
    )(gsum, cot, mid, proj, lines, fc_part)


def far_first(i, chips):
    return (i % 2) * (i // 2) + (1 - i % 2) * (chips - 1 - i // 2)


def line_sum(chip, chips, f, core, part, came, sems, ready=None):
    sent, left_sem, right_sem = sems

    def to_right(d):
        return send(
            part.at[d], came.at[d], sent.at[d], left_sem.at[d], (2 * (chip + 1) + core, f)
        )

    def to_left(d):
        place = jnp.where(d == chip - 1, chips, d)
        return send(
            part.at[d], came.at[place], sent.at[d], right_sem.at[d], (2 * (chip - 1) + core, f)
        )

    def from_left(d):
        send(part.at[d], came.at[d], sent.at[d], left_sem.at[d], (2 * chip + core, f)).wait_recv()
        add(d, d)

    def from_right(d, place):
        send(
            part.at[d], came.at[place], sent.at[d], right_sem.at[d], (2 * chip + core, f)
        ).wait_recv()
        add(d, place)

    def add(d, place):
        part[d] = (part[d].astype(F32) + came[place].astype(F32)).astype(BF16)

    def step(t):
        far = chips - 1 - t + chip
        near = t - (chips - 1 - chip)

        @pl.when(chip <= t)
        def _():
            if ready is not None:
                ready(far)

            @pl.when(chip > 0)
            def _():
                from_left(far)

            @pl.when(chip < t)
            def _():
                to_right(far + 1).wait_send()

            to_right(far).start()

        @pl.when(near >= 0)
        def _():
            if ready is not None:
                ready(near)

            @pl.when(chip < chips - 1)
            def _():
                from_right(near, near)

            @pl.when(near > 0)
            def _():
                to_left(near - 1).wait_send()

            to_left(near).start()

    def finish():
        if ready is not None:
            ready(chip)

        @pl.when(chip > 0)
        def _():
            from_left(chip)

        @pl.when(chip < chips - 1)
        def _():
            from_right(chip, chips)

    def done():
        @pl.when(chip < chips - 1)
        def _():
            to_right(chip + 1).wait_send()

        @pl.when(chip > 0)
        def _():
            to_left(chip - 1).wait_send()

    return step, finish, done


def line_gather(chip, chips, f, core, view, sems):
    right, left, twin_sent, got, twin_got = sems
    twin_id = (2 * chip + 1 - core, f)

    def hop(s, rightward):
        origin = chip - s if rightward else chip + s
        ref = view(origin, core)
        peer = (2 * (chip + 1 if rightward else chip - 1) + core, f)
        return send(ref, ref, (right if rightward else left).at[s], got.at[origin], peer)

    def twin(origin):
        ref = view(origin, core)
        return send(ref, ref, twin_sent.at[origin], twin_got.at[origin], twin_id)

    def arrived(origin):
        ref = view(origin, core)
        send(ref, ref, right.at[0], got.at[origin], twin_id).wait_recv()

    def step(s):
        @pl.when(chip - s >= 0)
        def _():
            if s:
                arrived(chip - s)

            @pl.when(chip < chips - 1)
            def _():
                hop(s, True).start()

            twin(chip - s).start()

        @pl.when(chip + s < chips)
        def _():
            if s:
                arrived(chip + s)

            @pl.when(chip > 0)
            def _():
                hop(s, False).start()

            if s:
                twin(chip + s).start()

    def done():
        for s in range(chips):
            if s < chips - 1:

                @pl.when((chip - s >= 0) & (chip < chips - 1))
                def _(s=s):
                    hop(s, True).wait_send()

                @pl.when((chip + s < chips) & (chip > 0))
                def _(s=s):
                    hop(s, False).wait_send()

            twin(s).wait_send()
            ref = view(s, 1 - core)
            send(ref, ref, twin_sent.at[s], twin_got.at[s], twin_id).wait_recv()

    return step, done


def back_kernel(
    n_ctx,
    n_fsdp,
    own_ref,
    rest_ref,
    w_ref,
    n_ref,
    fc_hbm,
    one_ref,
    cols_ref,
    fc_all,
    part,
    twin_out,
    twin_in,
    came,
    mine,
    theirs,
    twin_send,
    twin_recv,
    line_send,
    left_recv,
    right_recv,
    cols_send,
    cols_recv,
    fc_send,
    fc_recv,
    local,
):
    c = lax.axis_index("ctx")
    f = lax.axis_index("fsdp")
    chips = n_ctx // 2
    chip, core = c // 2, c % 2
    slots, width, cols = w_ref.shape
    count = own_ref.shape[2]
    base = own_ref.shape[0]
    shard = width // n_fsdp
    twin_id = (2 * chip + 1 - core, f)
    enter(
        [(lax.rem(c + i, n_ctx), f) for i in range(1, n_ctx)]
        + [(c, flip(f, k, n_fsdp)) for k in range(1, n_fsdp)]
    )

    def grad(s):
        return own_ref.at[s] if s < base else rest_ref.at[s - base]

    def for_block(b):
        total = dot_last(grad(0)[b], w_ref[0])
        for s in range(1, slots):
            total += dot_last(grad(s)[b], w_ref[s])
        return total.astype(BF16)

    def to_twin(d, slot):
        return send(twin_out.at[slot], twin_in.at[d], twin_send.at[slot], twin_recv.at[d], twin_id)

    def products(i, carry):
        d = far_first(i, chips)
        slot = i % 2
        product = for_block(2 * d + 1 - core)

        @pl.when(i > 1)
        def _():
            to_twin(d, slot).wait_send()

        twin_out[slot] = product
        to_twin(d, slot).start()
        part[d] = for_block(2 * d + core)
        return carry

    def ready(d):
        to_twin(d, 0).wait_recv()
        part[d] = (part[d].astype(F32) + twin_in[d].astype(F32)).astype(BF16)

    cut = count // 2
    streams = [
        line_sum(
            chip,
            chips,
            f,
            core,
            part.at[:, pl.ds(h * cut, cut)],
            came.at[h],
            (line_send.at[h], left_recv.at[h], right_recv.at[h]),
            None if h else ready,
        )
        for h in range(2)
    ]

    def step(t):
        for stream in streams:
            stream[0](t)

    def finish():
        for stream in streams:
            stream[1]()

    def done():
        for stream in streams:
            stream[2]()

    def cols_copy(src, dst, at):
        return send(mine.at[src], theirs.at[at], cols_send.at[src], cols_recv.at[at], (c, dst))

    def columns(j):
        left = n_ref[:, :, j * shard : (j + 1) * shard].reshape(n_ctx * count, shard)
        for s in range(slots):
            right = grad(s)[...].reshape(n_ctx * count, cols)
            mine[j, s] = dot_first(left, right).astype(BF16)

    def fc_copy(k):
        other = flip(f, k, n_fsdp)
        return send(fc_hbm.at[other], fc_all.at[f], fc_send.at[k], fc_recv.at[k], (c, other))

    for k in range(1, n_fsdp):
        fc_copy(k).start()
    own_fc = pltpu.make_async_copy(fc_hbm.at[f], fc_all.at[f], local)
    own_fc.start()
    lax.fori_loop(0, 2, products, 0)
    step(0)
    for j in range(n_fsdp):
        columns(j)
    for k in range(1, n_fsdp):
        other = flip(f, k, n_fsdp)
        cols_copy(other, other, f).start()
    lax.fori_loop(2, chips, products, 0)
    if chips > 2:
        step(1)
    for t in range(2, chips - 1):
        step(t)
    total = mine[f].astype(F32)
    for k in range(1, n_fsdp):
        other = flip(f, k, n_fsdp)
        cols_copy(other, other, other).wait_recv()
        total += theirs[other].astype(F32)
    cols_ref[...] = total.astype(BF16)
    finish()
    one_ref[...] = part[chip]
    own_fc.wait()
    for k in range(1, n_fsdp):
        fc_copy(k).wait()
    done()
    for slot in range(2):
        to_twin(0, slot).wait_send()
    for k in range(1, n_fsdp):
        other = flip(f, k, n_fsdp)
        cols_copy(other, other, other).wait_send()


def back_fits(n_ctx, n_fsdp, count, width, slots):
    blocks = (5 * (n_ctx // 2) + n_ctx) * count * width
    heads = slots * 256 * (n_ctx * count + 3 * width)
    return 2 * (blocks + heads) < 50 * 1024 * 1024


def back_call(n_ctx, n_fsdp, own, rest, w_slots, normed, fc_mine, cid):
    slots, width, cols = w_slots.shape
    count = normed.shape[1]
    chips = n_ctx // 2
    shard = width // n_fsdp
    vm = pl.BlockSpec(memory_space=pltpu.VMEM)
    anym = pl.BlockSpec(memory_space=pl.ANY)
    dma = pltpu.SemaphoreType.DMA
    block = pltpu.VMEM((chips, count, width), BF16)
    piece = pltpu.VMEM((n_fsdp, slots, shard, cols), BF16)
    return pl.pallas_call(
        functools.partial(back_kernel, n_ctx, n_fsdp),
        in_specs=[vm] * 4 + [anym],
        out_specs=[vm] * 2 + [anym],
        out_shape=[
            jax.ShapeDtypeStruct((count, width), BF16),
            jax.ShapeDtypeStruct((slots, shard, cols), BF16),
            jax.ShapeDtypeStruct(fc_mine.shape, BF16),
        ],
        scratch_shapes=[
            block,
            pltpu.VMEM((2, count, width), BF16),
            block,
            pltpu.VMEM((2, chips + 1, count // 2, width), BF16),
        ]
        + [piece] * 2
        + [dma((2,)), dma((chips,))]
        + [dma((2, chips))] * 3
        + [dma((n_fsdp,))] * 4
        + [dma(())],
        compiler_params=pltpu.CompilerParams(
            collective_id=cid, has_side_effects=True, vmem_limit_bytes=60 * 1024 * 1024
        ),
        cost_estimate=SHORT,
        name="qkv_back",
    )(own, rest, w_slots, normed, fc_mine)


def sums_kernel(n_ctx, n_fsdp, lead, *refs):
    rows_ref, cols_ref, extra_ref, att_ref, mid_ref, lines_in = refs[:6]
    outs, cols_all, lines_ref = refs[6:8], refs[8], refs[9]
    parts, cames = refs[10:12], refs[12:14]
    proj_part, proj_in, proj_got, lines_got = refs[14:18]
    lines_send, lines_recv, local, proj_send, proj_recv, pair_sem = refs[18:24]
    cols_sems = refs[24:29]
    sems = [(refs[29 + 8 * i : 32 + 8 * i], refs[32 + 8 * i : 37 + 8 * i]) for i in range(2)]
    c = lax.axis_index("ctx")
    f = lax.axis_index("fsdp")
    chips = n_ctx // 2
    chip, core = c // 2, c % 2
    width = att_ref.shape[1]
    shard = width // n_fsdp
    half = shard // 2
    high = proj_in.shape[1]
    twin_id = (2 * chip + 1 - core, f)
    enter(
        [(lax.rem(c + i, n_ctx), f) for i in range(1, n_ctx)]
        + [(c, flip(f, k, n_fsdp)) for k in range(1, n_fsdp)]
    )

    def line_ops(i):
        sum_sems, gather_sems = sems[i]
        gather = line_gather(chip, chips, f, core, lambda at, h: outs[i].at[h, at], gather_sems)
        return line_sum(chip, chips, f, core, parts[i], cames[i], sum_sems) + gather

    def proj_pair():
        return send(proj_part.at[1 - core], proj_in, pair_sem.at[0], pair_sem.at[1], twin_id)

    def proj_copy(k):
        other = flip(f, k, n_fsdp)
        return send(
            proj_part.at[core, other],
            proj_got.at[f],
            proj_send.at[k],
            proj_recv.at[k],
            (c, other),
        )

    def proj_products(j):
        for h in range(2):
            lo = j * shard + h * half
            proj_part[h, j, :half] = dot_first(att_ref[:, lo : lo + half], mid_ref[...]).astype(BF16)
            if half < high:
                proj_part[h, j, half:] = jnp.zeros((high - half, width), BF16)

    def proj_add(j, carry):
        proj_part[core, j] = (
            proj_part[core, j].astype(F32) + proj_in[j].astype(F32)
        ).astype(BF16)
        return carry

    def proj_total():
        total = proj_part[core, f].astype(F32)
        for k in range(1, n_fsdp):
            proj_copy(k).wait_recv()
            total += proj_got[flip(f, k, n_fsdp)].astype(F32)
        total = jnp.concatenate([total.astype(BF16), extra_ref[...]], axis=0)
        first = rows_ref.shape[1] - parts[0].shape[1]
        step, rows = parts[1].shape[1] - first, total.shape[0]
        for p in range(chips):
            lo, hi = min(p * step, rows), min((p + 1) * step, rows)
            end = first + hi - lo
            if hi > lo:
                parts[1][p, first:end] = total[lo:hi]
            if hi - lo < step:
                parts[1][p, end:] = jnp.zeros((step - hi + lo, width), BF16)

    peers = [(flip(c, 1 << i, n_ctx), f) for i in range(n_ctx.bit_length() - 1)]
    ctx_phases = len(peers)
    peers += [(c, flip(f, 1 << i, n_fsdp)) for i in range(n_fsdp.bit_length() - 1)]

    def line_copy(i):
        rows = lines_in.shape[0] if i < ctx_phases else lead
        return send(
            lines_ref.at[:rows],
            lines_got.at[i, :rows],
            lines_send.at[i],
            lines_recv.at[i],
            peers[i],
        )

    def line_phase(i):
        if 0 < i <= len(peers):
            rows = lines_in.shape[0] if i <= ctx_phases else lead
            line_copy(i - 1).wait()
            lines_ref[:rows] += lines_got[i - 1, :rows]
        if i < len(peers):
            line_copy(i).start()

    def settle(finish, i):
        finish()
        keep = pltpu.make_async_copy(parts[i].at[chip], outs[i].at[core, chip], local.at[0])
        keep.start()
        keep.wait()

    sum_a, finish_a, sums_a, gather_a, gathers_a = line_ops(0)
    sum_b, finish_b, sums_b, gather_b, gathers_b = line_ops(1)
    cols_step, cols_done = line_gather(
        chip, chips, f, core, lambda at, h: cols_all.at[2 * at + h], cols_sems
    )
    load = pltpu.make_async_copy(cols_ref, cols_all.at[c], local.at[1])
    load.start()
    cut = parts[0].shape[1]
    parts[0][...] = rows_ref[:, :cut]
    load.wait()
    cols_step(0)
    sum_a(0)
    parts[1][:, : rows_ref.shape[1] - cut] = rows_ref[:, cut:]
    lines_ref[...] = lines_in[...]
    for j in range(n_fsdp):
        proj_products(j)
    proj_pair().start()
    for t in range(1, chips - 1):
        cols_step(t)
        sum_a(t)
        if t == 1:
            proj_pair().wait()
            lax.fori_loop(0, n_fsdp, proj_add, 0)
            for k in range(1, n_fsdp):
                proj_copy(k).start()
    cols_step(chips - 1)
    settle(finish_a, 0)
    gather_a(0)
    proj_total()
    sum_b(0)
    phase = 0
    for s in range(1, chips):
        gather_a(s)
        if s < chips - 1:
            sum_b(s)
        line_phase(phase)
        phase += 1
    settle(finish_b, 1)
    for s in range(chips):
        gather_b(s)
        line_phase(phase)
        phase += 1
    while phase <= len(peers):
        line_phase(phase)
        phase += 1
    for done in (sums_a, sums_b, cols_done, gathers_a, gathers_b):
        done()
    for k in range(1, n_fsdp):
        proj_copy(k).wait_send()


def sums_call(n_ctx, n_fsdp, rows, cols, extra, attended, mid_low, lines, lead, cid):
    chips = n_ctx // 2
    count, width = attended.shape
    high = half_high(width // n_fsdp)
    per_chip = rows.shape[1]
    third = -(-(high + extra.shape[0]) // (16 * chips)) * 16
    cut = -(-(per_chip + third) // 32) * 16
    shapes = [(chips, size, width) for size in (cut, per_chip + third - cut)]
    phases = (n_ctx * n_fsdp).bit_length() - 1
    vm = pl.BlockSpec(memory_space=pltpu.VMEM)
    anym = pl.BlockSpec(memory_space=pl.ANY)
    dma = pltpu.SemaphoreType.DMA
    return pl.pallas_call(
        functools.partial(sums_kernel, n_ctx, n_fsdp, lead),
        in_specs=[vm, anym, vm, vm, vm, vm],
        out_specs=[vm, vm, anym, vm],
        out_shape=[jax.ShapeDtypeStruct((2,) + shape, BF16) for shape in shapes]
        + [jax.ShapeDtypeStruct((n_ctx,) + cols.shape, BF16)]
        + [jax.ShapeDtypeStruct(lines.shape, F32)],
        scratch_shapes=[pltpu.VMEM(shape, BF16) for shape in shapes]
        + [pltpu.VMEM((chips + 1,) + shape[1:], BF16) for shape in shapes]
        + [
            pltpu.VMEM((2, n_fsdp, high, width), BF16),
            pltpu.VMEM((n_fsdp, high, width), BF16),
            pltpu.VMEM((n_fsdp, high, width), BF16),
            pltpu.VMEM((phases,) + lines.shape, F32),
            dma((phases,)),
            dma((phases,)),
            dma((2,)),
            dma((n_fsdp,)),
            dma((n_fsdp,)),
            dma((2,)),
        ]
        + [dma((chips,))] * (5 + 2 * 8),
        compiler_params=pltpu.CompilerParams(
            collective_id=cid, has_side_effects=True, vmem_limit_bytes=56 * 1024 * 1024
        ),
        cost_estimate=SHORT,
        name="weight_sums",
    )(rows, cols, extra, attended, mid_low, lines)


def assemble_kernel(
    n_fsdp,
    own_ref,
    rest_ref,
    first_ref,
    second_ref,
    third_ref,
    out_ref,
    attn_hbm,
    fc_hbm,
    proj_hbm,
    wout_hbm,
    *scratch,
):
    attn_ref, fc_ref, proj_ref, wout_ref, low_ref, sem = scratch
    load = pltpu.make_async_copy(out_ref, low_ref, sem.at[4])
    load.start()
    hd = HEAD_DIM
    shard, hidden = fc_ref.shape[0], fc_ref.shape[1] // n_fsdp
    half = shard // 2
    width = proj_ref.shape[1]
    count = own_ref.shape[0]
    copies = [
        pltpu.make_async_copy(src, dst, sem.at[i])
        for i, (src, dst) in enumerate(
            ((wout_ref, wout_hbm), (fc_ref, fc_hbm), (proj_ref, proj_hbm), (attn_ref, attn_hbm))
        )
    ]
    for h in range(2):
        for j in range(n_fsdp):
            cut = min(first_ref.shape[2], half)
            at = slice(j * hidden, (j + 1) * hidden)
            fc_ref[h * half : h * half + cut, at] = first_ref[h, j, :cut].astype(F32)
            if cut < half:
                rows = second_ref[h, j, : half - cut].astype(F32)
                fc_ref[h * half + cut : (h + 1) * half, at] = rows
    copies[1].start()
    for h in range(2):
        proj_ref[h * half : (h + 1) * half] = third_ref[h, :half].astype(F32)
    copies[2].start()
    for h in range(width // hd):
        src = own_ref.at[h] if h < count else rest_ref.at[h - count]
        for part in range(3):
            at = part * width + h * hd
            attn_ref[:, at : at + hd] = src[:, part * hd : (part + 1) * hd].astype(F32)
    copies[3].start()
    load.wait()
    wout_ref[...] = low_ref[...].astype(F32)
    copies[0].start()
    for copy in copies:
        copy.wait()


def assemble(n_fsdp, own, rest, first, second, third, out_low, hidden):
    shard = own.shape[1]
    width = first.shape[3]
    vm = pl.BlockSpec(memory_space=pltpu.VMEM)
    anym = pl.BlockSpec(memory_space=pl.ANY)
    shapes = [(shard, 3 * width), (shard, n_fsdp * hidden), (shard, width), out_low.shape]
    return pl.pallas_call(
        functools.partial(assemble_kernel, n_fsdp),
        in_specs=[vm] * 5 + [anym],
        out_specs=[anym] * 4,
        out_shape=[jax.ShapeDtypeStruct(shape, F32) for shape in shapes],
        scratch_shapes=[pltpu.VMEM(shape, F32) for shape in shapes]
        + [pltpu.VMEM(out_low.shape, BF16), pltpu.SemaphoreType.DMA((5,))],
        compiler_params=pltpu.CompilerParams(vmem_limit_bytes=60 * 1024 * 1024),
        cost_estimate=SHORT,
        name="assemble",
    )(own, rest, first, second, third, out_low)


def swap(value, axis, size, k):
    return lax.ppermute(value, axis, [(i, i ^ k) for i in range(size)])


def shards(
    n_ctx,
    n_fsdp,
    tokens,
    block_order,
    w_attn,
    w_proj,
    w_fc,
    w_out,
    norm_gains,
    biases,
    fc_bias,
    cotangent,
):
    hd = HEAD_DIM
    count, width = tokens.shape[1:]
    shard = width // n_fsdp
    heads = width // hd
    base = heads // n_ctx
    rest = heads - base * n_ctx
    slots = base + rest
    own_blocks = count // BLOCK
    c = lax.axis_index("ctx")
    f = lax.axis_index("fsdp")

    order = block_order[0]
    inv = jnp.argsort(order).astype(jnp.int32)
    order_own = jnp.concatenate([order, (c * own_blocks)[None]])

    def head_cols(h):
        return jnp.concatenate(
            [
                lax.dynamic_slice(w_attn, (0, part * width + h * hd), (shard, hd))
                for part in range(3)
            ],
            axis=1,
        )

    slot_heads = [c * base + s for s in range(base)] + [n_ctx * base + r for r in range(rest)]
    w_slots = jnp.stack([head_cols(h) for h in slot_heads])
    small = jnp.concatenate([norm_gains, biases], axis=0).astype(F32)
    hidden_cols = w_fc.shape[1] // n_fsdp
    normed_one, qkv, full_proj, fc_parts, w_slots, small = start_call(
        n_ctx, n_fsdp, base, tokens[0], w_slots, small, w_proj, w_fc, 3
    )
    full_proj = full_proj.reshape(width, width)
    qkv = qkv.reshape(slots, n_ctx * own_blocks, BLOCK, 3 * hd)
    gains, shifts = small[:2], small[2:]
    cot = cotangent[0]

    cot_all = lax.all_gather(cot, "fsdp", axis=0)

    out_own, lse_own = attn_fwd(inv, qkv, base)
    if rest:
        out_rest, lse_rest = rest_fwd(order_own, qkv, base)
    else:
        out_rest = out_own
    attended, mid, normed_two, fc_cols = mix_call(
        n_ctx, n_fsdp, out_own, out_rest, tokens[0], full_proj, small, fc_parts, 6
    )
    fc_cols = fc_cols.reshape(width, hidden_cols)
    rows = tokens[0].astype(F32)

    normed_two_grad, fc_bias_part, out_part, w_out_part, w_fc_part = ffn(
        n_fsdp,
        normed_two,
        cot_all,
        fc_cols,
        w_out,
        fc_bias.astype(F32)[None],
    )
    out_rows = lax.psum_scatter(
        out_part.reshape(n_fsdp * count, width), "fsdp", scatter_dimension=0, tiled=True
    )
    w_out_low = lax.psum(w_out_part, "ctx")

    half, high = shard // 2, half_high(shard)
    core = c % 2
    main = n_ctx * base * hd
    mid_grad, mid_low, turn_sums, d_rest, fc_mine, d_out = turn_call(
        n_ctx, base, normed_two_grad, cot, mid, full_proj, small, w_fc_part, 7
    )

    d_own = attn_bwd(inv, qkv, d_out, out_own, lse_own, base)
    d_own = d_own.reshape(base, n_ctx, count, 3 * hd)
    if rest:
        d_rest = rest_bwd(order_own, qkv, d_rest, out_rest, lse_rest, base)
        d_rest = d_rest.reshape(rest, n_ctx, count, 3 * hd)
        sums = jnp.concatenate(
            [jnp.sum(d.astype(F32), axis=(1, 2)) for d in (d_own, d_rest)], axis=0
        )
    else:
        d_rest = d_own
        sums = jnp.sum(d_own.astype(F32), axis=(1, 2))
    if back_fits(n_ctx, n_fsdp, count, width, slots):
        normed_one_grad, cols_sum, fc_rows = back_call(
            n_ctx, n_fsdp, d_own, d_rest, w_slots, normed_one, fc_mine, 4
        )
        normed_one_grad = normed_one_grad.astype(F32)
    else:
        dqkv = jnp.concatenate([d_own, d_rest])[:slots].reshape(slots, n_ctx * count, 3 * hd)
        one_part = jnp.einsum("hte,hde->td", dqkv, w_slots, preferred_element_type=F32)
        normed_one_grad = lax.psum_scatter(
            one_part.astype(BF16), "ctx", scatter_dimension=0, tiled=True
        ).astype(F32)
        slot_part = jnp.einsum(
            "td,hte->hde",
            normed_one.reshape(n_ctx * count, width),
            dqkv,
            preferred_element_type=F32,
        ).astype(BF16)
        cols_sum = lax.psum_scatter(slot_part, "fsdp", scatter_dimension=1, tiled=True)
        fc_rows = lax.all_to_all(fc_mine, "fsdp", split_axis=0, concat_axis=0, tiled=True)

    xhat_one, rstd_one = norm_parts(rows)
    tokens_grad = (mid_grad + norm_back(xhat_one, rstd_one, gains[0], normed_one_grad)).astype(
        BF16
    )

    def placed(part):
        cols = sums[:, part * hd : (part + 1) * hd]
        line = lax.dynamic_update_slice_in_dim(
            jnp.zeros((width,), F32), cols[:base].reshape(-1), c * base * hd, 0
        )
        return line + jnp.pad(cols[base:].reshape(-1), (main, 0))

    lines = jnp.stack(
        [
            jnp.sum(normed_one_grad * xhat_one, axis=0),
            turn_sums[0],
            jnp.sum(normed_one_grad, axis=0),
            turn_sums[1],
            placed(0),
            placed(2),
            turn_sums[2],
            turn_sums[3],
        ]
    )
    lead = lines.shape[0]
    tail = jnp.pad(fc_bias_part, ((0, 7), (0, width - hidden_cols)))
    lines = jnp.concatenate([lines, tail])

    chips = n_ctx // 2
    fc_rows = fc_rows.reshape(-1, width)
    per_chip = -(-fc_rows.shape[0] // (16 * chips)) * 16
    fc_rows = jnp.pad(fc_rows, ((0, per_chip * chips - fc_rows.shape[0]), (0, 0)))
    fc_rows = fc_rows.reshape(chips, per_chip, width)
    extra = jnp.zeros((16, width), BF16)
    if rest:
        away = lax.dynamic_slice_in_dim(cols_sum[base:], (1 - core) * half, half, 1)
        here = lax.dynamic_slice_in_dim(cols_sum[base:], core * half, half, 1)
        extra = here.astype(F32) + swap(away, "ctx", n_ctx, 1).astype(F32)
        extra = extra.astype(BF16).reshape(-1, width)
        extra_rows = extra.shape[0]
        extra = jnp.pad(extra, ((0, -extra_rows % 16), (0, 0)))
    first, second, own_cols, lines = sums_call(
        n_ctx, n_fsdp, fc_rows, cols_sum[:base], extra, attended, mid_low, lines, lead, 5
    )
    out_rows, w_out_low, lines = lax.optimization_barrier((out_rows, w_out_low, lines))
    layer_rows = (mid + (out_rows.astype(F32) + shifts[5])).astype(BF16)
    split = per_chip - first.shape[2]
    third = second[:, :, split:].reshape(2, -1, width)
    second = second[:, :, :split]
    own_cols = own_cols.reshape(n_ctx * base, shard, 3 * hd)
    if rest:
        rest_cols = third[:, high : high + extra_rows].reshape(2, rest, half, 3 * hd)
        rest_cols = rest_cols.transpose(1, 0, 2, 3).reshape(rest, shard, 3 * hd)
    else:
        rest_cols = own_cols
    if hidden_cols == width and chips == n_fsdp:
        w_attn_grad, w_fc_grad, w_proj_grad, w_out_grad = assemble(
            n_fsdp, own_cols, rest_cols, first, second, third, w_out_low, hidden_cols
        )
    else:
        w_fc_low = jnp.concatenate([first, second], axis=2).reshape(2, -1, width)
        w_fc_low = w_fc_low[:, : n_fsdp * high * hidden_cols // width]
        w_fc_low = w_fc_low.reshape(2, n_fsdp, high, hidden_cols)[:, :, :half]
        w_fc_grad = w_fc_low.transpose(0, 2, 1, 3).reshape(shard, n_fsdp * hidden_cols)
        w_fc_grad = w_fc_grad.astype(F32)
        w_proj_grad = third[:, :half].reshape(shard, width).astype(F32)
        cols = jnp.concatenate([own_cols, rest_cols])[: width // hd]
        cols = cols.reshape(width // hd, shard, 3, hd).transpose(1, 2, 0, 3)
        w_attn_grad = cols.reshape(shard, 3 * width).astype(F32)
        w_out_grad = w_out_low.astype(F32)
    fc_bias_grad = lines[lead, :hidden_cols]
    lines = lax.dynamic_slice_in_dim(lines[:lead], f * shard, shard, 1)
    return (
        layer_rows[None],
        tokens_grad[None],
        w_attn_grad,
        w_proj_grad,
        w_fc_grad,
        w_out_grad,
        lines[:2],
        lines[2:],
        fc_bias_grad,
    )


def solution(mesh):
    rows = P("fsdp", "ctx", None)
    weight = P("fsdp", None)
    vectors = P(None, "fsdp")
    return jax.shard_map(
        functools.partial(shards, mesh.shape["ctx"], mesh.shape["fsdp"]),
        mesh=mesh,
        in_specs=(
            rows, weight, weight, weight, weight, weight, vectors, vectors, P("fsdp"), rows,
        ),
        out_specs=(
            rows, rows, weight, weight, weight, weight, vectors, vectors, P("fsdp"),
        ),
        check_vma=False,
    )
```

```python
import functools

import jax
import jax.numpy as jnp
from jax import lax
from jax.experimental import pallas as pl
from jax.experimental.pallas import tpu as pltpu
from jax.sharding import PartitionSpec as P

HEAD_DIM = 64
BLOCK = 128
QROWS = 256
EPS = 1e-05
SCALE = HEAD_DIM ** (-0.5)
F32 = jnp.float32
BF16 = jnp.bfloat16
VMEM_LIMIT = 56 * 1024 * 1024
LAST = (((1,), (1,)), ((), ()))
FIRST = (((0,), (0,)), ((), ()))
MESH = pl.DeviceIdType.MESH
TILE = 256


def dot_last(a, b):
    return lax.dot_general(a, b, LAST, preferred_element_type=F32)


def dot(a, b):
    return jnp.dot(a, b, preferred_element_type=F32)


def dot_first(a, b):
    return lax.dot_general(a, b, FIRST, preferred_element_type=F32)


SHORT = pl.CostEstimate(flops=1, bytes_accessed=1, transcendentals=0)


def norm_parts(rows):
    mean = jnp.mean(rows, axis=-1, keepdims=True)
    cen = rows - mean
    rstd = lax.rsqrt(jnp.mean(cen * cen, axis=-1, keepdims=True) + EPS)
    return cen * rstd, rstd


def norm_back(xhat, rstd, gain, grad):
    dxhat = grad * gain
    return rstd * (
        dxhat
        - jnp.mean(dxhat, axis=-1, keepdims=True)
        - xhat * jnp.mean(dxhat * xhat, axis=-1, keepdims=True)
    )


def flip(place, k, size):
    out = 0
    bit = 1
    while bit < size:
        out = out + (place // bit + k // bit) % 2 * bit
        bit *= 2
    return out

def half_high(shard):
    return -(-(shard // 2) // 16) * 16


def enter(peers):
    barrier = pltpu.get_barrier_semaphore()
    for peer in peers:
        pl.semaphore_signal(barrier, inc=1, device_id=peer, device_id_type=MESH)
    pl.semaphore_wait(barrier, len(peers))

def send(src, dst, send_sem, recv_sem, peer):
    return pltpu.make_async_remote_copy(
        src_ref=src, dst_ref=dst, send_sem=send_sem, recv_sem=recv_sem,
        device_id=peer, device_id_type=MESH)


def ffn_kernel(n, nt_hbm, cot_hbm, wfc_hbm, wout_hbm, bias_ref,
               gsum_ref, fcb_ref, out_hbm, wout_grad_hbm, wfc_grad_hbm,
               cot_ref, wfc_ref, wout_ref, all_ref, act_ref, hg_ref, ag_ref, part_ref, got_ref, stage_d, stage_h,
               s1, r1, s2, r2, local):
    c = lax.axis_index("ctx")
    f = lax.axis_index("fsdp")
    rows, width = nt_hbm.shape
    enter([(c, flip(f, k, n)) for k in range(1, n)])

    def rows_out(k):
        return send(nt_hbm, all_ref.at[f], s1.at[k], r1.at[k], (c, flip(f, k, n)))

    def grad_back(k):
        other = flip(f, k, n)
        return send(part_ref.at[other], got_ref.at[k], s2.at[k], r2.at[k], (c, other))

    near = [k for k in range(1, n) if k & (k - 1) == 0]
    far = [k for k in range(1, n) if k not in near]
    for k in near:
        rows_out(k).start()
    loads = [
        pltpu.make_async_copy(nt_hbm, all_ref.at[f], local.at[0]),
        pltpu.make_async_copy(wout_hbm, wout_ref, local.at[1]),
        pltpu.make_async_copy(cot_hbm, cot_ref, local.at[2]),
        pltpu.make_async_copy(wfc_hbm, wfc_ref, local.at[3]),
    ]
    for load in loads:
        load.start()
    fcb_ref[...] = jnp.zeros_like(fcb_ref)
    loads[1].wait()
    loads[2].wait()

    def active_grad(k, carry):
        ag_ref[k] = dot_last(cot_ref[k], wout_ref[...])
        return carry

    lax.fori_loop(0, n, active_grad, 0)
    for k in far:
        rows_out(k).start()
    loads[0].wait()
    loads[3].wait()

    def chunk(k, carry):
        src = flip(f, k, n)

        @pl.when(k > 0)
        def _():
            rows_out(k).wait_recv()

        hidden = dot(all_ref[src], wfc_ref[...]) + bias_ref[...]
        square = hidden * hidden
        tanh = jnp.tanh(0.7978845608028654 * (hidden + 0.044715 * square * hidden))
        act_ref[src] = (0.5 * hidden * (1.0 + tanh)).astype(BF16)
        slope = 0.5 * (1.0 + tanh) + 0.5 * hidden * (1.0 - tanh * tanh) * 0.7978845608028654 * (
            1.0 + 3.0 * 0.044715 * square
        )
        grad = (ag_ref[src] * slope).astype(BF16)
        hg_ref[src] = grad
        fcb_ref[...] += jnp.sum(grad.astype(F32), axis=0, keepdims=True)
        part_ref[src] = dot_last(grad, wfc_ref[...]).astype(BF16)

        @pl.when(k > 0)
        def _():
            grad_back(k).start()

        return carry

    lax.fori_loop(0, n, chunk, 0)

    def grads(left_ref, right_ref, tiles, stage_ref, base):
        right = right_ref[...].reshape(n * rows, right_ref.shape[2])
        copies = []
        for i, (lo, size, sent, dst) in enumerate(tiles):
            slot = i % 2
            if i >= 2:
                copies[i - 2].wait()
            left = left_ref[:, :, lo : lo + size].reshape(n * rows, size)
            stage_ref[slot, :size] = dot_first(left, right).astype(BF16)
            copies.append(
                pltpu.make_async_copy(stage_ref.at[slot, :sent], dst, local.at[base + slot])
            )
            copies[-1].start()
        for copy in copies[-2:]:
            copy.wait()

    half, high = width // n // 2, wfc_grad_hbm.shape[2]
    if half < high:
        stage_h[:, half:high] = jnp.zeros((2, high - half, stage_h.shape[2]), BF16)
    wide = act_ref.shape[2]
    sizes = [(lo, min(TILE, wide - lo)) for lo in range(0, wide, TILE)]
    grads(
        act_ref,
        cot_ref,
        [(lo, size, size, wout_grad_hbm.at[lo : lo + size]) for lo, size in sizes],
        stage_d,
        4,
    )
    grads(
        all_ref,
        hg_ref,
        [
            ((2 * j + h) * half, half, high, wfc_grad_hbm.at[h, j])
            for j in range(n)
            for h in range(2)
        ],
        stage_h,
        6,
    )

    def out_copy(k):
        return pltpu.make_async_copy(
            stage_d.at[k % 2, :rows], out_hbm.at[k], local.at[4 + k % 2]
        )

    for k in range(n):
        if k >= 2:
            out_copy(k - 2).wait()
        stage_d[k % 2, :rows] = dot(act_ref[k], wout_ref[...]).astype(BF16)
        out_copy(k).start()

    gsum_ref[...] = part_ref[f].astype(F32)
    for k in near + far:
        grad_back(k).wait_recv()
        gsum_ref[...] += got_ref[k].astype(F32)
    for k in range(1, n):
        rows_out(k).wait_send()
        grad_back(k).wait_send()
    for k in range(max(0, n - 2), n):
        out_copy(k).wait()


def ffn(n, nt, cot, wfc, wout, bias, cid=1):
    m, d = nt.shape
    h = wfc.shape[1]
    vm = pl.BlockSpec(memory_space=pltpu.VMEM)
    anym = pl.BlockSpec(memory_space=pl.ANY)
    return pl.pallas_call(
        functools.partial(ffn_kernel, n),
        in_specs=[anym] * 4 + [vm],
        out_specs=[vm, vm] + [anym] * 3,
        out_shape=[
            jax.ShapeDtypeStruct((m, d), F32),
            jax.ShapeDtypeStruct((1, h), F32),
            jax.ShapeDtypeStruct((n, m, d), BF16),
            jax.ShapeDtypeStruct((h, d), BF16),
            jax.ShapeDtypeStruct((2, n, half_high(d // n), h), BF16),
        ],
        scratch_shapes=[
            pltpu.VMEM((n, m, d), BF16),
            pltpu.VMEM((d, h), BF16),
            pltpu.VMEM((h, d), BF16),
            pltpu.VMEM((n, m, d), BF16),
            pltpu.VMEM((n, m, h), BF16),
            pltpu.VMEM((n, m, h), BF16),
            pltpu.VMEM((n, m, h), F32),
            pltpu.VMEM((n, m, d), BF16),
            pltpu.VMEM((n, m, d), BF16),
            pltpu.VMEM((2, max(TILE, m), d), BF16),
            pltpu.VMEM((2, half_high(d // n), h), BF16),
        ]
        + [pltpu.SemaphoreType.DMA((n,))] * 4
        + [pltpu.SemaphoreType.DMA((8,))],
        compiler_params=pltpu.CompilerParams(
            collective_id=cid, has_side_effects=True, vmem_limit_bytes=60 * 1024 * 1024
        ),
        cost_estimate=SHORT,
        name="feed_forward",
    )(nt, cot, wfc, wout, bias)


def weight_shares(c, f, core, n_fsdp, shard, source, dst, ss, rs):
    cut = shard // 32 * 16 if shard % 16 == 0 else 0
    shares = ((0, cut), (cut, shard)) if cut else ((0, shard), (0, shard))
    twin_id = (c + 1 - 2 * core, f)

    def copy(share, k, onward):
        lo, hi = share
        other = flip(f, k, n_fsdp)
        if onward:
            part = dst.at[other, lo:hi]
            return send(part, part, ss.at[1, k], rs.at[1, k], twin_id)
        return send(source(k).at[lo:hi], dst.at[f, lo:hi], ss.at[0, k], rs.at[0, k], (c, other))

    def by_core(act):
        for h in range(2):

            @pl.when(core == h)
            def _(h=h):
                for k in range(1, n_fsdp):
                    act(shares[h], shares[1 - h], k)

    def start(mine, theirs, k):
        copy(mine, k, False).start()

    def onward(mine, theirs, k):
        copy(mine, k, False).wait_recv()
        if cut:
            copy(mine, k, True).start()

    def done(mine, theirs, k):
        if cut:
            copy(theirs, k, True).wait_recv()
            copy(mine, k, True).wait_send()
        copy(mine, k, False).wait_send()

    return tuple(functools.partial(by_core, act) for act in (start, onward, done))


def start_kernel(
    n_ctx,
    n_fsdp,
    base,
    tok_hbm,
    w_hbm,
    small_ref,
    proj_hbm,
    fc_hbm,
    n_hbm,
    qkv_hbm,
    proj_all,
    fc_parts,
    w_ref,
    lines_ref,
    n_ref,
    qkv_ref,
    fc_ref,
    fc_cut,
    x_ref,
    wg_ref,
    sg_ref,
    tok_recv,
    right_sem,
    left_sem,
    twin_sem,
    w_send,
    w_recv,
    s_send,
    s_recv,
    proj_send,
    proj_recv,
    local,
):
    c = lax.axis_index("ctx")
    f = lax.axis_index("fsdp")
    chips = n_ctx // 2
    chip, core = c // 2, c % 2
    slots, width, cols = w_ref.shape
    shard = width // n_fsdp
    hd = HEAD_DIM
    enter(
        [(lax.rem(c + i, n_ctx), f) for i in range(1, n_ctx)]
        + [(c, flip(f, k, n_fsdp)) for k in range(1, n_fsdp)]
    )

    def block(at, same):
        return 2 * at + (core if same else 1 - core)

    cut = x_ref.shape[1] // 2

    def part(ref, h):
        return ref.at[pl.ds(h * cut, cut)]

    def hop(step, to_right, from_own, h):
        origin = block(chip - step if to_right else chip + step, True)
        src = tok_hbm if from_own else x_ref.at[origin]
        sem = (right_sem if to_right else left_sem).at[step, h]
        peer = (c + 2 if to_right else c - 2, f)
        dst = part(x_ref.at[origin], h)
        return send(part(src, h), dst, sem, tok_recv.at[origin, h], peer)

    def twin(at, from_own, h):
        origin = block(at, True)
        src = tok_hbm if from_own else x_ref.at[origin]
        dst = part(x_ref.at[origin], h)
        return send(
            part(src, h),
            dst,
            twin_sem.at[at, h],
            tok_recv.at[origin, h],
            (block(chip, False), f),
        )

    def w_copy(k):
        return send(w_hbm, wg_ref.at[f], w_send.at[k], w_recv.at[k], (c, flip(f, k, n_fsdp)))

    def s_copy(k):
        return send(small_ref, sg_ref.at[f], s_send.at[k], s_recv.at[k], (c, flip(f, k, n_fsdp)))

    weights_start, weights_onward, weights_done = weight_shares(
        c, f, core, n_fsdp, shard, lambda k: proj_hbm, proj_all, proj_send, proj_recv
    )

    for k in range(1, n_fsdp):
        s_copy(k).start()

    for h in range(2):

        @pl.when(chip < chips - 1)
        def _(h=h):
            hop(0, True, True, h).start()

        @pl.when(chip > 0)
        def _(h=h):
            hop(0, False, True, h).start()

    for k in range(1, n_fsdp):
        w_copy(k).start()
    for h in range(2):
        twin(chip, True, h).start()
    own_x = pltpu.make_async_copy(tok_hbm, x_ref.at[c], local.at[0])
    own_w = pltpu.make_async_copy(w_hbm, wg_ref.at[f], local.at[1])
    own_proj = pltpu.make_async_copy(proj_hbm, proj_all.at[f], local.at[2])
    load_fc = pltpu.make_async_copy(fc_hbm, fc_ref, local.at[3])
    for copy in (own_x, own_w, own_proj, load_fc):
        copy.start()
    sg_ref[f] = small_ref[...]
    for k in range(1, n_fsdp):
        s_copy(k).wait_recv()
    for j in range(n_fsdp):
        lines_ref[:, j * shard : (j + 1) * shard] = sg_ref[j]
    main = n_ctx * base * hd
    row_id = lax.broadcasted_iota(jnp.int32, (width, slots * hd), 0)
    col_id = lax.broadcasted_iota(jnp.int32, (width, slots * hd), 1)
    wanted = jnp.where(col_id < base * hd, c * base * hd + col_id, main + col_id - base * hd)
    picked = dot(lines_ref[...].astype(BF16), (row_id == wanted).astype(BF16))
    zero = jnp.zeros((1, hd), F32)
    bias = [
        jnp.concatenate(
            [picked[4:5, s * hd : (s + 1) * hd], zero, picked[5:6, s * hd : (s + 1) * hd]], axis=1
        )
        for s in range(slots)
    ]
    own_w.wait()
    own_x.wait()
    for k in range(1, n_fsdp):
        w_copy(k).wait_recv()
    weights_start()
    for j in range(n_fsdp):
        w_ref[:, j * shard : (j + 1) * shard, :] = wg_ref[j]

    load_fc.wait()
    hidden = fc_cut.shape[2]
    cuts = []
    for j in range(n_fsdp):
        if j >= 2:
            cuts[j - 2].wait()
        fc_cut[j % 2] = fc_ref[:, j * hidden : (j + 1) * hidden]
        cuts.append(pltpu.make_async_copy(fc_cut.at[j % 2], fc_parts.at[j], local.at[4 + j % 2]))
        cuts[-1].start()

    def results(origin):
        return (
            pltpu.make_async_copy(n_ref, n_hbm.at[origin], local.at[0]),
            pltpu.make_async_copy(qkv_ref, qkv_hbm.at[:, origin], local.at[1]),
        )

    def project(at, same, first=False):
        origin = block(at, same)
        rows = x_ref[origin].astype(F32)
        mean = jnp.mean(rows, axis=1, keepdims=True)
        cen = rows - mean
        var = jnp.mean(cen * cen, axis=1, keepdims=True)
        normed = cen * lax.rsqrt(var + EPS) * lines_ref[0:1] + lines_ref[2:3]
        normed = normed.astype(BF16)

        @pl.when(jnp.logical_not(first))
        def _():
            for copy in results(origin):
                copy.wait()

        n_ref[...] = normed
        for s in range(slots):
            qkv_ref[s] = (dot(normed, w_ref[s]) + bias[s]).astype(BF16)
        for copy in results(origin):
            copy.start()

    def arrived(at, same, h):
        origin = block(at, same)
        ref = part(x_ref.at[origin], h)
        pltpu.make_async_copy(ref, ref, tok_recv.at[origin, h]).wait()

    def step(s, carry):
        for h in range(2):

            @pl.when((s > 0) & (chip - s >= 0))
            def _(h=h):
                arrived(chip - s, True, h)

                @pl.when(chip < chips - 1)
                def _():
                    hop(s, True, False, h).start()

                twin(chip - s, False, h).start()

            @pl.when((s > 0) & (chip + s < chips))
            def _(h=h):
                arrived(chip + s, True, h)

                @pl.when(chip > 0)
                def _():
                    hop(s, False, False, h).start()

                twin(chip + s, False, h).start()

        @pl.when(s == chips - 1)
        def _():
            weights_onward()

        @pl.when(chip - s >= 0)
        def _():
            project(chip - s, True, s == 0)

        @pl.when((s > 0) & (chip + s < chips))
        def _():
            project(chip + s, True)

        @pl.when(chip - s >= 0)
        def _():
            for h in range(2):
                arrived(chip - s, False, h)
            project(chip - s, False)

        @pl.when((s > 0) & (chip + s < chips))
        def _():
            for h in range(2):
                arrived(chip + s, False, h)
            project(chip + s, False)

        return carry

    lax.fori_loop(0, chips, step, 0)
    for copy in results(c):
        copy.wait()
    own_proj.wait()
    for copy in cuts[-2:]:
        copy.wait()

    for s in range(chips):
        for h in range(2):
            if s < chips - 1:

                @pl.when((chip - s >= 0) & (chip < chips - 1))
                def _(s=s, h=h):
                    hop(s, True, False, h).wait_send()

                @pl.when((chip + s < chips) & (chip > 0))
                def _(s=s, h=h):
                    hop(s, False, False, h).wait_send()

            twin(s, False, h).wait_send()
    for k in range(1, n_fsdp):
        w_copy(k).wait_send()
        s_copy(k).wait_send()
    weights_done()


def start_call(n_ctx, n_fsdp, base, tok, w_slots, small, w_proj, w_fc, cid):
    count, width = tok.shape
    slots, shard, cols = w_slots.shape
    hidden = w_fc.shape[1] // n_fsdp
    vm = pl.BlockSpec(memory_space=pltpu.VMEM)
    anym = pl.BlockSpec(memory_space=pl.ANY)
    dma = pltpu.SemaphoreType.DMA
    return pl.pallas_call(
        functools.partial(start_kernel, n_ctx, n_fsdp, base),
        in_specs=[anym, anym, vm, anym, anym],
        out_specs=[anym, anym, anym, anym, vm, vm],
        out_shape=[
            jax.ShapeDtypeStruct((n_ctx, count, width), BF16),
            jax.ShapeDtypeStruct((slots, n_ctx, count, cols), BF16),
            jax.ShapeDtypeStruct((n_fsdp,) + w_proj.shape, BF16),
            jax.ShapeDtypeStruct((n_fsdp, shard, hidden), BF16),
            jax.ShapeDtypeStruct((slots, width, cols), BF16),
            jax.ShapeDtypeStruct((small.shape[0], width), F32),
        ],
        scratch_shapes=[
            pltpu.VMEM((count, width), BF16),
            pltpu.VMEM((slots, count, cols), BF16),
            pltpu.VMEM(w_fc.shape, BF16),
            pltpu.VMEM((2, shard, hidden), BF16),
            pltpu.VMEM((n_ctx, count, width), BF16),
            pltpu.VMEM((n_fsdp, slots, shard, cols), BF16),
            pltpu.VMEM((n_fsdp,) + small.shape, F32),
            dma((n_ctx, 2)),
            dma((n_ctx // 2, 2)),
            dma((n_ctx // 2, 2)),
            dma((n_ctx // 2, 2)),
            dma((n_fsdp,)),
            dma((n_fsdp,)),
            dma((n_fsdp,)),
            dma((n_fsdp,)),
            dma((2, n_fsdp)),
            dma((2, n_fsdp)),
            dma((6,)),
        ],
        compiler_params=pltpu.CompilerParams(
            collective_id=cid, has_side_effects=True, vmem_limit_bytes=VMEM_LIMIT
        ),
        cost_estimate=SHORT,
        name="tokens_qkv",
    )(tok, w_slots, small, w_proj, w_fc)


def causal_scores(k, q_rows, start):
    scores = dot_last(k, q_rows)
    keep = start
    tail = scores[keep:]
    key_id = lax.broadcasted_iota(jnp.int32, tail.shape, 0)
    query_id = lax.broadcasted_iota(jnp.int32, tail.shape, 1)
    tail = jnp.where(key_id <= query_id, tail, -1e30)
    if keep == 0:
        return tail
    return jnp.concatenate([scores[:keep], tail], axis=0)


def soft(scores, v_t):
    top = jnp.max(scores, axis=0, keepdims=True)
    weights = jnp.exp(scores - top)
    total = jnp.sum(weights, axis=0, keepdims=True)
    out = dot(v_t, weights.astype(BF16)) / total
    return out, top + jnp.log(total)


def causal(inv_ref, x_ref):
    return jnp.concatenate([x_ref[0, inv_ref[i]] for i in range(x_ref.shape[1])], axis=0)


def attn_fwd_kernel(inv_ref, x_ref, o_ref, l_ref):
    rows = l_ref.shape[2]
    hd = HEAD_DIM
    x = causal(inv_ref, x_ref)
    q = x[:, :hd] * BF16(SCALE)
    k = x[:, hd : 2 * hd]
    v_t = x[:, 2 * hd :].T
    for i in range(rows // QROWS):
        lo, hi = i * QROWS, (i + 1) * QROWS
        out, lse = soft(causal_scores(k[:hi], q[lo:hi], lo), v_t[:, :hi])
        l_ref[0, :, lo:hi] = lse
        out = out.astype(BF16)
        for b in range(QROWS // BLOCK):
            o_ref[inv_ref[2 * i + b]] = out[:, b * BLOCK : (b + 1) * BLOCK]


def attn_fwd(inv, qkv, heads):
    blocks, _, cols = qkv.shape[1:]
    rows = blocks * BLOCK
    return pl.pallas_call(
        attn_fwd_kernel,
        grid_spec=pltpu.PrefetchScalarGridSpec(
            num_scalar_prefetch=1,
            grid=(heads,),
            in_specs=[pl.BlockSpec((1, blocks, BLOCK, cols), lambda h, inv: (h, 0, 0, 0))],
            out_specs=[
                pl.BlockSpec((blocks, HEAD_DIM, BLOCK), lambda h, inv: (0, h, 0)),
                pl.BlockSpec((1, 1, rows), lambda h, inv: (h, 0, 0)),
            ],
        ),
        out_shape=[
            jax.ShapeDtypeStruct((blocks, heads * HEAD_DIM, BLOCK), BF16),
            jax.ShapeDtypeStruct((heads, 1, rows), F32),
        ],
        compiler_params=pltpu.CompilerParams(vmem_limit_bytes=VMEM_LIMIT),
        cost_estimate=SHORT,
        name="attn_fwd",
    )(inv, qkv)


def attn_bwd_kernel(inv_ref, x_ref, do_ref, o_ref, l_ref, dx_ref, dk_acc, dv_acc):
    rows = l_ref.shape[2]
    hd = HEAD_DIM
    x = causal(inv_ref, x_ref)
    q = x[:, :hd] * BF16(SCALE)
    k = x[:, hd : 2 * hd]
    v = x[:, 2 * hd :]
    k_t = k.T
    dk_acc[...] = jnp.zeros_like(dk_acc)
    dv_acc[...] = jnp.zeros_like(dv_acc)
    for i in range(rows // QROWS):
        lo, hi = i * QROWS, (i + 1) * QROWS
        ids = [inv_ref[2 * i + b] for b in range(QROWS // BLOCK)]
        do_t = jnp.concatenate([do_ref[b] for b in ids], axis=1)
        o_t = jnp.concatenate([o_ref[b] for b in ids], axis=1)
        inner = jnp.sum(do_t.astype(F32) * o_t.astype(F32), axis=0, keepdims=True)
        probs = jnp.exp(causal_scores(k[:hi], q[lo:hi], lo) - l_ref[0, :, lo:hi])
        dprobs = dot(v[:hi], do_t)
        dscores = (probs * (dprobs - inner)).astype(BF16)
        dv_acc[:hi] += dot_last(probs.astype(BF16), do_t)
        dk_acc[:hi] += dot(dscores, q[lo:hi])
        dq = (dot(k_t[:, :hi], dscores) * SCALE).T
        for n, b in enumerate(ids):
            dx_ref[0, b, :, :hd] = dq[n * BLOCK : (n + 1) * BLOCK].astype(BF16)
    for i in range(rows // BLOCK):
        lo, hi = i * BLOCK, (i + 1) * BLOCK
        dx_ref[0, inv_ref[i], :, hd : 2 * hd] = dk_acc[lo:hi].astype(BF16)
        dx_ref[0, inv_ref[i], :, 2 * hd :] = dv_acc[lo:hi].astype(BF16)


def attn_bwd(inv, qkv, d_out, out, lse, heads):
    blocks, _, cols = qkv.shape[1:]
    rows = blocks * BLOCK
    whole = pl.BlockSpec((1, blocks, BLOCK, cols), lambda h, inv: (h, 0, 0, 0))
    feat = pl.BlockSpec((blocks, HEAD_DIM, BLOCK), lambda h, inv: (0, h, 0))
    return pl.pallas_call(
        attn_bwd_kernel,
        grid_spec=pltpu.PrefetchScalarGridSpec(
            num_scalar_prefetch=1,
            grid=(heads,),
            in_specs=[
                whole,
                feat,
                feat,
                pl.BlockSpec((1, 1, rows), lambda h, inv: (h, 0, 0)),
            ],
            out_specs=whole,
            scratch_shapes=[pltpu.VMEM((rows, HEAD_DIM), F32)] * 2,
        ),
        out_shape=jax.ShapeDtypeStruct((heads, blocks, BLOCK, cols), BF16),
        compiler_params=pltpu.CompilerParams(vmem_limit_bytes=VMEM_LIMIT),
        cost_estimate=pl.CostEstimate(
            flops=24 * 10**9, bytes_accessed=24 * 10**6, transcendentals=0
        ),
        name="attn_bwd",
    )(inv, qkv, d_out, out, lse)


def own_scores(order_ref, x_ref, k):
    hd = HEAD_DIM
    blocks = x_ref.shape[1]
    first = order_ref[blocks]
    q = jnp.concatenate([x_ref[0, first], x_ref[0, first + 1]], axis=0)[:, :hd]
    q = q * BF16(SCALE)
    scores = dot_last(k, q)
    row = lax.broadcasted_iota(jnp.int32, (BLOCK, 1), 0)
    key_place = jnp.concatenate([order_ref[b] * BLOCK + row for b in range(blocks)], axis=0)
    lane = lax.broadcasted_iota(jnp.int32, (1, 2 * BLOCK), 1)
    low, high = order_ref[order_ref[blocks]], order_ref[order_ref[blocks] + 1]
    place = jnp.where(lane < BLOCK, low * BLOCK + lane, (high - 1) * BLOCK + lane)
    return q, first, jnp.where(key_place <= place, scores, -1e30)


def rest_fwd_kernel(order_ref, x_ref, o_ref, l_ref):
    hd = HEAD_DIM
    x = x_ref[0].reshape(-1, 3 * hd)
    _, _, scores = own_scores(order_ref, x_ref, x[:, hd : 2 * hd])
    out, lse = soft(scores, x[:, 2 * hd :].T)
    o_ref[0] = out.astype(BF16)
    l_ref[0] = lse


def rest_fwd(order, qkv, base):
    slots, blocks, _, cols = qkv.shape
    rest = slots - base
    return pl.pallas_call(
        rest_fwd_kernel,
        grid_spec=pltpu.PrefetchScalarGridSpec(
            num_scalar_prefetch=1,
            grid=(rest,),
            in_specs=[
                pl.BlockSpec((1, blocks, BLOCK, cols), lambda h, o: (base + h, 0, 0, 0))
            ],
            out_specs=[
                pl.BlockSpec((1, HEAD_DIM, QROWS), lambda h, o: (h, 0, 0)),
                pl.BlockSpec((1, 1, QROWS), lambda h, o: (h, 0, 0)),
            ],
        ),
        out_shape=[
            jax.ShapeDtypeStruct((rest, HEAD_DIM, QROWS), BF16),
            jax.ShapeDtypeStruct((rest, 1, QROWS), F32),
        ],
        compiler_params=pltpu.CompilerParams(vmem_limit_bytes=VMEM_LIMIT),
        cost_estimate=SHORT,
        name="rest_fwd",
    )(order, qkv)


def rest_bwd_kernel(order_ref, x_ref, do_ref, o_ref, l_ref, dx_ref):
    hd = HEAD_DIM
    x = x_ref[0].reshape(-1, 3 * hd)
    blocks = x_ref.shape[1]
    k = x[:, hd : 2 * hd]
    q, first, scores = own_scores(order_ref, x_ref, k)
    do_t = do_ref[0]
    inner = jnp.sum(do_t.astype(F32) * o_ref[0].astype(F32), axis=0, keepdims=True)
    probs = jnp.exp(scores - l_ref[0])
    dprobs = dot(x[:, 2 * hd :], do_t)
    dscores = (probs * (dprobs - inner)).astype(BF16)
    dv = dot_last(probs.astype(BF16), do_t).astype(BF16)
    dk = dot(dscores, q).astype(BF16)
    dq = (dot(k.T, dscores) * SCALE).T.astype(BF16)
    dx_ref[0, :, :, 2 * hd :] = dv.reshape(blocks, BLOCK, hd)
    dx_ref[0, :, :, hd : 2 * hd] = dk.reshape(blocks, BLOCK, hd)
    dx_ref[0, :, :, :hd] = jnp.zeros((blocks, BLOCK, hd), BF16)
    for b in range(2):
        dx_ref[0, first + b, :, :hd] = dq[b * BLOCK : (b + 1) * BLOCK]


def rest_bwd(order, qkv, d_out, out, lse, base):
    slots, blocks, _, cols = qkv.shape
    rest = slots - base
    feat = pl.BlockSpec((1, HEAD_DIM, QROWS), lambda h, o: (h, 0, 0))
    return pl.pallas_call(
        rest_bwd_kernel,
        grid_spec=pltpu.PrefetchScalarGridSpec(
            num_scalar_prefetch=1,
            grid=(rest,),
            in_specs=[
                pl.BlockSpec((1, blocks, BLOCK, cols), lambda h, o: (base + h, 0, 0, 0)),
                feat,
                feat,
                pl.BlockSpec((1, 1, QROWS), lambda h, o: (h, 0, 0)),
            ],
            out_specs=pl.BlockSpec((1, blocks, BLOCK, cols), lambda h, o: (h, 0, 0, 0)),
        ),
        out_shape=jax.ShapeDtypeStruct((rest, blocks, BLOCK, cols), BF16),
        compiler_params=pltpu.CompilerParams(vmem_limit_bytes=VMEM_LIMIT),
        cost_estimate=SHORT,
        name="rest_bwd",
    )(order, qkv, d_out, out, lse)


def mix_kernel(
    n_ctx,
    n_fsdp,
    out_hbm,
    rest_ref,
    tok_ref,
    proj_ref,
    lines_ref,
    fc_parts,
    att_ref,
    mid_ref,
    n_ref,
    fc_all,
    got_ref,
    out_send,
    out_recv,
    fc_send,
    fc_recv,
    local,
):
    c = lax.axis_index("ctx")
    f = lax.axis_index("fsdp")
    core = c % 2
    width = tok_ref.shape[1]
    shard = width // n_fsdp
    blocks, feats = got_ref.shape[1], got_ref.shape[2]
    enter(
        [(lax.rem(c + i, n_ctx), f) for i in range(1, n_ctx)]
        + [(c, flip(f, k, n_fsdp)) for k in range(1, n_fsdp)]
    )

    def out_copy(i):
        to = lax.rem(c + i, n_ctx)
        return send(
            out_hbm.at[pl.ds(to * blocks, blocks)],
            got_ref.at[c],
            out_send.at[i],
            out_recv.at[i],
            (to, f),
        )

    for i in range(n_ctx - 1, 0, -1):
        out_copy(i).start()
    weights_start, weights_onward, weights_done = weight_shares(
        c,
        f,
        core,
        n_fsdp,
        shard,
        lambda k: fc_parts.at[flip(f, k, n_fsdp)],
        fc_all,
        fc_send,
        fc_recv,
    )
    weights_start()
    own = pltpu.make_async_copy(
        out_hbm.at[pl.ds(c * blocks, blocks)], got_ref.at[c], local.at[0]
    )
    own_fc = pltpu.make_async_copy(fc_parts.at[f], fc_all.at[f], local.at[1])
    own.start()
    own_fc.start()
    main = n_ctx * feats
    if main < width:
        att_ref[:, main:] = rest_ref[...].reshape(width - main, -1).T
    own.wait()
    for i in range(1, n_ctx):
        out_copy(i).wait_recv()
    for src in range(n_ctx):
        block = jnp.concatenate([got_ref[src, b] for b in range(blocks)], axis=1)
        att_ref[:, src * feats : (src + 1) * feats] = block.T
    mid = tok_ref[...].astype(F32) + (dot(att_ref[...], proj_ref[...]) + lines_ref[6:7])
    mid_ref[...] = mid
    cen = mid - jnp.mean(mid, axis=1, keepdims=True)
    var = jnp.mean(cen * cen, axis=1, keepdims=True)
    n_ref[...] = (cen * lax.rsqrt(var + EPS) * lines_ref[1:2] + lines_ref[3:4]).astype(BF16)
    weights_onward()
    own_fc.wait()
    for i in range(1, n_ctx):
        out_copy(i).wait_send()
    weights_done()


def mix_call(n_ctx, n_fsdp, out_own, out_rest, tok, proj, lines, fc_parts, cid):
    count, width = tok.shape
    vm = pl.BlockSpec(memory_space=pltpu.VMEM)
    anym = pl.BlockSpec(memory_space=pl.ANY)
    dma = pltpu.SemaphoreType.DMA
    return pl.pallas_call(
        functools.partial(mix_kernel, n_ctx, n_fsdp),
        in_specs=[anym, vm, vm, vm, vm, anym],
        out_specs=[vm, vm, vm, anym],
        out_shape=[
            jax.ShapeDtypeStruct((count, width), BF16),
            jax.ShapeDtypeStruct((count, width), F32),
            jax.ShapeDtypeStruct((count, width), BF16),
            jax.ShapeDtypeStruct(fc_parts.shape, BF16),
        ],
        scratch_shapes=[
            pltpu.VMEM((n_ctx, out_own.shape[0] // n_ctx) + out_own.shape[1:], BF16),
            dma((n_ctx,)),
            dma((n_ctx,)),
            dma((2, n_fsdp)),
            dma((2, n_fsdp)),
            dma((2,)),
        ],
        compiler_params=pltpu.CompilerParams(
            collective_id=cid, has_side_effects=True, vmem_limit_bytes=VMEM_LIMIT
        ),
        cost_estimate=SHORT,
        name="mix_rows",
    )(out_own, out_rest, tok, proj, lines, fc_parts)


def turn_kernel(
    n_ctx,
    n_fsdp,
    gsum_ref,
    cot_ref,
    mid_ref,
    proj_ref,
    lines_ref,
    fc_hbm,
    parts_hbm,
    grad_ref,
    low_ref,
    sums_ref,
    rest_ref,
    fc_ref,
    rows_ref,
    got_hbm,
    out_ref,
    pair_in,
    rows_in,
    out_send,
    out_recv,
    pair_sem,
    rows_send,
    rows_recv,
    local,
):
    c = lax.axis_index("ctx")
    f = lax.axis_index("fsdp")
    core = c % 2
    width = mid_ref.shape[1]
    blocks, feats = out_ref.shape[0] // n_ctx, out_ref.shape[1]
    enter(
        [(lax.rem(c + i, n_ctx), f) for i in range(1, n_ctx)]
        + [(c, flip(f, k, n_fsdp)) for k in range(1, n_fsdp)]
    )

    def rows_copy(k):
        other = flip(f, k, n_fsdp)
        return send(
            parts_hbm.at[other], rows_in.at[f], rows_send.at[k], rows_recv.at[k], (c, other)
        )

    for k in range(1, n_fsdp):
        rows_copy(k).start()
    own_rows = pltpu.make_async_copy(parts_hbm.at[f], rows_in.at[f], local.at[2])
    own_rows.start()
    pair = send(fc_hbm.at[1 - core], pair_in, pair_sem.at[0], pair_sem.at[1], (c + 1 - 2 * core, f))
    pair.start()
    own_fc = pltpu.make_async_copy(fc_hbm.at[core], fc_ref, local.at[0])
    own_fc.start()

    xhat, rstd = norm_parts(mid_ref[...])
    grad = gsum_ref[...]
    cot = cot_ref[...].astype(F32)
    mid_grad = cot + norm_back(xhat, rstd, lines_ref[1:2], grad)
    grad_ref[...] = mid_grad
    low = mid_grad.astype(BF16)
    low_ref[...] = low
    att_t = dot_last(low, proj_ref[...]).astype(BF16).T
    for to in range(n_ctx):
        for b in range(blocks):
            out_ref[to * blocks + b] = att_t[
                to * feats : (to + 1) * feats, b * BLOCK : (b + 1) * BLOCK
            ]

    def out_copy(i):
        to = lax.rem(c + i, n_ctx)
        return send(
            out_ref.at[pl.ds(to * blocks, blocks)],
            got_hbm.at[pl.ds(c * blocks, blocks)],
            out_send.at[i],
            out_recv.at[i],
            (to, f),
        )

    for i in range(n_ctx - 1, 0, -1):
        out_copy(i).start()
    own = pltpu.make_async_copy(
        out_ref.at[pl.ds(c * blocks, blocks)], got_hbm.at[pl.ds(c * blocks, blocks)], local.at[1]
    )
    own.start()
    main = n_ctx * feats
    if main < width:
        rest_ref[...] = att_t[main:].reshape(rest_ref.shape)
    else:
        rest_ref[...] = jnp.zeros(rest_ref.shape, BF16)
    for r, line in enumerate((grad * xhat, grad, low.astype(F32), cot)):
        sums_ref[r : r + 1] = jnp.sum(line, axis=0, keepdims=True)
    sums_ref[4:] = jnp.zeros((4, width), F32)
    own_fc.wait()
    pair.wait()

    def add(j, carry):
        fc_ref[j] = (fc_ref[j].astype(F32) + pair_in[j].astype(F32)).astype(BF16)
        return carry

    lax.fori_loop(0, fc_ref.shape[0], add, 0)
    own.wait()
    for i in range(1, n_ctx):
        out_copy(i).wait()
    own_rows.wait()
    total = rows_in[f].astype(F32)
    for k in range(1, n_fsdp):
        rows_copy(k).wait()
        total += rows_in[flip(f, k, n_fsdp)].astype(F32)
    rows_ref[...] = (mid_ref[...] + (total + lines_ref[7:8])).astype(BF16)


def turn_call(n_ctx, n_fsdp, base, gsum, cot, mid, proj, lines, fc_part, out_part, cid):
    count, width = mid.shape
    heads = width // HEAD_DIM
    rest = max(heads - base * n_ctx, 1)
    out = (n_ctx * count // BLOCK, base * HEAD_DIM, BLOCK)
    vm = pl.BlockSpec(memory_space=pltpu.VMEM)
    anym = pl.BlockSpec(memory_space=pl.ANY)
    dma = pltpu.SemaphoreType.DMA
    return pl.pallas_call(
        functools.partial(turn_kernel, n_ctx, n_fsdp),
        in_specs=[vm] * 5 + [anym] * 2,
        out_specs=[vm] * 6 + [anym],
        out_shape=[
            jax.ShapeDtypeStruct((count, width), F32),
            jax.ShapeDtypeStruct((count, width), BF16),
            jax.ShapeDtypeStruct((8, width), F32),
            jax.ShapeDtypeStruct((rest, HEAD_DIM, count), BF16),
            jax.ShapeDtypeStruct(fc_part.shape[1:], BF16),
            jax.ShapeDtypeStruct((count, width), BF16),
            jax.ShapeDtypeStruct(out, BF16),
        ],
        scratch_shapes=[
            pltpu.VMEM(out, BF16),
            pltpu.VMEM(fc_part.shape[1:], BF16),
            pltpu.VMEM(out_part.shape, BF16),
            dma((n_ctx,)),
            dma((n_ctx,)),
            dma((2,)),
            dma((n_fsdp,)),
            dma((n_fsdp,)),
            dma((3,)),
        ],
        compiler_params=pltpu.CompilerParams(
            collective_id=cid, has_side_effects=True, vmem_limit_bytes=VMEM_LIMIT
        ),
        cost_estimate=SHORT,
        name="turn_rows",
    )(gsum, cot, mid, proj, lines, fc_part, out_part)


def far_first(i, chips):
    return (i % 2) * (i // 2) + (1 - i % 2) * (chips - 1 - i // 2)


def line_sum(chip, chips, f, core, part, came, sems, ready=None):
    sent, left_sem, right_sem = sems

    def to_right(d):
        return send(
            part.at[d], came.at[d], sent.at[d], left_sem.at[d], (2 * (chip + 1) + core, f)
        )

    def to_left(d):
        place = jnp.where(d == chip - 1, chips, d)
        return send(
            part.at[d], came.at[place], sent.at[d], right_sem.at[d], (2 * (chip - 1) + core, f)
        )

    def from_left(d):
        send(part.at[d], came.at[d], sent.at[d], left_sem.at[d], (2 * chip + core, f)).wait_recv()
        add(d, d)

    def from_right(d, place):
        send(
            part.at[d], came.at[place], sent.at[d], right_sem.at[d], (2 * chip + core, f)
        ).wait_recv()
        add(d, place)

    def add(d, place):
        part[d] = (part[d].astype(F32) + came[place].astype(F32)).astype(BF16)

    def step(t):
        far = chips - 1 - t + chip
        near = t - (chips - 1 - chip)

        @pl.when(chip <= t)
        def _():
            if ready is not None:
                ready(far)

            @pl.when(chip > 0)
            def _():
                from_left(far)

            @pl.when(chip < t)
            def _():
                to_right(far + 1).wait_send()

            to_right(far).start()

        @pl.when(near >= 0)
        def _():
            if ready is not None:
                ready(near)

            @pl.when(chip < chips - 1)
            def _():
                from_right(near, near)

            @pl.when(near > 0)
            def _():
                to_left(near - 1).wait_send()

            to_left(near).start()

    def finish():
        if ready is not None:
            ready(chip)

        @pl.when(chip > 0)
        def _():
            from_left(chip)

        @pl.when(chip < chips - 1)
        def _():
            from_right(chip, chips)

    def done():
        @pl.when(chip < chips - 1)
        def _():
            to_right(chip + 1).wait_send()

        @pl.when(chip > 0)
        def _():
            to_left(chip - 1).wait_send()

    return step, finish, done


def line_gather(chip, chips, f, core, view, sems):
    right, left, twin_sent, got, twin_got = sems
    twin_id = (2 * chip + 1 - core, f)

    def hop(s, rightward):
        origin = chip - s if rightward else chip + s
        ref = view(origin, core)
        peer = (2 * (chip + 1 if rightward else chip - 1) + core, f)
        return send(ref, ref, (right if rightward else left).at[s], got.at[origin], peer)

    def twin(origin):
        ref = view(origin, core)
        return send(ref, ref, twin_sent.at[origin], twin_got.at[origin], twin_id)

    def arrived(origin):
        ref = view(origin, core)
        send(ref, ref, right.at[0], got.at[origin], twin_id).wait_recv()

    def step(s):
        @pl.when(chip - s >= 0)
        def _():
            if s:
                arrived(chip - s)

            @pl.when(chip < chips - 1)
            def _():
                hop(s, True).start()

            twin(chip - s).start()

        @pl.when(chip + s < chips)
        def _():
            if s:
                arrived(chip + s)

            @pl.when(chip > 0)
            def _():
                hop(s, False).start()

            if s:
                twin(chip + s).start()

    def done():
        for s in range(chips):
            if s < chips - 1:

                @pl.when((chip - s >= 0) & (chip < chips - 1))
                def _(s=s):
                    hop(s, True).wait_send()

                @pl.when((chip + s < chips) & (chip > 0))
                def _(s=s):
                    hop(s, False).wait_send()

            twin(s).wait_send()
            ref = view(s, 1 - core)
            send(ref, ref, twin_sent.at[s], twin_got.at[s], twin_id).wait_recv()

    return step, done


def back_kernel(
    n_ctx,
    n_fsdp,
    own_ref,
    rest_ref,
    w_ref,
    n_ref,
    fc_hbm,
    one_ref,
    cols_ref,
    fc_all,
    part,
    twin_out,
    twin_in,
    came,
    mine,
    theirs,
    twin_send,
    twin_recv,
    line_send,
    left_recv,
    right_recv,
    cols_send,
    cols_recv,
    fc_send,
    fc_recv,
    local,
):
    c = lax.axis_index("ctx")
    f = lax.axis_index("fsdp")
    chips = n_ctx // 2
    chip, core = c // 2, c % 2
    slots, width, cols = w_ref.shape
    count = own_ref.shape[2]
    base = own_ref.shape[0]
    shard = width // n_fsdp
    twin_id = (2 * chip + 1 - core, f)
    enter(
        [(lax.rem(c + i, n_ctx), f) for i in range(1, n_ctx)]
        + [(c, flip(f, k, n_fsdp)) for k in range(1, n_fsdp)]
    )

    def grad(s):
        return own_ref.at[s] if s < base else rest_ref.at[s - base]

    def for_block(b):
        total = dot_last(grad(0)[b], w_ref[0])
        for s in range(1, slots):
            total += dot_last(grad(s)[b], w_ref[s])
        return total.astype(BF16)

    def to_twin(d, slot):
        return send(twin_out.at[slot], twin_in.at[d], twin_send.at[slot], twin_recv.at[d], twin_id)

    def products(i, carry):
        d = far_first(i, chips)
        slot = i % 2
        product = for_block(2 * d + 1 - core)

        @pl.when(i > 1)
        def _():
            to_twin(d, slot).wait_send()

        twin_out[slot] = product
        to_twin(d, slot).start()
        part[d] = for_block(2 * d + core)
        return carry

    def ready(d):
        to_twin(d, 0).wait_recv()
        part[d] = (part[d].astype(F32) + twin_in[d].astype(F32)).astype(BF16)

    cut = count // 2
    streams = [
        line_sum(
            chip,
            chips,
            f,
            core,
            part.at[:, pl.ds(h * cut, cut)],
            came.at[h],
            (line_send.at[h], left_recv.at[h], right_recv.at[h]),
            None if h else ready,
        )
        for h in range(2)
    ]

    def step(t):
        for stream in streams:
            stream[0](t)

    def finish():
        for stream in streams:
            stream[1]()

    def done():
        for stream in streams:
            stream[2]()

    def cols_copy(src, dst, at):
        return send(mine.at[src], theirs.at[at], cols_send.at[src], cols_recv.at[at], (c, dst))

    def columns(j):
        left = n_ref[:, :, j * shard : (j + 1) * shard].reshape(n_ctx * count, shard)
        for s in range(slots):
            right = grad(s)[...].reshape(n_ctx * count, cols)
            mine[j, s] = dot_first(left, right).astype(BF16)

    def fc_copy(k):
        other = flip(f, k, n_fsdp)
        return send(fc_hbm.at[other], fc_all.at[f], fc_send.at[k], fc_recv.at[k], (c, other))

    for k in range(1, n_fsdp):
        fc_copy(k).start()
    own_fc = pltpu.make_async_copy(fc_hbm.at[f], fc_all.at[f], local)
    own_fc.start()
    lax.fori_loop(0, 2, products, 0)
    step(0)
    for j in range(n_fsdp):
        columns(j)
    for k in range(1, n_fsdp):
        other = flip(f, k, n_fsdp)
        cols_copy(other, other, f).start()
    lax.fori_loop(2, chips, products, 0)
    if chips > 2:
        step(1)
    for t in range(2, chips - 1):
        step(t)
    total = mine[f].astype(F32)
    for k in range(1, n_fsdp):
        other = flip(f, k, n_fsdp)
        cols_copy(other, other, other).wait_recv()
        total += theirs[other].astype(F32)
    cols_ref[...] = total.astype(BF16)
    finish()
    one_ref[...] = part[chip]
    own_fc.wait()
    for k in range(1, n_fsdp):
        fc_copy(k).wait()
    done()
    for slot in range(2):
        to_twin(0, slot).wait_send()
    for k in range(1, n_fsdp):
        other = flip(f, k, n_fsdp)
        cols_copy(other, other, other).wait_send()


def back_fits(n_ctx, n_fsdp, count, width, slots):
    blocks = (5 * (n_ctx // 2) + n_ctx) * count * width
    heads = slots * 256 * (n_ctx * count + 3 * width)
    return 2 * (blocks + heads) < 50 * 1024 * 1024


def back_call(n_ctx, n_fsdp, own, rest, w_slots, normed, fc_mine, cid):
    slots, width, cols = w_slots.shape
    count = normed.shape[1]
    chips = n_ctx // 2
    shard = width // n_fsdp
    vm = pl.BlockSpec(memory_space=pltpu.VMEM)
    anym = pl.BlockSpec(memory_space=pl.ANY)
    dma = pltpu.SemaphoreType.DMA
    block = pltpu.VMEM((chips, count, width), BF16)
    piece = pltpu.VMEM((n_fsdp, slots, shard, cols), BF16)
    return pl.pallas_call(
        functools.partial(back_kernel, n_ctx, n_fsdp),
        in_specs=[vm] * 4 + [anym],
        out_specs=[vm] * 2 + [anym],
        out_shape=[
            jax.ShapeDtypeStruct((count, width), BF16),
            jax.ShapeDtypeStruct((slots, shard, cols), BF16),
            jax.ShapeDtypeStruct(fc_mine.shape, BF16),
        ],
        scratch_shapes=[
            block,
            pltpu.VMEM((2, count, width), BF16),
            block,
            pltpu.VMEM((2, chips + 1, count // 2, width), BF16),
        ]
        + [piece] * 2
        + [dma((2,)), dma((chips,))]
        + [dma((2, chips))] * 3
        + [dma((n_fsdp,))] * 4
        + [dma(())],
        compiler_params=pltpu.CompilerParams(
            collective_id=cid, has_side_effects=True, vmem_limit_bytes=60 * 1024 * 1024
        ),
        cost_estimate=SHORT,
        name="qkv_back",
    )(own, rest, w_slots, normed, fc_mine)


def sums_kernel(n_ctx, n_fsdp, lead, *refs):
    rows_ref, cols_ref, extra_ref, att_ref, mid_ref, lines_in = refs[:6]
    outs, cols_all, lines_ref = refs[6:8], refs[8], refs[9]
    parts, cames = refs[10:12], refs[12:14]
    proj_part, proj_in, proj_got, lines_got = refs[14:18]
    lines_send, lines_recv, local, proj_send, proj_recv, pair_sem = refs[18:24]
    cols_sems = refs[24:29]
    sems = [(refs[29 + 8 * i : 32 + 8 * i], refs[32 + 8 * i : 37 + 8 * i]) for i in range(2)]
    c = lax.axis_index("ctx")
    f = lax.axis_index("fsdp")
    chips = n_ctx // 2
    chip, core = c // 2, c % 2
    width = att_ref.shape[1]
    shard = width // n_fsdp
    half = shard // 2
    high = proj_in.shape[1]
    twin_id = (2 * chip + 1 - core, f)
    enter(
        [(lax.rem(c + i, n_ctx), f) for i in range(1, n_ctx)]
        + [(c, flip(f, k, n_fsdp)) for k in range(1, n_fsdp)]
    )

    def line_ops(i):
        sum_sems, gather_sems = sems[i]
        gather = line_gather(chip, chips, f, core, lambda at, h: outs[i].at[h, at], gather_sems)
        return line_sum(chip, chips, f, core, parts[i], cames[i], sum_sems) + gather

    def proj_pair():
        return send(proj_part.at[1 - core], proj_in, pair_sem.at[0], pair_sem.at[1], twin_id)

    def proj_copy(k):
        other = flip(f, k, n_fsdp)
        return send(
            proj_part.at[core, other],
            proj_got.at[f],
            proj_send.at[k],
            proj_recv.at[k],
            (c, other),
        )

    def proj_products(j):
        for h in range(2):
            lo = j * shard + h * half
            proj_part[h, j, :half] = dot_first(att_ref[:, lo : lo + half], mid_ref[...]).astype(BF16)
            if half < high:
                proj_part[h, j, half:] = jnp.zeros((high - half, width), BF16)

    def proj_add(j, carry):
        proj_part[core, j] = (
            proj_part[core, j].astype(F32) + proj_in[j].astype(F32)
        ).astype(BF16)
        return carry

    def proj_total():
        total = proj_part[core, f].astype(F32)
        for k in range(1, n_fsdp):
            proj_copy(k).wait_recv()
            total += proj_got[flip(f, k, n_fsdp)].astype(F32)
        total = jnp.concatenate([total.astype(BF16), extra_ref[...]], axis=0)
        first = rows_ref.shape[1] - parts[0].shape[1]
        step, rows = parts[1].shape[1] - first, total.shape[0]
        for p in range(chips):
            lo, hi = min(p * step, rows), min((p + 1) * step, rows)
            end = first + hi - lo
            if hi > lo:
                parts[1][p, first:end] = total[lo:hi]
            if hi - lo < step:
                parts[1][p, end:] = jnp.zeros((step - hi + lo, width), BF16)

    peers = [(flip(c, 1 << i, n_ctx), f) for i in range(n_ctx.bit_length() - 1)]
    ctx_phases = len(peers)
    peers += [(c, flip(f, 1 << i, n_fsdp)) for i in range(n_fsdp.bit_length() - 1)]

    def line_copy(i):
        rows = lines_in.shape[0] if i < ctx_phases else lead
        return send(
            lines_ref.at[:rows],
            lines_got.at[i, :rows],
            lines_send.at[i],
            lines_recv.at[i],
            peers[i],
        )

    def line_phase(i):
        if 0 < i <= len(peers):
            rows = lines_in.shape[0] if i <= ctx_phases else lead
            line_copy(i - 1).wait()
            lines_ref[:rows] += lines_got[i - 1, :rows]
        if i < len(peers):
            line_copy(i).start()

    def settle(finish, i):
        finish()
        keep = pltpu.make_async_copy(parts[i].at[chip], outs[i].at[core, chip], local.at[0])
        keep.start()
        keep.wait()

    sum_a, finish_a, sums_a, gather_a, gathers_a = line_ops(0)
    sum_b, finish_b, sums_b, gather_b, gathers_b = line_ops(1)
    cols_step, cols_done = line_gather(
        chip, chips, f, core, lambda at, h: cols_all.at[2 * at + h], cols_sems
    )
    load = pltpu.make_async_copy(cols_ref, cols_all.at[c], local.at[1])
    load.start()
    cut = parts[0].shape[1]
    parts[0][...] = rows_ref[:, :cut]
    load.wait()
    cols_step(0)
    sum_a(0)
    parts[1][:, : rows_ref.shape[1] - cut] = rows_ref[:, cut:]
    lines_ref[...] = lines_in[...]
    for j in range(n_fsdp):
        proj_products(j)
    proj_pair().start()
    for t in range(1, chips - 1):
        cols_step(t)
        sum_a(t)
        if t == 1:
            proj_pair().wait()
            lax.fori_loop(0, n_fsdp, proj_add, 0)
            for k in range(1, n_fsdp):
                proj_copy(k).start()
    cols_step(chips - 1)
    settle(finish_a, 0)
    gather_a(0)
    proj_total()
    sum_b(0)
    phase = 0
    for s in range(1, chips):
        gather_a(s)
        if s < chips - 1:
            sum_b(s)
        line_phase(phase)
        phase += 1
    settle(finish_b, 1)
    for s in range(chips):
        gather_b(s)
        line_phase(phase)
        phase += 1
    while phase <= len(peers):
        line_phase(phase)
        phase += 1
    for done in (sums_a, sums_b, cols_done, gathers_a, gathers_b):
        done()
    for k in range(1, n_fsdp):
        proj_copy(k).wait_send()


def sums_call(n_ctx, n_fsdp, rows, cols, extra, attended, mid_low, lines, lead, cid):
    chips = n_ctx // 2
    count, width = attended.shape
    high = half_high(width // n_fsdp)
    per_chip = rows.shape[1]
    third = -(-(high + extra.shape[0]) // (16 * chips)) * 16
    cut = -(-(per_chip + third) // 32) * 16
    shapes = [(chips, size, width) for size in (cut, per_chip + third - cut)]
    phases = (n_ctx * n_fsdp).bit_length() - 1
    vm = pl.BlockSpec(memory_space=pltpu.VMEM)
    anym = pl.BlockSpec(memory_space=pl.ANY)
    dma = pltpu.SemaphoreType.DMA
    return pl.pallas_call(
        functools.partial(sums_kernel, n_ctx, n_fsdp, lead),
        in_specs=[vm, anym, vm, vm, vm, vm],
        out_specs=[vm, vm, anym, vm],
        out_shape=[jax.ShapeDtypeStruct((2,) + shape, BF16) for shape in shapes]
        + [jax.ShapeDtypeStruct((n_ctx,) + cols.shape, BF16)]
        + [jax.ShapeDtypeStruct(lines.shape, F32)],
        scratch_shapes=[pltpu.VMEM(shape, BF16) for shape in shapes]
        + [pltpu.VMEM((chips + 1,) + shape[1:], BF16) for shape in shapes]
        + [
            pltpu.VMEM((2, n_fsdp, high, width), BF16),
            pltpu.VMEM((n_fsdp, high, width), BF16),
            pltpu.VMEM((n_fsdp, high, width), BF16),
            pltpu.VMEM((phases,) + lines.shape, F32),
            dma((phases,)),
            dma((phases,)),
            dma((2,)),
            dma((n_fsdp,)),
            dma((n_fsdp,)),
            dma((2,)),
        ]
        + [dma((chips,))] * (5 + 2 * 8),
        compiler_params=pltpu.CompilerParams(
            collective_id=cid, has_side_effects=True, vmem_limit_bytes=56 * 1024 * 1024
        ),
        cost_estimate=SHORT,
        name="weight_sums",
    )(rows, cols, extra, attended, mid_low, lines)


def assemble_kernel(
    n_fsdp,
    own_ref,
    rest_ref,
    first_ref,
    second_ref,
    third_ref,
    out_ref,
    attn_hbm,
    fc_hbm,
    proj_hbm,
    wout_hbm,
    *scratch,
):
    attn_ref, fc_ref, proj_ref, wout_ref, low_ref, sem = scratch
    load = pltpu.make_async_copy(out_ref, low_ref, sem.at[4])
    load.start()
    hd = HEAD_DIM
    shard, hidden = fc_ref.shape[0], fc_ref.shape[1] // n_fsdp
    half = shard // 2
    width = proj_ref.shape[1]
    count = own_ref.shape[0]
    copies = [
        pltpu.make_async_copy(src, dst, sem.at[i])
        for i, (src, dst) in enumerate(
            ((wout_ref, wout_hbm), (fc_ref, fc_hbm), (proj_ref, proj_hbm), (attn_ref, attn_hbm))
        )
    ]
    for h in range(2):
        for j in range(n_fsdp):
            cut = min(first_ref.shape[2], half)
            at = slice(j * hidden, (j + 1) * hidden)
            fc_ref[h * half : h * half + cut, at] = first_ref[h, j, :cut].astype(F32)
            if cut < half:
                rows = second_ref[h, j, : half - cut].astype(F32)
                fc_ref[h * half + cut : (h + 1) * half, at] = rows
    copies[1].start()
    for h in range(2):
        proj_ref[h * half : (h + 1) * half] = third_ref[h, :half].astype(F32)
    copies[2].start()
    for h in range(width // hd):
        src = own_ref.at[h] if h < count else rest_ref.at[h - count]
        for part in range(3):
            at = part * width + h * hd
            attn_ref[:, at : at + hd] = src[:, part * hd : (part + 1) * hd].astype(F32)
    copies[3].start()
    load.wait()
    wout_ref[...] = low_ref[...].astype(F32)
    copies[0].start()
    for copy in copies:
        copy.wait()


def assemble(n_fsdp, own, rest, first, second, third, out_low, hidden):
    shard = own.shape[1]
    width = first.shape[3]
    vm = pl.BlockSpec(memory_space=pltpu.VMEM)
    anym = pl.BlockSpec(memory_space=pl.ANY)
    shapes = [(shard, 3 * width), (shard, n_fsdp * hidden), (shard, width), out_low.shape]
    return pl.pallas_call(
        functools.partial(assemble_kernel, n_fsdp),
        in_specs=[vm] * 5 + [anym],
        out_specs=[anym] * 4,
        out_shape=[jax.ShapeDtypeStruct(shape, F32) for shape in shapes],
        scratch_shapes=[pltpu.VMEM(shape, F32) for shape in shapes]
        + [pltpu.VMEM(out_low.shape, BF16), pltpu.SemaphoreType.DMA((5,))],
        compiler_params=pltpu.CompilerParams(vmem_limit_bytes=60 * 1024 * 1024),
        cost_estimate=SHORT,
        name="assemble",
    )(own, rest, first, second, third, out_low)


def swap(value, axis, size, k):
    return lax.ppermute(value, axis, [(i, i ^ k) for i in range(size)])


def shards(
    n_ctx,
    n_fsdp,
    tokens,
    block_order,
    w_attn,
    w_proj,
    w_fc,
    w_out,
    norm_gains,
    biases,
    fc_bias,
    cotangent,
):
    hd = HEAD_DIM
    count, width = tokens.shape[1:]
    shard = width // n_fsdp
    heads = width // hd
    base = heads // n_ctx
    rest = heads - base * n_ctx
    slots = base + rest
    own_blocks = count // BLOCK
    c = lax.axis_index("ctx")
    f = lax.axis_index("fsdp")

    order = block_order[0]
    inv = jnp.argsort(order).astype(jnp.int32)
    order_own = jnp.concatenate([order, (c * own_blocks)[None]])

    def head_cols(h):
        return jnp.concatenate(
            [
                lax.dynamic_slice(w_attn, (0, part * width + h * hd), (shard, hd))
                for part in range(3)
            ],
            axis=1,
        )

    slot_heads = [c * base + s for s in range(base)] + [n_ctx * base + r for r in range(rest)]
    w_slots = jnp.stack([head_cols(h) for h in slot_heads])
    small = jnp.concatenate([norm_gains, biases], axis=0).astype(F32)
    hidden_cols = w_fc.shape[1] // n_fsdp
    normed_one, qkv, full_proj, fc_parts, w_slots, small = start_call(
        n_ctx, n_fsdp, base, tokens[0], w_slots, small, w_proj, w_fc, 3
    )
    full_proj = full_proj.reshape(width, width)
    qkv = qkv.reshape(slots, n_ctx * own_blocks, BLOCK, 3 * hd)
    gains, shifts = small[:2], small[2:]
    cot = cotangent[0]

    cot_late, _ = lax.optimization_barrier((cot, small))
    cot_all = lax.all_gather(cot_late, "fsdp", axis=0)

    out_own, lse_own = attn_fwd(inv, qkv, base)
    if rest:
        out_rest, lse_rest = rest_fwd(order_own, qkv, base)
    else:
        out_rest = out_own
    attended, mid, normed_two, fc_cols = mix_call(
        n_ctx, n_fsdp, out_own, out_rest, tokens[0], full_proj, small, fc_parts, 6
    )
    fc_cols = fc_cols.reshape(width, hidden_cols)
    rows = tokens[0].astype(F32)

    normed_two_grad, fc_bias_part, out_part, w_out_part, w_fc_part = ffn(
        n_fsdp,
        normed_two,
        cot_all,
        fc_cols,
        w_out,
        fc_bias.astype(F32)[None],
    )
    w_out_sum = lax.psum_scatter(w_out_part, "ctx", scatter_dimension=0, tiled=True)

    half, high = shard // 2, half_high(shard)
    core = c % 2
    main = n_ctx * base * hd
    mid_grad, mid_low, turn_sums, d_rest, fc_mine, layer_rows, d_out = turn_call(
        n_ctx,
        n_fsdp,
        base,
        normed_two_grad,
        cot,
        mid,
        full_proj,
        small,
        w_fc_part,
        out_part,
        7,
    )

    d_own = attn_bwd(inv, qkv, d_out, out_own, lse_own, base)
    d_own = d_own.reshape(base, n_ctx, count, 3 * hd)
    if rest:
        d_rest = rest_bwd(order_own, qkv, d_rest, out_rest, lse_rest, base)
        d_rest = d_rest.reshape(rest, n_ctx, count, 3 * hd)
        sums = jnp.concatenate(
            [jnp.sum(d.astype(F32), axis=(1, 2)) for d in (d_own, d_rest)], axis=0
        )
    else:
        d_rest = d_own
        sums = jnp.sum(d_own.astype(F32), axis=(1, 2))
    if back_fits(n_ctx, n_fsdp, count, width, slots):
        normed_one_grad, cols_sum, fc_rows = back_call(
            n_ctx, n_fsdp, d_own, d_rest, w_slots, normed_one, fc_mine, 4
        )
        normed_one_grad = normed_one_grad.astype(F32)
    else:
        dqkv = jnp.concatenate([d_own, d_rest])[:slots].reshape(slots, n_ctx * count, 3 * hd)
        one_part = jnp.einsum("hte,hde->td", dqkv, w_slots, preferred_element_type=F32)
        normed_one_grad = lax.psum_scatter(
            one_part.astype(BF16), "ctx", scatter_dimension=0, tiled=True
        ).astype(F32)
        slot_part = jnp.einsum(
            "td,hte->hde",
            normed_one.reshape(n_ctx * count, width),
            dqkv,
            preferred_element_type=F32,
        ).astype(BF16)
        cols_sum = lax.psum_scatter(slot_part, "fsdp", scatter_dimension=1, tiled=True)
        fc_rows = lax.all_to_all(fc_mine, "fsdp", split_axis=0, concat_axis=0, tiled=True)

    w_out_sum, fc_rows = lax.optimization_barrier((w_out_sum, fc_rows))
    w_out_low = lax.all_gather(w_out_sum, "ctx", axis=0, tiled=True)
    xhat_one, rstd_one = norm_parts(rows)
    tokens_grad = (mid_grad + norm_back(xhat_one, rstd_one, gains[0], normed_one_grad)).astype(
        BF16
    )

    def placed(part):
        cols = sums[:, part * hd : (part + 1) * hd]
        line = lax.dynamic_update_slice_in_dim(
            jnp.zeros((width,), F32), cols[:base].reshape(-1), c * base * hd, 0
        )
        return line + jnp.pad(cols[base:].reshape(-1), (main, 0))

    lines = jnp.stack(
        [
            jnp.sum(normed_one_grad * xhat_one, axis=0),
            turn_sums[0],
            jnp.sum(normed_one_grad, axis=0),
            turn_sums[1],
            placed(0),
            placed(2),
            turn_sums[2],
            turn_sums[3],
        ]
    )
    lead = lines.shape[0]
    tail = jnp.pad(fc_bias_part, ((0, 7), (0, width - hidden_cols)))
    lines = jnp.concatenate([lines, tail])

    chips = n_ctx // 2
    fc_rows = fc_rows.reshape(-1, width)
    per_chip = -(-fc_rows.shape[0] // (16 * chips)) * 16
    fc_rows = jnp.pad(fc_rows, ((0, per_chip * chips - fc_rows.shape[0]), (0, 0)))
    fc_rows = fc_rows.reshape(chips, per_chip, width)
    extra = jnp.zeros((16, width), BF16)
    if rest:
        away = lax.dynamic_slice_in_dim(cols_sum[base:], (1 - core) * half, half, 1)
        here = lax.dynamic_slice_in_dim(cols_sum[base:], core * half, half, 1)
        extra = here.astype(F32) + swap(away, "ctx", n_ctx, 1).astype(F32)
        extra = extra.astype(BF16).reshape(-1, width)
        extra_rows = extra.shape[0]
        extra = jnp.pad(extra, ((0, -extra_rows % 16), (0, 0)))
    first, second, own_cols, lines = sums_call(
        n_ctx, n_fsdp, fc_rows, cols_sum[:base], extra, attended, mid_low, lines, lead, 5
    )
    w_out_low, lines = lax.optimization_barrier((w_out_low, lines))
    split = per_chip - first.shape[2]
    third = second[:, :, split:].reshape(2, -1, width)
    second = second[:, :, :split]
    own_cols = own_cols.reshape(n_ctx * base, shard, 3 * hd)
    if rest:
        rest_cols = third[:, high : high + extra_rows].reshape(2, rest, half, 3 * hd)
        rest_cols = rest_cols.transpose(1, 0, 2, 3).reshape(rest, shard, 3 * hd)
    else:
        rest_cols = own_cols
    if hidden_cols == width and chips == n_fsdp:
        w_attn_grad, w_fc_grad, w_proj_grad, w_out_grad = assemble(
            n_fsdp, own_cols, rest_cols, first, second, third, w_out_low, hidden_cols
        )
    else:
        w_fc_low = jnp.concatenate([first, second], axis=2).reshape(2, -1, width)
        w_fc_low = w_fc_low[:, : n_fsdp * high * hidden_cols // width]
        w_fc_low = w_fc_low.reshape(2, n_fsdp, high, hidden_cols)[:, :, :half]
        w_fc_grad = w_fc_low.transpose(0, 2, 1, 3).reshape(shard, n_fsdp * hidden_cols)
        w_fc_grad = w_fc_grad.astype(F32)
        w_proj_grad = third[:, :half].reshape(shard, width).astype(F32)
        cols = jnp.concatenate([own_cols, rest_cols])[: width // hd]
        cols = cols.reshape(width // hd, shard, 3, hd).transpose(1, 2, 0, 3)
        w_attn_grad = cols.reshape(shard, 3 * width).astype(F32)
        w_out_grad = w_out_low.astype(F32)
    fc_bias_grad = lines[lead, :hidden_cols]
    lines = lax.dynamic_slice_in_dim(lines[:lead], f * shard, shard, 1)
    return (
        layer_rows[None],
        tokens_grad[None],
        w_attn_grad,
        w_proj_grad,
        w_fc_grad,
        w_out_grad,
        lines[:2],
        lines[2:],
        fc_bias_grad,
    )


def solution(mesh):
    rows = P("fsdp", "ctx", None)
    weight = P("fsdp", None)
    vectors = P(None, "fsdp")
    return jax.shard_map(
        functools.partial(shards, mesh.shape["ctx"], mesh.shape["fsdp"]),
        mesh=mesh,
        in_specs=(
            rows, weight, weight, weight, weight, weight, vectors, vectors, P("fsdp"), rows,
        ),
        out_specs=(
            rows, rows, weight, weight, weight, weight, vectors, vectors, P("fsdp"),
        ),
        check_vma=False,
    )
```

```python
import functools

import jax
import jax.numpy as jnp
from jax import lax
from jax.experimental import pallas as pl
from jax.experimental.pallas import tpu as pltpu
from jax.sharding import PartitionSpec as P

HEAD_DIM = 64
BLOCK = 128
QROWS = 256
EPS = 1e-05
SCALE = HEAD_DIM ** (-0.5)
F32 = jnp.float32
BF16 = jnp.bfloat16
VMEM_LIMIT = 56 * 1024 * 1024
LAST = (((1,), (1,)), ((), ()))
FIRST = (((0,), (0,)), ((), ()))
MESH = pl.DeviceIdType.MESH
TILE = 256


def dot_last(a, b):
    return lax.dot_general(a, b, LAST, preferred_element_type=F32)


def dot(a, b):
    return jnp.dot(a, b, preferred_element_type=F32)


def dot_first(a, b):
    return lax.dot_general(a, b, FIRST, preferred_element_type=F32)


SHORT = pl.CostEstimate(flops=1, bytes_accessed=1, transcendentals=0)


def norm_parts(rows):
    mean = jnp.mean(rows, axis=-1, keepdims=True)
    cen = rows - mean
    rstd = lax.rsqrt(jnp.mean(cen * cen, axis=-1, keepdims=True) + EPS)
    return cen * rstd, rstd


def norm_back(xhat, rstd, gain, grad):
    dxhat = grad * gain
    return rstd * (
        dxhat
        - jnp.mean(dxhat, axis=-1, keepdims=True)
        - xhat * jnp.mean(dxhat * xhat, axis=-1, keepdims=True)
    )


def flip(place, k, size):
    out = 0
    bit = 1
    while bit < size:
        out = out + (place // bit + k // bit) % 2 * bit
        bit *= 2
    return out

def half_high(shard):
    return -(-(shard // 2) // 16) * 16


def enter(peers):
    barrier = pltpu.get_barrier_semaphore()
    for peer in peers:
        pl.semaphore_signal(barrier, inc=1, device_id=peer, device_id_type=MESH)
    pl.semaphore_wait(barrier, len(peers))

def send(src, dst, send_sem, recv_sem, peer):
    return pltpu.make_async_remote_copy(
        src_ref=src, dst_ref=dst, send_sem=send_sem, recv_sem=recv_sem,
        device_id=peer, device_id_type=MESH)


def ffn_kernel(n, nt_hbm, cot_hbm, wfc_hbm, wout_hbm, bias_ref,
               gsum_ref, fcb_ref, out_hbm, wout_grad_hbm, wfc_grad_hbm,
               cot_ref, wfc_ref, wout_ref, all_ref, act_ref, hg_ref, ag_ref, part_ref, got_ref, stage_d, stage_h,
               s1, r1, s2, r2, local):
    c = lax.axis_index("ctx")
    f = lax.axis_index("fsdp")
    rows, width = nt_hbm.shape
    enter([(c, flip(f, k, n)) for k in range(1, n)])

    def rows_out(k):
        return send(nt_hbm, all_ref.at[f], s1.at[k], r1.at[k], (c, flip(f, k, n)))

    def grad_back(k):
        other = flip(f, k, n)
        return send(part_ref.at[other], got_ref.at[k], s2.at[k], r2.at[k], (c, other))

    near = [k for k in range(1, n) if k & (k - 1) == 0]
    far = [k for k in range(1, n) if k not in near]
    for k in near:
        rows_out(k).start()
    loads = [
        pltpu.make_async_copy(nt_hbm, all_ref.at[f], local.at[0]),
        pltpu.make_async_copy(wout_hbm, wout_ref, local.at[1]),
        pltpu.make_async_copy(cot_hbm, cot_ref, local.at[2]),
        pltpu.make_async_copy(wfc_hbm, wfc_ref, local.at[3]),
    ]
    for load in loads:
        load.start()
    fcb_ref[...] = jnp.zeros_like(fcb_ref)
    loads[1].wait()
    loads[2].wait()

    def active_grad(k, carry):
        ag_ref[k] = dot_last(cot_ref[k], wout_ref[...])
        return carry

    lax.fori_loop(0, n, active_grad, 0)
    for k in far:
        rows_out(k).start()
    loads[0].wait()
    loads[3].wait()

    def chunk(k, carry):
        src = flip(f, k, n)

        @pl.when(k > 0)
        def _():
            rows_out(k).wait_recv()

        hidden = dot(all_ref[src], wfc_ref[...]) + bias_ref[...]
        square = hidden * hidden
        tanh = jnp.tanh(0.7978845608028654 * (hidden + 0.044715 * square * hidden))
        act_ref[src] = (0.5 * hidden * (1.0 + tanh)).astype(BF16)
        slope = 0.5 * (1.0 + tanh) + 0.5 * hidden * (1.0 - tanh * tanh) * 0.7978845608028654 * (
            1.0 + 3.0 * 0.044715 * square
        )
        grad = (ag_ref[src] * slope).astype(BF16)
        hg_ref[src] = grad
        fcb_ref[...] += jnp.sum(grad.astype(F32), axis=0, keepdims=True)
        part_ref[src] = dot_last(grad, wfc_ref[...]).astype(BF16)

        @pl.when(k > 0)
        def _():
            grad_back(k).start()

        return carry

    lax.fori_loop(0, n, chunk, 0)

    def grads(left_ref, right_ref, tiles, stage_ref, base):
        right = right_ref[...].reshape(n * rows, right_ref.shape[2])
        copies = []
        for i, (lo, size, sent, dst) in enumerate(tiles):
            slot = i % 2
            if i >= 2:
                copies[i - 2].wait()
            left = left_ref[:, :, lo : lo + size].reshape(n * rows, size)
            stage_ref[slot, :size] = dot_first(left, right).astype(BF16)
            copies.append(
                pltpu.make_async_copy(stage_ref.at[slot, :sent], dst, local.at[base + slot])
            )
            copies[-1].start()
        for copy in copies[-2:]:
            copy.wait()

    half, high = width // n // 2, wfc_grad_hbm.shape[2]
    if half < high:
        stage_h[:, half:high] = jnp.zeros((2, high - half, stage_h.shape[2]), BF16)
    wide = act_ref.shape[2]
    sizes = [(lo, min(TILE, wide - lo)) for lo in range(0, wide, TILE)]
    grads(
        act_ref,
        cot_ref,
        [(lo, size, size, wout_grad_hbm.at[lo : lo + size]) for lo, size in sizes],
        stage_d,
        4,
    )
    grads(
        all_ref,
        hg_ref,
        [
            ((2 * j + h) * half, half, high, wfc_grad_hbm.at[h, j])
            for j in range(n)
            for h in range(2)
        ],
        stage_h,
        6,
    )

    def out_copy(k):
        return pltpu.make_async_copy(
            stage_d.at[k % 2, :rows], out_hbm.at[k], local.at[4 + k % 2]
        )

    for k in range(n):
        if k >= 2:
            out_copy(k - 2).wait()
        stage_d[k % 2, :rows] = dot(act_ref[k], wout_ref[...]).astype(BF16)
        out_copy(k).start()

    gsum_ref[...] = part_ref[f].astype(F32)
    for k in near + far:
        grad_back(k).wait_recv()
        gsum_ref[...] += got_ref[k].astype(F32)
    for k in range(1, n):
        rows_out(k).wait_send()
        grad_back(k).wait_send()
    for k in range(max(0, n - 2), n):
        out_copy(k).wait()


def ffn(n, nt, cot, wfc, wout, bias, cid=1):
    m, d = nt.shape
    h = wfc.shape[1]
    vm = pl.BlockSpec(memory_space=pltpu.VMEM)
    anym = pl.BlockSpec(memory_space=pl.ANY)
    return pl.pallas_call(
        functools.partial(ffn_kernel, n),
        in_specs=[anym] * 4 + [vm],
        out_specs=[vm, vm] + [anym] * 3,
        out_shape=[
            jax.ShapeDtypeStruct((m, d), F32),
            jax.ShapeDtypeStruct((1, h), F32),
            jax.ShapeDtypeStruct((n, m, d), BF16),
            jax.ShapeDtypeStruct((h, d), BF16),
            jax.ShapeDtypeStruct((2, n, half_high(d // n), h), BF16),
        ],
        scratch_shapes=[
            pltpu.VMEM((n, m, d), BF16),
            pltpu.VMEM((d, h), BF16),
            pltpu.VMEM((h, d), BF16),
            pltpu.VMEM((n, m, d), BF16),
            pltpu.VMEM((n, m, h), BF16),
            pltpu.VMEM((n, m, h), BF16),
            pltpu.VMEM((n, m, h), F32),
            pltpu.VMEM((n, m, d), BF16),
            pltpu.VMEM((n, m, d), BF16),
            pltpu.VMEM((2, max(TILE, m), d), BF16),
            pltpu.VMEM((2, half_high(d // n), h), BF16),
        ]
        + [pltpu.SemaphoreType.DMA((n,))] * 4
        + [pltpu.SemaphoreType.DMA((8,))],
        compiler_params=pltpu.CompilerParams(
            collective_id=cid, has_side_effects=True, vmem_limit_bytes=60 * 1024 * 1024
        ),
        cost_estimate=SHORT,
        name="feed_forward",
    )(nt, cot, wfc, wout, bias)


def weight_shares(c, f, core, n_fsdp, shard, source, dst, ss, rs):
    cut = shard // 32 * 16 if shard % 16 == 0 else 0
    shares = ((0, cut), (cut, shard)) if cut else ((0, shard), (0, shard))
    twin_id = (c + 1 - 2 * core, f)

    def copy(share, k, onward):
        lo, hi = share
        other = flip(f, k, n_fsdp)
        if onward:
            part = dst.at[other, lo:hi]
            return send(part, part, ss.at[1, k], rs.at[1, k], twin_id)
        return send(source(k).at[lo:hi], dst.at[f, lo:hi], ss.at[0, k], rs.at[0, k], (c, other))

    def by_core(act):
        for h in range(2):

            @pl.when(core == h)
            def _(h=h):
                for k in range(1, n_fsdp):
                    act(shares[h], shares[1 - h], k)

    def start(mine, theirs, k):
        copy(mine, k, False).start()

    def onward(mine, theirs, k):
        copy(mine, k, False).wait_recv()
        if cut:
            copy(mine, k, True).start()

    def done(mine, theirs, k):
        if cut:
            copy(theirs, k, True).wait_recv()
            copy(mine, k, True).wait_send()
        copy(mine, k, False).wait_send()

    return tuple(functools.partial(by_core, act) for act in (start, onward, done))


def start_kernel(
    n_ctx,
    n_fsdp,
    base,
    tok_hbm,
    w_hbm,
    small_ref,
    proj_hbm,
    fc_hbm,
    n_hbm,
    qkv_hbm,
    proj_all,
    fc_all,
    fc_parts,
    w_ref,
    lines_ref,
    n_ref,
    qkv_ref,
    fc_ref,
    fc_cut,
    x_ref,
    wg_ref,
    sg_ref,
    tok_recv,
    right_sem,
    left_sem,
    twin_sem,
    w_send,
    w_recv,
    s_send,
    s_recv,
    proj_send,
    proj_recv,
    fc_send,
    fc_recv,
    local,
):
    c = lax.axis_index("ctx")
    f = lax.axis_index("fsdp")
    chips = n_ctx // 2
    chip, core = c // 2, c % 2
    slots, width, cols = w_ref.shape
    shard = width // n_fsdp
    hd = HEAD_DIM
    enter(
        [(lax.rem(c + i, n_ctx), f) for i in range(1, n_ctx)]
        + [(c, flip(f, k, n_fsdp)) for k in range(1, n_fsdp)]
    )

    def block(at, same):
        return 2 * at + (core if same else 1 - core)

    cut = x_ref.shape[1] // 2

    def part(ref, h):
        return ref.at[pl.ds(h * cut, cut)]

    def hop(step, to_right, from_own, h):
        origin = block(chip - step if to_right else chip + step, True)
        src = tok_hbm if from_own else x_ref.at[origin]
        sem = (right_sem if to_right else left_sem).at[step, h]
        peer = (c + 2 if to_right else c - 2, f)
        dst = part(x_ref.at[origin], h)
        return send(part(src, h), dst, sem, tok_recv.at[origin, h], peer)

    def twin(at, from_own, h):
        origin = block(at, True)
        src = tok_hbm if from_own else x_ref.at[origin]
        dst = part(x_ref.at[origin], h)
        return send(
            part(src, h),
            dst,
            twin_sem.at[at, h],
            tok_recv.at[origin, h],
            (block(chip, False), f),
        )

    def w_copy(k):
        return send(w_hbm, wg_ref.at[f], w_send.at[k], w_recv.at[k], (c, flip(f, k, n_fsdp)))

    def s_copy(k):
        return send(small_ref, sg_ref.at[f], s_send.at[k], s_recv.at[k], (c, flip(f, k, n_fsdp)))

    weights_start, weights_onward, weights_done = weight_shares(
        c, f, core, n_fsdp, shard, lambda k: proj_hbm, proj_all, proj_send, proj_recv
    )
    fc_start, fc_onward, fc_done = weight_shares(
        c,
        f,
        core,
        n_fsdp,
        shard,
        lambda k: fc_parts.at[flip(f, k, n_fsdp)],
        fc_all,
        fc_send,
        fc_recv,
    )

    for k in range(1, n_fsdp):
        s_copy(k).start()

    for h in range(2):

        @pl.when(chip < chips - 1)
        def _(h=h):
            hop(0, True, True, h).start()

        @pl.when(chip > 0)
        def _(h=h):
            hop(0, False, True, h).start()

    for k in range(1, n_fsdp):
        w_copy(k).start()
    for h in range(2):
        twin(chip, True, h).start()
    own_x = pltpu.make_async_copy(tok_hbm, x_ref.at[c], local.at[0])
    own_w = pltpu.make_async_copy(w_hbm, wg_ref.at[f], local.at[1])
    own_proj = pltpu.make_async_copy(proj_hbm, proj_all.at[f], local.at[2])
    load_fc = pltpu.make_async_copy(fc_hbm, fc_ref, local.at[3])
    for copy in (own_x, own_w, own_proj, load_fc):
        copy.start()
    sg_ref[f] = small_ref[...]
    for k in range(1, n_fsdp):
        s_copy(k).wait_recv()
    for j in range(n_fsdp):
        lines_ref[:, j * shard : (j + 1) * shard] = sg_ref[j]
    main = n_ctx * base * hd
    row_id = lax.broadcasted_iota(jnp.int32, (width, slots * hd), 0)
    col_id = lax.broadcasted_iota(jnp.int32, (width, slots * hd), 1)
    wanted = jnp.where(col_id < base * hd, c * base * hd + col_id, main + col_id - base * hd)
    picked = dot(lines_ref[...].astype(BF16), (row_id == wanted).astype(BF16))
    zero = jnp.zeros((1, hd), F32)
    bias = [
        jnp.concatenate(
            [picked[4:5, s * hd : (s + 1) * hd], zero, picked[5:6, s * hd : (s + 1) * hd]], axis=1
        )
        for s in range(slots)
    ]
    own_w.wait()
    own_x.wait()
    for k in range(1, n_fsdp):
        w_copy(k).wait_recv()
    weights_start()
    for j in range(n_fsdp):
        w_ref[:, j * shard : (j + 1) * shard, :] = wg_ref[j]

    load_fc.wait()
    hidden = fc_cut.shape[2]
    cuts = []
    for j in range(n_fsdp):
        if j >= 2:
            cuts[j - 2].wait()
        fc_cut[j % 2] = fc_ref[:, j * hidden : (j + 1) * hidden]
        cuts.append(pltpu.make_async_copy(fc_cut.at[j % 2], fc_parts.at[j], local.at[4 + j % 2]))
        cuts[-1].start()

    for copy in cuts[-2:]:
        copy.wait()
    fc_start()
    own_fc = pltpu.make_async_copy(fc_parts.at[f], fc_all.at[f], local.at[3])
    own_fc.start()

    def results(origin):
        return (
            pltpu.make_async_copy(n_ref, n_hbm.at[origin], local.at[0]),
            pltpu.make_async_copy(qkv_ref, qkv_hbm.at[:, origin], local.at[1]),
        )

    def project(at, same, first=False):
        origin = block(at, same)
        rows = x_ref[origin].astype(F32)
        mean = jnp.mean(rows, axis=1, keepdims=True)
        cen = rows - mean
        var = jnp.mean(cen * cen, axis=1, keepdims=True)
        normed = cen * lax.rsqrt(var + EPS) * lines_ref[0:1] + lines_ref[2:3]
        normed = normed.astype(BF16)

        @pl.when(jnp.logical_not(first))
        def _():
            for copy in results(origin):
                copy.wait()

        n_ref[...] = normed
        for s in range(slots):
            qkv_ref[s] = (dot(normed, w_ref[s]) + bias[s]).astype(BF16)
        for copy in results(origin):
            copy.start()

    def arrived(at, same, h):
        origin = block(at, same)
        ref = part(x_ref.at[origin], h)
        pltpu.make_async_copy(ref, ref, tok_recv.at[origin, h]).wait()

    def step(s, carry):
        for h in range(2):

            @pl.when((s > 0) & (chip - s >= 0))
            def _(h=h):
                arrived(chip - s, True, h)

                @pl.when(chip < chips - 1)
                def _():
                    hop(s, True, False, h).start()

                twin(chip - s, False, h).start()

            @pl.when((s > 0) & (chip + s < chips))
            def _(h=h):
                arrived(chip + s, True, h)

                @pl.when(chip > 0)
                def _():
                    hop(s, False, False, h).start()

                twin(chip + s, False, h).start()

        @pl.when(s == chips - 1)
        def _():
            weights_onward()

        @pl.when(chip - s >= 0)
        def _():
            project(chip - s, True, s == 0)

        @pl.when((s > 0) & (chip + s < chips))
        def _():
            project(chip + s, True)

        @pl.when(chip - s >= 0)
        def _():
            for h in range(2):
                arrived(chip - s, False, h)
            project(chip - s, False)

        @pl.when((s > 0) & (chip + s < chips))
        def _():
            for h in range(2):
                arrived(chip + s, False, h)
            project(chip + s, False)

        return carry

    lax.fori_loop(0, chips, step, 0)
    fc_onward()
    for copy in results(c):
        copy.wait()
    own_proj.wait()
    own_fc.wait()

    for s in range(chips):
        for h in range(2):
            if s < chips - 1:

                @pl.when((chip - s >= 0) & (chip < chips - 1))
                def _(s=s, h=h):
                    hop(s, True, False, h).wait_send()

                @pl.when((chip + s < chips) & (chip > 0))
                def _(s=s, h=h):
                    hop(s, False, False, h).wait_send()

            twin(s, False, h).wait_send()
    for k in range(1, n_fsdp):
        w_copy(k).wait_send()
        s_copy(k).wait_send()
    weights_done()
    fc_done()


def start_call(n_ctx, n_fsdp, base, tok, w_slots, small, w_proj, w_fc, cid):
    count, width = tok.shape
    slots, shard, cols = w_slots.shape
    hidden = w_fc.shape[1] // n_fsdp
    vm = pl.BlockSpec(memory_space=pltpu.VMEM)
    anym = pl.BlockSpec(memory_space=pl.ANY)
    dma = pltpu.SemaphoreType.DMA
    return pl.pallas_call(
        functools.partial(start_kernel, n_ctx, n_fsdp, base),
        in_specs=[anym, anym, vm, anym, anym],
        out_specs=[anym, anym, anym, anym, anym, vm, vm],
        out_shape=[
            jax.ShapeDtypeStruct((n_ctx, count, width), BF16),
            jax.ShapeDtypeStruct((slots, n_ctx, count, cols), BF16),
            jax.ShapeDtypeStruct((n_fsdp,) + w_proj.shape, BF16),
            jax.ShapeDtypeStruct((n_fsdp, shard, hidden), BF16),
            jax.ShapeDtypeStruct((n_fsdp, shard, hidden), BF16),
            jax.ShapeDtypeStruct((slots, width, cols), BF16),
            jax.ShapeDtypeStruct((small.shape[0], width), F32),
        ],
        scratch_shapes=[
            pltpu.VMEM((count, width), BF16),
            pltpu.VMEM((slots, count, cols), BF16),
            pltpu.VMEM(w_fc.shape, BF16),
            pltpu.VMEM((2, shard, hidden), BF16),
            pltpu.VMEM((n_ctx, count, width), BF16),
            pltpu.VMEM((n_fsdp, slots, shard, cols), BF16),
            pltpu.VMEM((n_fsdp,) + small.shape, F32),
            dma((n_ctx, 2)),
            dma((n_ctx // 2, 2)),
            dma((n_ctx // 2, 2)),
            dma((n_ctx // 2, 2)),
            dma((n_fsdp,)),
            dma((n_fsdp,)),
            dma((n_fsdp,)),
            dma((n_fsdp,)),
            dma((2, n_fsdp)),
            dma((2, n_fsdp)),
            dma((2, n_fsdp)),
            dma((2, n_fsdp)),
            dma((6,)),
        ],
        compiler_params=pltpu.CompilerParams(
            collective_id=cid, has_side_effects=True, vmem_limit_bytes=VMEM_LIMIT
        ),
        cost_estimate=SHORT,
        name="tokens_qkv",
    )(tok, w_slots, small, w_proj, w_fc)


def causal_scores(k, q_rows, start):
    scores = dot_last(k, q_rows)
    keep = start
    tail = scores[keep:]
    key_id = lax.broadcasted_iota(jnp.int32, tail.shape, 0)
    query_id = lax.broadcasted_iota(jnp.int32, tail.shape, 1)
    tail = jnp.where(key_id <= query_id, tail, -1e30)
    if keep == 0:
        return tail
    return jnp.concatenate([scores[:keep], tail], axis=0)


def soft(scores, v_t):
    top = jnp.max(scores, axis=0, keepdims=True)
    weights = jnp.exp(scores - top)
    total = jnp.sum(weights, axis=0, keepdims=True)
    out = dot(v_t, weights.astype(BF16)) / total
    return out, top + jnp.log(total)


def causal(inv_ref, x_ref):
    return jnp.concatenate([x_ref[0, inv_ref[i]] for i in range(x_ref.shape[1])], axis=0)


def attn_fwd_kernel(inv_ref, x_ref, o_ref, l_ref):
    rows = l_ref.shape[2]
    hd = HEAD_DIM
    x = causal(inv_ref, x_ref)
    q = x[:, :hd] * BF16(SCALE)
    k = x[:, hd : 2 * hd]
    v_t = x[:, 2 * hd :].T
    for i in range(rows // QROWS):
        lo, hi = i * QROWS, (i + 1) * QROWS
        out, lse = soft(causal_scores(k[:hi], q[lo:hi], lo), v_t[:, :hi])
        l_ref[0, :, lo:hi] = lse
        out = out.astype(BF16)
        for b in range(QROWS // BLOCK):
            o_ref[inv_ref[2 * i + b]] = out[:, b * BLOCK : (b + 1) * BLOCK]


def attn_fwd(inv, qkv, heads):
    blocks, _, cols = qkv.shape[1:]
    rows = blocks * BLOCK
    return pl.pallas_call(
        attn_fwd_kernel,
        grid_spec=pltpu.PrefetchScalarGridSpec(
            num_scalar_prefetch=1,
            grid=(heads,),
            in_specs=[pl.BlockSpec((1, blocks, BLOCK, cols), lambda h, inv: (h, 0, 0, 0))],
            out_specs=[
                pl.BlockSpec((blocks, HEAD_DIM, BLOCK), lambda h, inv: (0, h, 0)),
                pl.BlockSpec((1, 1, rows), lambda h, inv: (h, 0, 0)),
            ],
        ),
        out_shape=[
            jax.ShapeDtypeStruct((blocks, heads * HEAD_DIM, BLOCK), BF16),
            jax.ShapeDtypeStruct((heads, 1, rows), F32),
        ],
        compiler_params=pltpu.CompilerParams(vmem_limit_bytes=VMEM_LIMIT),
        cost_estimate=SHORT,
        name="attn_fwd",
    )(inv, qkv)


def attn_bwd_kernel(inv_ref, x_ref, do_ref, o_ref, l_ref, dx_ref, dk_acc, dv_acc):
    rows = l_ref.shape[2]
    hd = HEAD_DIM
    x = causal(inv_ref, x_ref)
    q = x[:, :hd] * BF16(SCALE)
    k = x[:, hd : 2 * hd]
    v = x[:, 2 * hd :]
    k_t = k.T
    dk_acc[...] = jnp.zeros_like(dk_acc)
    dv_acc[...] = jnp.zeros_like(dv_acc)
    for i in range(rows // QROWS):
        lo, hi = i * QROWS, (i + 1) * QROWS
        ids = [inv_ref[2 * i + b] for b in range(QROWS // BLOCK)]
        do_t = jnp.concatenate([do_ref[b] for b in ids], axis=1)
        o_t = jnp.concatenate([o_ref[b] for b in ids], axis=1)
        inner = jnp.sum(do_t.astype(F32) * o_t.astype(F32), axis=0, keepdims=True)
        probs = jnp.exp(causal_scores(k[:hi], q[lo:hi], lo) - l_ref[0, :, lo:hi])
        dprobs = dot(v[:hi], do_t)
        dscores = (probs * (dprobs - inner)).astype(BF16)
        dv_acc[:hi] += dot_last(probs.astype(BF16), do_t)
        dk_acc[:hi] += dot(dscores, q[lo:hi])
        dq = (dot(k_t[:, :hi], dscores) * SCALE).T
        for n, b in enumerate(ids):
            dx_ref[0, b, :, :hd] = dq[n * BLOCK : (n + 1) * BLOCK].astype(BF16)
    for i in range(rows // BLOCK):
        lo, hi = i * BLOCK, (i + 1) * BLOCK
        dx_ref[0, inv_ref[i], :, hd : 2 * hd] = dk_acc[lo:hi].astype(BF16)
        dx_ref[0, inv_ref[i], :, 2 * hd :] = dv_acc[lo:hi].astype(BF16)


def attn_bwd(inv, qkv, d_out, out, lse, heads):
    blocks, _, cols = qkv.shape[1:]
    rows = blocks * BLOCK
    whole = pl.BlockSpec((1, blocks, BLOCK, cols), lambda h, inv: (h, 0, 0, 0))
    feat = pl.BlockSpec((blocks, HEAD_DIM, BLOCK), lambda h, inv: (0, h, 0))
    return pl.pallas_call(
        attn_bwd_kernel,
        grid_spec=pltpu.PrefetchScalarGridSpec(
            num_scalar_prefetch=1,
            grid=(heads,),
            in_specs=[
                whole,
                feat,
                feat,
                pl.BlockSpec((1, 1, rows), lambda h, inv: (h, 0, 0)),
            ],
            out_specs=whole,
            scratch_shapes=[pltpu.VMEM((rows, HEAD_DIM), F32)] * 2,
        ),
        out_shape=jax.ShapeDtypeStruct((heads, blocks, BLOCK, cols), BF16),
        compiler_params=pltpu.CompilerParams(vmem_limit_bytes=VMEM_LIMIT),
        cost_estimate=pl.CostEstimate(
            flops=24 * 10**9, bytes_accessed=24 * 10**6, transcendentals=0
        ),
        name="attn_bwd",
    )(inv, qkv, d_out, out, lse)


def own_scores(order_ref, x_ref, k):
    hd = HEAD_DIM
    blocks = x_ref.shape[1]
    first = order_ref[blocks]
    q = jnp.concatenate([x_ref[0, first], x_ref[0, first + 1]], axis=0)[:, :hd]
    q = q * BF16(SCALE)
    scores = dot_last(k, q)
    row = lax.broadcasted_iota(jnp.int32, (BLOCK, 1), 0)
    key_place = jnp.concatenate([order_ref[b] * BLOCK + row for b in range(blocks)], axis=0)
    lane = lax.broadcasted_iota(jnp.int32, (1, 2 * BLOCK), 1)
    low, high = order_ref[order_ref[blocks]], order_ref[order_ref[blocks] + 1]
    place = jnp.where(lane < BLOCK, low * BLOCK + lane, (high - 1) * BLOCK + lane)
    return q, first, jnp.where(key_place <= place, scores, -1e30)


def rest_fwd_kernel(order_ref, x_ref, o_ref, l_ref):
    hd = HEAD_DIM
    x = x_ref[0].reshape(-1, 3 * hd)
    _, _, scores = own_scores(order_ref, x_ref, x[:, hd : 2 * hd])
    out, lse = soft(scores, x[:, 2 * hd :].T)
    o_ref[0] = out.astype(BF16)
    l_ref[0] = lse


def rest_fwd(order, qkv, base):
    slots, blocks, _, cols = qkv.shape
    rest = slots - base
    return pl.pallas_call(
        rest_fwd_kernel,
        grid_spec=pltpu.PrefetchScalarGridSpec(
            num_scalar_prefetch=1,
            grid=(rest,),
            in_specs=[
                pl.BlockSpec((1, blocks, BLOCK, cols), lambda h, o: (base + h, 0, 0, 0))
            ],
            out_specs=[
                pl.BlockSpec((1, HEAD_DIM, QROWS), lambda h, o: (h, 0, 0)),
                pl.BlockSpec((1, 1, QROWS), lambda h, o: (h, 0, 0)),
            ],
        ),
        out_shape=[
            jax.ShapeDtypeStruct((rest, HEAD_DIM, QROWS), BF16),
            jax.ShapeDtypeStruct((rest, 1, QROWS), F32),
        ],
        compiler_params=pltpu.CompilerParams(vmem_limit_bytes=VMEM_LIMIT),
        cost_estimate=SHORT,
        name="rest_fwd",
    )(order, qkv)


def rest_bwd_kernel(order_ref, x_ref, do_ref, o_ref, l_ref, dx_ref):
    hd = HEAD_DIM
    x = x_ref[0].reshape(-1, 3 * hd)
    blocks = x_ref.shape[1]
    k = x[:, hd : 2 * hd]
    q, first, scores = own_scores(order_ref, x_ref, k)
    do_t = do_ref[0]
    inner = jnp.sum(do_t.astype(F32) * o_ref[0].astype(F32), axis=0, keepdims=True)
    probs = jnp.exp(scores - l_ref[0])
    dprobs = dot(x[:, 2 * hd :], do_t)
    dscores = (probs * (dprobs - inner)).astype(BF16)
    dv = dot_last(probs.astype(BF16), do_t).astype(BF16)
    dk = dot(dscores, q).astype(BF16)
    dq = (dot(k.T, dscores) * SCALE).T.astype(BF16)
    dx_ref[0, :, :, 2 * hd :] = dv.reshape(blocks, BLOCK, hd)
    dx_ref[0, :, :, hd : 2 * hd] = dk.reshape(blocks, BLOCK, hd)
    dx_ref[0, :, :, :hd] = jnp.zeros((blocks, BLOCK, hd), BF16)
    for b in range(2):
        dx_ref[0, first + b, :, :hd] = dq[b * BLOCK : (b + 1) * BLOCK]


def rest_bwd(order, qkv, d_out, out, lse, base):
    slots, blocks, _, cols = qkv.shape
    rest = slots - base
    feat = pl.BlockSpec((1, HEAD_DIM, QROWS), lambda h, o: (h, 0, 0))
    return pl.pallas_call(
        rest_bwd_kernel,
        grid_spec=pltpu.PrefetchScalarGridSpec(
            num_scalar_prefetch=1,
            grid=(rest,),
            in_specs=[
                pl.BlockSpec((1, blocks, BLOCK, cols), lambda h, o: (base + h, 0, 0, 0)),
                feat,
                feat,
                pl.BlockSpec((1, 1, QROWS), lambda h, o: (h, 0, 0)),
            ],
            out_specs=pl.BlockSpec((1, blocks, BLOCK, cols), lambda h, o: (h, 0, 0, 0)),
        ),
        out_shape=jax.ShapeDtypeStruct((rest, blocks, BLOCK, cols), BF16),
        compiler_params=pltpu.CompilerParams(vmem_limit_bytes=VMEM_LIMIT),
        cost_estimate=SHORT,
        name="rest_bwd",
    )(order, qkv, d_out, out, lse)


def mix_kernel(
    n_ctx,
    out_hbm,
    rest_ref,
    tok_ref,
    proj_ref,
    lines_ref,
    att_ref,
    mid_ref,
    n_ref,
    got_ref,
    out_send,
    out_recv,
    local,
):
    c = lax.axis_index("ctx")
    f = lax.axis_index("fsdp")
    width = tok_ref.shape[1]
    blocks, feats = got_ref.shape[1], got_ref.shape[2]
    enter([(lax.rem(c + i, n_ctx), f) for i in range(1, n_ctx)])

    def out_copy(i):
        to = lax.rem(c + i, n_ctx)
        return send(
            out_hbm.at[pl.ds(to * blocks, blocks)],
            got_ref.at[c],
            out_send.at[i],
            out_recv.at[i],
            (to, f),
        )

    for i in range(n_ctx - 1, 0, -1):
        out_copy(i).start()
    own = pltpu.make_async_copy(
        out_hbm.at[pl.ds(c * blocks, blocks)], got_ref.at[c], local
    )
    own.start()
    main = n_ctx * feats
    if main < width:
        att_ref[:, main:] = rest_ref[...].reshape(width - main, -1).T
    own.wait()
    for i in range(1, n_ctx):
        out_copy(i).wait_recv()
    for src in range(n_ctx):
        block = jnp.concatenate([got_ref[src, b] for b in range(blocks)], axis=1)
        att_ref[:, src * feats : (src + 1) * feats] = block.T
    mid = tok_ref[...].astype(F32) + (dot(att_ref[...], proj_ref[...]) + lines_ref[6:7])
    mid_ref[...] = mid
    cen = mid - jnp.mean(mid, axis=1, keepdims=True)
    var = jnp.mean(cen * cen, axis=1, keepdims=True)
    n_ref[...] = (cen * lax.rsqrt(var + EPS) * lines_ref[1:2] + lines_ref[3:4]).astype(BF16)
    for i in range(1, n_ctx):
        out_copy(i).wait_send()


def mix_call(n_ctx, out_own, out_rest, tok, proj, lines, cid):
    count, width = tok.shape
    vm = pl.BlockSpec(memory_space=pltpu.VMEM)
    anym = pl.BlockSpec(memory_space=pl.ANY)
    dma = pltpu.SemaphoreType.DMA
    return pl.pallas_call(
        functools.partial(mix_kernel, n_ctx),
        in_specs=[anym, vm, vm, vm, vm],
        out_specs=[vm, vm, vm],
        out_shape=[
            jax.ShapeDtypeStruct((count, width), BF16),
            jax.ShapeDtypeStruct((count, width), F32),
            jax.ShapeDtypeStruct((count, width), BF16),
        ],
        scratch_shapes=[
            pltpu.VMEM((n_ctx, out_own.shape[0] // n_ctx) + out_own.shape[1:], BF16),
            dma((n_ctx,)),
            dma((n_ctx,)),
            dma(()),
        ],
        compiler_params=pltpu.CompilerParams(
            collective_id=cid, has_side_effects=True, vmem_limit_bytes=VMEM_LIMIT
        ),
        cost_estimate=SHORT,
        name="mix_rows",
    )(out_own, out_rest, tok, proj, lines)


def turn_kernel(
    n_ctx,
    n_fsdp,
    gsum_ref,
    cot_ref,
    mid_ref,
    proj_ref,
    lines_ref,
    fc_hbm,
    parts_hbm,
    grad_ref,
    low_ref,
    sums_ref,
    rest_ref,
    fc_ref,
    rows_ref,
    got_hbm,
    out_ref,
    pair_in,
    rows_in,
    out_send,
    out_recv,
    pair_sem,
    rows_send,
    rows_recv,
    local,
):
    c = lax.axis_index("ctx")
    f = lax.axis_index("fsdp")
    core = c % 2
    width = mid_ref.shape[1]
    blocks, feats = out_ref.shape[0] // n_ctx, out_ref.shape[1]
    enter(
        [(lax.rem(c + i, n_ctx), f) for i in range(1, n_ctx)]
        + [(c, flip(f, k, n_fsdp)) for k in range(1, n_fsdp)]
    )

    def rows_copy(k):
        other = flip(f, k, n_fsdp)
        return send(
            parts_hbm.at[other], rows_in.at[f], rows_send.at[k], rows_recv.at[k], (c, other)
        )

    for k in range(1, n_fsdp):
        rows_copy(k).start()
    own_rows = pltpu.make_async_copy(parts_hbm.at[f], rows_in.at[f], local.at[2])
    own_rows.start()
    pair = send(fc_hbm.at[1 - core], pair_in, pair_sem.at[0], pair_sem.at[1], (c + 1 - 2 * core, f))
    pair.start()
    own_fc = pltpu.make_async_copy(fc_hbm.at[core], fc_ref, local.at[0])
    own_fc.start()

    xhat, rstd = norm_parts(mid_ref[...])
    grad = gsum_ref[...]
    cot = cot_ref[...].astype(F32)
    mid_grad = cot + norm_back(xhat, rstd, lines_ref[1:2], grad)
    grad_ref[...] = mid_grad
    low = mid_grad.astype(BF16)
    low_ref[...] = low
    att_t = dot_last(low, proj_ref[...]).astype(BF16).T
    for to in range(n_ctx):
        for b in range(blocks):
            out_ref[to * blocks + b] = att_t[
                to * feats : (to + 1) * feats, b * BLOCK : (b + 1) * BLOCK
            ]

    def out_copy(i):
        to = lax.rem(c + i, n_ctx)
        return send(
            out_ref.at[pl.ds(to * blocks, blocks)],
            got_hbm.at[pl.ds(c * blocks, blocks)],
            out_send.at[i],
            out_recv.at[i],
            (to, f),
        )

    for i in range(n_ctx - 1, 0, -1):
        out_copy(i).start()
    own = pltpu.make_async_copy(
        out_ref.at[pl.ds(c * blocks, blocks)], got_hbm.at[pl.ds(c * blocks, blocks)], local.at[1]
    )
    own.start()
    main = n_ctx * feats
    if main < width:
        rest_ref[...] = att_t[main:].reshape(rest_ref.shape)
    else:
        rest_ref[...] = jnp.zeros(rest_ref.shape, BF16)
    for r, line in enumerate((grad * xhat, grad, low.astype(F32), cot)):
        sums_ref[r : r + 1] = jnp.sum(line, axis=0, keepdims=True)
    sums_ref[4:] = jnp.zeros((4, width), F32)
    own_fc.wait()
    pair.wait()

    def add(j, carry):
        fc_ref[j] = (fc_ref[j].astype(F32) + pair_in[j].astype(F32)).astype(BF16)
        return carry

    lax.fori_loop(0, fc_ref.shape[0], add, 0)
    own.wait()
    for i in range(1, n_ctx):
        out_copy(i).wait()
    own_rows.wait()
    total = rows_in[f].astype(F32)
    for k in range(1, n_fsdp):
        rows_copy(k).wait()
        total += rows_in[flip(f, k, n_fsdp)].astype(F32)
    rows_ref[...] = (mid_ref[...] + (total + lines_ref[7:8])).astype(BF16)


def turn_call(n_ctx, n_fsdp, base, gsum, cot, mid, proj, lines, fc_part, out_part, cid):
    count, width = mid.shape
    heads = width // HEAD_DIM
    rest = max(heads - base * n_ctx, 1)
    out = (n_ctx * count // BLOCK, base * HEAD_DIM, BLOCK)
    vm = pl.BlockSpec(memory_space=pltpu.VMEM)
    anym = pl.BlockSpec(memory_space=pl.ANY)
    dma = pltpu.SemaphoreType.DMA
    return pl.pallas_call(
        functools.partial(turn_kernel, n_ctx, n_fsdp),
        in_specs=[vm] * 5 + [anym] * 2,
        out_specs=[vm] * 6 + [anym],
        out_shape=[
            jax.ShapeDtypeStruct((count, width), F32),
            jax.ShapeDtypeStruct((count, width), BF16),
            jax.ShapeDtypeStruct((8, width), F32),
            jax.ShapeDtypeStruct((rest, HEAD_DIM, count), BF16),
            jax.ShapeDtypeStruct(fc_part.shape[1:], BF16),
            jax.ShapeDtypeStruct((count, width), BF16),
            jax.ShapeDtypeStruct(out, BF16),
        ],
        scratch_shapes=[
            pltpu.VMEM(out, BF16),
            pltpu.VMEM(fc_part.shape[1:], BF16),
            pltpu.VMEM(out_part.shape, BF16),
            dma((n_ctx,)),
            dma((n_ctx,)),
            dma((2,)),
            dma((n_fsdp,)),
            dma((n_fsdp,)),
            dma((3,)),
        ],
        compiler_params=pltpu.CompilerParams(
            collective_id=cid, has_side_effects=True, vmem_limit_bytes=VMEM_LIMIT
        ),
        cost_estimate=SHORT,
        name="turn_rows",
    )(gsum, cot, mid, proj, lines, fc_part, out_part)


def far_first(i, chips):
    return (i % 2) * (i // 2) + (1 - i % 2) * (chips - 1 - i // 2)


def line_sum(chip, chips, f, core, part, came, sems, ready=None):
    sent, left_sem, right_sem = sems

    def to_right(d):
        return send(
            part.at[d], came.at[d], sent.at[d], left_sem.at[d], (2 * (chip + 1) + core, f)
        )

    def to_left(d):
        place = jnp.where(d == chip - 1, chips, d)
        return send(
            part.at[d], came.at[place], sent.at[d], right_sem.at[d], (2 * (chip - 1) + core, f)
        )

    def from_left(d):
        send(part.at[d], came.at[d], sent.at[d], left_sem.at[d], (2 * chip + core, f)).wait_recv()
        add(d, d)

    def from_right(d, place):
        send(
            part.at[d], came.at[place], sent.at[d], right_sem.at[d], (2 * chip + core, f)
        ).wait_recv()
        add(d, place)

    def add(d, place):
        part[d] = (part[d].astype(F32) + came[place].astype(F32)).astype(BF16)

    def step(t):
        far = chips - 1 - t + chip
        near = t - (chips - 1 - chip)

        @pl.when(chip <= t)
        def _():
            if ready is not None:
                ready(far)

            @pl.when(chip > 0)
            def _():
                from_left(far)

            @pl.when(chip < t)
            def _():
                to_right(far + 1).wait_send()

            to_right(far).start()

        @pl.when(near >= 0)
        def _():
            if ready is not None:
                ready(near)

            @pl.when(chip < chips - 1)
            def _():
                from_right(near, near)

            @pl.when(near > 0)
            def _():
                to_left(near - 1).wait_send()

            to_left(near).start()

    def finish():
        if ready is not None:
            ready(chip)

        @pl.when(chip > 0)
        def _():
            from_left(chip)

        @pl.when(chip < chips - 1)
        def _():
            from_right(chip, chips)

    def done():
        @pl.when(chip < chips - 1)
        def _():
            to_right(chip + 1).wait_send()

        @pl.when(chip > 0)
        def _():
            to_left(chip - 1).wait_send()

    return step, finish, done


def line_gather(chip, chips, f, core, view, sems):
    right, left, twin_sent, got, twin_got = sems
    twin_id = (2 * chip + 1 - core, f)

    def hop(s, rightward):
        origin = chip - s if rightward else chip + s
        ref = view(origin, core)
        peer = (2 * (chip + 1 if rightward else chip - 1) + core, f)
        return send(ref, ref, (right if rightward else left).at[s], got.at[origin], peer)

    def twin(origin):
        ref = view(origin, core)
        return send(ref, ref, twin_sent.at[origin], twin_got.at[origin], twin_id)

    def arrived(origin):
        ref = view(origin, core)
        send(ref, ref, right.at[0], got.at[origin], twin_id).wait_recv()

    def step(s):
        @pl.when(chip - s >= 0)
        def _():
            if s:
                arrived(chip - s)

            @pl.when(chip < chips - 1)
            def _():
                hop(s, True).start()

            twin(chip - s).start()

        @pl.when(chip + s < chips)
        def _():
            if s:
                arrived(chip + s)

            @pl.when(chip > 0)
            def _():
                hop(s, False).start()

            if s:
                twin(chip + s).start()

    def done():
        for s in range(chips):
            if s < chips - 1:

                @pl.when((chip - s >= 0) & (chip < chips - 1))
                def _(s=s):
                    hop(s, True).wait_send()

                @pl.when((chip + s < chips) & (chip > 0))
                def _(s=s):
                    hop(s, False).wait_send()

            twin(s).wait_send()
            ref = view(s, 1 - core)
            send(ref, ref, twin_sent.at[s], twin_got.at[s], twin_id).wait_recv()

    return step, done


def back_kernel(
    n_ctx,
    n_fsdp,
    own_ref,
    rest_ref,
    w_ref,
    n_ref,
    fc_hbm,
    one_ref,
    cols_ref,
    fc_all,
    part,
    twin_out,
    twin_in,
    came,
    mine,
    theirs,
    twin_send,
    twin_recv,
    line_send,
    left_recv,
    right_recv,
    cols_send,
    cols_recv,
    fc_send,
    fc_recv,
    local,
):
    c = lax.axis_index("ctx")
    f = lax.axis_index("fsdp")
    chips = n_ctx // 2
    chip, core = c // 2, c % 2
    slots, width, cols = w_ref.shape
    count = own_ref.shape[2]
    base = own_ref.shape[0]
    shard = width // n_fsdp
    twin_id = (2 * chip + 1 - core, f)
    enter(
        [(lax.rem(c + i, n_ctx), f) for i in range(1, n_ctx)]
        + [(c, flip(f, k, n_fsdp)) for k in range(1, n_fsdp)]
    )

    def grad(s):
        return own_ref.at[s] if s < base else rest_ref.at[s - base]

    def for_block(b):
        total = dot_last(grad(0)[b], w_ref[0])
        for s in range(1, slots):
            total += dot_last(grad(s)[b], w_ref[s])
        return total.astype(BF16)

    def to_twin(d, slot):
        return send(twin_out.at[slot], twin_in.at[d], twin_send.at[slot], twin_recv.at[d], twin_id)

    def products(i, carry):
        d = far_first(i, chips)
        slot = i % 2
        product = for_block(2 * d + 1 - core)

        @pl.when(i > 1)
        def _():
            to_twin(d, slot).wait_send()

        twin_out[slot] = product
        to_twin(d, slot).start()
        part[d] = for_block(2 * d + core)
        return carry

    def ready(d):
        to_twin(d, 0).wait_recv()
        part[d] = (part[d].astype(F32) + twin_in[d].astype(F32)).astype(BF16)

    cut = count // 2
    streams = [
        line_sum(
            chip,
            chips,
            f,
            core,
            part.at[:, pl.ds(h * cut, cut)],
            came.at[h],
            (line_send.at[h], left_recv.at[h], right_recv.at[h]),
            None if h else ready,
        )
        for h in range(2)
    ]

    def step(t):
        for stream in streams:
            stream[0](t)

    def finish():
        for stream in streams:
            stream[1]()

    def done():
        for stream in streams:
            stream[2]()

    def cols_copy(src, dst, at):
        return send(mine.at[src], theirs.at[at], cols_send.at[src], cols_recv.at[at], (c, dst))

    def columns(j):
        left = n_ref[:, :, j * shard : (j + 1) * shard].reshape(n_ctx * count, shard)
        for s in range(slots):
            right = grad(s)[...].reshape(n_ctx * count, cols)
            mine[j, s] = dot_first(left, right).astype(BF16)

    def fc_copy(k):
        other = flip(f, k, n_fsdp)
        return send(fc_hbm.at[other], fc_all.at[f], fc_send.at[k], fc_recv.at[k], (c, other))

    for k in range(1, n_fsdp):
        fc_copy(k).start()
    own_fc = pltpu.make_async_copy(fc_hbm.at[f], fc_all.at[f], local)
    own_fc.start()
    lax.fori_loop(0, 2, products, 0)
    step(0)
    for j in range(n_fsdp):
        columns(j)
    for k in range(1, n_fsdp):
        other = flip(f, k, n_fsdp)
        cols_copy(other, other, f).start()
    lax.fori_loop(2, chips, products, 0)
    if chips > 2:
        step(1)
    for t in range(2, chips - 1):
        step(t)
    total = mine[f].astype(F32)
    for k in range(1, n_fsdp):
        other = flip(f, k, n_fsdp)
        cols_copy(other, other, other).wait_recv()
        total += theirs[other].astype(F32)
    cols_ref[...] = total.astype(BF16)
    finish()
    one_ref[...] = part[chip]
    own_fc.wait()
    for k in range(1, n_fsdp):
        fc_copy(k).wait()
    done()
    for slot in range(2):
        to_twin(0, slot).wait_send()
    for k in range(1, n_fsdp):
        other = flip(f, k, n_fsdp)
        cols_copy(other, other, other).wait_send()


def back_fits(n_ctx, n_fsdp, count, width, slots):
    blocks = (5 * (n_ctx // 2) + n_ctx) * count * width
    heads = slots * 256 * (n_ctx * count + 3 * width)
    return 2 * (blocks + heads) < 50 * 1024 * 1024


def back_call(n_ctx, n_fsdp, own, rest, w_slots, normed, fc_mine, cid):
    slots, width, cols = w_slots.shape
    count = normed.shape[1]
    chips = n_ctx // 2
    shard = width // n_fsdp
    vm = pl.BlockSpec(memory_space=pltpu.VMEM)
    anym = pl.BlockSpec(memory_space=pl.ANY)
    dma = pltpu.SemaphoreType.DMA
    block = pltpu.VMEM((chips, count, width), BF16)
    piece = pltpu.VMEM((n_fsdp, slots, shard, cols), BF16)
    return pl.pallas_call(
        functools.partial(back_kernel, n_ctx, n_fsdp),
        in_specs=[vm] * 4 + [anym],
        out_specs=[vm] * 2 + [anym],
        out_shape=[
            jax.ShapeDtypeStruct((count, width), BF16),
            jax.ShapeDtypeStruct((slots, shard, cols), BF16),
            jax.ShapeDtypeStruct(fc_mine.shape, BF16),
        ],
        scratch_shapes=[
            block,
            pltpu.VMEM((2, count, width), BF16),
            block,
            pltpu.VMEM((2, chips + 1, count // 2, width), BF16),
        ]
        + [piece] * 2
        + [dma((2,)), dma((chips,))]
        + [dma((2, chips))] * 3
        + [dma((n_fsdp,))] * 4
        + [dma(())],
        compiler_params=pltpu.CompilerParams(
            collective_id=cid, has_side_effects=True, vmem_limit_bytes=60 * 1024 * 1024
        ),
        cost_estimate=SHORT,
        name="qkv_back",
    )(own, rest, w_slots, normed, fc_mine)


def sums_kernel(n_ctx, n_fsdp, lead, *refs):
    rows_ref, cols_ref, extra_ref, att_ref, mid_ref, lines_in = refs[:6]
    outs, cols_all, lines_ref = refs[6:8], refs[8], refs[9]
    parts, cames = refs[10:12], refs[12:14]
    proj_part, proj_in, proj_got, lines_got = refs[14:18]
    lines_send, lines_recv, local, proj_send, proj_recv, pair_sem = refs[18:24]
    cols_sems = refs[24:29]
    sems = [(refs[29 + 8 * i : 32 + 8 * i], refs[32 + 8 * i : 37 + 8 * i]) for i in range(2)]
    c = lax.axis_index("ctx")
    f = lax.axis_index("fsdp")
    chips = n_ctx // 2
    chip, core = c // 2, c % 2
    width = att_ref.shape[1]
    shard = width // n_fsdp
    half = shard // 2
    high = proj_in.shape[1]
    twin_id = (2 * chip + 1 - core, f)
    enter(
        [(lax.rem(c + i, n_ctx), f) for i in range(1, n_ctx)]
        + [(c, flip(f, k, n_fsdp)) for k in range(1, n_fsdp)]
    )

    def line_ops(i):
        sum_sems, gather_sems = sems[i]
        gather = line_gather(chip, chips, f, core, lambda at, h: outs[i].at[h, at], gather_sems)
        return line_sum(chip, chips, f, core, parts[i], cames[i], sum_sems) + gather

    def proj_pair():
        return send(proj_part.at[1 - core], proj_in, pair_sem.at[0], pair_sem.at[1], twin_id)

    def proj_copy(k):
        other = flip(f, k, n_fsdp)
        return send(
            proj_part.at[core, other],
            proj_got.at[f],
            proj_send.at[k],
            proj_recv.at[k],
            (c, other),
        )

    def proj_products(j):
        for h in range(2):
            lo = j * shard + h * half
            proj_part[h, j, :half] = dot_first(att_ref[:, lo : lo + half], mid_ref[...]).astype(BF16)
            if half < high:
                proj_part[h, j, half:] = jnp.zeros((high - half, width), BF16)

    def proj_add(j, carry):
        proj_part[core, j] = (
            proj_part[core, j].astype(F32) + proj_in[j].astype(F32)
        ).astype(BF16)
        return carry

    def proj_total():
        total = proj_part[core, f].astype(F32)
        for k in range(1, n_fsdp):
            proj_copy(k).wait_recv()
            total += proj_got[flip(f, k, n_fsdp)].astype(F32)
        total = jnp.concatenate([total.astype(BF16), extra_ref[...]], axis=0)
        first = rows_ref.shape[1] - parts[0].shape[1]
        step, rows = parts[1].shape[1] - first, total.shape[0]
        for p in range(chips):
            lo, hi = min(p * step, rows), min((p + 1) * step, rows)
            end = first + hi - lo
            if hi > lo:
                parts[1][p, first:end] = total[lo:hi]
            if hi - lo < step:
                parts[1][p, end:] = jnp.zeros((step - hi + lo, width), BF16)

    peers = [(flip(c, 1 << i, n_ctx), f) for i in range(n_ctx.bit_length() - 1)]
    ctx_phases = len(peers)
    peers += [(c, flip(f, 1 << i, n_fsdp)) for i in range(n_fsdp.bit_length() - 1)]

    def line_copy(i):
        rows = lines_in.shape[0] if i < ctx_phases else lead
        return send(
            lines_ref.at[:rows],
            lines_got.at[i, :rows],
            lines_send.at[i],
            lines_recv.at[i],
            peers[i],
        )

    def line_phase(i):
        if 0 < i <= len(peers):
            rows = lines_in.shape[0] if i <= ctx_phases else lead
            line_copy(i - 1).wait()
            lines_ref[:rows] += lines_got[i - 1, :rows]
        if i < len(peers):
            line_copy(i).start()

    def settle(finish, i):
        finish()
        keep = pltpu.make_async_copy(parts[i].at[chip], outs[i].at[core, chip], local.at[0])
        keep.start()
        keep.wait()

    sum_a, finish_a, sums_a, gather_a, gathers_a = line_ops(0)
    sum_b, finish_b, sums_b, gather_b, gathers_b = line_ops(1)
    cols_step, cols_done = line_gather(
        chip, chips, f, core, lambda at, h: cols_all.at[2 * at + h], cols_sems
    )
    load = pltpu.make_async_copy(cols_ref, cols_all.at[c], local.at[1])
    load.start()
    cut = parts[0].shape[1]
    parts[0][...] = rows_ref[:, :cut]
    load.wait()
    cols_step(0)
    sum_a(0)
    parts[1][:, : rows_ref.shape[1] - cut] = rows_ref[:, cut:]
    lines_ref[...] = lines_in[...]
    for j in range(n_fsdp):
        proj_products(j)
    proj_pair().start()
    for t in range(1, chips - 1):
        cols_step(t)
        sum_a(t)
        if t == 1:
            proj_pair().wait()
            lax.fori_loop(0, n_fsdp, proj_add, 0)
            for k in range(1, n_fsdp):
                proj_copy(k).start()
    cols_step(chips - 1)
    settle(finish_a, 0)
    gather_a(0)
    proj_total()
    sum_b(0)
    phase = 0
    for s in range(1, chips):
        gather_a(s)
        if s < chips - 1:
            sum_b(s)
        line_phase(phase)
        phase += 1
    settle(finish_b, 1)
    for s in range(chips):
        gather_b(s)
        line_phase(phase)
        phase += 1
    while phase <= len(peers):
        line_phase(phase)
        phase += 1
    for done in (sums_a, sums_b, cols_done, gathers_a, gathers_b):
        done()
    for k in range(1, n_fsdp):
        proj_copy(k).wait_send()


def sums_call(n_ctx, n_fsdp, rows, cols, extra, attended, mid_low, lines, lead, cid):
    chips = n_ctx // 2
    count, width = attended.shape
    high = half_high(width // n_fsdp)
    per_chip = rows.shape[1]
    third = -(-(high + extra.shape[0]) // (16 * chips)) * 16
    cut = -(-(per_chip + third) // 32) * 16
    shapes = [(chips, size, width) for size in (cut, per_chip + third - cut)]
    phases = (n_ctx * n_fsdp).bit_length() - 1
    vm = pl.BlockSpec(memory_space=pltpu.VMEM)
    anym = pl.BlockSpec(memory_space=pl.ANY)
    dma = pltpu.SemaphoreType.DMA
    return pl.pallas_call(
        functools.partial(sums_kernel, n_ctx, n_fsdp, lead),
        in_specs=[vm, anym, vm, vm, vm, vm],
        out_specs=[vm, vm, anym, vm],
        out_shape=[jax.ShapeDtypeStruct((2,) + shape, BF16) for shape in shapes]
        + [jax.ShapeDtypeStruct((n_ctx,) + cols.shape, BF16)]
        + [jax.ShapeDtypeStruct(lines.shape, F32)],
        scratch_shapes=[pltpu.VMEM(shape, BF16) for shape in shapes]
        + [pltpu.VMEM((chips + 1,) + shape[1:], BF16) for shape in shapes]
        + [
            pltpu.VMEM((2, n_fsdp, high, width), BF16),
            pltpu.VMEM((n_fsdp, high, width), BF16),
            pltpu.VMEM((n_fsdp, high, width), BF16),
            pltpu.VMEM((phases,) + lines.shape, F32),
            dma((phases,)),
            dma((phases,)),
            dma((2,)),
            dma((n_fsdp,)),
            dma((n_fsdp,)),
            dma((2,)),
        ]
        + [dma((chips,))] * (5 + 2 * 8),
        compiler_params=pltpu.CompilerParams(
            collective_id=cid, has_side_effects=True, vmem_limit_bytes=56 * 1024 * 1024
        ),
        cost_estimate=SHORT,
        name="weight_sums",
    )(rows, cols, extra, attended, mid_low, lines)


def assemble_kernel(
    n_fsdp,
    own_ref,
    rest_ref,
    first_ref,
    second_ref,
    third_ref,
    out_ref,
    attn_hbm,
    fc_hbm,
    proj_hbm,
    wout_hbm,
    *scratch,
):
    attn_ref, fc_ref, proj_ref, wout_ref, low_ref, sem = scratch
    load = pltpu.make_async_copy(out_ref, low_ref, sem.at[4])
    load.start()
    hd = HEAD_DIM
    shard, hidden = fc_ref.shape[0], fc_ref.shape[1] // n_fsdp
    half = shard // 2
    width = proj_ref.shape[1]
    count = own_ref.shape[0]
    copies = [
        pltpu.make_async_copy(src, dst, sem.at[i])
        for i, (src, dst) in enumerate(
            ((wout_ref, wout_hbm), (fc_ref, fc_hbm), (proj_ref, proj_hbm), (attn_ref, attn_hbm))
        )
    ]
    for h in range(2):
        for j in range(n_fsdp):
            cut = min(first_ref.shape[2], half)
            at = slice(j * hidden, (j + 1) * hidden)
            fc_ref[h * half : h * half + cut, at] = first_ref[h, j, :cut].astype(F32)
            if cut < half:
                rows = second_ref[h, j, : half - cut].astype(F32)
                fc_ref[h * half + cut : (h + 1) * half, at] = rows
    copies[1].start()
    for h in range(2):
        proj_ref[h * half : (h + 1) * half] = third_ref[h, :half].astype(F32)
    copies[2].start()
    for h in range(width // hd):
        src = own_ref.at[h] if h < count else rest_ref.at[h - count]
        for part in range(3):
            at = part * width + h * hd
            attn_ref[:, at : at + hd] = src[:, part * hd : (part + 1) * hd].astype(F32)
    copies[3].start()
    load.wait()
    wout_ref[...] = low_ref[...].astype(F32)
    copies[0].start()
    for copy in copies:
        copy.wait()


def assemble(n_fsdp, own, rest, first, second, third, out_low, hidden):
    shard = own.shape[1]
    width = first.shape[3]
    vm = pl.BlockSpec(memory_space=pltpu.VMEM)
    anym = pl.BlockSpec(memory_space=pl.ANY)
    shapes = [(shard, 3 * width), (shard, n_fsdp * hidden), (shard, width), out_low.shape]
    return pl.pallas_call(
        functools.partial(assemble_kernel, n_fsdp),
        in_specs=[vm] * 5 + [anym],
        out_specs=[anym] * 4,
        out_shape=[jax.ShapeDtypeStruct(shape, F32) for shape in shapes],
        scratch_shapes=[pltpu.VMEM(shape, F32) for shape in shapes]
        + [pltpu.VMEM(out_low.shape, BF16), pltpu.SemaphoreType.DMA((5,))],
        compiler_params=pltpu.CompilerParams(vmem_limit_bytes=60 * 1024 * 1024),
        cost_estimate=SHORT,
        name="assemble",
    )(own, rest, first, second, third, out_low)


def swap(value, axis, size, k):
    return lax.ppermute(value, axis, [(i, i ^ k) for i in range(size)])


def shards(
    n_ctx,
    n_fsdp,
    tokens,
    block_order,
    w_attn,
    w_proj,
    w_fc,
    w_out,
    norm_gains,
    biases,
    fc_bias,
    cotangent,
):
    hd = HEAD_DIM
    count, width = tokens.shape[1:]
    shard = width // n_fsdp
    heads = width // hd
    base = heads // n_ctx
    rest = heads - base * n_ctx
    slots = base + rest
    own_blocks = count // BLOCK
    c = lax.axis_index("ctx")
    f = lax.axis_index("fsdp")

    order = block_order[0]
    inv = jnp.argsort(order).astype(jnp.int32)
    order_own = jnp.concatenate([order, (c * own_blocks)[None]])

    def head_cols(h):
        return jnp.concatenate(
            [
                lax.dynamic_slice(w_attn, (0, part * width + h * hd), (shard, hd))
                for part in range(3)
            ],
            axis=1,
        )

    slot_heads = [c * base + s for s in range(base)] + [n_ctx * base + r for r in range(rest)]
    w_slots = jnp.stack([head_cols(h) for h in slot_heads])
    small = jnp.concatenate([norm_gains, biases], axis=0).astype(F32)
    hidden_cols = w_fc.shape[1] // n_fsdp
    normed_one, qkv, full_proj, fc_cols, _, w_slots, small = start_call(
        n_ctx, n_fsdp, base, tokens[0], w_slots, small, w_proj, w_fc, 3
    )
    full_proj = full_proj.reshape(width, width)
    qkv = qkv.reshape(slots, n_ctx * own_blocks, BLOCK, 3 * hd)
    gains, shifts = small[:2], small[2:]
    cot = cotangent[0]

    cot_late, _ = lax.optimization_barrier((cot, small))
    cot_all = lax.all_gather(cot_late, "fsdp", axis=0)

    out_own, lse_own = attn_fwd(inv, qkv, base)
    if rest:
        out_rest, lse_rest = rest_fwd(order_own, qkv, base)
    else:
        out_rest = out_own
    attended, mid, normed_two = mix_call(
        n_ctx, out_own, out_rest, tokens[0], full_proj, small, 6
    )
    fc_cols = fc_cols.reshape(width, hidden_cols)
    rows = tokens[0].astype(F32)

    normed_two_grad, fc_bias_part, out_part, w_out_part, w_fc_part = ffn(
        n_fsdp,
        normed_two,
        cot_all,
        fc_cols,
        w_out,
        fc_bias.astype(F32)[None],
    )
    w_out_sum = lax.psum_scatter(w_out_part, "ctx", scatter_dimension=0, tiled=True)

    half, high = shard // 2, half_high(shard)
    core = c % 2
    main = n_ctx * base * hd
    mid_grad, mid_low, turn_sums, d_rest, fc_mine, layer_rows, d_out = turn_call(
        n_ctx,
        n_fsdp,
        base,
        normed_two_grad,
        cot,
        mid,
        full_proj,
        small,
        w_fc_part,
        out_part,
        7,
    )

    d_own = attn_bwd(inv, qkv, d_out, out_own, lse_own, base)
    d_own = d_own.reshape(base, n_ctx, count, 3 * hd)
    if rest:
        d_rest = rest_bwd(order_own, qkv, d_rest, out_rest, lse_rest, base)
        d_rest = d_rest.reshape(rest, n_ctx, count, 3 * hd)
        sums = jnp.concatenate(
            [jnp.sum(d.astype(F32), axis=(1, 2)) for d in (d_own, d_rest)], axis=0
        )
    else:
        d_rest = d_own
        sums = jnp.sum(d_own.astype(F32), axis=(1, 2))
    if back_fits(n_ctx, n_fsdp, count, width, slots):
        normed_one_grad, cols_sum, fc_rows = back_call(
            n_ctx, n_fsdp, d_own, d_rest, w_slots, normed_one, fc_mine, 4
        )
        normed_one_grad = normed_one_grad.astype(F32)
    else:
        dqkv = jnp.concatenate([d_own, d_rest])[:slots].reshape(slots, n_ctx * count, 3 * hd)
        one_part = jnp.einsum("hte,hde->td", dqkv, w_slots, preferred_element_type=F32)
        normed_one_grad = lax.psum_scatter(
            one_part.astype(BF16), "ctx", scatter_dimension=0, tiled=True
        ).astype(F32)
        slot_part = jnp.einsum(
            "td,hte->hde",
            normed_one.reshape(n_ctx * count, width),
            dqkv,
            preferred_element_type=F32,
        ).astype(BF16)
        cols_sum = lax.psum_scatter(slot_part, "fsdp", scatter_dimension=1, tiled=True)
        fc_rows = lax.all_to_all(fc_mine, "fsdp", split_axis=0, concat_axis=0, tiled=True)

    w_out_sum, fc_rows = lax.optimization_barrier((w_out_sum, fc_rows))
    w_out_low = lax.all_gather(w_out_sum, "ctx", axis=0, tiled=True)
    xhat_one, rstd_one = norm_parts(rows)
    tokens_grad = (mid_grad + norm_back(xhat_one, rstd_one, gains[0], normed_one_grad)).astype(
        BF16
    )

    def placed(part):
        cols = sums[:, part * hd : (part + 1) * hd]
        line = lax.dynamic_update_slice_in_dim(
            jnp.zeros((width,), F32), cols[:base].reshape(-1), c * base * hd, 0
        )
        return line + jnp.pad(cols[base:].reshape(-1), (main, 0))

    lines = jnp.stack(
        [
            jnp.sum(normed_one_grad * xhat_one, axis=0),
            turn_sums[0],
            jnp.sum(normed_one_grad, axis=0),
            turn_sums[1],
            placed(0),
            placed(2),
            turn_sums[2],
            turn_sums[3],
        ]
    )
    lead = lines.shape[0]
    tail = jnp.pad(fc_bias_part, ((0, 7), (0, width - hidden_cols)))
    lines = jnp.concatenate([lines, tail])

    chips = n_ctx // 2
    fc_rows = fc_rows.reshape(-1, width)
    per_chip = -(-fc_rows.shape[0] // (16 * chips)) * 16
    fc_rows = jnp.pad(fc_rows, ((0, per_chip * chips - fc_rows.shape[0]), (0, 0)))
    fc_rows = fc_rows.reshape(chips, per_chip, width)
    extra = jnp.zeros((16, width), BF16)
    if rest:
        away = lax.dynamic_slice_in_dim(cols_sum[base:], (1 - core) * half, half, 1)
        here = lax.dynamic_slice_in_dim(cols_sum[base:], core * half, half, 1)
        extra = here.astype(F32) + swap(away, "ctx", n_ctx, 1).astype(F32)
        extra = extra.astype(BF16).reshape(-1, width)
        extra_rows = extra.shape[0]
        extra = jnp.pad(extra, ((0, -extra_rows % 16), (0, 0)))
    first, second, own_cols, lines = sums_call(
        n_ctx, n_fsdp, fc_rows, cols_sum[:base], extra, attended, mid_low, lines, lead, 5
    )
    w_out_low, lines = lax.optimization_barrier((w_out_low, lines))
    split = per_chip - first.shape[2]
    third = second[:, :, split:].reshape(2, -1, width)
    second = second[:, :, :split]
    own_cols = own_cols.reshape(n_ctx * base, shard, 3 * hd)
    if rest:
        rest_cols = third[:, high : high + extra_rows].reshape(2, rest, half, 3 * hd)
        rest_cols = rest_cols.transpose(1, 0, 2, 3).reshape(rest, shard, 3 * hd)
    else:
        rest_cols = own_cols
    if hidden_cols == width and chips == n_fsdp:
        w_attn_grad, w_fc_grad, w_proj_grad, w_out_grad = assemble(
            n_fsdp, own_cols, rest_cols, first, second, third, w_out_low, hidden_cols
        )
    else:
        w_fc_low = jnp.concatenate([first, second], axis=2).reshape(2, -1, width)
        w_fc_low = w_fc_low[:, : n_fsdp * high * hidden_cols // width]
        w_fc_low = w_fc_low.reshape(2, n_fsdp, high, hidden_cols)[:, :, :half]
        w_fc_grad = w_fc_low.transpose(0, 2, 1, 3).reshape(shard, n_fsdp * hidden_cols)
        w_fc_grad = w_fc_grad.astype(F32)
        w_proj_grad = third[:, :half].reshape(shard, width).astype(F32)
        cols = jnp.concatenate([own_cols, rest_cols])[: width // hd]
        cols = cols.reshape(width // hd, shard, 3, hd).transpose(1, 2, 0, 3)
        w_attn_grad = cols.reshape(shard, 3 * width).astype(F32)
        w_out_grad = w_out_low.astype(F32)
    fc_bias_grad = lines[lead, :hidden_cols]
    lines = lax.dynamic_slice_in_dim(lines[:lead], f * shard, shard, 1)
    return (
        layer_rows[None],
        tokens_grad[None],
        w_attn_grad,
        w_proj_grad,
        w_fc_grad,
        w_out_grad,
        lines[:2],
        lines[2:],
        fc_bias_grad,
    )


def solution(mesh):
    rows = P("fsdp", "ctx", None)
    weight = P("fsdp", None)
    vectors = P(None, "fsdp")
    return jax.shard_map(
        functools.partial(shards, mesh.shape["ctx"], mesh.shape["fsdp"]),
        mesh=mesh,
        in_specs=(
            rows, weight, weight, weight, weight, weight, vectors, vectors, P("fsdp"), rows,
        ),
        out_specs=(
            rows, rows, weight, weight, weight, weight, vectors, vectors, P("fsdp"),
        ),
        check_vma=False,
    )
```

```python
import functools

import jax
import jax.numpy as jnp
from jax import lax
from jax.experimental import pallas as pl
from jax.experimental.pallas import tpu as pltpu
from jax.sharding import PartitionSpec as P

HEAD_DIM = 64
BLOCK = 128
QROWS = 256
EPS = 1e-05
SCALE = HEAD_DIM ** (-0.5)
F32 = jnp.float32
BF16 = jnp.bfloat16
VMEM_LIMIT = 56 * 1024 * 1024
LAST = (((1,), (1,)), ((), ()))
FIRST = (((0,), (0,)), ((), ()))
MESH = pl.DeviceIdType.MESH
TILE = 256


def dot_last(a, b):
    return lax.dot_general(a, b, LAST, preferred_element_type=F32)


def dot(a, b):
    return jnp.dot(a, b, preferred_element_type=F32)


def dot_first(a, b):
    return lax.dot_general(a, b, FIRST, preferred_element_type=F32)


SHORT = pl.CostEstimate(flops=1, bytes_accessed=1, transcendentals=0)


def norm_parts(rows):
    mean = jnp.mean(rows, axis=-1, keepdims=True)
    cen = rows - mean
    rstd = lax.rsqrt(jnp.mean(cen * cen, axis=-1, keepdims=True) + EPS)
    return cen * rstd, rstd


def norm_back(xhat, rstd, gain, grad):
    dxhat = grad * gain
    return rstd * (
        dxhat
        - jnp.mean(dxhat, axis=-1, keepdims=True)
        - xhat * jnp.mean(dxhat * xhat, axis=-1, keepdims=True)
    )


def flip(place, k, size):
    out = 0
    bit = 1
    while bit < size:
        out = out + (place // bit + k // bit) % 2 * bit
        bit *= 2
    return out

def half_high(shard):
    return -(-(shard // 2) // 16) * 16


def enter(peers):
    barrier = pltpu.get_barrier_semaphore()
    for peer in peers:
        pl.semaphore_signal(barrier, inc=1, device_id=peer, device_id_type=MESH)
    pl.semaphore_wait(barrier, len(peers))

def send(src, dst, send_sem, recv_sem, peer):
    return pltpu.make_async_remote_copy(
        src_ref=src, dst_ref=dst, send_sem=send_sem, recv_sem=recv_sem,
        device_id=peer, device_id_type=MESH)


def ffn_kernel(n, nt_hbm, cot_hbm, wfc_hbm, wout_hbm, bias_ref,
               gsum_ref, fcb_ref, out_hbm, wout_grad_hbm, wfc_grad_hbm,
               cot_ref, wfc_ref, wout_ref, all_ref, act_ref, hg_ref, ag_ref, part_ref, got_ref, stage_d, stage_h,
               s1, r1, s2, r2, local):
    c = lax.axis_index("ctx")
    f = lax.axis_index("fsdp")
    rows, width = nt_hbm.shape
    enter([(c, flip(f, k, n)) for k in range(1, n)])

    def rows_out(k):
        return send(nt_hbm, all_ref.at[f], s1.at[k], r1.at[k], (c, flip(f, k, n)))

    def grad_back(k):
        other = flip(f, k, n)
        return send(part_ref.at[other], got_ref.at[k], s2.at[k], r2.at[k], (c, other))

    near = [k for k in range(1, n) if k & (k - 1) == 0]
    far = [k for k in range(1, n) if k not in near]
    for k in near:
        rows_out(k).start()
    loads = [
        pltpu.make_async_copy(nt_hbm, all_ref.at[f], local.at[0]),
        pltpu.make_async_copy(wout_hbm, wout_ref, local.at[1]),
        pltpu.make_async_copy(cot_hbm, cot_ref, local.at[2]),
        pltpu.make_async_copy(wfc_hbm, wfc_ref, local.at[3]),
    ]
    for load in loads:
        load.start()
    fcb_ref[...] = jnp.zeros_like(fcb_ref)
    loads[1].wait()
    loads[2].wait()

    def active_grad(k, carry):
        ag_ref[k] = dot_last(cot_ref[k], wout_ref[...])
        return carry

    lax.fori_loop(0, n, active_grad, 0)
    for k in far:
        rows_out(k).start()
    loads[0].wait()
    loads[3].wait()

    def chunk(k, carry):
        src = flip(f, k, n)

        @pl.when(k > 0)
        def _():
            rows_out(k).wait_recv()

        hidden = dot(all_ref[src], wfc_ref[...]) + bias_ref[...]
        square = hidden * hidden
        tanh = jnp.tanh(0.7978845608028654 * (hidden + 0.044715 * square * hidden))
        act_ref[src] = (0.5 * hidden * (1.0 + tanh)).astype(BF16)
        slope = 0.5 * (1.0 + tanh) + 0.5 * hidden * (1.0 - tanh * tanh) * 0.7978845608028654 * (
            1.0 + 3.0 * 0.044715 * square
        )
        grad = (ag_ref[src] * slope).astype(BF16)
        hg_ref[src] = grad
        fcb_ref[...] += jnp.sum(grad.astype(F32), axis=0, keepdims=True)
        part_ref[src] = dot_last(grad, wfc_ref[...]).astype(BF16)

        @pl.when(k > 0)
        def _():
            grad_back(k).start()

        return carry

    lax.fori_loop(0, n, chunk, 0)

    def grads(left_ref, right_ref, tiles, stage_ref, base):
        right = right_ref[...].reshape(n * rows, right_ref.shape[2])
        copies = []
        for i, (lo, size, sent, dst) in enumerate(tiles):
            slot = i % 2
            if i >= 2:
                copies[i - 2].wait()
            left = left_ref[:, :, lo : lo + size].reshape(n * rows, size)
            stage_ref[slot, :size] = dot_first(left, right).astype(BF16)
            copies.append(
                pltpu.make_async_copy(stage_ref.at[slot, :sent], dst, local.at[base + slot])
            )
            copies[-1].start()
        for copy in copies[-2:]:
            copy.wait()

    half, high = width // n // 2, wfc_grad_hbm.shape[2]
    if half < high:
        stage_h[:, half:high] = jnp.zeros((2, high - half, stage_h.shape[2]), BF16)
    wide = act_ref.shape[2]
    sizes = [(lo, min(TILE, wide - lo)) for lo in range(0, wide, TILE)]
    grads(
        act_ref,
        cot_ref,
        [(lo, size, size, wout_grad_hbm.at[lo : lo + size]) for lo, size in sizes],
        stage_d,
        4,
    )
    grads(
        all_ref,
        hg_ref,
        [
            ((2 * j + h) * half, half, high, wfc_grad_hbm.at[h, j])
            for j in range(n)
            for h in range(2)
        ],
        stage_h,
        6,
    )

    def out_copy(k):
        return pltpu.make_async_copy(
            stage_d.at[k % 2, :rows], out_hbm.at[k], local.at[4 + k % 2]
        )

    for k in range(n):
        if k >= 2:
            out_copy(k - 2).wait()
        stage_d[k % 2, :rows] = dot(act_ref[k], wout_ref[...]).astype(BF16)
        out_copy(k).start()

    gsum_ref[...] = part_ref[f].astype(F32)
    for k in near + far:
        grad_back(k).wait_recv()
        gsum_ref[...] += got_ref[k].astype(F32)
    for k in range(1, n):
        rows_out(k).wait_send()
        grad_back(k).wait_send()
    for k in range(max(0, n - 2), n):
        out_copy(k).wait()


def ffn(n, nt, cot, wfc, wout, bias, cid=1):
    m, d = nt.shape
    h = wfc.shape[1]
    vm = pl.BlockSpec(memory_space=pltpu.VMEM)
    anym = pl.BlockSpec(memory_space=pl.ANY)
    return pl.pallas_call(
        functools.partial(ffn_kernel, n),
        in_specs=[anym] * 4 + [vm],
        out_specs=[vm, vm] + [anym] * 3,
        out_shape=[
            jax.ShapeDtypeStruct((m, d), F32),
            jax.ShapeDtypeStruct((1, h), F32),
            jax.ShapeDtypeStruct((n, m, d), BF16),
            jax.ShapeDtypeStruct((h, d), BF16),
            jax.ShapeDtypeStruct((2, n, half_high(d // n), h), BF16),
        ],
        scratch_shapes=[
            pltpu.VMEM((n, m, d), BF16),
            pltpu.VMEM((d, h), BF16),
            pltpu.VMEM((h, d), BF16),
            pltpu.VMEM((n, m, d), BF16),
            pltpu.VMEM((n, m, h), BF16),
            pltpu.VMEM((n, m, h), BF16),
            pltpu.VMEM((n, m, h), F32),
            pltpu.VMEM((n, m, d), BF16),
            pltpu.VMEM((n, m, d), BF16),
            pltpu.VMEM((2, max(TILE, m), d), BF16),
            pltpu.VMEM((2, half_high(d // n), h), BF16),
        ]
        + [pltpu.SemaphoreType.DMA((n,))] * 4
        + [pltpu.SemaphoreType.DMA((8,))],
        compiler_params=pltpu.CompilerParams(
            collective_id=cid, has_side_effects=True, vmem_limit_bytes=60 * 1024 * 1024
        ),
        cost_estimate=SHORT,
        name="feed_forward",
    )(nt, cot, wfc, wout, bias)


def weight_shares(c, f, core, n_fsdp, shard, source, dst, ss, rs):
    cut = shard // 32 * 16 if shard % 16 == 0 else 0
    shares = ((0, cut), (cut, shard)) if cut else ((0, shard), (0, shard))
    twin_id = (c + 1 - 2 * core, f)

    def copy(share, k, onward):
        lo, hi = share
        other = flip(f, k, n_fsdp)
        if onward:
            part = dst.at[other, lo:hi]
            return send(part, part, ss.at[1, k], rs.at[1, k], twin_id)
        return send(source(k).at[lo:hi], dst.at[f, lo:hi], ss.at[0, k], rs.at[0, k], (c, other))

    def by_core(act):
        for h in range(2):

            @pl.when(core == h)
            def _(h=h):
                for k in range(1, n_fsdp):
                    act(shares[h], shares[1 - h], k)

    def start(mine, theirs, k):
        copy(mine, k, False).start()

    def onward(mine, theirs, k):
        copy(mine, k, False).wait_recv()
        if cut:
            copy(mine, k, True).start()

    def done(mine, theirs, k):
        if cut:
            copy(theirs, k, True).wait_recv()
            copy(mine, k, True).wait_send()
        copy(mine, k, False).wait_send()

    return tuple(functools.partial(by_core, act) for act in (start, onward, done))


def start_kernel(
    n_ctx,
    n_fsdp,
    base,
    tok_hbm,
    w_hbm,
    small_ref,
    proj_hbm,
    fc_hbm,
    n_hbm,
    qkv_hbm,
    proj_all,
    fc_all,
    fc_parts,
    w_ref,
    lines_ref,
    n_ref,
    qkv_ref,
    fc_ref,
    fc_cut,
    x_ref,
    wg_ref,
    sg_ref,
    tok_recv,
    right_sem,
    left_sem,
    twin_sem,
    w_send,
    w_recv,
    s_send,
    s_recv,
    proj_send,
    proj_recv,
    fc_send,
    fc_recv,
    local,
):
    c = lax.axis_index("ctx")
    f = lax.axis_index("fsdp")
    chips = n_ctx // 2
    chip, core = c // 2, c % 2
    slots, width, cols = w_ref.shape
    shard = width // n_fsdp
    hd = HEAD_DIM
    enter(
        [(lax.rem(c + i, n_ctx), f) for i in range(1, n_ctx)]
        + [(c, flip(f, k, n_fsdp)) for k in range(1, n_fsdp)]
    )

    def block(at, same):
        return 2 * at + (core if same else 1 - core)

    cut = x_ref.shape[1] // 2

    def part(ref, h):
        return ref.at[pl.ds(h * cut, cut)]

    def hop(step, to_right, from_own, h):
        origin = block(chip - step if to_right else chip + step, True)
        src = tok_hbm if from_own else x_ref.at[origin]
        sem = (right_sem if to_right else left_sem).at[step, h]
        peer = (c + 2 if to_right else c - 2, f)
        dst = part(x_ref.at[origin], h)
        return send(part(src, h), dst, sem, tok_recv.at[origin, h], peer)

    def twin(at, from_own, h):
        origin = block(at, True)
        src = tok_hbm if from_own else x_ref.at[origin]
        dst = part(x_ref.at[origin], h)
        return send(
            part(src, h),
            dst,
            twin_sem.at[at, h],
            tok_recv.at[origin, h],
            (block(chip, False), f),
        )

    def w_copy(k):
        return send(w_hbm, wg_ref.at[f], w_send.at[k], w_recv.at[k], (c, flip(f, k, n_fsdp)))

    def s_copy(k):
        return send(small_ref, sg_ref.at[f], s_send.at[k], s_recv.at[k], (c, flip(f, k, n_fsdp)))

    weights_start, weights_onward, weights_done = weight_shares(
        c, f, core, n_fsdp, shard, lambda k: proj_hbm, proj_all, proj_send, proj_recv
    )
    fc_start, fc_onward, fc_done = weight_shares(
        c,
        f,
        core,
        n_fsdp,
        shard,
        lambda k: fc_parts.at[flip(f, k, n_fsdp)],
        fc_all,
        fc_send,
        fc_recv,
    )

    for k in range(1, n_fsdp):
        s_copy(k).start()

    for h in range(2):

        @pl.when(chip < chips - 1)
        def _(h=h):
            hop(0, True, True, h).start()

        @pl.when(chip > 0)
        def _(h=h):
            hop(0, False, True, h).start()

    for k in range(1, n_fsdp):
        w_copy(k).start()
    for h in range(2):
        twin(chip, True, h).start()
    own_x = pltpu.make_async_copy(tok_hbm, x_ref.at[c], local.at[0])
    own_w = pltpu.make_async_copy(w_hbm, wg_ref.at[f], local.at[1])
    own_proj = pltpu.make_async_copy(proj_hbm, proj_all.at[f], local.at[2])
    load_fc = pltpu.make_async_copy(fc_hbm, fc_ref, local.at[3])
    for copy in (own_x, own_w, own_proj, load_fc):
        copy.start()
    sg_ref[f] = small_ref[...]
    for k in range(1, n_fsdp):
        s_copy(k).wait_recv()
    for j in range(n_fsdp):
        lines_ref[:, j * shard : (j + 1) * shard] = sg_ref[j]
    main = n_ctx * base * hd
    row_id = lax.broadcasted_iota(jnp.int32, (width, slots * hd), 0)
    col_id = lax.broadcasted_iota(jnp.int32, (width, slots * hd), 1)
    wanted = jnp.where(col_id < base * hd, c * base * hd + col_id, main + col_id - base * hd)
    picked = dot(lines_ref[...].astype(BF16), (row_id == wanted).astype(BF16))
    zero = jnp.zeros((1, hd), F32)
    bias = [
        jnp.concatenate(
            [picked[4:5, s * hd : (s + 1) * hd], zero, picked[5:6, s * hd : (s + 1) * hd]], axis=1
        )
        for s in range(slots)
    ]
    own_w.wait()
    own_x.wait()
    for k in range(1, n_fsdp):
        w_copy(k).wait_recv()
    weights_start()
    for j in range(n_fsdp):
        w_ref[:, j * shard : (j + 1) * shard, :] = wg_ref[j]

    load_fc.wait()
    hidden = fc_cut.shape[2]
    cuts = []
    for j in range(n_fsdp):
        if j >= 2:
            cuts[j - 2].wait()
        fc_cut[j % 2] = fc_ref[:, j * hidden : (j + 1) * hidden]
        cuts.append(pltpu.make_async_copy(fc_cut.at[j % 2], fc_parts.at[j], local.at[4 + j % 2]))
        cuts[-1].start()

    for copy in cuts[-2:]:
        copy.wait()
    fc_start()
    own_fc = pltpu.make_async_copy(fc_parts.at[f], fc_all.at[f], local.at[3])
    own_fc.start()

    def results(origin):
        return (
            pltpu.make_async_copy(n_ref, n_hbm.at[origin], local.at[0]),
            pltpu.make_async_copy(qkv_ref, qkv_hbm.at[:, origin], local.at[1]),
        )

    def project(at, same, first=False):
        origin = block(at, same)
        rows = x_ref[origin].astype(F32)
        mean = jnp.mean(rows, axis=1, keepdims=True)
        cen = rows - mean
        var = jnp.mean(cen * cen, axis=1, keepdims=True)
        normed = cen * lax.rsqrt(var + EPS) * lines_ref[0:1] + lines_ref[2:3]
        normed = normed.astype(BF16)

        @pl.when(jnp.logical_not(first))
        def _():
            for copy in results(origin):
                copy.wait()

        n_ref[...] = normed
        for s in range(slots):
            qkv_ref[s] = (dot(normed, w_ref[s]) + bias[s]).astype(BF16)
        for copy in results(origin):
            copy.start()

    def arrived(at, same, h):
        origin = block(at, same)
        ref = part(x_ref.at[origin], h)
        pltpu.make_async_copy(ref, ref, tok_recv.at[origin, h]).wait()

    def step(s, carry):
        for h in range(2):

            @pl.when((s > 0) & (chip - s >= 0))
            def _(h=h):
                arrived(chip - s, True, h)

                @pl.when(chip < chips - 1)
                def _():
                    hop(s, True, False, h).start()

                twin(chip - s, False, h).start()

            @pl.when((s > 0) & (chip + s < chips))
            def _(h=h):
                arrived(chip + s, True, h)

                @pl.when(chip > 0)
                def _():
                    hop(s, False, False, h).start()

                twin(chip + s, False, h).start()

        @pl.when(s == chips - 1)
        def _():
            weights_onward()

        @pl.when(chip - s >= 0)
        def _():
            project(chip - s, True, s == 0)

        @pl.when((s > 0) & (chip + s < chips))
        def _():
            project(chip + s, True)

        @pl.when(chip - s >= 0)
        def _():
            for h in range(2):
                arrived(chip - s, False, h)
            project(chip - s, False)

        @pl.when((s > 0) & (chip + s < chips))
        def _():
            for h in range(2):
                arrived(chip + s, False, h)
            project(chip + s, False)

        return carry

    lax.fori_loop(0, chips, step, 0)
    fc_onward()
    for copy in results(c):
        copy.wait()
    own_proj.wait()
    own_fc.wait()

    for s in range(chips):
        for h in range(2):
            if s < chips - 1:

                @pl.when((chip - s >= 0) & (chip < chips - 1))
                def _(s=s, h=h):
                    hop(s, True, False, h).wait_send()

                @pl.when((chip + s < chips) & (chip > 0))
                def _(s=s, h=h):
                    hop(s, False, False, h).wait_send()

            twin(s, False, h).wait_send()
    for k in range(1, n_fsdp):
        w_copy(k).wait_send()
        s_copy(k).wait_send()
    weights_done()
    fc_done()


def start_call(n_ctx, n_fsdp, base, tok, w_slots, small, w_proj, w_fc, cid):
    count, width = tok.shape
    slots, shard, cols = w_slots.shape
    hidden = w_fc.shape[1] // n_fsdp
    vm = pl.BlockSpec(memory_space=pltpu.VMEM)
    anym = pl.BlockSpec(memory_space=pl.ANY)
    dma = pltpu.SemaphoreType.DMA
    return pl.pallas_call(
        functools.partial(start_kernel, n_ctx, n_fsdp, base),
        in_specs=[anym, anym, vm, anym, anym],
        out_specs=[anym, anym, anym, anym, anym, vm, vm],
        out_shape=[
            jax.ShapeDtypeStruct((n_ctx, count, width), BF16),
            jax.ShapeDtypeStruct((slots, n_ctx, count, cols), BF16),
            jax.ShapeDtypeStruct((n_fsdp,) + w_proj.shape, BF16),
            jax.ShapeDtypeStruct((n_fsdp, shard, hidden), BF16),
            jax.ShapeDtypeStruct((n_fsdp, shard, hidden), BF16),
            jax.ShapeDtypeStruct((slots, width, cols), BF16),
            jax.ShapeDtypeStruct((small.shape[0], width), F32),
        ],
        scratch_shapes=[
            pltpu.VMEM((count, width), BF16),
            pltpu.VMEM((slots, count, cols), BF16),
            pltpu.VMEM(w_fc.shape, BF16),
            pltpu.VMEM((2, shard, hidden), BF16),
            pltpu.VMEM((n_ctx, count, width), BF16),
            pltpu.VMEM((n_fsdp, slots, shard, cols), BF16),
            pltpu.VMEM((n_fsdp,) + small.shape, F32),
            dma((n_ctx, 2)),
            dma((n_ctx // 2, 2)),
            dma((n_ctx // 2, 2)),
            dma((n_ctx // 2, 2)),
            dma((n_fsdp,)),
            dma((n_fsdp,)),
            dma((n_fsdp,)),
            dma((n_fsdp,)),
            dma((2, n_fsdp)),
            dma((2, n_fsdp)),
            dma((2, n_fsdp)),
            dma((2, n_fsdp)),
            dma((6,)),
        ],
        compiler_params=pltpu.CompilerParams(
            collective_id=cid, has_side_effects=True, vmem_limit_bytes=VMEM_LIMIT
        ),
        cost_estimate=SHORT,
        name="tokens_qkv",
    )(tok, w_slots, small, w_proj, w_fc)


def causal_scores(k, q_rows, start):
    scores = dot_last(k, q_rows)
    keep = start
    tail = scores[keep:]
    key_id = lax.broadcasted_iota(jnp.int32, tail.shape, 0)
    query_id = lax.broadcasted_iota(jnp.int32, tail.shape, 1)
    tail = jnp.where(key_id <= query_id, tail, -1e30)
    if keep == 0:
        return tail
    return jnp.concatenate([scores[:keep], tail], axis=0)


def soft(scores, v_t):
    top = jnp.max(scores, axis=0, keepdims=True)
    weights = jnp.exp(scores - top)
    total = jnp.sum(weights, axis=0, keepdims=True)
    out = dot(v_t, weights.astype(BF16)) / total
    return out, top + jnp.log(total)


def causal(inv_ref, x_ref):
    return jnp.concatenate([x_ref[0, inv_ref[i]] for i in range(x_ref.shape[1])], axis=0)


def attn_fwd_kernel(inv_ref, x_ref, o_ref, l_ref):
    rows = l_ref.shape[2]
    hd = HEAD_DIM
    x = causal(inv_ref, x_ref)
    q = x[:, :hd] * BF16(SCALE)
    k = x[:, hd : 2 * hd]
    v_t = x[:, 2 * hd :].T
    for i in range(rows // QROWS):
        lo, hi = i * QROWS, (i + 1) * QROWS
        out, lse = soft(causal_scores(k[:hi], q[lo:hi], lo), v_t[:, :hi])
        l_ref[0, :, lo:hi] = lse
        out = out.astype(BF16)
        for b in range(QROWS // BLOCK):
            o_ref[inv_ref[2 * i + b]] = out[:, b * BLOCK : (b + 1) * BLOCK]


def attn_fwd(inv, qkv, heads):
    blocks, _, cols = qkv.shape[1:]
    rows = blocks * BLOCK
    return pl.pallas_call(
        attn_fwd_kernel,
        grid_spec=pltpu.PrefetchScalarGridSpec(
            num_scalar_prefetch=1,
            grid=(heads,),
            in_specs=[pl.BlockSpec((1, blocks, BLOCK, cols), lambda h, inv: (h, 0, 0, 0))],
            out_specs=[
                pl.BlockSpec((blocks, HEAD_DIM, BLOCK), lambda h, inv: (0, h, 0)),
                pl.BlockSpec((1, 1, rows), lambda h, inv: (h, 0, 0)),
            ],
        ),
        out_shape=[
            jax.ShapeDtypeStruct((blocks, heads * HEAD_DIM, BLOCK), BF16),
            jax.ShapeDtypeStruct((heads, 1, rows), F32),
        ],
        compiler_params=pltpu.CompilerParams(vmem_limit_bytes=VMEM_LIMIT),
        cost_estimate=SHORT,
        name="attn_fwd",
    )(inv, qkv)


def attn_bwd_kernel(inv_ref, x_ref, do_ref, o_ref, l_ref, dx_ref, dk_acc, dv_acc):
    rows = l_ref.shape[2]
    hd = HEAD_DIM
    x = causal(inv_ref, x_ref)
    q = x[:, :hd] * BF16(SCALE)
    k = x[:, hd : 2 * hd]
    v = x[:, 2 * hd :]
    k_t = k.T
    dk_acc[...] = jnp.zeros_like(dk_acc)
    dv_acc[...] = jnp.zeros_like(dv_acc)
    for i in range(rows // QROWS):
        lo, hi = i * QROWS, (i + 1) * QROWS
        ids = [inv_ref[2 * i + b] for b in range(QROWS // BLOCK)]
        do_t = jnp.concatenate([do_ref[b] for b in ids], axis=1)
        o_t = jnp.concatenate([o_ref[b] for b in ids], axis=1)
        inner = jnp.sum(do_t.astype(F32) * o_t.astype(F32), axis=0, keepdims=True)
        probs = jnp.exp(causal_scores(k[:hi], q[lo:hi], lo) - l_ref[0, :, lo:hi])
        dprobs = dot(v[:hi], do_t)
        dscores = (probs * (dprobs - inner)).astype(BF16)
        dv_acc[:hi] += dot_last(probs.astype(BF16), do_t)
        dk_acc[:hi] += dot(dscores, q[lo:hi])
        dq = (dot(k_t[:, :hi], dscores) * SCALE).T
        for n, b in enumerate(ids):
            dx_ref[0, b, :, :hd] = dq[n * BLOCK : (n + 1) * BLOCK].astype(BF16)
    for i in range(rows // BLOCK):
        lo, hi = i * BLOCK, (i + 1) * BLOCK
        dx_ref[0, inv_ref[i], :, hd : 2 * hd] = dk_acc[lo:hi].astype(BF16)
        dx_ref[0, inv_ref[i], :, 2 * hd :] = dv_acc[lo:hi].astype(BF16)


def attn_bwd(inv, qkv, d_out, out, lse, heads):
    blocks, _, cols = qkv.shape[1:]
    rows = blocks * BLOCK
    whole = pl.BlockSpec((1, blocks, BLOCK, cols), lambda h, inv: (h, 0, 0, 0))
    feat = pl.BlockSpec((blocks, HEAD_DIM, BLOCK), lambda h, inv: (0, h, 0))
    return pl.pallas_call(
        attn_bwd_kernel,
        grid_spec=pltpu.PrefetchScalarGridSpec(
            num_scalar_prefetch=1,
            grid=(heads,),
            in_specs=[
                whole,
                feat,
                feat,
                pl.BlockSpec((1, 1, rows), lambda h, inv: (h, 0, 0)),
            ],
            out_specs=whole,
            scratch_shapes=[pltpu.VMEM((rows, HEAD_DIM), F32)] * 2,
        ),
        out_shape=jax.ShapeDtypeStruct((heads, blocks, BLOCK, cols), BF16),
        compiler_params=pltpu.CompilerParams(vmem_limit_bytes=VMEM_LIMIT),
        cost_estimate=pl.CostEstimate(
            flops=24 * 10**9, bytes_accessed=24 * 10**6, transcendentals=0
        ),
        name="attn_bwd",
    )(inv, qkv, d_out, out, lse)


def own_scores(order_ref, x_ref, k):
    hd = HEAD_DIM
    blocks = x_ref.shape[1]
    first = order_ref[blocks]
    q = jnp.concatenate([x_ref[0, first], x_ref[0, first + 1]], axis=0)[:, :hd]
    q = q * BF16(SCALE)
    scores = dot_last(k, q)
    row = lax.broadcasted_iota(jnp.int32, (BLOCK, 1), 0)
    key_place = jnp.concatenate([order_ref[b] * BLOCK + row for b in range(blocks)], axis=0)
    lane = lax.broadcasted_iota(jnp.int32, (1, 2 * BLOCK), 1)
    low, high = order_ref[order_ref[blocks]], order_ref[order_ref[blocks] + 1]
    place = jnp.where(lane < BLOCK, low * BLOCK + lane, (high - 1) * BLOCK + lane)
    return q, first, jnp.where(key_place <= place, scores, -1e30)


def rest_fwd_kernel(order_ref, x_ref, o_ref, l_ref):
    hd = HEAD_DIM
    x = x_ref[0].reshape(-1, 3 * hd)
    _, _, scores = own_scores(order_ref, x_ref, x[:, hd : 2 * hd])
    out, lse = soft(scores, x[:, 2 * hd :].T)
    o_ref[0] = out.astype(BF16)
    l_ref[0] = lse


def rest_fwd(order, qkv, base):
    slots, blocks, _, cols = qkv.shape
    rest = slots - base
    return pl.pallas_call(
        rest_fwd_kernel,
        grid_spec=pltpu.PrefetchScalarGridSpec(
            num_scalar_prefetch=1,
            grid=(rest,),
            in_specs=[
                pl.BlockSpec((1, blocks, BLOCK, cols), lambda h, o: (base + h, 0, 0, 0))
            ],
            out_specs=[
                pl.BlockSpec((1, HEAD_DIM, QROWS), lambda h, o: (h, 0, 0)),
                pl.BlockSpec((1, 1, QROWS), lambda h, o: (h, 0, 0)),
            ],
        ),
        out_shape=[
            jax.ShapeDtypeStruct((rest, HEAD_DIM, QROWS), BF16),
            jax.ShapeDtypeStruct((rest, 1, QROWS), F32),
        ],
        compiler_params=pltpu.CompilerParams(vmem_limit_bytes=VMEM_LIMIT),
        cost_estimate=SHORT,
        name="rest_fwd",
    )(order, qkv)


def rest_bwd_kernel(order_ref, x_ref, do_ref, o_ref, l_ref, dx_ref):
    hd = HEAD_DIM
    x = x_ref[0].reshape(-1, 3 * hd)
    blocks = x_ref.shape[1]
    k = x[:, hd : 2 * hd]
    q, first, scores = own_scores(order_ref, x_ref, k)
    do_t = do_ref[0]
    inner = jnp.sum(do_t.astype(F32) * o_ref[0].astype(F32), axis=0, keepdims=True)
    probs = jnp.exp(scores - l_ref[0])
    dprobs = dot(x[:, 2 * hd :], do_t)
    dscores = (probs * (dprobs - inner)).astype(BF16)
    dv = dot_last(probs.astype(BF16), do_t).astype(BF16)
    dk = dot(dscores, q).astype(BF16)
    dq = (dot(k.T, dscores) * SCALE).T.astype(BF16)
    dx_ref[0, :, :, 2 * hd :] = dv.reshape(blocks, BLOCK, hd)
    dx_ref[0, :, :, hd : 2 * hd] = dk.reshape(blocks, BLOCK, hd)
    dx_ref[0, :, :, :hd] = jnp.zeros((blocks, BLOCK, hd), BF16)
    for b in range(2):
        dx_ref[0, first + b, :, :hd] = dq[b * BLOCK : (b + 1) * BLOCK]


def rest_bwd(order, qkv, d_out, out, lse, base):
    slots, blocks, _, cols = qkv.shape
    rest = slots - base
    feat = pl.BlockSpec((1, HEAD_DIM, QROWS), lambda h, o: (h, 0, 0))
    return pl.pallas_call(
        rest_bwd_kernel,
        grid_spec=pltpu.PrefetchScalarGridSpec(
            num_scalar_prefetch=1,
            grid=(rest,),
            in_specs=[
                pl.BlockSpec((1, blocks, BLOCK, cols), lambda h, o: (base + h, 0, 0, 0)),
                feat,
                feat,
                pl.BlockSpec((1, 1, QROWS), lambda h, o: (h, 0, 0)),
            ],
            out_specs=pl.BlockSpec((1, blocks, BLOCK, cols), lambda h, o: (h, 0, 0, 0)),
        ),
        out_shape=jax.ShapeDtypeStruct((rest, blocks, BLOCK, cols), BF16),
        compiler_params=pltpu.CompilerParams(vmem_limit_bytes=VMEM_LIMIT),
        cost_estimate=SHORT,
        name="rest_bwd",
    )(order, qkv, d_out, out, lse)


def mix_kernel(
    n_ctx,
    out_hbm,
    rest_ref,
    tok_ref,
    proj_ref,
    lines_ref,
    att_ref,
    mid_ref,
    n_ref,
    got_ref,
    out_send,
    out_recv,
    local,
):
    c = lax.axis_index("ctx")
    f = lax.axis_index("fsdp")
    width = tok_ref.shape[1]
    blocks, feats = got_ref.shape[1], got_ref.shape[2]
    enter([(lax.rem(c + i, n_ctx), f) for i in range(1, n_ctx)])

    def out_copy(i):
        to = lax.rem(c + i, n_ctx)
        return send(
            out_hbm.at[pl.ds(to * blocks, blocks)],
            got_ref.at[c],
            out_send.at[i],
            out_recv.at[i],
            (to, f),
        )

    for i in range(n_ctx - 1, 0, -1):
        out_copy(i).start()
    own = pltpu.make_async_copy(
        out_hbm.at[pl.ds(c * blocks, blocks)], got_ref.at[c], local
    )
    own.start()
    main = n_ctx * feats
    if main < width:
        att_ref[:, main:] = rest_ref[...].reshape(width - main, -1).T
    own.wait()
    for i in range(1, n_ctx):
        out_copy(i).wait_recv()
    for src in range(n_ctx):
        block = jnp.concatenate([got_ref[src, b] for b in range(blocks)], axis=1)
        att_ref[:, src * feats : (src + 1) * feats] = block.T
    mid = tok_ref[...].astype(F32) + (dot(att_ref[...], proj_ref[...]) + lines_ref[6:7])
    mid_ref[...] = mid
    cen = mid - jnp.mean(mid, axis=1, keepdims=True)
    var = jnp.mean(cen * cen, axis=1, keepdims=True)
    n_ref[...] = (cen * lax.rsqrt(var + EPS) * lines_ref[1:2] + lines_ref[3:4]).astype(BF16)
    for i in range(1, n_ctx):
        out_copy(i).wait_send()


def mix_call(n_ctx, out_own, out_rest, tok, proj, lines, cid):
    count, width = tok.shape
    vm = pl.BlockSpec(memory_space=pltpu.VMEM)
    anym = pl.BlockSpec(memory_space=pl.ANY)
    dma = pltpu.SemaphoreType.DMA
    return pl.pallas_call(
        functools.partial(mix_kernel, n_ctx),
        in_specs=[anym, vm, vm, vm, vm],
        out_specs=[vm, vm, vm],
        out_shape=[
            jax.ShapeDtypeStruct((count, width), BF16),
            jax.ShapeDtypeStruct((count, width), F32),
            jax.ShapeDtypeStruct((count, width), BF16),
        ],
        scratch_shapes=[
            pltpu.VMEM((n_ctx, out_own.shape[0] // n_ctx) + out_own.shape[1:], BF16),
            dma((n_ctx,)),
            dma((n_ctx,)),
            dma(()),
        ],
        compiler_params=pltpu.CompilerParams(
            collective_id=cid, has_side_effects=True, vmem_limit_bytes=VMEM_LIMIT
        ),
        cost_estimate=SHORT,
        name="mix_rows",
    )(out_own, out_rest, tok, proj, lines)


def turn_kernel(
    n_ctx,
    gsum_ref,
    cot_ref,
    mid_ref,
    proj_ref,
    lines_ref,
    fc_hbm,
    grad_ref,
    low_ref,
    sums_ref,
    rest_ref,
    fc_ref,
    got_hbm,
    out_ref,
    pair_in,
    out_send,
    out_recv,
    pair_sem,
    local,
):
    c = lax.axis_index("ctx")
    f = lax.axis_index("fsdp")
    core = c % 2
    width = mid_ref.shape[1]
    blocks, feats = out_ref.shape[0] // n_ctx, out_ref.shape[1]
    enter([(lax.rem(c + i, n_ctx), f) for i in range(1, n_ctx)])
    pair = send(fc_hbm.at[1 - core], pair_in, pair_sem.at[0], pair_sem.at[1], (c + 1 - 2 * core, f))
    pair.start()
    own_fc = pltpu.make_async_copy(fc_hbm.at[core], fc_ref, local.at[0])
    own_fc.start()

    xhat, rstd = norm_parts(mid_ref[...])
    grad = gsum_ref[...]
    cot = cot_ref[...].astype(F32)
    mid_grad = cot + norm_back(xhat, rstd, lines_ref[1:2], grad)
    grad_ref[...] = mid_grad
    low = mid_grad.astype(BF16)
    low_ref[...] = low
    att_t = dot_last(low, proj_ref[...]).astype(BF16).T
    for to in range(n_ctx):
        for b in range(blocks):
            out_ref[to * blocks + b] = att_t[
                to * feats : (to + 1) * feats, b * BLOCK : (b + 1) * BLOCK
            ]

    def out_copy(i):
        to = lax.rem(c + i, n_ctx)
        return send(
            out_ref.at[pl.ds(to * blocks, blocks)],
            got_hbm.at[pl.ds(c * blocks, blocks)],
            out_send.at[i],
            out_recv.at[i],
            (to, f),
        )

    for i in range(n_ctx - 1, 0, -1):
        out_copy(i).start()
    own = pltpu.make_async_copy(
        out_ref.at[pl.ds(c * blocks, blocks)], got_hbm.at[pl.ds(c * blocks, blocks)], local.at[1]
    )
    own.start()
    main = n_ctx * feats
    if main < width:
        rest_ref[...] = att_t[main:].reshape(rest_ref.shape)
    else:
        rest_ref[...] = jnp.zeros(rest_ref.shape, BF16)
    for r, line in enumerate((grad * xhat, grad, low.astype(F32), cot)):
        sums_ref[r : r + 1] = jnp.sum(line, axis=0, keepdims=True)
    sums_ref[4:] = jnp.zeros((4, width), F32)
    own_fc.wait()
    pair.wait()

    def add(j, carry):
        fc_ref[j] = (fc_ref[j].astype(F32) + pair_in[j].astype(F32)).astype(BF16)
        return carry

    lax.fori_loop(0, fc_ref.shape[0], add, 0)
    own.wait()
    for i in range(1, n_ctx):
        out_copy(i).wait()


def turn_call(n_ctx, base, gsum, cot, mid, proj, lines, fc_part, cid):
    count, width = mid.shape
    heads = width // HEAD_DIM
    rest = max(heads - base * n_ctx, 1)
    out = (n_ctx * count // BLOCK, base * HEAD_DIM, BLOCK)
    vm = pl.BlockSpec(memory_space=pltpu.VMEM)
    anym = pl.BlockSpec(memory_space=pl.ANY)
    dma = pltpu.SemaphoreType.DMA
    return pl.pallas_call(
        functools.partial(turn_kernel, n_ctx),
        in_specs=[vm] * 5 + [anym],
        out_specs=[vm] * 5 + [anym],
        out_shape=[
            jax.ShapeDtypeStruct((count, width), F32),
            jax.ShapeDtypeStruct((count, width), BF16),
            jax.ShapeDtypeStruct((8, width), F32),
            jax.ShapeDtypeStruct((rest, HEAD_DIM, count), BF16),
            jax.ShapeDtypeStruct(fc_part.shape[1:], BF16),
            jax.ShapeDtypeStruct(out, BF16),
        ],
        scratch_shapes=[
            pltpu.VMEM(out, BF16),
            pltpu.VMEM(fc_part.shape[1:], BF16),
            dma((n_ctx,)),
            dma((n_ctx,)),
            dma((2,)),
            dma((2,)),
        ],
        compiler_params=pltpu.CompilerParams(
            collective_id=cid, has_side_effects=True, vmem_limit_bytes=VMEM_LIMIT
        ),
        cost_estimate=SHORT,
        name="turn_rows",
    )(gsum, cot, mid, proj, lines, fc_part)


def far_first(i, chips):
    return (i % 2) * (i // 2) + (1 - i % 2) * (chips - 1 - i // 2)


def line_sum(chip, chips, f, core, part, came, sems, ready=None):
    sent, left_sem, right_sem = sems

    def to_right(d):
        return send(
            part.at[d], came.at[d], sent.at[d], left_sem.at[d], (2 * (chip + 1) + core, f)
        )

    def to_left(d):
        place = jnp.where(d == chip - 1, chips, d)
        return send(
            part.at[d], came.at[place], sent.at[d], right_sem.at[d], (2 * (chip - 1) + core, f)
        )

    def from_left(d):
        send(part.at[d], came.at[d], sent.at[d], left_sem.at[d], (2 * chip + core, f)).wait_recv()
        add(d, d)

    def from_right(d, place):
        send(
            part.at[d], came.at[place], sent.at[d], right_sem.at[d], (2 * chip + core, f)
        ).wait_recv()
        add(d, place)

    def add(d, place):
        part[d] = (part[d].astype(F32) + came[place].astype(F32)).astype(BF16)

    def step(t):
        far = chips - 1 - t + chip
        near = t - (chips - 1 - chip)

        @pl.when(chip <= t)
        def _():
            if ready is not None:
                ready(far)

            @pl.when(chip > 0)
            def _():
                from_left(far)

            @pl.when(chip < t)
            def _():
                to_right(far + 1).wait_send()

            to_right(far).start()

        @pl.when(near >= 0)
        def _():
            if ready is not None:
                ready(near)

            @pl.when(chip < chips - 1)
            def _():
                from_right(near, near)

            @pl.when(near > 0)
            def _():
                to_left(near - 1).wait_send()

            to_left(near).start()

    def finish():
        if ready is not None:
            ready(chip)

        @pl.when(chip > 0)
        def _():
            from_left(chip)

        @pl.when(chip < chips - 1)
        def _():
            from_right(chip, chips)

    def done():
        @pl.when(chip < chips - 1)
        def _():
            to_right(chip + 1).wait_send()

        @pl.when(chip > 0)
        def _():
            to_left(chip - 1).wait_send()

    return step, finish, done


def line_gather(chip, chips, f, core, view, sems):
    right, left, twin_sent, got, twin_got = sems
    twin_id = (2 * chip + 1 - core, f)

    def hop(s, rightward):
        origin = chip - s if rightward else chip + s
        ref = view(origin, core)
        peer = (2 * (chip + 1 if rightward else chip - 1) + core, f)
        return send(ref, ref, (right if rightward else left).at[s], got.at[origin], peer)

    def twin(origin):
        ref = view(origin, core)
        return send(ref, ref, twin_sent.at[origin], twin_got.at[origin], twin_id)

    def arrived(origin):
        ref = view(origin, core)
        send(ref, ref, right.at[0], got.at[origin], twin_id).wait_recv()

    def step(s):
        @pl.when(chip - s >= 0)
        def _():
            if s:
                arrived(chip - s)

            @pl.when(chip < chips - 1)
            def _():
                hop(s, True).start()

            twin(chip - s).start()

        @pl.when(chip + s < chips)
        def _():
            if s:
                arrived(chip + s)

            @pl.when(chip > 0)
            def _():
                hop(s, False).start()

            if s:
                twin(chip + s).start()

    def done():
        for s in range(chips):
            if s < chips - 1:

                @pl.when((chip - s >= 0) & (chip < chips - 1))
                def _(s=s):
                    hop(s, True).wait_send()

                @pl.when((chip + s < chips) & (chip > 0))
                def _(s=s):
                    hop(s, False).wait_send()

            twin(s).wait_send()
            ref = view(s, 1 - core)
            send(ref, ref, twin_sent.at[s], twin_got.at[s], twin_id).wait_recv()

    return step, done


def back_kernel(
    n_ctx,
    n_fsdp,
    own_ref,
    rest_ref,
    w_ref,
    n_ref,
    fc_hbm,
    one_ref,
    cols_ref,
    fc_all,
    part,
    twin_out,
    twin_in,
    came,
    mine,
    theirs,
    twin_send,
    twin_recv,
    line_send,
    left_recv,
    right_recv,
    cols_send,
    cols_recv,
    fc_send,
    fc_recv,
    local,
):
    c = lax.axis_index("ctx")
    f = lax.axis_index("fsdp")
    chips = n_ctx // 2
    chip, core = c // 2, c % 2
    slots, width, cols = w_ref.shape
    count = own_ref.shape[2]
    base = own_ref.shape[0]
    shard = width // n_fsdp
    twin_id = (2 * chip + 1 - core, f)
    enter(
        [(lax.rem(c + i, n_ctx), f) for i in range(1, n_ctx)]
        + [(c, flip(f, k, n_fsdp)) for k in range(1, n_fsdp)]
    )

    def grad(s):
        return own_ref.at[s] if s < base else rest_ref.at[s - base]

    def for_block(b):
        total = dot_last(grad(0)[b], w_ref[0])
        for s in range(1, slots):
            total += dot_last(grad(s)[b], w_ref[s])
        return total.astype(BF16)

    def to_twin(d, slot):
        return send(twin_out.at[slot], twin_in.at[d], twin_send.at[slot], twin_recv.at[d], twin_id)

    def products(i, carry):
        d = far_first(i, chips)
        slot = i % 2
        product = for_block(2 * d + 1 - core)

        @pl.when(i > 1)
        def _():
            to_twin(d, slot).wait_send()

        twin_out[slot] = product
        to_twin(d, slot).start()
        part[d] = for_block(2 * d + core)
        return carry

    def ready(d):
        to_twin(d, 0).wait_recv()
        part[d] = (part[d].astype(F32) + twin_in[d].astype(F32)).astype(BF16)

    cut = count // 2
    streams = [
        line_sum(
            chip,
            chips,
            f,
            core,
            part.at[:, pl.ds(h * cut, cut)],
            came.at[h],
            (line_send.at[h], left_recv.at[h], right_recv.at[h]),
            None if h else ready,
        )
        for h in range(2)
    ]

    def step(t):
        for stream in streams:
            stream[0](t)

    def finish():
        for stream in streams:
            stream[1]()

    def done():
        for stream in streams:
            stream[2]()

    def cols_copy(src, dst, at):
        return send(mine.at[src], theirs.at[at], cols_send.at[src], cols_recv.at[at], (c, dst))

    def columns(j):
        left = n_ref[:, :, j * shard : (j + 1) * shard].reshape(n_ctx * count, shard)
        for s in range(slots):
            right = grad(s)[...].reshape(n_ctx * count, cols)
            mine[j, s] = dot_first(left, right).astype(BF16)

    def fc_copy(k):
        other = flip(f, k, n_fsdp)
        return send(fc_hbm.at[other], fc_all.at[f], fc_send.at[k], fc_recv.at[k], (c, other))

    for k in range(1, n_fsdp):
        fc_copy(k).start()
    own_fc = pltpu.make_async_copy(fc_hbm.at[f], fc_all.at[f], local)
    own_fc.start()
    lax.fori_loop(0, 2, products, 0)
    step(0)
    for j in range(n_fsdp):
        columns(j)
    for k in range(1, n_fsdp):
        other = flip(f, k, n_fsdp)
        cols_copy(other, other, f).start()
    lax.fori_loop(2, chips, products, 0)
    if chips > 2:
        step(1)
    for t in range(2, chips - 1):
        step(t)
    total = mine[f].astype(F32)
    for k in range(1, n_fsdp):
        other = flip(f, k, n_fsdp)
        cols_copy(other, other, other).wait_recv()
        total += theirs[other].astype(F32)
    cols_ref[...] = total.astype(BF16)
    finish()
    one_ref[...] = part[chip]
    own_fc.wait()
    for k in range(1, n_fsdp):
        fc_copy(k).wait()
    done()
    for slot in range(2):
        to_twin(0, slot).wait_send()
    for k in range(1, n_fsdp):
        other = flip(f, k, n_fsdp)
        cols_copy(other, other, other).wait_send()


def back_fits(n_ctx, n_fsdp, count, width, slots):
    blocks = (5 * (n_ctx // 2) + n_ctx) * count * width
    heads = slots * 256 * (n_ctx * count + 3 * width)
    return 2 * (blocks + heads) < 50 * 1024 * 1024


def back_call(n_ctx, n_fsdp, own, rest, w_slots, normed, fc_mine, cid):
    slots, width, cols = w_slots.shape
    count = normed.shape[1]
    chips = n_ctx // 2
    shard = width // n_fsdp
    vm = pl.BlockSpec(memory_space=pltpu.VMEM)
    anym = pl.BlockSpec(memory_space=pl.ANY)
    dma = pltpu.SemaphoreType.DMA
    block = pltpu.VMEM((chips, count, width), BF16)
    piece = pltpu.VMEM((n_fsdp, slots, shard, cols), BF16)
    return pl.pallas_call(
        functools.partial(back_kernel, n_ctx, n_fsdp),
        in_specs=[vm] * 4 + [anym],
        out_specs=[vm] * 2 + [anym],
        out_shape=[
            jax.ShapeDtypeStruct((count, width), BF16),
            jax.ShapeDtypeStruct((slots, shard, cols), BF16),
            jax.ShapeDtypeStruct(fc_mine.shape, BF16),
        ],
        scratch_shapes=[
            block,
            pltpu.VMEM((2, count, width), BF16),
            block,
            pltpu.VMEM((2, chips + 1, count // 2, width), BF16),
        ]
        + [piece] * 2
        + [dma((2,)), dma((chips,))]
        + [dma((2, chips))] * 3
        + [dma((n_fsdp,))] * 4
        + [dma(())],
        compiler_params=pltpu.CompilerParams(
            collective_id=cid, has_side_effects=True, vmem_limit_bytes=60 * 1024 * 1024
        ),
        cost_estimate=SHORT,
        name="qkv_back",
    )(own, rest, w_slots, normed, fc_mine)


def sums_kernel(n_ctx, n_fsdp, lead, *refs):
    rows_ref, cols_ref, extra_ref, att_ref, mid_ref, lines_in = refs[:6]
    share_hbm, resid_ref, small_ref = refs[6:9]
    outs, cols_all, lines_ref, layer_ref = refs[9:11], refs[11], refs[12], refs[13]
    parts, cames = refs[14:16], refs[16:18]
    proj_part, proj_in, proj_got, lines_got, share_in = refs[18:23]
    lines_send, lines_recv, local, proj_send, proj_recv, pair_sem = refs[23:29]
    share_send, share_recv = refs[29:31]
    cols_sems = refs[31:36]
    sems = [(refs[36 + 8 * i : 39 + 8 * i], refs[39 + 8 * i : 44 + 8 * i]) for i in range(2)]
    c = lax.axis_index("ctx")
    f = lax.axis_index("fsdp")
    chips = n_ctx // 2
    chip, core = c // 2, c % 2
    width = att_ref.shape[1]
    shard = width // n_fsdp
    half = shard // 2
    high = proj_in.shape[1]
    twin_id = (2 * chip + 1 - core, f)
    enter(
        [(lax.rem(c + i, n_ctx), f) for i in range(1, n_ctx)]
        + [(c, flip(f, k, n_fsdp)) for k in range(1, n_fsdp)]
    )

    def line_ops(i):
        sum_sems, gather_sems = sems[i]
        gather = line_gather(chip, chips, f, core, lambda at, h: outs[i].at[h, at], gather_sems)
        return line_sum(chip, chips, f, core, parts[i], cames[i], sum_sems) + gather

    def proj_pair():
        return send(proj_part.at[1 - core], proj_in, pair_sem.at[0], pair_sem.at[1], twin_id)

    def proj_copy(k):
        other = flip(f, k, n_fsdp)
        return send(
            proj_part.at[core, other],
            proj_got.at[f],
            proj_send.at[k],
            proj_recv.at[k],
            (c, other),
        )

    def share_copy(k):
        other = flip(f, k, n_fsdp)
        return send(
            share_hbm.at[other], share_in.at[f], share_send.at[k], share_recv.at[k], (c, other)
        )

    def proj_products(j):
        for h in range(2):
            lo = j * shard + h * half
            proj_part[h, j, :half] = dot_first(att_ref[:, lo : lo + half], mid_ref[...]).astype(BF16)
            if half < high:
                proj_part[h, j, half:] = jnp.zeros((high - half, width), BF16)

    def proj_add(j, carry):
        proj_part[core, j] = (
            proj_part[core, j].astype(F32) + proj_in[j].astype(F32)
        ).astype(BF16)
        return carry

    def proj_total():
        total = proj_part[core, f].astype(F32)
        for k in range(1, n_fsdp):
            proj_copy(k).wait_recv()
            total += proj_got[flip(f, k, n_fsdp)].astype(F32)
        total = jnp.concatenate([total.astype(BF16), extra_ref[...]], axis=0)
        first = rows_ref.shape[1] - parts[0].shape[1]
        step, rows = parts[1].shape[1] - first, total.shape[0]
        for p in range(chips):
            lo, hi = min(p * step, rows), min((p + 1) * step, rows)
            end = first + hi - lo
            if hi > lo:
                parts[1][p, first:end] = total[lo:hi]
            if hi - lo < step:
                parts[1][p, end:] = jnp.zeros((step - hi + lo, width), BF16)

    peers = [(flip(c, 1 << i, n_ctx), f) for i in range(n_ctx.bit_length() - 1)]
    ctx_phases = len(peers)
    peers += [(c, flip(f, 1 << i, n_fsdp)) for i in range(n_fsdp.bit_length() - 1)]

    def line_copy(i):
        rows = lines_in.shape[0] if i < ctx_phases else lead
        return send(
            lines_ref.at[:rows],
            lines_got.at[i, :rows],
            lines_send.at[i],
            lines_recv.at[i],
            peers[i],
        )

    def line_phase(i):
        if 0 < i <= len(peers):
            rows = lines_in.shape[0] if i <= ctx_phases else lead
            line_copy(i - 1).wait()
            lines_ref[:rows] += lines_got[i - 1, :rows]
        if i < len(peers):
            line_copy(i).start()

    def settle(finish, i):
        finish()
        keep = pltpu.make_async_copy(parts[i].at[chip], outs[i].at[core, chip], local.at[0])
        keep.start()
        keep.wait()

    sum_a, finish_a, sums_a, gather_a, gathers_a = line_ops(0)
    sum_b, finish_b, sums_b, gather_b, gathers_b = line_ops(1)
    cols_step, cols_done = line_gather(
        chip, chips, f, core, lambda at, h: cols_all.at[2 * at + h], cols_sems
    )
    load = pltpu.make_async_copy(cols_ref, cols_all.at[c], local.at[1])
    load.start()
    cut = parts[0].shape[1]
    parts[0][...] = rows_ref[:, :cut]
    load.wait()
    cols_step(0)
    sum_a(0)
    parts[1][:, : rows_ref.shape[1] - cut] = rows_ref[:, cut:]
    lines_ref[...] = lines_in[...]
    for j in range(n_fsdp):
        proj_products(j)
    proj_pair().start()
    for t in range(1, chips - 1):
        cols_step(t)
        sum_a(t)
        if t == 1:
            proj_pair().wait()
            lax.fori_loop(0, n_fsdp, proj_add, 0)
            for k in range(1, n_fsdp):
                proj_copy(k).start()
            for k in range(1, n_fsdp):
                share_copy(k).start()
            own_share = pltpu.make_async_copy(share_hbm.at[f], share_in.at[f], local.at[2])
            own_share.start()
    cols_step(chips - 1)
    settle(finish_a, 0)
    gather_a(0)
    proj_total()
    sum_b(0)
    phase = 0
    for s in range(1, chips):
        gather_a(s)
        if s < chips - 1:
            sum_b(s)
        line_phase(phase)
        phase += 1
    settle(finish_b, 1)
    for s in range(chips):
        gather_b(s)
        line_phase(phase)
        phase += 1
    while phase <= len(peers):
        line_phase(phase)
        phase += 1
    own_share.wait()
    total = share_in[f].astype(F32)
    for k in range(1, n_fsdp):
        share_copy(k).wait()
        total += share_in[flip(f, k, n_fsdp)].astype(F32)
    layer_ref[...] = (resid_ref[...] + (total + small_ref[7:8])).astype(BF16)
    for done in (sums_a, sums_b, cols_done, gathers_a, gathers_b):
        done()
    for k in range(1, n_fsdp):
        proj_copy(k).wait_send()


def sums_call(
    n_ctx, n_fsdp, rows, cols, extra, attended, mid_low, lines, shares, mid, small, lead, cid
):
    chips = n_ctx // 2
    count, width = attended.shape
    high = half_high(width // n_fsdp)
    per_chip = rows.shape[1]
    third = -(-(high + extra.shape[0]) // (16 * chips)) * 16
    cut = -(-(per_chip + third) // 32) * 16
    shapes = [(chips, size, width) for size in (cut, per_chip + third - cut)]
    phases = (n_ctx * n_fsdp).bit_length() - 1
    vm = pl.BlockSpec(memory_space=pltpu.VMEM)
    anym = pl.BlockSpec(memory_space=pl.ANY)
    dma = pltpu.SemaphoreType.DMA
    return pl.pallas_call(
        functools.partial(sums_kernel, n_ctx, n_fsdp, lead),
        in_specs=[vm, anym, vm, vm, vm, vm, anym, vm, vm],
        out_specs=[vm, vm, anym, vm, vm],
        out_shape=[jax.ShapeDtypeStruct((2,) + shape, BF16) for shape in shapes]
        + [jax.ShapeDtypeStruct((n_ctx,) + cols.shape, BF16)]
        + [jax.ShapeDtypeStruct(lines.shape, F32), jax.ShapeDtypeStruct(mid.shape, BF16)],
        scratch_shapes=[pltpu.VMEM(shape, BF16) for shape in shapes]
        + [pltpu.VMEM((chips + 1,) + shape[1:], BF16) for shape in shapes]
        + [
            pltpu.VMEM((2, n_fsdp, high, width), BF16),
            pltpu.VMEM((n_fsdp, high, width), BF16),
            pltpu.VMEM((n_fsdp, high, width), BF16),
            pltpu.VMEM((phases,) + lines.shape, F32),
            pltpu.VMEM(shares.shape, BF16),
            dma((phases,)),
            dma((phases,)),
            dma((3,)),
            dma((n_fsdp,)),
            dma((n_fsdp,)),
            dma((2,)),
            dma((n_fsdp,)),
            dma((n_fsdp,)),
        ]
        + [dma((chips,))] * (5 + 2 * 8),
        compiler_params=pltpu.CompilerParams(
            collective_id=cid, has_side_effects=True, vmem_limit_bytes=56 * 1024 * 1024
        ),
        cost_estimate=SHORT,
        name="weight_sums",
    )(rows, cols, extra, attended, mid_low, lines, shares, mid, small)


def assemble_kernel(
    n_fsdp,
    own_ref,
    rest_ref,
    first_ref,
    second_ref,
    third_ref,
    out_ref,
    attn_hbm,
    fc_hbm,
    proj_hbm,
    wout_hbm,
    *scratch,
):
    attn_ref, fc_ref, proj_ref, wout_ref, low_ref, sem = scratch
    load = pltpu.make_async_copy(out_ref, low_ref, sem.at[4])
    load.start()
    hd = HEAD_DIM
    shard, hidden = fc_ref.shape[0], fc_ref.shape[1] // n_fsdp
    half = shard // 2
    width = proj_ref.shape[1]
    count = own_ref.shape[0]
    copies = [
        pltpu.make_async_copy(src, dst, sem.at[i])
        for i, (src, dst) in enumerate(
            ((wout_ref, wout_hbm), (fc_ref, fc_hbm), (proj_ref, proj_hbm), (attn_ref, attn_hbm))
        )
    ]
    for h in range(2):
        for j in range(n_fsdp):
            cut = min(first_ref.shape[2], half)
            at = slice(j * hidden, (j + 1) * hidden)
            fc_ref[h * half : h * half + cut, at] = first_ref[h, j, :cut].astype(F32)
            if cut < half:
                rows = second_ref[h, j, : half - cut].astype(F32)
                fc_ref[h * half + cut : (h + 1) * half, at] = rows
    copies[1].start()
    for h in range(2):
        proj_ref[h * half : (h + 1) * half] = third_ref[h, :half].astype(F32)
    copies[2].start()
    for h in range(width // hd):
        src = own_ref.at[h] if h < count else rest_ref.at[h - count]
        for part in range(3):
            at = part * width + h * hd
            attn_ref[:, at : at + hd] = src[:, part * hd : (part + 1) * hd].astype(F32)
    copies[3].start()
    load.wait()
    wout_ref[...] = low_ref[...].astype(F32)
    copies[0].start()
    for copy in copies:
        copy.wait()


def assemble(n_fsdp, own, rest, first, second, third, out_low, hidden):
    shard = own.shape[1]
    width = first.shape[3]
    vm = pl.BlockSpec(memory_space=pltpu.VMEM)
    anym = pl.BlockSpec(memory_space=pl.ANY)
    shapes = [(shard, 3 * width), (shard, n_fsdp * hidden), (shard, width), out_low.shape]
    return pl.pallas_call(
        functools.partial(assemble_kernel, n_fsdp),
        in_specs=[vm] * 5 + [anym],
        out_specs=[anym] * 4,
        out_shape=[jax.ShapeDtypeStruct(shape, F32) for shape in shapes],
        scratch_shapes=[pltpu.VMEM(shape, F32) for shape in shapes]
        + [pltpu.VMEM(out_low.shape, BF16), pltpu.SemaphoreType.DMA((5,))],
        compiler_params=pltpu.CompilerParams(vmem_limit_bytes=60 * 1024 * 1024),
        cost_estimate=SHORT,
        name="assemble",
    )(own, rest, first, second, third, out_low)


def swap(value, axis, size, k):
    return lax.ppermute(value, axis, [(i, i ^ k) for i in range(size)])


def shards(
    n_ctx,
    n_fsdp,
    tokens,
    block_order,
    w_attn,
    w_proj,
    w_fc,
    w_out,
    norm_gains,
    biases,
    fc_bias,
    cotangent,
):
    hd = HEAD_DIM
    count, width = tokens.shape[1:]
    shard = width // n_fsdp
    heads = width // hd
    base = heads // n_ctx
    rest = heads - base * n_ctx
    slots = base + rest
    own_blocks = count // BLOCK
    c = lax.axis_index("ctx")
    f = lax.axis_index("fsdp")

    order = block_order[0]
    inv = jnp.argsort(order).astype(jnp.int32)
    order_own = jnp.concatenate([order, (c * own_blocks)[None]])

    def head_cols(h):
        return jnp.concatenate(
            [
                lax.dynamic_slice(w_attn, (0, part * width + h * hd), (shard, hd))
                for part in range(3)
            ],
            axis=1,
        )

    slot_heads = [c * base + s for s in range(base)] + [n_ctx * base + r for r in range(rest)]
    w_slots = jnp.stack([head_cols(h) for h in slot_heads])
    small = jnp.concatenate([norm_gains, biases], axis=0).astype(F32)
    hidden_cols = w_fc.shape[1] // n_fsdp
    normed_one, qkv, full_proj, fc_cols, _, w_slots, small = start_call(
        n_ctx, n_fsdp, base, tokens[0], w_slots, small, w_proj, w_fc, 3
    )
    full_proj = full_proj.reshape(width, width)
    qkv = qkv.reshape(slots, n_ctx * own_blocks, BLOCK, 3 * hd)
    gains, shifts = small[:2], small[2:]
    cot = cotangent[0]

    cot_late, _ = lax.optimization_barrier((cot, small))
    cot_all = lax.all_gather(cot_late, "fsdp", axis=0)

    out_own, lse_own = attn_fwd(inv, qkv, base)
    if rest:
        out_rest, lse_rest = rest_fwd(order_own, qkv, base)
    else:
        out_rest = out_own
    attended, mid, normed_two = mix_call(
        n_ctx, out_own, out_rest, tokens[0], full_proj, small, 6
    )
    fc_cols = fc_cols.reshape(width, hidden_cols)
    rows = tokens[0].astype(F32)

    normed_two_grad, fc_bias_part, out_part, w_out_part, w_fc_part = ffn(
        n_fsdp,
        normed_two,
        cot_all,
        fc_cols,
        w_out,
        fc_bias.astype(F32)[None],
    )
    w_out_sum = lax.psum_scatter(w_out_part, "ctx", scatter_dimension=0, tiled=True)

    half, high = shard // 2, half_high(shard)
    core = c % 2
    main = n_ctx * base * hd
    mid_grad, mid_low, turn_sums, d_rest, fc_mine, d_out = turn_call(
        n_ctx, base, normed_two_grad, cot, mid, full_proj, small, w_fc_part, 7
    )

    d_own = attn_bwd(inv, qkv, d_out, out_own, lse_own, base)
    d_own = d_own.reshape(base, n_ctx, count, 3 * hd)
    if rest:
        d_rest = rest_bwd(order_own, qkv, d_rest, out_rest, lse_rest, base)
        d_rest = d_rest.reshape(rest, n_ctx, count, 3 * hd)
        sums = jnp.concatenate(
            [jnp.sum(d.astype(F32), axis=(1, 2)) for d in (d_own, d_rest)], axis=0
        )
    else:
        d_rest = d_own
        sums = jnp.sum(d_own.astype(F32), axis=(1, 2))
    if back_fits(n_ctx, n_fsdp, count, width, slots):
        normed_one_grad, cols_sum, fc_rows = back_call(
            n_ctx, n_fsdp, d_own, d_rest, w_slots, normed_one, fc_mine, 4
        )
        normed_one_grad = normed_one_grad.astype(F32)
    else:
        dqkv = jnp.concatenate([d_own, d_rest])[:slots].reshape(slots, n_ctx * count, 3 * hd)
        one_part = jnp.einsum("hte,hde->td", dqkv, w_slots, preferred_element_type=F32)
        normed_one_grad = lax.psum_scatter(
            one_part.astype(BF16), "ctx", scatter_dimension=0, tiled=True
        ).astype(F32)
        slot_part = jnp.einsum(
            "td,hte->hde",
            normed_one.reshape(n_ctx * count, width),
            dqkv,
            preferred_element_type=F32,
        ).astype(BF16)
        cols_sum = lax.psum_scatter(slot_part, "fsdp", scatter_dimension=1, tiled=True)
        fc_rows = lax.all_to_all(fc_mine, "fsdp", split_axis=0, concat_axis=0, tiled=True)

    w_out_sum, fc_rows = lax.optimization_barrier((w_out_sum, fc_rows))
    w_out_low = lax.all_gather(w_out_sum, "ctx", axis=0, tiled=True)
    xhat_one, rstd_one = norm_parts(rows)
    tokens_grad = (mid_grad + norm_back(xhat_one, rstd_one, gains[0], normed_one_grad)).astype(
        BF16
    )

    def placed(part):
        cols = sums[:, part * hd : (part + 1) * hd]
        line = lax.dynamic_update_slice_in_dim(
            jnp.zeros((width,), F32), cols[:base].reshape(-1), c * base * hd, 0
        )
        return line + jnp.pad(cols[base:].reshape(-1), (main, 0))

    lines = jnp.stack(
        [
            jnp.sum(normed_one_grad * xhat_one, axis=0),
            turn_sums[0],
            jnp.sum(normed_one_grad, axis=0),
            turn_sums[1],
            placed(0),
            placed(2),
            turn_sums[2],
            turn_sums[3],
        ]
    )
    lead = lines.shape[0]
    tail = jnp.pad(fc_bias_part, ((0, 7), (0, width - hidden_cols)))
    lines = jnp.concatenate([lines, tail])

    chips = n_ctx // 2
    fc_rows = fc_rows.reshape(-1, width)
    per_chip = -(-fc_rows.shape[0] // (16 * chips)) * 16
    fc_rows = jnp.pad(fc_rows, ((0, per_chip * chips - fc_rows.shape[0]), (0, 0)))
    fc_rows = fc_rows.reshape(chips, per_chip, width)
    extra = jnp.zeros((16, width), BF16)
    if rest:
        away = lax.dynamic_slice_in_dim(cols_sum[base:], (1 - core) * half, half, 1)
        here = lax.dynamic_slice_in_dim(cols_sum[base:], core * half, half, 1)
        extra = here.astype(F32) + swap(away, "ctx", n_ctx, 1).astype(F32)
        extra = extra.astype(BF16).reshape(-1, width)
        extra_rows = extra.shape[0]
        extra = jnp.pad(extra, ((0, -extra_rows % 16), (0, 0)))
    first, second, own_cols, lines, layer_rows = sums_call(
        n_ctx,
        n_fsdp,
        fc_rows,
        cols_sum[:base],
        extra,
        attended,
        mid_low,
        lines,
        out_part,
        mid,
        small,
        lead,
        5,
    )
    w_out_low, lines = lax.optimization_barrier((w_out_low, lines))
    split = per_chip - first.shape[2]
    third = second[:, :, split:].reshape(2, -1, width)
    second = second[:, :, :split]
    own_cols = own_cols.reshape(n_ctx * base, shard, 3 * hd)
    if rest:
        rest_cols = third[:, high : high + extra_rows].reshape(2, rest, half, 3 * hd)
        rest_cols = rest_cols.transpose(1, 0, 2, 3).reshape(rest, shard, 3 * hd)
    else:
        rest_cols = own_cols
    if hidden_cols == width and chips == n_fsdp:
        w_attn_grad, w_fc_grad, w_proj_grad, w_out_grad = assemble(
            n_fsdp, own_cols, rest_cols, first, second, third, w_out_low, hidden_cols
        )
    else:
        w_fc_low = jnp.concatenate([first, second], axis=2).reshape(2, -1, width)
        w_fc_low = w_fc_low[:, : n_fsdp * high * hidden_cols // width]
        w_fc_low = w_fc_low.reshape(2, n_fsdp, high, hidden_cols)[:, :, :half]
        w_fc_grad = w_fc_low.transpose(0, 2, 1, 3).reshape(shard, n_fsdp * hidden_cols)
        w_fc_grad = w_fc_grad.astype(F32)
        w_proj_grad = third[:, :half].reshape(shard, width).astype(F32)
        cols = jnp.concatenate([own_cols, rest_cols])[: width // hd]
        cols = cols.reshape(width // hd, shard, 3, hd).transpose(1, 2, 0, 3)
        w_attn_grad = cols.reshape(shard, 3 * width).astype(F32)
        w_out_grad = w_out_low.astype(F32)
    fc_bias_grad = lines[lead, :hidden_cols]
    lines = lax.dynamic_slice_in_dim(lines[:lead], f * shard, shard, 1)
    return (
        layer_rows[None],
        tokens_grad[None],
        w_attn_grad,
        w_proj_grad,
        w_fc_grad,
        w_out_grad,
        lines[:2],
        lines[2:],
        fc_bias_grad,
    )


def solution(mesh):
    rows = P("fsdp", "ctx", None)
    weight = P("fsdp", None)
    vectors = P(None, "fsdp")
    return jax.shard_map(
        functools.partial(shards, mesh.shape["ctx"], mesh.shape["fsdp"]),
        mesh=mesh,
        in_specs=(
            rows, weight, weight, weight, weight, weight, vectors, vectors, P("fsdp"), rows,
        ),
        out_specs=(
            rows, rows, weight, weight, weight, weight, vectors, vectors, P("fsdp"),
        ),
        check_vma=False,
    )
```

```python
import functools

import jax
import jax.numpy as jnp
from jax import lax
from jax.experimental import pallas as pl
from jax.experimental.pallas import tpu as pltpu
from jax.sharding import PartitionSpec as P

HEAD_DIM = 64
BLOCK = 128
QROWS = 256
EPS = 1e-05
SCALE = HEAD_DIM ** (-0.5)
F32 = jnp.float32
BF16 = jnp.bfloat16
VMEM_LIMIT = 56 * 1024 * 1024
LAST = (((1,), (1,)), ((), ()))
FIRST = (((0,), (0,)), ((), ()))
MESH = pl.DeviceIdType.MESH
TILE = 256


def dot_last(a, b):
    return lax.dot_general(a, b, LAST, preferred_element_type=F32)


def dot(a, b):
    return jnp.dot(a, b, preferred_element_type=F32)


def dot_first(a, b):
    return lax.dot_general(a, b, FIRST, preferred_element_type=F32)


SHORT = pl.CostEstimate(flops=1, bytes_accessed=1, transcendentals=0)


def norm_parts(rows):
    mean = jnp.mean(rows, axis=-1, keepdims=True)
    cen = rows - mean
    rstd = lax.rsqrt(jnp.mean(cen * cen, axis=-1, keepdims=True) + EPS)
    return cen * rstd, rstd


def norm_back(xhat, rstd, gain, grad):
    dxhat = grad * gain
    return rstd * (
        dxhat
        - jnp.mean(dxhat, axis=-1, keepdims=True)
        - xhat * jnp.mean(dxhat * xhat, axis=-1, keepdims=True)
    )


def flip(place, k, size):
    out = 0
    bit = 1
    while bit < size:
        out = out + (place // bit + k // bit) % 2 * bit
        bit *= 2
    return out

def half_high(shard):
    return -(-(shard // 2) // 16) * 16


def enter(peers):
    barrier = pltpu.get_barrier_semaphore()
    for peer in peers:
        pl.semaphore_signal(barrier, inc=1, device_id=peer, device_id_type=MESH)
    pl.semaphore_wait(barrier, len(peers))

def send(src, dst, send_sem, recv_sem, peer):
    return pltpu.make_async_remote_copy(
        src_ref=src, dst_ref=dst, send_sem=send_sem, recv_sem=recv_sem,
        device_id=peer, device_id_type=MESH)


def ffn_kernel(n, nt_hbm, cot_hbm, wfc_hbm, wout_hbm, bias_ref,
               gsum_ref, fcb_ref, out_hbm, wout_grad_hbm, wfc_grad_hbm,
               cot_ref, wfc_ref, wout_ref, all_ref, act_ref, hg_ref, ag_ref, part_ref, got_ref, stage_d, stage_h,
               s1, r1, s2, r2, local):
    c = lax.axis_index("ctx")
    f = lax.axis_index("fsdp")
    rows, width = nt_hbm.shape
    enter([(c, flip(f, k, n)) for k in range(1, n)])

    def rows_out(k):
        return send(nt_hbm, all_ref.at[f], s1.at[k], r1.at[k], (c, flip(f, k, n)))

    def grad_back(k):
        other = flip(f, k, n)
        return send(part_ref.at[other], got_ref.at[k], s2.at[k], r2.at[k], (c, other))

    near = [k for k in range(1, n) if k & (k - 1) == 0]
    far = [k for k in range(1, n) if k not in near]
    for k in near:
        rows_out(k).start()
    loads = [
        pltpu.make_async_copy(nt_hbm, all_ref.at[f], local.at[0]),
        pltpu.make_async_copy(wout_hbm, wout_ref, local.at[1]),
        pltpu.make_async_copy(cot_hbm, cot_ref, local.at[2]),
        pltpu.make_async_copy(wfc_hbm, wfc_ref, local.at[3]),
    ]
    for load in loads:
        load.start()
    fcb_ref[...] = jnp.zeros_like(fcb_ref)
    loads[1].wait()
    loads[2].wait()

    def active_grad(k, carry):
        ag_ref[k] = dot_last(cot_ref[k], wout_ref[...])
        return carry

    lax.fori_loop(0, n, active_grad, 0)
    for k in far:
        rows_out(k).start()
    loads[0].wait()
    loads[3].wait()

    def chunk(k, carry):
        src = flip(f, k, n)

        @pl.when(k > 0)
        def _():
            rows_out(k).wait_recv()

        hidden = dot(all_ref[src], wfc_ref[...]) + bias_ref[...]
        square = hidden * hidden
        tanh = jnp.tanh(0.7978845608028654 * (hidden + 0.044715 * square * hidden))
        act_ref[src] = (0.5 * hidden * (1.0 + tanh)).astype(BF16)
        slope = 0.5 * (1.0 + tanh) + 0.5 * hidden * (1.0 - tanh * tanh) * 0.7978845608028654 * (
            1.0 + 3.0 * 0.044715 * square
        )
        grad = (ag_ref[src] * slope).astype(BF16)
        hg_ref[src] = grad
        fcb_ref[...] += jnp.sum(grad.astype(F32), axis=0, keepdims=True)
        part_ref[src] = dot_last(grad, wfc_ref[...]).astype(BF16)

        @pl.when(k > 0)
        def _():
            grad_back(k).start()

        return carry

    lax.fori_loop(0, n, chunk, 0)

    def grads(left_ref, right_ref, tiles, stage_ref, base):
        right = right_ref[...].reshape(n * rows, right_ref.shape[2])
        copies = []
        for i, (lo, size, sent, dst) in enumerate(tiles):
            slot = i % 2
            if i >= 2:
                copies[i - 2].wait()
            left = left_ref[:, :, lo : lo + size].reshape(n * rows, size)
            stage_ref[slot, :size] = dot_first(left, right).astype(BF16)
            copies.append(
                pltpu.make_async_copy(stage_ref.at[slot, :sent], dst, local.at[base + slot])
            )
            copies[-1].start()
        for copy in copies[-2:]:
            copy.wait()

    half, high = width // n // 2, wfc_grad_hbm.shape[2]
    if half < high:
        stage_h[:, half:high] = jnp.zeros((2, high - half, stage_h.shape[2]), BF16)
    wide = act_ref.shape[2]
    sizes = [(lo, min(TILE, wide - lo)) for lo in range(0, wide, TILE)]
    grads(
        act_ref,
        cot_ref,
        [(lo, size, size, wout_grad_hbm.at[lo : lo + size]) for lo, size in sizes],
        stage_d,
        4,
    )
    grads(
        all_ref,
        hg_ref,
        [
            ((2 * j + h) * half, half, high, wfc_grad_hbm.at[h, j])
            for j in range(n)
            for h in range(2)
        ],
        stage_h,
        6,
    )

    def out_copy(k):
        return pltpu.make_async_copy(
            stage_d.at[k % 2, :rows], out_hbm.at[k], local.at[4 + k % 2]
        )

    for k in range(n):
        if k >= 2:
            out_copy(k - 2).wait()
        stage_d[k % 2, :rows] = dot(act_ref[k], wout_ref[...]).astype(BF16)
        out_copy(k).start()

    gsum_ref[...] = part_ref[f].astype(F32)
    for k in near + far:
        grad_back(k).wait_recv()
        gsum_ref[...] += got_ref[k].astype(F32)
    for k in range(1, n):
        rows_out(k).wait_send()
        grad_back(k).wait_send()
    for k in range(max(0, n - 2), n):
        out_copy(k).wait()


def ffn(n, nt, cot, wfc, wout, bias, cid=1):
    m, d = nt.shape
    h = wfc.shape[1]
    vm = pl.BlockSpec(memory_space=pltpu.VMEM)
    anym = pl.BlockSpec(memory_space=pl.ANY)
    return pl.pallas_call(
        functools.partial(ffn_kernel, n),
        in_specs=[anym] * 4 + [vm],
        out_specs=[vm, vm] + [anym] * 3,
        out_shape=[
            jax.ShapeDtypeStruct((m, d), F32),
            jax.ShapeDtypeStruct((1, h), F32),
            jax.ShapeDtypeStruct((n, m, d), BF16),
            jax.ShapeDtypeStruct((h, d), BF16),
            jax.ShapeDtypeStruct((2, n, half_high(d // n), h), BF16),
        ],
        scratch_shapes=[
            pltpu.VMEM((n, m, d), BF16),
            pltpu.VMEM((d, h), BF16),
            pltpu.VMEM((h, d), BF16),
            pltpu.VMEM((n, m, d), BF16),
            pltpu.VMEM((n, m, h), BF16),
            pltpu.VMEM((n, m, h), BF16),
            pltpu.VMEM((n, m, h), F32),
            pltpu.VMEM((n, m, d), BF16),
            pltpu.VMEM((n, m, d), BF16),
            pltpu.VMEM((2, max(TILE, m), d), BF16),
            pltpu.VMEM((2, half_high(d // n), h), BF16),
        ]
        + [pltpu.SemaphoreType.DMA((n,))] * 4
        + [pltpu.SemaphoreType.DMA((8,))],
        compiler_params=pltpu.CompilerParams(
            collective_id=cid, has_side_effects=True, vmem_limit_bytes=60 * 1024 * 1024
        ),
        cost_estimate=SHORT,
        name="feed_forward",
    )(nt, cot, wfc, wout, bias)


def weight_shares(c, f, core, n_fsdp, shard, source, dst, ss, rs):
    cut = shard // 32 * 16 if shard % 16 == 0 else 0
    shares = ((0, cut), (cut, shard)) if cut else ((0, shard), (0, shard))
    twin_id = (c + 1 - 2 * core, f)

    def copy(share, k, onward):
        lo, hi = share
        other = flip(f, k, n_fsdp)
        if onward:
            part = dst.at[other, lo:hi]
            return send(part, part, ss.at[1, k], rs.at[1, k], twin_id)
        return send(source(k).at[lo:hi], dst.at[f, lo:hi], ss.at[0, k], rs.at[0, k], (c, other))

    def by_core(act):
        for h in range(2):

            @pl.when(core == h)
            def _(h=h):
                for k in range(1, n_fsdp):
                    act(shares[h], shares[1 - h], k)

    def start(mine, theirs, k):
        copy(mine, k, False).start()

    def onward(mine, theirs, k):
        copy(mine, k, False).wait_recv()
        if cut:
            copy(mine, k, True).start()

    def done(mine, theirs, k):
        if cut:
            copy(theirs, k, True).wait_recv()
            copy(mine, k, True).wait_send()
        copy(mine, k, False).wait_send()

    return tuple(functools.partial(by_core, act) for act in (start, onward, done))


def start_kernel(
    n_ctx,
    n_fsdp,
    base,
    tok_hbm,
    w_hbm,
    small_ref,
    proj_hbm,
    fc_hbm,
    n_hbm,
    qkv_hbm,
    proj_all,
    fc_all,
    fc_parts,
    w_ref,
    lines_ref,
    n_ref,
    qkv_ref,
    fc_ref,
    fc_cut,
    x_ref,
    wg_ref,
    sg_ref,
    tok_recv,
    right_sem,
    left_sem,
    twin_sem,
    w_send,
    w_recv,
    s_send,
    s_recv,
    proj_send,
    proj_recv,
    fc_send,
    fc_recv,
    local,
):
    c = lax.axis_index("ctx")
    f = lax.axis_index("fsdp")
    chips = n_ctx // 2
    chip, core = c // 2, c % 2
    slots, width, cols = w_ref.shape
    shard = width // n_fsdp
    hd = HEAD_DIM
    enter(
        [(lax.rem(c + i, n_ctx), f) for i in range(1, n_ctx)]
        + [(c, flip(f, k, n_fsdp)) for k in range(1, n_fsdp)]
    )

    def block(at, same):
        return 2 * at + (core if same else 1 - core)

    cut = x_ref.shape[1] // 2

    def part(ref, h):
        return ref.at[pl.ds(h * cut, cut)]

    def hop(step, to_right, from_own, h):
        origin = block(chip - step if to_right else chip + step, True)
        src = tok_hbm if from_own else x_ref.at[origin]
        sem = (right_sem if to_right else left_sem).at[step, h]
        peer = (c + 2 if to_right else c - 2, f)
        dst = part(x_ref.at[origin], h)
        return send(part(src, h), dst, sem, tok_recv.at[origin, h], peer)

    def twin(at, from_own, h):
        origin = block(at, True)
        src = tok_hbm if from_own else x_ref.at[origin]
        dst = part(x_ref.at[origin], h)
        return send(
            part(src, h),
            dst,
            twin_sem.at[at, h],
            tok_recv.at[origin, h],
            (block(chip, False), f),
        )

    def w_copy(k):
        return send(w_hbm, wg_ref.at[f], w_send.at[k], w_recv.at[k], (c, flip(f, k, n_fsdp)))

    def s_copy(k):
        return send(small_ref, sg_ref.at[f], s_send.at[k], s_recv.at[k], (c, flip(f, k, n_fsdp)))

    weights_start, weights_onward, weights_done = weight_shares(
        c, f, core, n_fsdp, shard, lambda k: proj_hbm, proj_all, proj_send, proj_recv
    )
    fc_start, fc_onward, fc_done = weight_shares(
        c,
        f,
        core,
        n_fsdp,
        shard,
        lambda k: fc_parts.at[flip(f, k, n_fsdp)],
        fc_all,
        fc_send,
        fc_recv,
    )

    for k in range(1, n_fsdp):
        s_copy(k).start()

    for h in range(2):

        @pl.when(chip < chips - 1)
        def _(h=h):
            hop(0, True, True, h).start()

        @pl.when(chip > 0)
        def _(h=h):
            hop(0, False, True, h).start()

    for k in range(1, n_fsdp):
        w_copy(k).start()
    for h in range(2):
        twin(chip, True, h).start()
    own_x = pltpu.make_async_copy(tok_hbm, x_ref.at[c], local.at[0])
    own_w = pltpu.make_async_copy(w_hbm, wg_ref.at[f], local.at[1])
    own_proj = pltpu.make_async_copy(proj_hbm, proj_all.at[f], local.at[2])
    load_fc = pltpu.make_async_copy(fc_hbm, fc_ref, local.at[3])
    for copy in (own_x, own_w, own_proj, load_fc):
        copy.start()
    sg_ref[f] = small_ref[...]
    for k in range(1, n_fsdp):
        s_copy(k).wait_recv()
    for j in range(n_fsdp):
        lines_ref[:, j * shard : (j + 1) * shard] = sg_ref[j]
    main = n_ctx * base * hd
    row_id = lax.broadcasted_iota(jnp.int32, (width, slots * hd), 0)
    col_id = lax.broadcasted_iota(jnp.int32, (width, slots * hd), 1)
    wanted = jnp.where(col_id < base * hd, c * base * hd + col_id, main + col_id - base * hd)
    picked = dot(lines_ref[...].astype(BF16), (row_id == wanted).astype(BF16))
    zero = jnp.zeros((1, hd), F32)
    bias = [
        jnp.concatenate(
            [picked[4:5, s * hd : (s + 1) * hd], zero, picked[5:6, s * hd : (s + 1) * hd]], axis=1
        )
        for s in range(slots)
    ]
    own_w.wait()
    own_x.wait()
    for k in range(1, n_fsdp):
        w_copy(k).wait_recv()
    weights_start()
    for j in range(n_fsdp):
        w_ref[:, j * shard : (j + 1) * shard, :] = wg_ref[j]

    load_fc.wait()
    hidden = fc_cut.shape[2]
    cuts = []
    for j in range(n_fsdp):
        if j >= 2:
            cuts[j - 2].wait()
        fc_cut[j % 2] = fc_ref[:, j * hidden : (j + 1) * hidden]
        cuts.append(pltpu.make_async_copy(fc_cut.at[j % 2], fc_parts.at[j], local.at[4 + j % 2]))
        cuts[-1].start()

    for copy in cuts[-2:]:
        copy.wait()
    fc_start()
    own_fc = pltpu.make_async_copy(fc_parts.at[f], fc_all.at[f], local.at[3])
    own_fc.start()

    def results(origin):
        return (
            pltpu.make_async_copy(n_ref, n_hbm.at[origin], local.at[0]),
            pltpu.make_async_copy(qkv_ref, qkv_hbm.at[:, origin], local.at[1]),
        )

    def project(at, same, first=False):
        origin = block(at, same)
        rows = x_ref[origin].astype(F32)
        mean = jnp.mean(rows, axis=1, keepdims=True)
        cen = rows - mean
        var = jnp.mean(cen * cen, axis=1, keepdims=True)
        normed = cen * lax.rsqrt(var + EPS) * lines_ref[0:1] + lines_ref[2:3]
        normed = normed.astype(BF16)

        @pl.when(jnp.logical_not(first))
        def _():
            for copy in results(origin):
                copy.wait()

        n_ref[...] = normed
        for s in range(slots):
            qkv_ref[s] = (dot(normed, w_ref[s]) + bias[s]).astype(BF16)
        for copy in results(origin):
            copy.start()

    def arrived(at, same, h):
        origin = block(at, same)
        ref = part(x_ref.at[origin], h)
        pltpu.make_async_copy(ref, ref, tok_recv.at[origin, h]).wait()

    def step(s, carry):
        for h in range(2):

            @pl.when((s > 0) & (chip - s >= 0))
            def _(h=h):
                arrived(chip - s, True, h)

                @pl.when(chip < chips - 1)
                def _():
                    hop(s, True, False, h).start()

                twin(chip - s, False, h).start()

            @pl.when((s > 0) & (chip + s < chips))
            def _(h=h):
                arrived(chip + s, True, h)

                @pl.when(chip > 0)
                def _():
                    hop(s, False, False, h).start()

                twin(chip + s, False, h).start()

        @pl.when(s == chips - 1)
        def _():
            weights_onward()

        @pl.when(chip - s >= 0)
        def _():
            project(chip - s, True, s == 0)

        @pl.when((s > 0) & (chip + s < chips))
        def _():
            project(chip + s, True)

        @pl.when(chip - s >= 0)
        def _():
            for h in range(2):
                arrived(chip - s, False, h)
            project(chip - s, False)

        @pl.when((s > 0) & (chip + s < chips))
        def _():
            for h in range(2):
                arrived(chip + s, False, h)
            project(chip + s, False)

        return carry

    lax.fori_loop(0, chips, step, 0)
    fc_onward()
    for copy in results(c):
        copy.wait()
    own_proj.wait()
    own_fc.wait()

    for s in range(chips):
        for h in range(2):
            if s < chips - 1:

                @pl.when((chip - s >= 0) & (chip < chips - 1))
                def _(s=s, h=h):
                    hop(s, True, False, h).wait_send()

                @pl.when((chip + s < chips) & (chip > 0))
                def _(s=s, h=h):
                    hop(s, False, False, h).wait_send()

            twin(s, False, h).wait_send()
    for k in range(1, n_fsdp):
        w_copy(k).wait_send()
        s_copy(k).wait_send()
    weights_done()
    fc_done()


def start_call(n_ctx, n_fsdp, base, tok, w_slots, small, w_proj, w_fc, cid):
    count, width = tok.shape
    slots, shard, cols = w_slots.shape
    hidden = w_fc.shape[1] // n_fsdp
    vm = pl.BlockSpec(memory_space=pltpu.VMEM)
    anym = pl.BlockSpec(memory_space=pl.ANY)
    dma = pltpu.SemaphoreType.DMA
    return pl.pallas_call(
        functools.partial(start_kernel, n_ctx, n_fsdp, base),
        in_specs=[anym, anym, vm, anym, anym],
        out_specs=[anym, anym, anym, anym, anym, vm, vm],
        out_shape=[
            jax.ShapeDtypeStruct((n_ctx, count, width), BF16),
            jax.ShapeDtypeStruct((slots, n_ctx, count, cols), BF16),
            jax.ShapeDtypeStruct((n_fsdp,) + w_proj.shape, BF16),
            jax.ShapeDtypeStruct((n_fsdp, shard, hidden), BF16),
            jax.ShapeDtypeStruct((n_fsdp, shard, hidden), BF16),
            jax.ShapeDtypeStruct((slots, width, cols), BF16),
            jax.ShapeDtypeStruct((small.shape[0], width), F32),
        ],
        scratch_shapes=[
            pltpu.VMEM((count, width), BF16),
            pltpu.VMEM((slots, count, cols), BF16),
            pltpu.VMEM(w_fc.shape, BF16),
            pltpu.VMEM((2, shard, hidden), BF16),
            pltpu.VMEM((n_ctx, count, width), BF16),
            pltpu.VMEM((n_fsdp, slots, shard, cols), BF16),
            pltpu.VMEM((n_fsdp,) + small.shape, F32),
            dma((n_ctx, 2)),
            dma((n_ctx // 2, 2)),
            dma((n_ctx // 2, 2)),
            dma((n_ctx // 2, 2)),
            dma((n_fsdp,)),
            dma((n_fsdp,)),
            dma((n_fsdp,)),
            dma((n_fsdp,)),
            dma((2, n_fsdp)),
            dma((2, n_fsdp)),
            dma((2, n_fsdp)),
            dma((2, n_fsdp)),
            dma((6,)),
        ],
        compiler_params=pltpu.CompilerParams(
            collective_id=cid, has_side_effects=True, vmem_limit_bytes=VMEM_LIMIT
        ),
        cost_estimate=SHORT,
        name="tokens_qkv",
    )(tok, w_slots, small, w_proj, w_fc)


def causal_scores(k, q_rows, start):
    scores = dot_last(k, q_rows)
    keep = start
    tail = scores[keep:]
    key_id = lax.broadcasted_iota(jnp.int32, tail.shape, 0)
    query_id = lax.broadcasted_iota(jnp.int32, tail.shape, 1)
    tail = jnp.where(key_id <= query_id, tail, -1e30)
    if keep == 0:
        return tail
    return jnp.concatenate([scores[:keep], tail], axis=0)


def soft(scores, v_t):
    top = jnp.max(scores, axis=0, keepdims=True)
    weights = jnp.exp(scores - top)
    total = jnp.sum(weights, axis=0, keepdims=True)
    out = dot(v_t, weights.astype(BF16)) / total
    return out, top + jnp.log(total)


def causal(inv_ref, x_ref):
    return jnp.concatenate([x_ref[0, inv_ref[i]] for i in range(x_ref.shape[1])], axis=0)


def attn_fwd_kernel(inv_ref, x_ref, o_ref, l_ref):
    rows = l_ref.shape[2]
    hd = HEAD_DIM
    x = causal(inv_ref, x_ref)
    q = x[:, :hd] * BF16(SCALE)
    k = x[:, hd : 2 * hd]
    v_t = x[:, 2 * hd :].T
    for i in range(rows // QROWS):
        lo, hi = i * QROWS, (i + 1) * QROWS
        out, lse = soft(causal_scores(k[:hi], q[lo:hi], lo), v_t[:, :hi])
        l_ref[0, :, lo:hi] = lse
        out = out.astype(BF16)
        for b in range(QROWS // BLOCK):
            o_ref[inv_ref[2 * i + b]] = out[:, b * BLOCK : (b + 1) * BLOCK]


def attn_fwd(inv, qkv, heads):
    blocks, _, cols = qkv.shape[1:]
    rows = blocks * BLOCK
    return pl.pallas_call(
        attn_fwd_kernel,
        grid_spec=pltpu.PrefetchScalarGridSpec(
            num_scalar_prefetch=1,
            grid=(heads,),
            in_specs=[pl.BlockSpec((1, blocks, BLOCK, cols), lambda h, inv: (h, 0, 0, 0))],
            out_specs=[
                pl.BlockSpec((blocks, HEAD_DIM, BLOCK), lambda h, inv: (0, h, 0)),
                pl.BlockSpec((1, 1, rows), lambda h, inv: (h, 0, 0)),
            ],
        ),
        out_shape=[
            jax.ShapeDtypeStruct((blocks, heads * HEAD_DIM, BLOCK), BF16),
            jax.ShapeDtypeStruct((heads, 1, rows), F32),
        ],
        compiler_params=pltpu.CompilerParams(vmem_limit_bytes=VMEM_LIMIT),
        cost_estimate=SHORT,
        name="attn_fwd",
    )(inv, qkv)


def attn_bwd_kernel(inv_ref, x_ref, do_ref, o_ref, l_ref, dx_ref, dk_acc, dv_acc):
    rows = l_ref.shape[2]
    hd = HEAD_DIM
    x = causal(inv_ref, x_ref)
    q = x[:, :hd] * BF16(SCALE)
    k = x[:, hd : 2 * hd]
    v = x[:, 2 * hd :]
    k_t = k.T
    dk_acc[...] = jnp.zeros_like(dk_acc)
    dv_acc[...] = jnp.zeros_like(dv_acc)
    for i in range(rows // QROWS):
        lo, hi = i * QROWS, (i + 1) * QROWS
        ids = [inv_ref[2 * i + b] for b in range(QROWS // BLOCK)]
        do_t = jnp.concatenate([do_ref[b] for b in ids], axis=1)
        o_t = jnp.concatenate([o_ref[b] for b in ids], axis=1)
        inner = jnp.sum(do_t.astype(F32) * o_t.astype(F32), axis=0, keepdims=True)
        probs = jnp.exp(causal_scores(k[:hi], q[lo:hi], lo) - l_ref[0, :, lo:hi])
        dprobs = dot(v[:hi], do_t)
        dscores = (probs * (dprobs - inner)).astype(BF16)
        dv_acc[:hi] += dot_last(probs.astype(BF16), do_t)
        dk_acc[:hi] += dot(dscores, q[lo:hi])
        dq = (dot(k_t[:, :hi], dscores) * SCALE).T
        for n, b in enumerate(ids):
            dx_ref[0, b, :, :hd] = dq[n * BLOCK : (n + 1) * BLOCK].astype(BF16)
    for i in range(rows // BLOCK):
        lo, hi = i * BLOCK, (i + 1) * BLOCK
        dx_ref[0, inv_ref[i], :, hd : 2 * hd] = dk_acc[lo:hi].astype(BF16)
        dx_ref[0, inv_ref[i], :, 2 * hd :] = dv_acc[lo:hi].astype(BF16)


def attn_bwd(inv, qkv, d_out, out, lse, heads):
    blocks, _, cols = qkv.shape[1:]
    rows = blocks * BLOCK
    whole = pl.BlockSpec((1, blocks, BLOCK, cols), lambda h, inv: (h, 0, 0, 0))
    feat = pl.BlockSpec((blocks, HEAD_DIM, BLOCK), lambda h, inv: (0, h, 0))
    return pl.pallas_call(
        attn_bwd_kernel,
        grid_spec=pltpu.PrefetchScalarGridSpec(
            num_scalar_prefetch=1,
            grid=(heads,),
            in_specs=[
                whole,
                feat,
                feat,
                pl.BlockSpec((1, 1, rows), lambda h, inv: (h, 0, 0)),
            ],
            out_specs=whole,
            scratch_shapes=[pltpu.VMEM((rows, HEAD_DIM), F32)] * 2,
        ),
        out_shape=jax.ShapeDtypeStruct((heads, blocks, BLOCK, cols), BF16),
        compiler_params=pltpu.CompilerParams(vmem_limit_bytes=VMEM_LIMIT),
        cost_estimate=pl.CostEstimate(
            flops=24 * 10**9, bytes_accessed=24 * 10**6, transcendentals=0
        ),
        name="attn_bwd",
    )(inv, qkv, d_out, out, lse)


def own_scores(order_ref, x_ref, k):
    hd = HEAD_DIM
    blocks = x_ref.shape[1]
    first = order_ref[blocks]
    q = jnp.concatenate([x_ref[0, first], x_ref[0, first + 1]], axis=0)[:, :hd]
    q = q * BF16(SCALE)
    scores = dot_last(k, q)
    row = lax.broadcasted_iota(jnp.int32, (BLOCK, 1), 0)
    key_place = jnp.concatenate([order_ref[b] * BLOCK + row for b in range(blocks)], axis=0)
    lane = lax.broadcasted_iota(jnp.int32, (1, 2 * BLOCK), 1)
    low, high = order_ref[order_ref[blocks]], order_ref[order_ref[blocks] + 1]
    place = jnp.where(lane < BLOCK, low * BLOCK + lane, (high - 1) * BLOCK + lane)
    return q, first, jnp.where(key_place <= place, scores, -1e30)


def rest_fwd_kernel(order_ref, x_ref, o_ref, l_ref):
    hd = HEAD_DIM
    x = x_ref[0].reshape(-1, 3 * hd)
    _, _, scores = own_scores(order_ref, x_ref, x[:, hd : 2 * hd])
    out, lse = soft(scores, x[:, 2 * hd :].T)
    o_ref[0] = out.astype(BF16)
    l_ref[0] = lse


def rest_fwd(order, qkv, base):
    slots, blocks, _, cols = qkv.shape
    rest = slots - base
    return pl.pallas_call(
        rest_fwd_kernel,
        grid_spec=pltpu.PrefetchScalarGridSpec(
            num_scalar_prefetch=1,
            grid=(rest,),
            in_specs=[
                pl.BlockSpec((1, blocks, BLOCK, cols), lambda h, o: (base + h, 0, 0, 0))
            ],
            out_specs=[
                pl.BlockSpec((1, HEAD_DIM, QROWS), lambda h, o: (h, 0, 0)),
                pl.BlockSpec((1, 1, QROWS), lambda h, o: (h, 0, 0)),
            ],
        ),
        out_shape=[
            jax.ShapeDtypeStruct((rest, HEAD_DIM, QROWS), BF16),
            jax.ShapeDtypeStruct((rest, 1, QROWS), F32),
        ],
        compiler_params=pltpu.CompilerParams(vmem_limit_bytes=VMEM_LIMIT),
        cost_estimate=SHORT,
        name="rest_fwd",
    )(order, qkv)


def rest_bwd_kernel(order_ref, x_ref, do_ref, o_ref, l_ref, dx_ref):
    hd = HEAD_DIM
    x = x_ref[0].reshape(-1, 3 * hd)
    blocks = x_ref.shape[1]
    k = x[:, hd : 2 * hd]
    q, first, scores = own_scores(order_ref, x_ref, k)
    do_t = do_ref[0]
    inner = jnp.sum(do_t.astype(F32) * o_ref[0].astype(F32), axis=0, keepdims=True)
    probs = jnp.exp(scores - l_ref[0])
    dprobs = dot(x[:, 2 * hd :], do_t)
    dscores = (probs * (dprobs - inner)).astype(BF16)
    dv = dot_last(probs.astype(BF16), do_t).astype(BF16)
    dk = dot(dscores, q).astype(BF16)
    dq = (dot(k.T, dscores) * SCALE).T.astype(BF16)
    dx_ref[0, :, :, 2 * hd :] = dv.reshape(blocks, BLOCK, hd)
    dx_ref[0, :, :, hd : 2 * hd] = dk.reshape(blocks, BLOCK, hd)
    dx_ref[0, :, :, :hd] = jnp.zeros((blocks, BLOCK, hd), BF16)
    for b in range(2):
        dx_ref[0, first + b, :, :hd] = dq[b * BLOCK : (b + 1) * BLOCK]


def rest_bwd(order, qkv, d_out, out, lse, base):
    slots, blocks, _, cols = qkv.shape
    rest = slots - base
    feat = pl.BlockSpec((1, HEAD_DIM, QROWS), lambda h, o: (h, 0, 0))
    return pl.pallas_call(
        rest_bwd_kernel,
        grid_spec=pltpu.PrefetchScalarGridSpec(
            num_scalar_prefetch=1,
            grid=(rest,),
            in_specs=[
                pl.BlockSpec((1, blocks, BLOCK, cols), lambda h, o: (base + h, 0, 0, 0)),
                feat,
                feat,
                pl.BlockSpec((1, 1, QROWS), lambda h, o: (h, 0, 0)),
            ],
            out_specs=pl.BlockSpec((1, blocks, BLOCK, cols), lambda h, o: (h, 0, 0, 0)),
        ),
        out_shape=jax.ShapeDtypeStruct((rest, blocks, BLOCK, cols), BF16),
        compiler_params=pltpu.CompilerParams(vmem_limit_bytes=VMEM_LIMIT),
        cost_estimate=SHORT,
        name="rest_bwd",
    )(order, qkv, d_out, out, lse)


def mix_kernel(
    n_ctx,
    out_hbm,
    rest_ref,
    tok_ref,
    proj_ref,
    lines_ref,
    att_ref,
    mid_ref,
    n_ref,
    got_ref,
    out_send,
    out_recv,
    local,
):
    c = lax.axis_index("ctx")
    f = lax.axis_index("fsdp")
    width = tok_ref.shape[1]
    blocks, feats = got_ref.shape[1], got_ref.shape[2]
    enter([(lax.rem(c + i, n_ctx), f) for i in range(1, n_ctx)])

    def out_copy(i):
        to = lax.rem(c + i, n_ctx)
        return send(
            out_hbm.at[pl.ds(to * blocks, blocks)],
            got_ref.at[c],
            out_send.at[i],
            out_recv.at[i],
            (to, f),
        )

    for i in range(n_ctx - 1, 0, -1):
        out_copy(i).start()
    own = pltpu.make_async_copy(
        out_hbm.at[pl.ds(c * blocks, blocks)], got_ref.at[c], local
    )
    own.start()
    main = n_ctx * feats
    if main < width:
        att_ref[:, main:] = rest_ref[...].reshape(width - main, -1).T
    own.wait()
    for i in range(1, n_ctx):
        out_copy(i).wait_recv()
    for src in range(n_ctx):
        block = jnp.concatenate([got_ref[src, b] for b in range(blocks)], axis=1)
        att_ref[:, src * feats : (src + 1) * feats] = block.T
    mid = tok_ref[...].astype(F32) + (dot(att_ref[...], proj_ref[...]) + lines_ref[6:7])
    mid_ref[...] = mid
    cen = mid - jnp.mean(mid, axis=1, keepdims=True)
    var = jnp.mean(cen * cen, axis=1, keepdims=True)
    n_ref[...] = (cen * lax.rsqrt(var + EPS) * lines_ref[1:2] + lines_ref[3:4]).astype(BF16)
    for i in range(1, n_ctx):
        out_copy(i).wait_send()


def mix_call(n_ctx, out_own, out_rest, tok, proj, lines, cid):
    count, width = tok.shape
    vm = pl.BlockSpec(memory_space=pltpu.VMEM)
    anym = pl.BlockSpec(memory_space=pl.ANY)
    dma = pltpu.SemaphoreType.DMA
    return pl.pallas_call(
        functools.partial(mix_kernel, n_ctx),
        in_specs=[anym, vm, vm, vm, vm],
        out_specs=[vm, vm, vm],
        out_shape=[
            jax.ShapeDtypeStruct((count, width), BF16),
            jax.ShapeDtypeStruct((count, width), F32),
            jax.ShapeDtypeStruct((count, width), BF16),
        ],
        scratch_shapes=[
            pltpu.VMEM((n_ctx, out_own.shape[0] // n_ctx) + out_own.shape[1:], BF16),
            dma((n_ctx,)),
            dma((n_ctx,)),
            dma(()),
        ],
        compiler_params=pltpu.CompilerParams(
            collective_id=cid, has_side_effects=True, vmem_limit_bytes=VMEM_LIMIT
        ),
        cost_estimate=SHORT,
        name="mix_rows",
    )(out_own, out_rest, tok, proj, lines)


def turn_kernel(
    n_ctx,
    gsum_ref,
    cot_ref,
    mid_ref,
    proj_ref,
    lines_ref,
    fc_hbm,
    grad_ref,
    low_ref,
    sums_ref,
    rest_ref,
    fc_ref,
    got_hbm,
    out_ref,
    pair_in,
    out_send,
    out_recv,
    pair_sem,
    local,
):
    c = lax.axis_index("ctx")
    f = lax.axis_index("fsdp")
    core = c % 2
    width = mid_ref.shape[1]
    blocks, feats = out_ref.shape[0] // n_ctx, out_ref.shape[1]
    enter([(lax.rem(c + i, n_ctx), f) for i in range(1, n_ctx)])
    pair = send(fc_hbm.at[1 - core], pair_in, pair_sem.at[0], pair_sem.at[1], (c + 1 - 2 * core, f))
    pair.start()
    own_fc = pltpu.make_async_copy(fc_hbm.at[core], fc_ref, local.at[0])
    own_fc.start()

    xhat, rstd = norm_parts(mid_ref[...])
    grad = gsum_ref[...]
    cot = cot_ref[...].astype(F32)
    mid_grad = cot + norm_back(xhat, rstd, lines_ref[1:2], grad)
    grad_ref[...] = mid_grad
    low = mid_grad.astype(BF16)
    low_ref[...] = low
    att_t = dot_last(low, proj_ref[...]).astype(BF16).T
    for to in range(n_ctx):
        for b in range(blocks):
            out_ref[to * blocks + b] = att_t[
                to * feats : (to + 1) * feats, b * BLOCK : (b + 1) * BLOCK
            ]

    def out_copy(i):
        to = lax.rem(c + i, n_ctx)
        return send(
            out_ref.at[pl.ds(to * blocks, blocks)],
            got_hbm.at[pl.ds(c * blocks, blocks)],
            out_send.at[i],
            out_recv.at[i],
            (to, f),
        )

    for i in range(n_ctx - 1, 0, -1):
        out_copy(i).start()
    own = pltpu.make_async_copy(
        out_ref.at[pl.ds(c * blocks, blocks)], got_hbm.at[pl.ds(c * blocks, blocks)], local.at[1]
    )
    own.start()
    main = n_ctx * feats
    if main < width:
        rest_ref[...] = att_t[main:].reshape(rest_ref.shape)
    else:
        rest_ref[...] = jnp.zeros(rest_ref.shape, BF16)
    for r, line in enumerate((grad * xhat, grad, low.astype(F32), cot)):
        sums_ref[r : r + 1] = jnp.sum(line, axis=0, keepdims=True)
    sums_ref[4:] = jnp.zeros((4, width), F32)
    own_fc.wait()
    pair.wait()

    def add(j, carry):
        fc_ref[j] = (fc_ref[j].astype(F32) + pair_in[j].astype(F32)).astype(BF16)
        return carry

    lax.fori_loop(0, fc_ref.shape[0], add, 0)
    own.wait()
    for i in range(1, n_ctx):
        out_copy(i).wait()


def turn_call(n_ctx, base, gsum, cot, mid, proj, lines, fc_part, cid):
    count, width = mid.shape
    heads = width // HEAD_DIM
    rest = max(heads - base * n_ctx, 1)
    out = (n_ctx * count // BLOCK, base * HEAD_DIM, BLOCK)
    vm = pl.BlockSpec(memory_space=pltpu.VMEM)
    anym = pl.BlockSpec(memory_space=pl.ANY)
    dma = pltpu.SemaphoreType.DMA
    return pl.pallas_call(
        functools.partial(turn_kernel, n_ctx),
        in_specs=[vm] * 5 + [anym],
        out_specs=[vm] * 5 + [anym],
        out_shape=[
            jax.ShapeDtypeStruct((count, width), F32),
            jax.ShapeDtypeStruct((count, width), BF16),
            jax.ShapeDtypeStruct((8, width), F32),
            jax.ShapeDtypeStruct((rest, HEAD_DIM, count), BF16),
            jax.ShapeDtypeStruct(fc_part.shape[1:], BF16),
            jax.ShapeDtypeStruct(out, BF16),
        ],
        scratch_shapes=[
            pltpu.VMEM(out, BF16),
            pltpu.VMEM(fc_part.shape[1:], BF16),
            dma((n_ctx,)),
            dma((n_ctx,)),
            dma((2,)),
            dma((2,)),
        ],
        compiler_params=pltpu.CompilerParams(
            collective_id=cid, has_side_effects=True, vmem_limit_bytes=VMEM_LIMIT
        ),
        cost_estimate=SHORT,
        name="turn_rows",
    )(gsum, cot, mid, proj, lines, fc_part)


def far_first(i, chips):
    return (i % 2) * (i // 2) + (1 - i % 2) * (chips - 1 - i // 2)


def line_sum(chip, chips, f, core, part, came, sems, ready=None):
    sent, left_sem, right_sem = sems

    def to_right(d):
        return send(
            part.at[d], came.at[d], sent.at[d], left_sem.at[d], (2 * (chip + 1) + core, f)
        )

    def to_left(d):
        place = jnp.where(d == chip - 1, chips, d)
        return send(
            part.at[d], came.at[place], sent.at[d], right_sem.at[d], (2 * (chip - 1) + core, f)
        )

    def from_left(d):
        send(part.at[d], came.at[d], sent.at[d], left_sem.at[d], (2 * chip + core, f)).wait_recv()
        add(d, d)

    def from_right(d, place):
        send(
            part.at[d], came.at[place], sent.at[d], right_sem.at[d], (2 * chip + core, f)
        ).wait_recv()
        add(d, place)

    def add(d, place):
        part[d] = (part[d].astype(F32) + came[place].astype(F32)).astype(BF16)

    def step(t):
        far = chips - 1 - t + chip
        near = t - (chips - 1 - chip)

        @pl.when(chip <= t)
        def _():
            if ready is not None:
                ready(far)

            @pl.when(chip > 0)
            def _():
                from_left(far)

            @pl.when(chip < t)
            def _():
                to_right(far + 1).wait_send()

            to_right(far).start()

        @pl.when(near >= 0)
        def _():
            if ready is not None:
                ready(near)

            @pl.when(chip < chips - 1)
            def _():
                from_right(near, near)

            @pl.when(near > 0)
            def _():
                to_left(near - 1).wait_send()

            to_left(near).start()

    def finish():
        if ready is not None:
            ready(chip)

        @pl.when(chip > 0)
        def _():
            from_left(chip)

        @pl.when(chip < chips - 1)
        def _():
            from_right(chip, chips)

    def done():
        @pl.when(chip < chips - 1)
        def _():
            to_right(chip + 1).wait_send()

        @pl.when(chip > 0)
        def _():
            to_left(chip - 1).wait_send()

    return step, finish, done


def line_gather(chip, chips, f, core, view, sems):
    right, left, twin_sent, got, twin_got = sems
    twin_id = (2 * chip + 1 - core, f)

    def hop(s, rightward):
        origin = chip - s if rightward else chip + s
        ref = view(origin, core)
        peer = (2 * (chip + 1 if rightward else chip - 1) + core, f)
        return send(ref, ref, (right if rightward else left).at[s], got.at[origin], peer)

    def twin(origin):
        ref = view(origin, core)
        return send(ref, ref, twin_sent.at[origin], twin_got.at[origin], twin_id)

    def arrived(origin):
        ref = view(origin, core)
        send(ref, ref, right.at[0], got.at[origin], twin_id).wait_recv()

    def step(s):
        @pl.when(chip - s >= 0)
        def _():
            if s:
                arrived(chip - s)

            @pl.when(chip < chips - 1)
            def _():
                hop(s, True).start()

            twin(chip - s).start()

        @pl.when(chip + s < chips)
        def _():
            if s:
                arrived(chip + s)

            @pl.when(chip > 0)
            def _():
                hop(s, False).start()

            if s:
                twin(chip + s).start()

    def done():
        for s in range(chips):
            if s < chips - 1:

                @pl.when((chip - s >= 0) & (chip < chips - 1))
                def _(s=s):
                    hop(s, True).wait_send()

                @pl.when((chip + s < chips) & (chip > 0))
                def _(s=s):
                    hop(s, False).wait_send()

            twin(s).wait_send()
            ref = view(s, 1 - core)
            send(ref, ref, twin_sent.at[s], twin_got.at[s], twin_id).wait_recv()

    return step, done


def back_kernel(
    n_ctx,
    n_fsdp,
    own_ref,
    rest_ref,
    w_ref,
    n_ref,
    fc_hbm,
    one_ref,
    cols_ref,
    fc_all,
    part,
    twin_out,
    twin_in,
    came,
    mine,
    theirs,
    twin_send,
    twin_recv,
    line_send,
    left_recv,
    right_recv,
    cols_send,
    cols_recv,
    fc_send,
    fc_recv,
    local,
    extra_in,
    extra_sem,
):
    c = lax.axis_index("ctx")
    f = lax.axis_index("fsdp")
    chips = n_ctx // 2
    chip, core = c // 2, c % 2
    slots, width, cols = w_ref.shape
    count = own_ref.shape[2]
    base = own_ref.shape[0]
    shard = width // n_fsdp
    twin_id = (2 * chip + 1 - core, f)
    enter(
        [(lax.rem(c + i, n_ctx), f) for i in range(1, n_ctx)]
        + [(c, flip(f, k, n_fsdp)) for k in range(1, n_fsdp)]
    )

    def grad(s):
        return own_ref.at[s] if s < base else rest_ref.at[s - base]

    def for_block(b):
        total = dot_last(grad(0)[b], w_ref[0])
        for s in range(1, slots):
            total += dot_last(grad(s)[b], w_ref[s])
        return total.astype(BF16)

    def to_twin(d, slot):
        return send(twin_out.at[slot], twin_in.at[d], twin_send.at[slot], twin_recv.at[d], twin_id)

    def products(i, carry):
        d = far_first(i, chips)
        slot = i % 2
        product = for_block(2 * d + 1 - core)

        @pl.when(i > 1)
        def _():
            to_twin(d, slot).wait_send()

        twin_out[slot] = product
        to_twin(d, slot).start()
        part[d] = for_block(2 * d + core)
        return carry

    def ready(d):
        to_twin(d, 0).wait_recv()
        part[d] = (part[d].astype(F32) + twin_in[d].astype(F32)).astype(BF16)

    cut = count // 2
    streams = [
        line_sum(
            chip,
            chips,
            f,
            core,
            part.at[:, pl.ds(h * cut, cut)],
            came.at[h],
            (line_send.at[h], left_recv.at[h], right_recv.at[h]),
            None if h else ready,
        )
        for h in range(2)
    ]

    def step(t):
        for stream in streams:
            stream[0](t)

    def finish():
        for stream in streams:
            stream[1]()

    def done():
        for stream in streams:
            stream[2]()

    def cols_copy(src, dst, at):
        return send(mine.at[src], theirs.at[at], cols_send.at[src], cols_recv.at[at], (c, dst))

    def columns(j):
        left = n_ref[:, :, j * shard : (j + 1) * shard].reshape(n_ctx * count, shard)
        for s in range(slots):
            right = grad(s)[...].reshape(n_ctx * count, cols)
            mine[j, s] = dot_first(left, right).astype(BF16)

    def fc_copy(k):
        other = flip(f, k, n_fsdp)
        return send(fc_hbm.at[other], fc_all.at[f], fc_send.at[k], fc_recv.at[k], (c, other))

    for k in range(1, n_fsdp):
        fc_copy(k).start()
    own_fc = pltpu.make_async_copy(fc_hbm.at[f], fc_all.at[f], local)
    own_fc.start()
    lax.fori_loop(0, 2, products, 0)
    step(0)
    for j in range(n_fsdp):
        columns(j)
    for k in range(1, n_fsdp):
        other = flip(f, k, n_fsdp)
        cols_copy(other, other, f).start()
    lax.fori_loop(2, chips, products, 0)
    if chips > 2:
        step(1)
    for t in range(2, chips - 1):
        step(t)
    total = mine[f].astype(F32)
    for k in range(1, n_fsdp):
        other = flip(f, k, n_fsdp)
        cols_copy(other, other, other).wait_recv()
        total += theirs[other].astype(F32)
    cols_ref[...] = total.astype(BF16)
    if slots > base:
        pair = send(
            cols_ref.at[pl.ds(base, slots - base)],
            extra_in,
            extra_sem.at[0],
            extra_sem.at[1],
            twin_id,
        )
        pair.start()
    finish()
    if slots > base:
        pair.wait()
        cols_ref[base:] = (cols_ref[base:].astype(F32) + extra_in[...].astype(F32)).astype(BF16)
    one_ref[...] = part[chip]
    own_fc.wait()
    for k in range(1, n_fsdp):
        fc_copy(k).wait()
    done()
    for slot in range(2):
        to_twin(0, slot).wait_send()
    for k in range(1, n_fsdp):
        other = flip(f, k, n_fsdp)
        cols_copy(other, other, other).wait_send()


def back_fits(n_ctx, n_fsdp, count, width, slots):
    blocks = (5 * (n_ctx // 2) + n_ctx) * count * width
    heads = slots * 256 * (n_ctx * count + 3 * width)
    return 2 * (blocks + heads) < 50 * 1024 * 1024


def back_call(n_ctx, n_fsdp, own, rest, w_slots, normed, fc_mine, cid):
    slots, width, cols = w_slots.shape
    count = normed.shape[1]
    chips = n_ctx // 2
    shard = width // n_fsdp
    vm = pl.BlockSpec(memory_space=pltpu.VMEM)
    anym = pl.BlockSpec(memory_space=pl.ANY)
    dma = pltpu.SemaphoreType.DMA
    block = pltpu.VMEM((chips, count, width), BF16)
    piece = pltpu.VMEM((n_fsdp, slots, shard, cols), BF16)
    return pl.pallas_call(
        functools.partial(back_kernel, n_ctx, n_fsdp),
        in_specs=[vm] * 4 + [anym],
        out_specs=[vm] * 2 + [anym],
        out_shape=[
            jax.ShapeDtypeStruct((count, width), BF16),
            jax.ShapeDtypeStruct((slots, shard, cols), BF16),
            jax.ShapeDtypeStruct(fc_mine.shape, BF16),
        ],
        scratch_shapes=[
            block,
            pltpu.VMEM((2, count, width), BF16),
            block,
            pltpu.VMEM((2, chips + 1, count // 2, width), BF16),
        ]
        + [piece] * 2
        + [dma((2,)), dma((chips,))]
        + [dma((2, chips))] * 3
        + [dma((n_fsdp,))] * 4
        + [dma(())]
        + [pltpu.VMEM((max(slots - own.shape[0], 1), shard, cols), BF16), dma((2,))],
        compiler_params=pltpu.CompilerParams(
            collective_id=cid, has_side_effects=True, vmem_limit_bytes=60 * 1024 * 1024
        ),
        cost_estimate=SHORT,
        name="qkv_back",
    )(own, rest, w_slots, normed, fc_mine)


def sums_kernel(n_ctx, n_fsdp, lead, *refs):
    rows_ref, cols_ref, extra_ref, att_ref, mid_ref, lines_in = refs[:6]
    share_hbm, resid_ref, small_ref = refs[6:9]
    outs, cols_all, lines_ref, layer_ref = refs[9:11], refs[11], refs[12], refs[13]
    parts, cames = refs[14:16], refs[16:18]
    proj_part, proj_in, proj_got, lines_got, share_in = refs[18:23]
    lines_send, lines_recv, local, proj_send, proj_recv, pair_sem = refs[23:29]
    share_send, share_recv = refs[29:31]
    cols_sems = refs[31:36]
    sems = [(refs[36 + 8 * i : 39 + 8 * i], refs[39 + 8 * i : 44 + 8 * i]) for i in range(2)]
    c = lax.axis_index("ctx")
    f = lax.axis_index("fsdp")
    chips = n_ctx // 2
    chip, core = c // 2, c % 2
    width = att_ref.shape[1]
    shard = width // n_fsdp
    half = shard // 2
    high = proj_in.shape[1]
    twin_id = (2 * chip + 1 - core, f)
    enter(
        [(lax.rem(c + i, n_ctx), f) for i in range(1, n_ctx)]
        + [(c, flip(f, k, n_fsdp)) for k in range(1, n_fsdp)]
    )

    def line_ops(i):
        sum_sems, gather_sems = sems[i]
        gather = line_gather(chip, chips, f, core, lambda at, h: outs[i].at[h, at], gather_sems)
        return line_sum(chip, chips, f, core, parts[i], cames[i], sum_sems) + gather

    def proj_pair():
        return send(proj_part.at[1 - core], proj_in, pair_sem.at[0], pair_sem.at[1], twin_id)

    def proj_copy(k):
        other = flip(f, k, n_fsdp)
        return send(
            proj_part.at[core, other],
            proj_got.at[f],
            proj_send.at[k],
            proj_recv.at[k],
            (c, other),
        )

    def share_copy(k):
        other = flip(f, k, n_fsdp)
        return send(
            share_hbm.at[other], share_in.at[f], share_send.at[k], share_recv.at[k], (c, other)
        )

    def proj_products(j):
        for h in range(2):
            lo = j * shard + h * half
            proj_part[h, j, :half] = dot_first(att_ref[:, lo : lo + half], mid_ref[...]).astype(BF16)
            if half < high:
                proj_part[h, j, half:] = jnp.zeros((high - half, width), BF16)

    def proj_add(j, carry):
        proj_part[core, j] = (
            proj_part[core, j].astype(F32) + proj_in[j].astype(F32)
        ).astype(BF16)
        return carry

    def proj_total():
        total = proj_part[core, f].astype(F32)
        for k in range(1, n_fsdp):
            proj_copy(k).wait_recv()
            total += proj_got[flip(f, k, n_fsdp)].astype(F32)
        total = jnp.concatenate([total.astype(BF16), extra_ref[...]], axis=0)
        first = rows_ref.shape[1] - parts[0].shape[1]
        step, rows = parts[1].shape[1] - first, total.shape[0]
        for p in range(chips):
            lo, hi = min(p * step, rows), min((p + 1) * step, rows)
            end = first + hi - lo
            if hi > lo:
                parts[1][p, first:end] = total[lo:hi]
            if hi - lo < step:
                parts[1][p, end:] = jnp.zeros((step - hi + lo, width), BF16)

    peers = [(flip(c, 1 << i, n_ctx), f) for i in range(n_ctx.bit_length() - 1)]
    ctx_phases = len(peers)
    peers += [(c, flip(f, 1 << i, n_fsdp)) for i in range(n_fsdp.bit_length() - 1)]

    def line_copy(i):
        rows = lines_in.shape[0] if i < ctx_phases else lead
        return send(
            lines_ref.at[:rows],
            lines_got.at[i, :rows],
            lines_send.at[i],
            lines_recv.at[i],
            peers[i],
        )

    def line_phase(i):
        if 0 < i <= len(peers):
            rows = lines_in.shape[0] if i <= ctx_phases else lead
            line_copy(i - 1).wait()
            lines_ref[:rows] += lines_got[i - 1, :rows]
        if i < len(peers):
            line_copy(i).start()

    def settle(finish, i):
        finish()
        keep = pltpu.make_async_copy(parts[i].at[chip], outs[i].at[core, chip], local.at[0])
        keep.start()
        keep.wait()

    sum_a, finish_a, sums_a, gather_a, gathers_a = line_ops(0)
    sum_b, finish_b, sums_b, gather_b, gathers_b = line_ops(1)
    cols_step, cols_done = line_gather(
        chip, chips, f, core, lambda at, h: cols_all.at[2 * at + h], cols_sems
    )
    load = pltpu.make_async_copy(cols_ref, cols_all.at[c], local.at[1])
    load.start()
    cut = parts[0].shape[1]
    parts[0][...] = rows_ref[:, :cut]
    load.wait()
    cols_step(0)
    sum_a(0)
    parts[1][:, : rows_ref.shape[1] - cut] = rows_ref[:, cut:]
    lines_ref[...] = lines_in[...]
    for j in range(n_fsdp):
        proj_products(j)
    proj_pair().start()
    for t in range(1, chips - 1):
        cols_step(t)
        sum_a(t)
        if t == 1:
            proj_pair().wait()
            lax.fori_loop(0, n_fsdp, proj_add, 0)
            for k in range(1, n_fsdp):
                proj_copy(k).start()
            for k in range(1, n_fsdp):
                share_copy(k).start()
            own_share = pltpu.make_async_copy(share_hbm.at[f], share_in.at[f], local.at[2])
            own_share.start()
    cols_step(chips - 1)
    settle(finish_a, 0)
    gather_a(0)
    proj_total()
    sum_b(0)
    phase = 0
    for s in range(1, chips):
        gather_a(s)
        if s < chips - 1:
            sum_b(s)
        line_phase(phase)
        phase += 1
    settle(finish_b, 1)
    for s in range(chips):
        gather_b(s)
        line_phase(phase)
        phase += 1
    while phase <= len(peers):
        line_phase(phase)
        phase += 1
    own_share.wait()
    total = share_in[f].astype(F32)
    for k in range(1, n_fsdp):
        share_copy(k).wait()
        total += share_in[flip(f, k, n_fsdp)].astype(F32)
    layer_ref[...] = (resid_ref[...] + (total + small_ref[7:8])).astype(BF16)
    for done in (sums_a, sums_b, cols_done, gathers_a, gathers_b):
        done()
    for k in range(1, n_fsdp):
        proj_copy(k).wait_send()


def sums_call(
    n_ctx, n_fsdp, rows, cols, extra, attended, mid_low, lines, shares, mid, small, lead, cid
):
    chips = n_ctx // 2
    count, width = attended.shape
    high = half_high(width // n_fsdp)
    per_chip = rows.shape[1]
    third = -(-(high + extra.shape[0]) // (16 * chips)) * 16
    cut = -(-(per_chip + third) // 32) * 16
    shapes = [(chips, size, width) for size in (cut, per_chip + third - cut)]
    phases = (n_ctx * n_fsdp).bit_length() - 1
    vm = pl.BlockSpec(memory_space=pltpu.VMEM)
    anym = pl.BlockSpec(memory_space=pl.ANY)
    dma = pltpu.SemaphoreType.DMA
    return pl.pallas_call(
        functools.partial(sums_kernel, n_ctx, n_fsdp, lead),
        in_specs=[vm, anym, vm, vm, vm, vm, anym, vm, vm],
        out_specs=[vm, vm, anym, vm, vm],
        out_shape=[jax.ShapeDtypeStruct((2,) + shape, BF16) for shape in shapes]
        + [jax.ShapeDtypeStruct((n_ctx,) + cols.shape, BF16)]
        + [jax.ShapeDtypeStruct(lines.shape, F32), jax.ShapeDtypeStruct(mid.shape, BF16)],
        scratch_shapes=[pltpu.VMEM(shape, BF16) for shape in shapes]
        + [pltpu.VMEM((chips + 1,) + shape[1:], BF16) for shape in shapes]
        + [
            pltpu.VMEM((2, n_fsdp, high, width), BF16),
            pltpu.VMEM((n_fsdp, high, width), BF16),
            pltpu.VMEM((n_fsdp, high, width), BF16),
            pltpu.VMEM((phases,) + lines.shape, F32),
            pltpu.VMEM(shares.shape, BF16),
            dma((phases,)),
            dma((phases,)),
            dma((3,)),
            dma((n_fsdp,)),
            dma((n_fsdp,)),
            dma((2,)),
            dma((n_fsdp,)),
            dma((n_fsdp,)),
        ]
        + [dma((chips,))] * (5 + 2 * 8),
        compiler_params=pltpu.CompilerParams(
            collective_id=cid, has_side_effects=True, vmem_limit_bytes=56 * 1024 * 1024
        ),
        cost_estimate=SHORT,
        name="weight_sums",
    )(rows, cols, extra, attended, mid_low, lines, shares, mid, small)


def assemble_kernel(
    n_fsdp,
    own_ref,
    rest_ref,
    first_ref,
    second_ref,
    third_ref,
    out_ref,
    attn_hbm,
    fc_hbm,
    proj_hbm,
    wout_hbm,
    *scratch,
):
    attn_ref, fc_ref, proj_ref, wout_ref, low_ref, sem = scratch
    load = pltpu.make_async_copy(out_ref, low_ref, sem.at[4])
    load.start()
    hd = HEAD_DIM
    shard, hidden = fc_ref.shape[0], fc_ref.shape[1] // n_fsdp
    half = shard // 2
    width = proj_ref.shape[1]
    count = own_ref.shape[0]
    copies = [
        pltpu.make_async_copy(src, dst, sem.at[i])
        for i, (src, dst) in enumerate(
            ((wout_ref, wout_hbm), (fc_ref, fc_hbm), (proj_ref, proj_hbm), (attn_ref, attn_hbm))
        )
    ]
    for h in range(2):
        for j in range(n_fsdp):
            cut = min(first_ref.shape[2], half)
            at = slice(j * hidden, (j + 1) * hidden)
            fc_ref[h * half : h * half + cut, at] = first_ref[h, j, :cut].astype(F32)
            if cut < half:
                rows = second_ref[h, j, : half - cut].astype(F32)
                fc_ref[h * half + cut : (h + 1) * half, at] = rows
    copies[1].start()
    for h in range(2):
        proj_ref[h * half : (h + 1) * half] = third_ref[h, :half].astype(F32)
    copies[2].start()
    for h in range(width // hd):
        src = own_ref.at[h] if h < count else rest_ref.at[h - count]
        for part in range(3):
            at = part * width + h * hd
            attn_ref[:, at : at + hd] = src[:, part * hd : (part + 1) * hd].astype(F32)
    copies[3].start()
    load.wait()
    wout_ref[...] = low_ref[...].astype(F32)
    copies[0].start()
    for copy in copies:
        copy.wait()


def assemble(n_fsdp, own, rest, first, second, third, out_low, hidden):
    shard = own.shape[1]
    width = first.shape[3]
    vm = pl.BlockSpec(memory_space=pltpu.VMEM)
    anym = pl.BlockSpec(memory_space=pl.ANY)
    shapes = [(shard, 3 * width), (shard, n_fsdp * hidden), (shard, width), out_low.shape]
    return pl.pallas_call(
        functools.partial(assemble_kernel, n_fsdp),
        in_specs=[vm] * 5 + [anym],
        out_specs=[anym] * 4,
        out_shape=[jax.ShapeDtypeStruct(shape, F32) for shape in shapes],
        scratch_shapes=[pltpu.VMEM(shape, F32) for shape in shapes]
        + [pltpu.VMEM(out_low.shape, BF16), pltpu.SemaphoreType.DMA((5,))],
        compiler_params=pltpu.CompilerParams(vmem_limit_bytes=60 * 1024 * 1024),
        cost_estimate=SHORT,
        name="assemble",
    )(own, rest, first, second, third, out_low)


def swap(value, axis, size, k):
    return lax.ppermute(value, axis, [(i, i ^ k) for i in range(size)])


def shards(
    n_ctx,
    n_fsdp,
    tokens,
    block_order,
    w_attn,
    w_proj,
    w_fc,
    w_out,
    norm_gains,
    biases,
    fc_bias,
    cotangent,
):
    hd = HEAD_DIM
    count, width = tokens.shape[1:]
    shard = width // n_fsdp
    heads = width // hd
    base = heads // n_ctx
    rest = heads - base * n_ctx
    slots = base + rest
    own_blocks = count // BLOCK
    c = lax.axis_index("ctx")
    f = lax.axis_index("fsdp")

    order = block_order[0]
    inv = jnp.argsort(order).astype(jnp.int32)
    order_own = jnp.concatenate([order, (c * own_blocks)[None]])

    def head_cols(h):
        return jnp.concatenate(
            [
                lax.dynamic_slice(w_attn, (0, part * width + h * hd), (shard, hd))
                for part in range(3)
            ],
            axis=1,
        )

    slot_heads = [c * base + s for s in range(base)] + [n_ctx * base + r for r in range(rest)]
    w_slots = jnp.stack([head_cols(h) for h in slot_heads])
    small = jnp.concatenate([norm_gains, biases], axis=0).astype(F32)
    hidden_cols = w_fc.shape[1] // n_fsdp
    normed_one, qkv, full_proj, fc_cols, _, w_slots, small = start_call(
        n_ctx, n_fsdp, base, tokens[0], w_slots, small, w_proj, w_fc, 3
    )
    full_proj = full_proj.reshape(width, width)
    qkv = qkv.reshape(slots, n_ctx * own_blocks, BLOCK, 3 * hd)
    gains, shifts = small[:2], small[2:]
    cot = cotangent[0]

    cot_late, _ = lax.optimization_barrier((cot, small))
    cot_all = lax.all_gather(cot_late, "fsdp", axis=0)

    out_own, lse_own = attn_fwd(inv, qkv, base)
    if rest:
        out_rest, lse_rest = rest_fwd(order_own, qkv, base)
    else:
        out_rest = out_own
    attended, mid, normed_two = mix_call(
        n_ctx, out_own, out_rest, tokens[0], full_proj, small, 6
    )
    fc_cols = fc_cols.reshape(width, hidden_cols)
    rows = tokens[0].astype(F32)

    normed_two_grad, fc_bias_part, out_part, w_out_part, w_fc_part = ffn(
        n_fsdp,
        normed_two,
        cot_all,
        fc_cols,
        w_out,
        fc_bias.astype(F32)[None],
    )
    w_out_sum = lax.psum_scatter(w_out_part, "ctx", scatter_dimension=0, tiled=True)

    half, high = shard // 2, half_high(shard)
    core = c % 2
    main = n_ctx * base * hd
    mid_grad, mid_low, turn_sums, d_rest, fc_mine, d_out = turn_call(
        n_ctx, base, normed_two_grad, cot, mid, full_proj, small, w_fc_part, 7
    )

    d_own = attn_bwd(inv, qkv, d_out, out_own, lse_own, base)
    d_own = d_own.reshape(base, n_ctx, count, 3 * hd)
    if rest:
        d_rest = rest_bwd(order_own, qkv, d_rest, out_rest, lse_rest, base)
        d_rest = d_rest.reshape(rest, n_ctx, count, 3 * hd)
        sums = jnp.concatenate(
            [jnp.sum(d.astype(F32), axis=(1, 2)) for d in (d_own, d_rest)], axis=0
        )
    else:
        d_rest = d_own
        sums = jnp.sum(d_own.astype(F32), axis=(1, 2))
    if back_fits(n_ctx, n_fsdp, count, width, slots):
        normed_one_grad, cols_sum, fc_rows = back_call(
            n_ctx, n_fsdp, d_own, d_rest, w_slots, normed_one, fc_mine, 4
        )
        normed_one_grad = normed_one_grad.astype(F32)
    else:
        dqkv = jnp.concatenate([d_own, d_rest])[:slots].reshape(slots, n_ctx * count, 3 * hd)
        one_part = jnp.einsum("hte,hde->td", dqkv, w_slots, preferred_element_type=F32)
        normed_one_grad = lax.psum_scatter(
            one_part.astype(BF16), "ctx", scatter_dimension=0, tiled=True
        ).astype(F32)
        slot_part = jnp.einsum(
            "td,hte->hde",
            normed_one.reshape(n_ctx * count, width),
            dqkv,
            preferred_element_type=F32,
        ).astype(BF16)
        cols_sum = lax.psum_scatter(slot_part, "fsdp", scatter_dimension=1, tiled=True)
        fc_rows = lax.all_to_all(fc_mine, "fsdp", split_axis=0, concat_axis=0, tiled=True)

    w_out_sum, fc_rows = lax.optimization_barrier((w_out_sum, fc_rows))
    w_out_low = lax.all_gather(w_out_sum, "ctx", axis=0, tiled=True)
    xhat_one, rstd_one = norm_parts(rows)
    tokens_grad = (mid_grad + norm_back(xhat_one, rstd_one, gains[0], normed_one_grad)).astype(
        BF16
    )

    def placed(part):
        cols = sums[:, part * hd : (part + 1) * hd]
        line = lax.dynamic_update_slice_in_dim(
            jnp.zeros((width,), F32), cols[:base].reshape(-1), c * base * hd, 0
        )
        return line + jnp.pad(cols[base:].reshape(-1), (main, 0))

    lines = jnp.stack(
        [
            jnp.sum(normed_one_grad * xhat_one, axis=0),
            turn_sums[0],
            jnp.sum(normed_one_grad, axis=0),
            turn_sums[1],
            placed(0),
            placed(2),
            turn_sums[2],
            turn_sums[3],
        ]
    )
    lead = lines.shape[0]
    tail = jnp.pad(fc_bias_part, ((0, 7), (0, width - hidden_cols)))
    lines = jnp.concatenate([lines, tail])

    chips = n_ctx // 2
    fc_rows = fc_rows.reshape(-1, width)
    per_chip = -(-fc_rows.shape[0] // (16 * chips)) * 16
    fc_rows = jnp.pad(fc_rows, ((0, per_chip * chips - fc_rows.shape[0]), (0, 0)))
    fc_rows = fc_rows.reshape(chips, per_chip, width)
    extra = jnp.zeros((16, width), BF16)
    if rest:
        extra = lax.dynamic_slice_in_dim(cols_sum[base:], core * half, half, 1)
        if not back_fits(n_ctx, n_fsdp, count, width, slots):
            away = lax.dynamic_slice_in_dim(cols_sum[base:], (1 - core) * half, half, 1)
            extra = extra.astype(F32) + swap(away, "ctx", n_ctx, 1).astype(F32)
        extra = extra.astype(BF16).reshape(-1, width)
        extra_rows = extra.shape[0]
        extra = jnp.pad(extra, ((0, -extra_rows % 16), (0, 0)))
    first, second, own_cols, lines, layer_rows = sums_call(
        n_ctx,
        n_fsdp,
        fc_rows,
        cols_sum[:base],
        extra,
        attended,
        mid_low,
        lines,
        out_part,
        mid,
        small,
        lead,
        5,
    )
    w_out_low, lines = lax.optimization_barrier((w_out_low, lines))
    split = per_chip - first.shape[2]
    third = second[:, :, split:].reshape(2, -1, width)
    second = second[:, :, :split]
    own_cols = own_cols.reshape(n_ctx * base, shard, 3 * hd)
    if rest:
        rest_cols = third[:, high : high + extra_rows].reshape(2, rest, half, 3 * hd)
        rest_cols = rest_cols.transpose(1, 0, 2, 3).reshape(rest, shard, 3 * hd)
    else:
        rest_cols = own_cols
    if hidden_cols == width and chips == n_fsdp:
        w_attn_grad, w_fc_grad, w_proj_grad, w_out_grad = assemble(
            n_fsdp, own_cols, rest_cols, first, second, third, w_out_low, hidden_cols
        )
    else:
        w_fc_low = jnp.concatenate([first, second], axis=2).reshape(2, -1, width)
        w_fc_low = w_fc_low[:, : n_fsdp * high * hidden_cols // width]
        w_fc_low = w_fc_low.reshape(2, n_fsdp, high, hidden_cols)[:, :, :half]
        w_fc_grad = w_fc_low.transpose(0, 2, 1, 3).reshape(shard, n_fsdp * hidden_cols)
        w_fc_grad = w_fc_grad.astype(F32)
        w_proj_grad = third[:, :half].reshape(shard, width).astype(F32)
        cols = jnp.concatenate([own_cols, rest_cols])[: width // hd]
        cols = cols.reshape(width // hd, shard, 3, hd).transpose(1, 2, 0, 3)
        w_attn_grad = cols.reshape(shard, 3 * width).astype(F32)
        w_out_grad = w_out_low.astype(F32)
    fc_bias_grad = lines[lead, :hidden_cols]
    lines = lax.dynamic_slice_in_dim(lines[:lead], f * shard, shard, 1)
    return (
        layer_rows[None],
        tokens_grad[None],
        w_attn_grad,
        w_proj_grad,
        w_fc_grad,
        w_out_grad,
        lines[:2],
        lines[2:],
        fc_bias_grad,
    )


def solution(mesh):
    rows = P("fsdp", "ctx", None)
    weight = P("fsdp", None)
    vectors = P(None, "fsdp")
    return jax.shard_map(
        functools.partial(shards, mesh.shape["ctx"], mesh.shape["fsdp"]),
        mesh=mesh,
        in_specs=(
            rows, weight, weight, weight, weight, weight, vectors, vectors, P("fsdp"), rows,
        ),
        out_specs=(
            rows, rows, weight, weight, weight, weight, vectors, vectors, P("fsdp"),
        ),
        check_vma=False,
    )
```
